32 devices in a mesh: batch: 4 (over y, x), seq: 8 (over z, core).
Axes of the slice: x: 2, y: 2, z: 4, core: 2. Of those that a mesh axis runs over, the one named last changes fastest.
Arguments:
- tokens: bfloat16 [8, 2048, 1280], P('batch', 'seq'), may hold values from -6 to 6
- cotangent: bfloat16 [8, 2048, 1280], P('batch', 'seq'), may hold values from -6 to 6
- weights: float32 [6, 1280, 1280], P(None, ('batch', 'seq'))
- gains: float32 [2, 1280], P(None, ('batch', 'seq'))
- query_scale: float32 [80], replicated, may hold values from 0 to 2
- first_weights: float32 [6, 1280, 1280], P(None, ('batch', 'seq')), may hold values from -0.00048828125 to 0.00048828125
- second_weights: float32 [6, 1280, 1280], P(None, ('batch', 'seq')), may hold values from 5.0848974e-11 to 8.135836e-10
- first_gains: float32 [2, 1280], P(None, ('batch', 'seq')), may hold values from -0.0009765625 to 0.0009765625
- second_gains: float32 [2, 1280], P(None, ('batch', 'seq')), may hold values from 2.033959e-10 to 3.2543344e-09
- first_scale: float32 [80], replicated, may hold values from -0.0078125 to 0.0078125
- second_scale: float32 [80], replicated, may hold values from 1.0169795e-09 to 5.0848974e-09
- lengths: int32 [8], P('batch'), may hold values from 256 to 2048, as said below
Outputs:
- block_out: bfloat16 [8, 2048, 1280], P('batch', 'seq')
- input_grad: float32 [8, 2048, 1280], P('batch', 'seq')
- grad_norm: float32 [], replicated
- new_weights: float32 [6, 1280, 1280], P(None, ('batch', 'seq'))
- new_first_weights: float32 [6, 1280, 1280], P(None, ('batch', 'seq'))
- new_second_weights: float32 [6, 1280, 1280], P(None, ('batch', 'seq'))
- new_gains: float32 [2, 1280], P(None, ('batch', 'seq'))
- new_first_gains: float32 [2, 1280], P(None, ('batch', 'seq'))
- new_second_gains: float32 [2, 1280], P(None, ('batch', 'seq'))
- new_scale: float32 [80], replicated
- new_first_scale: float32 [80], replicated
- new_second_scale: float32 [80], replicated
- rms_stats: float32 [3], replicated
The draws below stay inside these ranges and needn't reach their ends.
Inputs may be any that keep to these rules, and one draw needn't show every extreme that they name: `lengths`: in each run of 2 consecutive series (those of one index of batch) one series, drawn from the seed, has length 2048.
All inputs are finite; a program needn't handle non-finite values.
Results may differ from the reference program's by a relative error of at most 0.014.
The reference program's roundings to bfloat16 on the way count: a program that leaves them out, or rounds other values in their place, can miss the bound.
Values may be sent and summed in bfloat16 or wider, within the bound.
A program may use at most 512 MiB of HBM per device.

```python
import math
import jax
import jax.numpy as jnp
from jax import lax

D = 1280
HD = 80
SER_GRP = 2
STEP = 10
LENGTH = 2048
SERIES = 8
PARAMS = 9833040
N_BATCH = 4


OUT_BOOST = 5.0


def draw_weights(key, part):
    key = jax.random.fold_in(key, 3)
    boosts = jnp.array([1.0, 1.0, 1.0, OUT_BOOST, 1.0, 1.0], jnp.float32)
    drawn = jax.random.normal(key, (6, D, D), jnp.float32)
    return drawn * boosts[:, None, None] * D ** (-0.5)


def draw_gains(key, part):
    key = jax.random.fold_in(key, 5)
    block_rows = D // N_BATCH
    places = jnp.arange(D)
    inner = (places % block_rows).astype(jnp.float32) / block_rows
    outer = (places // block_rows).astype(jnp.float32) / N_BATCH
    rising = 0.55 * jnp.sqrt((1.0 + 2.0 * inner) * (1.0 + 2.0 * outer))
    jitter = 1.0 + 0.08 * jnp.clip(jax.random.normal(key, (2, D), jnp.float32), -2.0, 2.0)
    return rising[None, :] * jitter


def draw_lengths(key, part):
    key = jax.random.fold_in(key, 11)
    first_key, second_key = jax.random.split(key)
    drawn = jax.random.randint(first_key, (SERIES,), LENGTH // 8, LENGTH + 1)
    chosen = jax.random.randint(second_key, (SERIES // SER_GRP,), 0, SER_GRP)
    slots = jnp.arange(SERIES) % SER_GRP
    owners = jnp.repeat(chosen, SER_GRP)
    return jnp.where(slots == owners, LENGTH, drawn).astype(jnp.int32)


def level_of(own_key, shape, pieces, smallest, high):
    gain = 1.0
    for axis_at, parts in pieces:
        heights = jax.random.uniform(jax.random.fold_in(jax.random.fold_in(own_key, 6), axis_at), (parts,), jnp.float32, smallest / len(pieces), high / len(pieces))
        gain = gain * jnp.repeat(jnp.exp(heights), shape[axis_at] // parts).reshape((-1,) + (1,) * (len(shape) - 1 - axis_at))
    return gain


def centred(stream_key, dims, deviation, limit, shards=(), kind=jnp.bfloat16):
    loudness = level_of(stream_key, dims, shards, -0.22, 0.18) if shards else 1.0
    values = jax.random.normal(stream_key, dims, jnp.float32) * deviation * loudness
    return jnp.minimum(jnp.maximum(values, -limit), limit).astype(kind)


def setup_inputs(seed: int = 0) -> dict:
    arg_keys = jax.random.split(jax.random.key(seed), 13)
    tokens = centred(arg_keys[0], (SERIES, LENGTH, D), 1.0, 6.0, ((0, 4), (1, 8)))
    cotangent = centred(arg_keys[1], (SERIES, LENGTH, D), 1.0, 6.0, ((0, 4), (1, 8)))
    weights = draw_weights(jax.random.fold_in(arg_keys[12], 71), 0)
    gains = draw_gains(jax.random.fold_in(arg_keys[12], 71), 0)
    query_scale = jnp.clip(jax.random.uniform(arg_keys[4], (HD,), jnp.float32, 0.0, 2.0), 0.0, 2.0)
    first_weights = centred(arg_keys[5], (6, D, D), (0.111 * PARAMS ** -0.5), 0.00048828125, ((1, 32),), jnp.float32)
    second_weights = jnp.clip(jnp.exp(math.log(8.135835893874344e-10) - 2.7725887 * jax.random.uniform(arg_keys[6], (6, D, D), jnp.float32) ** level_of(arg_keys[6], (6, D, D), ((1, 32),), -0.2, 0.2)), 5.084897433671465e-11, 8.135835893874344e-10)
    first_gains = centred(arg_keys[7], (2, D), (0.222 * PARAMS ** -0.5), 0.0009765625, ((1, 32),), jnp.float32)
    second_gains = jnp.clip(jnp.exp(math.log(3.2543343575497374e-09) - 2.7725887 * jax.random.uniform(arg_keys[8], (2, D), jnp.float32) ** level_of(arg_keys[8], (2, D), ((1, 32),), -0.2, 0.2)), 2.033958973468586e-10, 3.2543343575497374e-09)
    first_scale = centred(arg_keys[9], (HD,), (1.8 * PARAMS ** -0.5), 0.0078125, (), jnp.float32)
    second_scale = jnp.clip(jnp.exp(jax.random.uniform(arg_keys[10], (HD,), jnp.float32, math.log(1.0169795006120808e-09), math.log(5.084897392038101e-09))), 1.0169795006120808e-09, 5.084897392038101e-09)
    lengths = draw_lengths(jax.random.fold_in(arg_keys[12], 71), 0)
    return {"tokens": tokens, "cotangent": cotangent, "weights": weights, "gains": gains, "query_scale": query_scale, "first_weights": first_weights, "second_weights": second_weights, "first_gains": first_gains, "second_gains": second_gains, "first_scale": first_scale, "second_scale": second_scale, "lengths": lengths}


NORM_EPS = 1e-06
LOG_TWO_E = 1.442695
BETA_FIRST = 0.9
BETA_SECOND = 0.999
ADAM_EPS = 1e-08
MATRIX_RATE = 0.05
GAIN_RATE = 0.5
MATRIX_DECAY = 0.1
CLIP_NORM = 1.0
MASKED = -1e+30

@jax.custom_vjp
def low(v):
    return lax.optimization_barrier(v.astype(jnp.bfloat16)).astype(jnp.float32)

@jax.custom_vjp
def low_back(v):
    return v

def low_keep(v):
    return (low(v), None)

def low_pass(kept, grad):
    return (grad,)

def back_keep(v):
    return (v, None)

def back_low(kept, grad):
    return (low(grad),)
low.defvjp(low_keep, low_pass)
low_back.defvjp(back_keep, back_low)

def matmul(left, right):
    return jnp.dot(left, right, precision=lax.Precision.HIGHEST)

def rms_normed(values):
    return values * lax.rsqrt(lax.optimization_barrier(jnp.mean(values * values, axis=-1, keepdims=True)) + NORM_EPS)

def attend_block(bundle, keys_heads, values_heads, length):
    rows_q, query_pos = bundle
    scores = jnp.einsum('qhd,khd->hqk', rows_q, keys_heads, precision=lax.Precision.HIGHEST)
    scores = low_back(scores)
    key_pos = jnp.arange(keys_heads.shape[0])
    visible = (key_pos[None, :] <= query_pos[:, None]) & (key_pos[None, :] < length)
    scores = jnp.where(visible[None], scores, MASKED)
    log_total = jax.nn.logsumexp(scores, axis=-1, keepdims=True)
    attn_probs = low(jnp.exp(scores - log_total))
    return jnp.einsum('hqk,khd->qhd', attn_probs, values_heads, precision=lax.Precision.HIGHEST)

def series_forward(weights, gains, query_scale, inputs, length):
    low_weights = low(weights)
    low_gains = low(gains)
    seq_len, model_width = inputs.shape
    head_size = query_scale.shape[0]
    head_count = model_width // head_size
    normed_one = rms_normed(inputs)
    normed_in = low(normed_one * low_gains[0])
    query_full = low_back(matmul(normed_in, low_weights[0]))
    keys_full = low(low_back(matmul(normed_in, low_weights[1])))
    values_full = low(low_back(matmul(normed_in, low_weights[2])))
    coef_row = jnp.tile(LOG_TWO_E / math.sqrt(head_size) * jax.nn.softplus(query_scale), head_count)
    scaled = low(low_back(query_full * coef_row))
    block_rows = math.gcd(seq_len, 512)
    block_count = seq_len // block_rows
    query_blocks = scaled.reshape(block_count, block_rows, head_count, head_size)
    pos_blocks = jnp.arange(seq_len).reshape(block_count, block_rows)
    keys_heads = keys_full.reshape(seq_len, head_count, head_size)
    values_heads = values_full.reshape(seq_len, head_count, head_size)

    def one_block(bundle):
        return attend_block(bundle, keys_heads, values_heads, length)
    attended = lax.map(jax.checkpoint(one_block), (query_blocks, pos_blocks))
    attended = low(low_back(attended.reshape(seq_len, model_width)))
    branch_one = low_back(matmul(attended, low_weights[3]))
    middle = inputs + branch_one
    normed_two = rms_normed(middle)
    hidden_in = low(normed_two * low_gains[1])
    pre_act = low_back(matmul(hidden_in, low_weights[4]))
    activated = low(jax.nn.silu(pre_act))
    branch_two = low_back(matmul(activated, low_weights[5]))
    block_out = middle + branch_two
    stats = jnp.stack([jnp.sum(branch_one * branch_one), jnp.sum(branch_two * branch_two), jnp.sum(block_out * block_out)])
    return (block_out, stats)

def adam_update(current, gradient, moment_one, moment_two, step_rate, decay_rate):
    new_one = BETA_FIRST * moment_one + (1.0 - BETA_FIRST) * gradient
    new_two = BETA_SECOND * moment_two + (1.0 - BETA_SECOND) * gradient * gradient
    first_hat = new_one / (1.0 - BETA_FIRST ** STEP)
    second_hat = new_two / (1.0 - BETA_SECOND ** STEP)
    updated = current - step_rate * (first_hat / (jnp.sqrt(second_hat) + ADAM_EPS) + decay_rate * current)
    return (updated, new_one, new_two)

def reference(tokens, cotangent, weights, gains, query_scale, first_weights, second_weights, first_gains, second_gains, first_scale, second_scale, lengths):
    model_width = tokens.shape[-1]

    def step_series(carry, bundle):
        grad_weights, grad_gains, grad_scale, stat_sum = carry
        inputs, grad_out, length = bundle

        def forward(weight_in, gain_in, scale_in, input_in):
            return series_forward(weight_in, gain_in, scale_in, input_in, length)
        outputs, pullback, stats = jax.vjp(forward, weights, gains, query_scale, inputs.astype(jnp.float32), has_aux=True)
        part_weights, part_gains, part_scale, part_input = pullback(grad_out.astype(jnp.float32))
        carry_out = (grad_weights + part_weights, grad_gains + part_gains, grad_scale + part_scale, stat_sum + stats)
        return (carry_out, (outputs.astype(jnp.bfloat16), part_input))
    start = (jnp.zeros(weights.shape, jnp.float32), jnp.zeros(gains.shape, jnp.float32), jnp.zeros(query_scale.shape, jnp.float32), jnp.zeros((3,), jnp.float32))
    totals, stacked = lax.scan(step_series, start, (tokens, cotangent, lengths))
    grad_weights, grad_gains, grad_scale, stat_sum = totals
    block_out, input_grad = stacked
    grad_norm = jnp.sqrt(jnp.sum(grad_weights * grad_weights) + jnp.sum(grad_gains * grad_gains) + jnp.sum(grad_scale * grad_scale))
    clip_factor = CLIP_NORM / jnp.maximum(grad_norm, CLIP_NORM)
    new_weights, new_first_weights, new_second_weights = adam_update(weights, grad_weights * clip_factor, first_weights, second_weights, MATRIX_RATE, MATRIX_DECAY)
    new_gains, new_first_gains, new_second_gains = adam_update(gains, grad_gains * clip_factor, first_gains, second_gains, GAIN_RATE, 0.0)
    new_scale, new_first_scale, new_second_scale = adam_update(query_scale, grad_scale * clip_factor, first_scale, second_scale, GAIN_RATE, 0.0)
    rms_stats = jnp.sqrt(stat_sum / (tokens.shape[0] * tokens.shape[1] * model_width))
    return (block_out, input_grad, grad_norm, new_weights, new_first_weights, new_second_weights, new_gains, new_first_gains, new_second_gains, new_scale, new_first_scale, new_second_scale, rms_stats)
```

```python
import functools
import math

import jax
import jax.numpy as jnp
from jax import lax
from jax.experimental import pallas as pl
from jax.experimental.pallas import tpu as pltpu
from jax.sharding import PartitionSpec as P

STEP = 10

NORM_EPS = 1e-06
LOG_TWO_E = 1.442695
BETA_FIRST = 0.9
BETA_SECOND = 0.999
ADAM_EPS = 1e-08
MATRIX_RATE = 0.05
GAIN_RATE = 0.5
MATRIX_DECAY = 0.1
CLIP_NORM = 1.0
MASKED = -1e30

MESH = pl.DeviceIdType.MESH
LANES = 128
F32 = jnp.float32
LOW = jnp.bfloat16
MIB = 1024 * 1024


def rms_factor(values):
    return lax.rsqrt(jnp.mean(values * values, axis=-1, keepdims=True) + NORM_EPS)


def norm_back(grad_normed, normed, factor):
    return factor * (grad_normed - normed * jnp.mean(grad_normed * normed, axis=-1, keepdims=True))


def silu_slope(values):
    logistic = jax.nn.sigmoid(values)
    return logistic * (1.0 + values * (1.0 - logistic))


def adam_update(current, gradient, moment_one, moment_two, step_rate, decay_rate):
    new_one = BETA_FIRST * moment_one + (1.0 - BETA_FIRST) * gradient
    new_two = BETA_SECOND * moment_two + (1.0 - BETA_SECOND) * gradient * gradient
    first_hat = new_one / (1.0 - BETA_FIRST**STEP)
    second_hat = new_two / (1.0 - BETA_SECOND**STEP)
    updated = current - step_rate * (
        first_hat / (jnp.sqrt(second_hat) + ADAM_EPS) + decay_rate * current
    )
    return (updated, new_one, new_two)


def dot(left, right, left_axis=1, right_axis=0):
    return lax.dot_general(
        left, right, (((left_axis,), (right_axis,)), ((), ())), preferred_element_type=F32
    )


def greet(seq_count, batch_count):
    barrier = pltpu.get_barrier_semaphore()
    me_seq, me_batch = lax.axis_index("seq"), lax.axis_index("batch")
    for k in range(1, seq_count):
        pl.semaphore_signal(
            barrier,
            inc=1,
            device_id={"seq": lax.rem(me_seq + k, seq_count)},
            device_id_type=MESH,
        )
    for k in range(1, batch_count):
        pl.semaphore_signal(
            barrier,
            inc=1,
            device_id={"batch": lax.rem(me_batch + k, batch_count)},
            device_id_type=MESH,
        )
    pl.semaphore_wait(barrier, seq_count - 1 + batch_count - 1)


def push(source, target, send_sem, recv_sem, **where):
    return pltpu.make_async_remote_copy(
        source, target, send_sem, recv_sem, device_id=where, device_id_type=MESH
    )


def place(seq_count):
    me = lax.axis_index("seq")
    chips = seq_count // 2
    half_chips = chips // 2
    core = lax.rem(me, 2)
    chip = me // 2
    half = chip // half_chips
    base = half * half_chips
    gate_mine = half_chips - 1 + half
    gate_other = half_chips - half
    return me, core, chip, half, base, gate_mine, gate_other


def far_chip(step, half, half_chips):
    return (1 - half) * (half_chips + step) + half * (half_chips - 1 - step)


def gather_kernel(
    n, nb, chunks, tok, slab, xg, wout, far_sem, own_sem, pass_sem, sib_sem, same_recv, sib_recv,
    z_send, z_recv, b_send, b_recv, local_sem,
):
    chips, half_chips = n // 2, n // 4
    me, core, chip, half, base, gate_mine, gate_other = place(n)
    group_count = n // 2
    batch = lax.axis_index("batch")
    rows = tok.shape[1] // chunks
    sibling = 2 * chip + 1 - core
    greet(n, nb)

    z_copies = []
    for k in range(1, n):
        target = lax.rem(me + k, n)
        copy = push(
            slab.at[lax.rem(target, group_count)], wout.at[batch, me], z_send.at[k],
            z_recv.at[k], seq=target,
        )
        copy.start()
        z_copies.append(copy)

    def part(ref, lead, c):
        return ref.at[lead, pl.ds(c * rows, rows)]

    def tok_copy(source, slot, c, send_sem, recv_sem, target):
        return push(source, part(xg, slot, c), send_sem, recv_sem.at[slot, c], seq=target)

    sends = []
    for c in range(chunks):
        copy = tok_copy(
            part(tok, 1 - half, c), me, c, far_sem.at[c], same_recv, 2 * gate_other + core
        )
        copy.start()
        sends.append(copy)
        for k in range(1, half_chips):
            other = base + lax.rem(chip - base + k, half_chips)
            copy = tok_copy(
                part(tok, half, c), me, c, own_sem.at[k, c], same_recv, 2 * other + core
            )
            copy.start()
            sends.append(copy)
        copy = tok_copy(part(tok, half, c), me, c, sib_sem.at[0, c], sib_recv, sibling)
        copy.start()
        sends.append(copy)
    own_copy = pltpu.make_async_copy(tok.at[half], xg.at[me], local_sem.at[0])
    own_copy.start()
    slab_copy = pltpu.make_async_copy(
        slab.at[lax.rem(me, group_count)], wout.at[batch, me], local_sem.at[1]
    )
    slab_copy.start()
    slab_copy.wait()

    b_copies = []

    def spread(source, index):
        for j in range(1, nb):
            copy = push(
                wout.at[batch, source], wout.at[batch, source], b_send.at[j, index],
                b_recv.at[j, index], batch=lax.rem(batch + j, nb),
            )
            copy.start()
            b_copies.append(copy)

    spread(me, 0)
    for k in range(1, n):
        z_copies[k - 1].wait_recv()
        spread(lax.rem(me + n - k, n), k)

    for c in range(chunks):
        for k in range(1, half_chips):
            slot = 2 * (base + lax.rem(chip - base + half_chips - k, half_chips)) + core
            arrived = tok_copy(part(xg, slot, c), slot, c, sib_sem.at[k, c], same_recv, sibling)
            arrived.wait_recv()
            copy = tok_copy(part(xg, slot, c), slot, c, sib_sem.at[k, c], sib_recv, sibling)
            copy.start()
            sends.append(copy)
        for k in range(half_chips):
            slot = 2 * far_chip(k, half, half_chips) + core
            lane = half_chips + k
            tok_copy(part(xg, slot, c), slot, c, sib_sem.at[lane, c], same_recv, sibling).wait_recv()

            @pl.when(chip == gate_mine)
            def _():
                for j in range(1, half_chips):
                    other = base + lax.rem(chip - base + j, half_chips)
                    tok_copy(
                        part(xg, slot, c), slot, c, pass_sem.at[k, j, c], same_recv,
                        2 * other + core,
                    ).start()

            copy = tok_copy(part(xg, slot, c), slot, c, sib_sem.at[lane, c], sib_recv, sibling)
            copy.start()
            sends.append(copy)

    for c in range(chunks):
        for q in range(chips):
            slot = 2 * q + 1 - core
            tok_copy(part(xg, slot, c), slot, c, sib_sem.at[0, c], sib_recv, sibling).wait_recv()
    own_copy.wait()
    for copy in b_copies:
        copy.wait_recv()
    for copy in sends + b_copies + z_copies:
        copy.wait_send()

    @pl.when(chip == gate_mine)
    def _():
        for c in range(chunks):
            for k in range(half_chips):
                for j in range(1, half_chips):
                    tok_copy(
                        part(xg, me, c), me, c, pass_sem.at[k, j, c], same_recv, sibling
                    ).wait_send()


def gather_tokens(n, nb, tokens, slab):
    chunks = 4
    chips, half_chips = n // 2, n // 4
    dma = pltpu.SemaphoreType.DMA
    return pl.pallas_call(
        functools.partial(gather_kernel, n, nb, chunks),
        out_shape=(
            jax.ShapeDtypeStruct((n,) + tokens.shape[1:], tokens.dtype),
            jax.ShapeDtypeStruct((nb, n) + slab.shape[1:], slab.dtype),
        ),
        in_specs=[pl.BlockSpec(memory_space=pl.ANY)] * 2,
        out_specs=[pl.BlockSpec(memory_space=pl.ANY)] * 2,
        scratch_shapes=[
            dma((chunks,)),
            dma((half_chips, chunks)),
            dma((half_chips, half_chips, chunks)),
            dma((chips, chunks)),
            dma((n, chunks)),
            dma((n, chunks)),
            dma((n,)),
            dma((n,)),
            dma((nb, n)),
            dma((nb, n)),
            dma((2,)),
        ],
        compiler_params=pltpu.CompilerParams(collective_id=1, has_side_effects=True),
        name="gather_tokens",
    )(tokens, slab)


def swap_kernel(n, source, target, send_sem, recv_sem, local_sem):
    me = lax.axis_index("seq")
    greet(n, 1)
    copies = []
    for k in range(1, n):
        other = lax.rem(me + k, n)
        copy = push(source.at[other], target.at[me], send_sem.at[k], recv_sem.at[k], seq=other)
        copy.start()
        copies.append(copy)
    own = pltpu.make_async_copy(source.at[me], target.at[me], local_sem)
    own.start()
    own.wait()
    for copy in copies:
        copy.wait()


def swap_blocks(n, blocks, collective_id):
    return pl.pallas_call(
        functools.partial(swap_kernel, n),
        out_shape=jax.ShapeDtypeStruct(blocks.shape, blocks.dtype),
        in_specs=[pl.BlockSpec(memory_space=pl.ANY)],
        out_specs=pl.BlockSpec(memory_space=pl.ANY),
        scratch_shapes=[
            pltpu.SemaphoreType.DMA((n,)),
            pltpu.SemaphoreType.DMA((n,)),
            pltpu.SemaphoreType.DMA,
        ],
        compiler_params=pltpu.CompilerParams(collective_id=collective_id, has_side_effects=True),
        name="swap_blocks",
    )(blocks)


def widen(values):
    rows, width = values.shape
    return jnp.concatenate([values, jnp.zeros((rows, LANES - width), values.dtype)], axis=1)


def project_kernel(heads, size, x_ref, w_ref, gain_ref, coef_ref, h_ref, qkv_ref, q_ref):
    x = x_ref[0].astype(F32)
    normed = x * rms_factor(x)
    h = (normed * gain_ref[...]).astype(LOW)
    h_ref[0] = h
    out = dot(h, w_ref[...])
    for a in range(heads):
        q = widen(out[:, a * size : (a + 1) * size])
        q_ref[a] = q
        qkv_ref[a] = (q * coef_ref[...]).astype(LOW)
    for a in range(heads, 3 * heads):
        qkv_ref[a] = widen(out[:, a * size : (a + 1) * size].astype(LOW))


def project(heads, size, xg, weights, gain, coef):
    n, rows, width = xg.shape
    return pl.pallas_call(
        functools.partial(project_kernel, heads, size),
        grid=(n,),
        out_shape=(
            jax.ShapeDtypeStruct(xg.shape, LOW),
            jax.ShapeDtypeStruct((3 * heads, n * rows, LANES), LOW),
            jax.ShapeDtypeStruct((heads, n * rows, LANES), F32),
        ),
        in_specs=[
            pl.BlockSpec((1, rows, width), lambda i: (i, 0, 0)),
            pl.BlockSpec(weights.shape, lambda i: (0, 0)),
            pl.BlockSpec(gain.shape, lambda i: (0, 0)),
            pl.BlockSpec(coef.shape, lambda i: (0, 0)),
        ],
        out_specs=[
            pl.BlockSpec((1, rows, width), lambda i: (i, 0, 0)),
            pl.BlockSpec((3 * heads, rows, LANES), lambda i: (0, i, 0)),
            pl.BlockSpec((heads, rows, LANES), lambda i: (0, i, 0)),
        ],
        compiler_params=pltpu.CompilerParams(vmem_limit_bytes=48 * MIB),
        name="project",
    )(xg, weights, gain, coef)


def attend_kernel(
    heads, size, fold, len_ref, q_ref, k_ref, v_ref, o_ref, keep_ref, lse_ref, s_ref, m_ref, acc_ref,
    sum_ref,
):
    i = pl.program_id(0)
    block = q_ref.shape[1]
    length = len_ref[0]
    whole = jnp.minimum(i, length // block)
    total = jnp.minimum(i + 1, pl.cdiv(length, block))
    m_ref[...] = jnp.full_like(m_ref, MASKED)
    sum_ref[...] = jnp.zeros_like(sum_ref)
    acc_ref[...] = jnp.zeros_like(acc_ref)

    def score(j, masked):
        keys = pl.ds(pl.multiple_of(j * block, block), block)
        if masked:
            row = i * block + lax.broadcasted_iota(jnp.int32, (block, block), 0)
            col = j * block + lax.broadcasted_iota(jnp.int32, (block, block), 1)
            visible = (col <= row) & (col < length)
        for a in range(heads):
            s = dot(q_ref[a], k_ref[a, keys], 1, 1)
            if masked:
                s = jnp.where(visible, s, MASKED)
            s_ref[a, j] = s
            best = m_ref[a]
            for part in range(block // LANES):
                best = jnp.maximum(best, s[:, part * LANES : (part + 1) * LANES])
            m_ref[a] = best

    pl.loop(0, whole)(lambda j: score(j, False))
    pl.loop(whole, total)(lambda j: score(j, True))
    for a in range(heads):
        m_ref[a] = jnp.broadcast_to(jnp.max(m_ref[a], axis=1, keepdims=True), (block, LANES))

    @pl.loop(0, total)
    def _(j):
        keys = pl.ds(pl.multiple_of(j * block, block), block)
        for a in range(heads):
            best = m_ref[a]
            count = sum_ref[a]
            pieces = []
            for part in range(block // LANES):
                e = jnp.exp(s_ref[a, j, :, part * LANES : (part + 1) * LANES] - best)
                count = count + e
                pieces.append(e.astype(LOW))
            sum_ref[a] = count
            acc_ref[a] += dot(jnp.concatenate(pieces, axis=1), v_ref[a, keys])

    outs = []
    for a in range(heads):
        count = jnp.sum(sum_ref[a], axis=1, keepdims=True)
        out = acc_ref[a] / count
        keep_ref[a] = out
        outs.append(out[:, :size])
        lse = m_ref[a] + jnp.log(count)
        lse_ref[a] = lse.T[:8]
    low = jnp.concatenate(outs, axis=1).astype(LOW)
    piece = block // fold
    o_ref[0] = jnp.concatenate([low[f * piece : (f + 1) * piece] for f in range(fold)], axis=1)


def attend(heads, size, fold, length, qkv, n):
    full = qkv.shape[1]
    block = full // n
    width = heads * size * fold
    return pl.pallas_call(
        functools.partial(attend_kernel, heads, size, fold),
        grid=(n,),
        out_shape=(
            jax.ShapeDtypeStruct((n, block // fold, width), LOW),
            jax.ShapeDtypeStruct((heads, full, LANES), F32),
            jax.ShapeDtypeStruct((heads, 8, full), F32),
        ),
        in_specs=[
            pl.BlockSpec(memory_space=pltpu.SMEM),
            pl.BlockSpec((heads, block, LANES), lambda i: (0, i, 0)),
            pl.BlockSpec((heads, full, LANES), lambda i: (1, 0, 0)),
            pl.BlockSpec((heads, full, LANES), lambda i: (2, 0, 0)),
        ],
        out_specs=[
            pl.BlockSpec((1, block // fold, width), lambda i: (i, 0, 0)),
            pl.BlockSpec((heads, block, LANES), lambda i: (0, i, 0)),
            pl.BlockSpec((heads, 8, block), lambda i: (0, 0, i)),
        ],
        scratch_shapes=[
            pltpu.VMEM((heads, n, block, block), F32),
            pltpu.VMEM((heads, block, LANES), F32),
            pltpu.VMEM((heads, block, LANES), F32),
            pltpu.VMEM((heads, block, LANES), F32),
        ],
        compiler_params=pltpu.CompilerParams(vmem_limit_bytes=48 * MIB),
        name="attend",
    )(length, qkv, qkv, qkv)


def attend_back_kernel(
    heads, size, fold, n, len_ref, coef_ref, q_ref, k_ref, v_ref, go_ref, keep_ref, lse_ref, qf_ref,
    out_ref, scale_ref, kt_ref, gq_ref, gqt_ref, gk_ref, gv_ref, g_ref, delta_ref,
):
    i = pl.program_id(0)
    block = q_ref.shape[1]
    length = len_ref[0]
    whole = jnp.minimum(i, length // block)
    total = jnp.minimum(i + 1, pl.cdiv(length, block))

    @pl.when(i == 0)
    def _():
        gk_ref[...] = jnp.zeros_like(gk_ref)
        gv_ref[...] = jnp.zeros_like(gv_ref)
        scale_ref[...] = jnp.zeros_like(scale_ref)

        @pl.loop(0, n)
        def _(j):
            keys = pl.ds(pl.multiple_of(j * block, block), block)
            for a in range(heads):
                kt_ref[a, j] = k_ref[a, keys].T

    gqt_ref[...] = jnp.zeros_like(gqt_ref)
    for a in range(heads):
        g = widen(
            jnp.concatenate(
                [
                    go_ref[0, :, (f * heads + a) * size : (f * heads + a + 1) * size]
                    for f in range(fold)
                ],
                axis=0,
            )
        )
        g_ref[a] = g
        delta_ref[a] = jnp.broadcast_to(
            jnp.sum((g.astype(F32) * keep_ref[a]).T, axis=0, keepdims=True), (8, block)
        )

    def back(j, masked):
        keys = pl.ds(pl.multiple_of(j * block, block), block)
        if masked:
            col = j * block + lax.broadcasted_iota(jnp.int32, (block, block), 0)
            row = i * block + lax.broadcasted_iota(jnp.int32, (block, block), 1)
            visible = (col <= row) & (col < length)
        for a in range(heads):
            s = dot(k_ref[a, keys], q_ref[a], 1, 1)
            p = jnp.exp(s - lse_ref[a, :1])
            if masked:
                p = jnp.where(visible, p, 0.0)
            dp = dot(v_ref[a, keys], g_ref[a], 1, 1)
            ds = (p * (dp - delta_ref[a, :1])).astype(LOW)
            gk_ref[a, keys] += dot(ds, q_ref[a])
            gv_ref[a, keys] += dot(p.astype(LOW), g_ref[a])
            gqt_ref[a] += dot(kt_ref[a, j], ds)

    pl.loop(0, whole)(lambda j: back(j, False))
    pl.loop(whole, total)(lambda j: back(j, True))

    rows = pl.ds(pl.multiple_of(i * block, block), block)
    for a in range(heads):
        grad = gqt_ref[a].T.astype(LOW).astype(F32)
        scale_ref[...] += jnp.sum((grad * qf_ref[a]).reshape(block // 8, 8, LANES), axis=0)
        gq_ref[a, rows] = (grad * coef_ref[...]).astype(LOW)

    @pl.when(i == n - 1)
    def _():
        @pl.loop(0, n)
        def _(j):
            keys = pl.ds(pl.multiple_of(j * block, block), block)
            pieces = [gq_ref[a, keys][:, :size] for a in range(heads)]
            pieces += [gk_ref[a, keys][:, :size].astype(LOW) for a in range(heads)]
            pieces += [gv_ref[a, keys][:, :size].astype(LOW) for a in range(heads)]
            spare = out_ref.shape[2] - 3 * heads * size
            pieces.append(jnp.zeros((block, spare), LOW))
            out_ref[j] = jnp.concatenate(pieces, axis=1)


def attend_back(heads, size, fold, length, coef, qkv, go, keep, lse, q_full, n, slab_width):
    full = qkv.shape[1]
    block = full // n
    width = heads * size * fold
    return pl.pallas_call(
        functools.partial(attend_back_kernel, heads, size, fold, n),
        grid=(n,),
        out_shape=(
            jax.ShapeDtypeStruct((n, block, slab_width), LOW),
            jax.ShapeDtypeStruct((8, LANES), F32),
        ),
        in_specs=[
            pl.BlockSpec(memory_space=pltpu.SMEM),
            pl.BlockSpec(coef.shape, lambda i: (0, 0)),
            pl.BlockSpec((heads, block, LANES), lambda i: (0, i, 0)),
            pl.BlockSpec((heads, full, LANES), lambda i: (1, 0, 0)),
            pl.BlockSpec((heads, full, LANES), lambda i: (2, 0, 0)),
            pl.BlockSpec((1, block // fold, width), lambda i: (i, 0, 0)),
            pl.BlockSpec((heads, block, LANES), lambda i: (0, i, 0)),
            pl.BlockSpec((heads, 8, block), lambda i: (0, 0, i)),
            pl.BlockSpec((heads, block, LANES), lambda i: (0, i, 0)),
        ],
        out_specs=[
            pl.BlockSpec((n, block, slab_width), lambda i: (0, 0, 0)),
            pl.BlockSpec((8, LANES), lambda i: (0, 0)),
        ],
        scratch_shapes=[
            pltpu.VMEM((heads, n, LANES, block), LOW),
            pltpu.VMEM((heads, full, LANES), LOW),
            pltpu.VMEM((heads, LANES, block), F32),
            pltpu.VMEM((heads, full, LANES), F32),
            pltpu.VMEM((heads, full, LANES), F32),
            pltpu.VMEM((heads, block, LANES), LOW),
            pltpu.VMEM((heads, 8, block), F32),
        ],
        compiler_params=pltpu.CompilerParams(vmem_limit_bytes=56 * MIB),
        name="attend_back",
    )(length, coef, qkv, qkv, qkv, go, keep, lse, q_full)


def reduce_kernel(
    n, nb, chunks, gh, gw, out, own_gw, from_sib, total, gate_in, peer_in, batch_in, line_out, line_in,
    sib_send, sib_recv, gate_send, gate_recv, peer_send, peer_recv, far_send, far_recv,
    b_send, b_recv, z_send, z_recv,
):
    chips, half_chips = n // 2, n // 4
    me, core, chip, half, base, gate_mine, gate_other = place(n)
    group_count = n // 2
    batch = lax.axis_index("batch")
    rows = gh.shape[1] // chunks
    sibling = 2 * chip + 1 - core
    greet(n, nb)

    b_copies = []
    for k in range(1, nb):
        target = lax.rem(batch + k, nb)
        copy = push(gw.at[target], batch_in.at[k], b_send.at[k], b_recv.at[k], batch=target)
        copy.start()
        b_copies.append(copy)

    order = [far_chip(half_chips - 1 - k, half, half_chips) for k in range(half_chips)]
    order += [base + lax.rem(chip - base + k, half_chips) for k in range(1, half_chips)]
    order += [chip]
    sib_copies = []
    for k, q in enumerate(order):
        copy = push(
            gh.at[2 * q + 1 - core], from_sib.at[q], sib_send.at[q], sib_recv.at[q], seq=sibling
        )
        copy.start()
        sib_copies.append(copy)

    def part(ref, lead, c):
        return ref.at[lead, pl.ds(c * rows, rows)]

    def add_sibling(k):
        q = order[k]
        sib_copies[k].wait_recv()
        total[q] = (gh[2 * q + core].astype(F32) + from_sib[q].astype(F32)).astype(LOW)

    def send_peer(k):
        q = order[half_chips + k - 1]
        copy = push(
            total.at[q], peer_in.at[k], peer_send.at[k], peer_recv.at[k], seq=2 * q + core
        )
        copy.start()
        return copy

    def gate_copy(j, k, c):
        return push(
            part(total, order[k], c), gate_in.at[j, k, pl.ds(c * rows, rows)],
            gate_send.at[k, c], gate_recv.at[j, k, c], seq=2 * gate_mine + core,
        )

    def far_copy(k, c):
        return push(
            part(total, order[k], c), part(out, half, c), far_send.at[k, c], far_recv.at[c],
            seq=2 * order[k] + core,
        )

    @pl.when(chip == gate_mine)
    def _():
        for k in range(1, half_chips):
            add_sibling(half_chips + k - 1)
            send_peer(k)
        for k in range(half_chips):
            add_sibling(k)
        for k in range(half_chips):
            for c in range(chunks):
                span = pl.ds(c * rows, rows)
                value = total[order[k], span].astype(F32)
                for j in range(1, half_chips):
                    gate_copy(j, k, c).wait_recv()
                    value = value + gate_in[j, k, span].astype(F32)
                total[order[k], span] = value.astype(LOW)
                far_copy(k, c).start()

    @pl.when(chip != gate_mine)
    def _():
        after = lax.rem(chip - gate_mine + half_chips, half_chips)
        for k in range(half_chips):
            add_sibling(k)
            for c in range(chunks):
                gate_copy(after, k, c).start()
        for k in range(1, half_chips):
            add_sibling(half_chips + k - 1)
            send_peer(k)

    add_sibling(chips - 1)

    for copy in b_copies:
        copy.wait_recv()

    @pl.loop(0, n)
    def _(s):
        value = gw[batch, s].astype(F32)
        for k in range(1, nb):
            value = value + batch_in[k, s].astype(F32)
        line_out[s] = value.astype(LOW)

    z_copies = []
    for k in range(1, n):
        target = lax.rem(me + k, n)
        copy = push(line_out.at[target], line_in.at[me], z_send.at[k], z_recv.at[k], seq=target)
        copy.start()
        z_copies.append(copy)
    line_in[me] = line_out[me]

    value = total[chip].astype(F32)
    for k in range(1, half_chips):
        push(
            total.at[chip], peer_in.at[k], peer_send.at[k], peer_recv.at[k], seq=sibling
        ).wait_recv()
        value = value + peer_in[k].astype(F32)
    out[half] = value.astype(LOW)
    for c in range(chunks):
        push(
            part(total, 0, c), part(out, 1 - half, c), far_send.at[0, c], far_recv.at[c], seq=sibling
        ).wait_recv()
    for copy in z_copies:
        copy.wait_recv()
    for g in range(group_count):
        own_gw[g] = line_in[g].astype(F32) + line_in[g + group_count].astype(F32)

    for copy in b_copies + sib_copies + z_copies:
        copy.wait_send()
    for k in range(1, half_chips):
        push(
            total.at[chip], peer_in.at[k], peer_send.at[k], peer_recv.at[k], seq=sibling
        ).wait_send()

    @pl.when(chip == gate_mine)
    def _():
        for k in range(half_chips):
            for c in range(chunks):
                far_copy(k, c).wait_send()

    @pl.when(chip != gate_mine)
    def _():
        for k in range(half_chips):
            for c in range(chunks):
                gate_copy(1, k, c).wait_send()


def reduce_grads(n, nb, gh, gw):
    chunks = 4
    chips, half_chips = n // 2, n // 4
    _, rows, width = gh.shape
    slab = gw.shape[2:]
    dma = pltpu.SemaphoreType.DMA
    return pl.pallas_call(
        functools.partial(reduce_kernel, n, nb, chunks),
        out_shape=(
            jax.ShapeDtypeStruct((2, rows, width), LOW),
            jax.ShapeDtypeStruct((n // 2,) + slab, F32),
        ),
        in_specs=[pl.BlockSpec(memory_space=pltpu.VMEM)] * 2,
        out_specs=[pl.BlockSpec(memory_space=pltpu.VMEM)] * 2,
        scratch_shapes=[
            pltpu.VMEM((chips, rows, width), LOW),
            pltpu.VMEM((chips, rows, width), LOW),
            pltpu.VMEM((half_chips, half_chips, rows, width), LOW),
            pltpu.VMEM((half_chips, rows, width), LOW),
            pltpu.VMEM((nb, n) + slab, LOW),
            pltpu.VMEM((n,) + slab, LOW),
            pltpu.VMEM((n,) + slab, LOW),
            dma((chips,)),
            dma((chips,)),
            dma((half_chips, chunks)),
            dma((half_chips, half_chips, chunks)),
            dma((half_chips,)),
            dma((half_chips,)),
            dma((half_chips, chunks)),
            dma((chunks,)),
            dma((nb,)),
            dma((nb,)),
            dma((n,)),
            dma((n,)),
        ],
        compiler_params=pltpu.CompilerParams(
            collective_id=4, has_side_effects=True, vmem_limit_bytes=60 * MIB
        ),
        name="reduce_grads",
    )(gh, gw)


def total_kernel(n, nb, value, out, mine, line_in, batch_in, z_send, z_recv, b_send, b_recv):
    me, batch = lax.axis_index("seq"), lax.axis_index("batch")
    greet(n, nb)
    copies = []
    for k in range(1, n):
        copy = push(
            value, line_in.at[k], z_send.at[k], z_recv.at[k], seq=lax.rem(me + k, n)
        )
        copy.start()
        copies.append(copy)
    line_in[0] = value[...]
    for copy in copies:
        copy.wait_recv()
    part = jnp.zeros_like(value)
    for s in range(n):
        part = part + line_in[lax.rem(me - s + n, n)]
    mine[...] = part
    for k in range(1, nb):
        copy = push(
            mine, batch_in.at[k], b_send.at[k], b_recv.at[k], batch=lax.rem(batch + k, nb)
        )
        copy.start()
        copies.append(copy)
    batch_in[0] = part
    for copy in copies[n - 1 :]:
        copy.wait_recv()
    part = jnp.zeros_like(part)
    for s in range(nb):
        part = part + batch_in[lax.rem(batch - s + nb, nb)]
    out[...] = part
    for copy in copies:
        copy.wait_send()


def total_all(n, nb, value):
    dma = pltpu.SemaphoreType.DMA
    return pl.pallas_call(
        functools.partial(total_kernel, n, nb),
        out_shape=jax.ShapeDtypeStruct(value.shape, F32),
        in_specs=[pl.BlockSpec(memory_space=pltpu.VMEM)],
        out_specs=pl.BlockSpec(memory_space=pltpu.VMEM),
        scratch_shapes=[
            pltpu.VMEM(value.shape, F32),
            pltpu.VMEM((n,) + value.shape, F32),
            pltpu.VMEM((nb,) + value.shape, F32),
            dma((n,)),
            dma((n,)),
            dma((nb,)),
            dma((nb,)),
        ],
        compiler_params=pltpu.CompilerParams(collective_id=5, has_side_effects=True),
        name="total_all",
    )(value)


def body(
    n,
    nb,
    tokens,
    cotangent,
    weights,
    gains,
    query_scale,
    first_weights,
    second_weights,
    first_gains,
    second_gains,
    first_scale,
    second_scale,
    lengths,
):
    series_count, rows, width = tokens.shape
    size = query_scale.shape[0]
    group_count = n // 2
    heads = width // size // group_count
    group_width = heads * size
    fold = 640 // group_width
    shard = weights.shape[1]
    slab_width = (3 * group_width + 2 + LANES - 1) // LANES * LANES
    half = lax.axis_index("seq") // group_count
    length = lax.dynamic_slice(lengths, (half,), (1,))

    low_weights = weights.astype(LOW)
    slab = (
        low_weights[:3]
        .reshape(3, shard, group_count, group_width)
        .transpose(2, 1, 0, 3)
        .reshape(group_count, shard, 3 * group_width)
    )
    low_gains = jnp.broadcast_to(gains.astype(LOW).T[None], (group_count, shard, 2))
    spare = jnp.zeros((group_count, shard, slab_width - 3 * group_width - 2), LOW)
    slab = jnp.concatenate([slab, low_gains, spare], axis=2)
    full_weights = lax.all_gather(low_weights[3:], ("batch", "seq"), axis=1, tiled=True)

    xg, wout = gather_tokens(n, nb, tokens, slab)
    wqkv = wout.reshape(nb * n * shard, slab_width)
    gain_rows = wqkv[:, 3 * group_width : 3 * group_width + 2].astype(F32).T
    gain_one, gain_two = gain_rows[0:1], gain_rows[1]

    coef = LOG_TWO_E / math.sqrt(size) * jax.nn.softplus(query_scale)
    coef_row = jnp.concatenate([coef, jnp.zeros((LANES - size,), F32)])[None]
    normed_in, qkv, q_full = project(heads, size, xg, wqkv, gain_one, coef_row)
    o_send, o_keep, lse = attend(heads, size, fold, length, qkv, n)
    o_recv = swap_blocks(n, o_send, 2)
    attended_low = (
        o_recv.reshape(2, group_count, rows // fold, fold, group_width)
        .transpose(0, 3, 2, 1, 4)
        .reshape(2, rows, width)
    )

    inputs = tokens.astype(F32)
    factor_one = rms_factor(inputs)
    normed_one = inputs * factor_one
    branch_one = jnp.einsum("std,de->ste", attended_low, full_weights[0], preferred_element_type=F32)
    middle = inputs + branch_one
    factor_two = rms_factor(middle)
    normed_two = middle * factor_two
    hidden_in = (normed_two * gain_two).astype(LOW)
    pre_act = jnp.einsum("std,de->ste", hidden_in, full_weights[1], preferred_element_type=F32)
    activated = jax.nn.silu(pre_act).astype(LOW)
    branch_two = jnp.einsum("std,de->ste", activated, full_weights[2], preferred_element_type=F32)
    final_sum = middle + branch_two
    block_out = final_sum.astype(LOW)
    stat_terms = jnp.stack(
        [
            jnp.sum(branch_one * branch_one),
            jnp.sum(branch_two * branch_two),
            jnp.sum(final_sum * final_sum),
        ]
    )
    grad_out = cotangent.astype(F32)
    grad_down = jnp.einsum("std,ste->de", activated, cotangent, preferred_element_type=F32)
    grad_act = jnp.einsum("ste,de->std", cotangent, full_weights[2], preferred_element_type=F32)
    grad_pre = (grad_act * silu_slope(pre_act)).astype(LOW)
    grad_up = jnp.einsum("std,ste->de", hidden_in, grad_pre, preferred_element_type=F32)
    grad_hidden = jnp.einsum("ste,de->std", grad_pre, full_weights[1], preferred_element_type=F32)
    grad_gain_two = jnp.sum(grad_hidden * normed_two, axis=(0, 1))
    grad_middle = grad_out + norm_back(grad_hidden * gain_two, normed_two, factor_two)
    grad_branch = grad_middle.astype(LOW)
    grad_out_proj = jnp.einsum("std,ste->de", attended_low, grad_branch, preferred_element_type=F32)
    grad_attended = jnp.einsum(
        "ste,de->std", grad_branch, full_weights[0], preferred_element_type=F32
    ).astype(LOW)
    go_send = (
        grad_attended.reshape(2, fold, rows // fold, group_count, group_width)
        .transpose(0, 3, 2, 1, 4)
        .reshape(n, rows // fold, fold * group_width)
    )
    go_recv = swap_blocks(n, go_send, 3)
    own_three = lax.psum_scatter(
        jnp.stack([grad_out_proj, grad_up, grad_down]).astype(LOW),
        ("batch", "seq"),
        scatter_dimension=1,
        tiled=True,
    ).astype(F32)

    grad_proj, scale_part = attend_back(
        heads, size, fold, length, coef_row, qkv, go_recv, o_keep, lse, q_full, n, slab_width
    )
    grad_slab = jnp.einsum("nrd,nrc->dc", normed_in, grad_proj, preferred_element_type=F32)
    grad_normed_part = jnp.einsum("nrc,dc->nrd", grad_proj, wqkv, preferred_element_type=F32)
    grad_normed, own_slab = reduce_grads(
        n, nb, grad_normed_part.astype(LOW), grad_slab.astype(LOW).reshape(nb, n, shard, slab_width)
    )
    grad_normed = grad_normed.astype(F32)
    own_qkv = (
        own_slab[:, :, : 3 * group_width]
        .reshape(group_count, shard, 3, group_width)
        .transpose(2, 1, 0, 3)
        .reshape(3, shard, width)
    )
    own_grads = jnp.concatenate([own_qkv, own_three], axis=0)

    grad_gain_one = jnp.sum(grad_normed * normed_one, axis=(0, 1))
    input_grad = grad_middle + norm_back(grad_normed * gain_one, normed_one, factor_one)
    own_squares = jnp.sum(own_grads * own_grads)
    scale_slope = LOG_TWO_E / math.sqrt(size) * jax.nn.sigmoid(query_scale)
    scale_part = jnp.sum(scale_part, axis=0)[:size] * scale_slope
    small = jnp.concatenate(
        [grad_gain_one, grad_gain_two, scale_part, stat_terms, own_squares[None]]
    )
    small_rows = (small.shape[0] + 8 * LANES - 1) // (8 * LANES) * 8
    small = jnp.pad(small, (0, small_rows * LANES - small.shape[0])).reshape(small_rows, LANES)
    sums = total_all(n, nb, small).reshape(-1)
    gain_sums = sums[: 2 * width].reshape(2, width)
    scale_grad = sums[2 * width : 2 * width + size]
    stat_sums = sums[2 * width + size : 2 * width + size + 3]
    total_squares = (
        sums[2 * width + size + 3] + jnp.sum(gain_sums * gain_sums) + jnp.sum(scale_grad * scale_grad)
    )
    index = lax.axis_index("batch") * n + lax.axis_index("seq")
    own_gain_grads = lax.dynamic_slice(gain_sums, (0, index * shard), (2, shard))

    grad_norm = jnp.sqrt(total_squares)
    clip_factor = CLIP_NORM / jnp.maximum(grad_norm, CLIP_NORM)
    new_weights, new_first_weights, new_second_weights = adam_update(
        weights, own_grads * clip_factor, first_weights, second_weights, MATRIX_RATE, MATRIX_DECAY
    )
    new_gains, new_first_gains, new_second_gains = adam_update(
        gains, own_gain_grads * clip_factor, first_gains, second_gains, GAIN_RATE, 0.0
    )
    new_scale, new_first_scale, new_second_scale = adam_update(
        query_scale, scale_grad * clip_factor, first_scale, second_scale, GAIN_RATE, 0.0
    )
    rms_stats = jnp.sqrt(stat_sums / float(series_count * rows * width * nb * n))
    return (
        block_out,
        input_grad,
        grad_norm,
        new_weights,
        new_first_weights,
        new_second_weights,
        new_gains,
        new_first_gains,
        new_second_gains,
        new_scale,
        new_first_scale,
        new_second_scale,
        rms_stats,
    )


def solution(mesh):
    return jax.shard_map(
        functools.partial(body, mesh.shape["seq"], mesh.shape["batch"]),
        mesh=mesh,
        in_specs=(
            P("batch", "seq", None),
            P("batch", "seq", None),
            P(None, ("batch", "seq"), None),
            P(None, ("batch", "seq")),
            P(),
            P(None, ("batch", "seq"), None),
            P(None, ("batch", "seq"), None),
            P(None, ("batch", "seq")),
            P(None, ("batch", "seq")),
            P(),
            P(),
            P("batch"),
        ),
        out_specs=(
            P("batch", "seq", None),
            P("batch", "seq", None),
            P(),
            P(None, ("batch", "seq"), None),
            P(None, ("batch", "seq"), None),
            P(None, ("batch", "seq"), None),
            P(None, ("batch", "seq")),
            P(None, ("batch", "seq")),
            P(None, ("batch", "seq")),
            P(),
            P(),
            P(),
            P(),
        ),
        check_vma=False,
    )
```

```python
import functools
import math

import jax
import jax.numpy as jnp
from jax import lax
from jax.experimental import pallas as pl
from jax.experimental.pallas import tpu as pltpu
from jax.sharding import PartitionSpec as P

STEP = 10

NORM_EPS = 1e-06
LOG_TWO_E = 1.442695
BETA_FIRST = 0.9
BETA_SECOND = 0.999
ADAM_EPS = 1e-08
MATRIX_RATE = 0.05
GAIN_RATE = 0.5
MATRIX_DECAY = 0.1
CLIP_NORM = 1.0
MASKED = -1e30

MESH = pl.DeviceIdType.MESH
LANES = 128
F32 = jnp.float32
LOW = jnp.bfloat16
MIB = 1024 * 1024


def rms_factor(values):
    return lax.rsqrt(jnp.mean(values * values, axis=-1, keepdims=True) + NORM_EPS)


def norm_back(grad_normed, normed, factor):
    return factor * (grad_normed - normed * jnp.mean(grad_normed * normed, axis=-1, keepdims=True))


def silu_slope(values):
    logistic = jax.nn.sigmoid(values)
    return logistic * (1.0 + values * (1.0 - logistic))


def adam_update(current, gradient, moment_one, moment_two, step_rate, decay_rate):
    new_one = BETA_FIRST * moment_one + (1.0 - BETA_FIRST) * gradient
    new_two = BETA_SECOND * moment_two + (1.0 - BETA_SECOND) * gradient * gradient
    first_hat = new_one / (1.0 - BETA_FIRST**STEP)
    second_hat = new_two / (1.0 - BETA_SECOND**STEP)
    updated = current - step_rate * (
        first_hat / (jnp.sqrt(second_hat) + ADAM_EPS) + decay_rate * current
    )
    return (updated, new_one, new_two)


def dot(left, right, left_axis=1, right_axis=0):
    return lax.dot_general(
        left, right, (((left_axis,), (right_axis,)), ((), ())), preferred_element_type=F32
    )


def greet(seq_count, batch_count):
    barrier = pltpu.get_barrier_semaphore()
    me_seq, me_batch = lax.axis_index("seq"), lax.axis_index("batch")
    for k in range(1, seq_count):
        pl.semaphore_signal(
            barrier,
            inc=1,
            device_id={"seq": lax.rem(me_seq + k, seq_count)},
            device_id_type=MESH,
        )
    for k in range(1, batch_count):
        pl.semaphore_signal(
            barrier,
            inc=1,
            device_id={"batch": lax.rem(me_batch + k, batch_count)},
            device_id_type=MESH,
        )
    pl.semaphore_wait(barrier, seq_count - 1 + batch_count - 1)


def push(source, target, send_sem, recv_sem, **where):
    return pltpu.make_async_remote_copy(
        source, target, send_sem, recv_sem, device_id=where, device_id_type=MESH
    )


def place(seq_count):
    me = lax.axis_index("seq")
    chips = seq_count // 2
    half_chips = chips // 2
    core = lax.rem(me, 2)
    chip = me // 2
    half = chip // half_chips
    base = half * half_chips
    gate_mine = half_chips - 1 + half
    gate_other = half_chips - half
    return me, core, chip, half, base, gate_mine, gate_other


def far_chip(step, half, half_chips):
    return (1 - half) * (half_chips + step) + half * (half_chips - 1 - step)


def batch_neighbours(batch):
    across = lax.rem(batch, 2)
    first = batch + 1 - 2 * across
    second = lax.rem(batch + 2, 4)
    return (first, second), lax.rem(first + 2, 4)


class Spread:
    def __init__(self, nb, ref, send, recv):
        self.nb, self.ref, self.send, self.recv = nb, ref, send, recv
        self.batch = lax.axis_index("batch")
        self.copies = []

    def copy(self, owner, slot, j, lane, target):
        block = self.ref.at[owner, slot]
        return push(block, block, self.send.at[j, lane], self.recv.at[j, lane], batch=target)

    def route(self, lane):
        sides, across = batch_neighbours(self.batch)
        return sides[lane % 2], sides[1 - lane % 2], across

    def begin(self, slot, lane):
        if self.nb == 4:
            first, second, _ = self.route(lane)
            new = [self.copy(self.batch, slot, 0, lane, first), self.copy(self.batch, slot, 1, lane, second)]
        else:
            new = [
                self.copy(self.batch, slot, j - 1, lane, lax.rem(self.batch + j, self.nb))
                for j in range(1, self.nb)
            ]
        for copy in new:
            copy.start()
        self.copies += new

    def relay(self, slot, lane):
        if self.nb == 4:
            first, second, _ = self.route(lane)
            self.copy(first, slot, 0, lane, first).wait_recv()
            copy = self.copy(first, slot, 2, lane, second)
            copy.start()
            self.copies.append(copy)
            return [first]
        return []

    def finish(self, slot, lane):
        if self.nb == 4:
            _, second, across = self.route(lane)
            self.copy(second, slot, 1, lane, second).wait_recv()
            self.copy(across, slot, 2, lane, second).wait_recv()
            return [second, across]
        owners = []
        for j in range(1, self.nb):
            owner = lax.rem(self.batch + self.nb - j, self.nb)
            self.copy(owner, slot, j - 1, lane, owner).wait_recv()
            owners.append(owner)
        return owners

    def drain(self):
        for copy in self.copies:
            copy.wait_send()


def gather_kernel(
    n, nb, chunks, tok, slab, own_w, xg, wout, w_all, far_sem, own_sem, pass_sem, sib_sem, same_recv,
    sib_recv, z_send, z_recv, b_send, b_recv, wz_send, wz_recv, wb_send, wb_recv, ws_send, ws_recv,
    local_sem,
):
    chips, half_chips = n // 2, n // 4
    me, core, chip, half, base, gate_mine, gate_other = place(n)
    group_count = n // 2
    batch = lax.axis_index("batch")
    rows = tok.shape[1] // chunks
    sibling = 2 * chip + 1 - core
    greet(n, nb)

    sends = []
    z_copies = []
    for k in range(1, n):
        target = lax.rem(me + k, n)
        copy = push(
            slab.at[lax.rem(target, group_count)], wout.at[batch, me], z_send.at[k],
            z_recv.at[k], seq=target,
        )
        copy.start()
        z_copies.append(copy)
    w_copies = []
    for k in range(1, chips):
        target = 2 * lax.rem(chip + k, chips) + core
        copy = push(own_w, w_all.at[batch, me], wz_send.at[k], wz_recv.at[k], seq=target)
        copy.start()
        w_copies.append(copy)

    def part(ref, lead, c):
        return ref.at[lead, pl.ds(c * rows, rows)]

    def tok_copy(source, slot, c, send_sem, recv_sem, target):
        return push(source, part(xg, slot, c), send_sem, recv_sem.at[slot, c], seq=target)

    for c in range(chunks):
        copy = tok_copy(
            part(tok, 1 - half, c), me, c, far_sem.at[c], same_recv, 2 * gate_other + core
        )
        copy.start()
        sends.append(copy)
        for k in range(1, half_chips):
            other = base + lax.rem(chip - base + k, half_chips)
            copy = tok_copy(
                part(tok, half, c), me, c, own_sem.at[k, c], same_recv, 2 * other + core
            )
            copy.start()
            sends.append(copy)
        copy = tok_copy(part(tok, half, c), me, c, sib_sem.at[0, c], sib_recv, sibling)
        copy.start()
        sends.append(copy)
    own_copy = pltpu.make_async_copy(tok.at[half], xg.at[me], local_sem.at[0])
    own_copy.start()
    slab_copy = pltpu.make_async_copy(
        slab.at[lax.rem(me, group_count)], wout.at[batch, me], local_sem.at[1]
    )
    slab_copy.start()
    w_copy = pltpu.make_async_copy(own_w, w_all.at[batch, me], local_sem.at[2])
    w_copy.start()
    slab_copy.wait()
    w_copy.wait()

    slices = Spread(nb, wout, b_send, b_recv)
    whole = Spread(nb, w_all, wb_send, wb_recv)

    def line_slot(k):
        return lax.rem(me + n - k, n)

    def chip_slot(k):
        return 2 * lax.rem(chip + chips - k, chips) + core

    def to_sibling(owner, lane, slot, j):
        block = w_all.at[owner, slot]
        copy = push(block, block, ws_send.at[j, lane], ws_recv.at[owner, slot], seq=sibling)
        copy.start()
        sends.append(copy)

    def pass_tokens(c):
        for k in range(1, half_chips):
            slot = 2 * (base + lax.rem(chip - base + half_chips - k, half_chips)) + core
            tok_copy(part(xg, slot, c), slot, c, sib_sem.at[k, c], same_recv, sibling).wait_recv()
            copy = tok_copy(part(xg, slot, c), slot, c, sib_sem.at[k, c], sib_recv, sibling)
            copy.start()
            sends.append(copy)
        for k in range(half_chips):
            slot = 2 * far_chip(k, half, half_chips) + core
            lane = half_chips + k
            tok_copy(part(xg, slot, c), slot, c, sib_sem.at[lane, c], same_recv, sibling).wait_recv()

            @pl.when(chip == gate_mine)
            def _():
                for j in range(1, half_chips):
                    other = base + lax.rem(chip - base + j, half_chips)
                    tok_copy(
                        part(xg, slot, c), slot, c, pass_sem.at[k, j, c], same_recv,
                        2 * other + core,
                    ).start()

            copy = tok_copy(part(xg, slot, c), slot, c, sib_sem.at[lane, c], sib_recv, sibling)
            copy.start()
            sends.append(copy)

    slices.begin(me, 0)
    whole.begin(me, 0)
    to_sibling(batch, 0, me, 0)
    for k in range(1, n):
        z_copies[k - 1].wait_recv()
        slices.begin(line_slot(k), k)
    pass_tokens(0)
    for k in range(1, chips):
        w_copies[k - 1].wait_recv()
        whole.begin(chip_slot(k), k)
        to_sibling(batch, k, chip_slot(k), 0)
    pass_tokens(1)
    for k in range(n):
        slices.relay(line_slot(k), k)
    pass_tokens(2)
    for k in range(chips):
        for j, owner in enumerate(whole.relay(chip_slot(k), k)):
            to_sibling(owner, k, chip_slot(k), 1 + j)
    pass_tokens(3)
    for k in range(n):
        slices.finish(line_slot(k), k)
    for k in range(chips):
        owners = whole.finish(chip_slot(k), k)
        for j, owner in enumerate(owners):
            to_sibling(owner, k, chip_slot(k), nb - len(owners) + j)

    for c in range(chunks):
        for q in range(chips):
            slot = 2 * q + 1 - core
            tok_copy(part(xg, slot, c), slot, c, sib_sem.at[0, c], sib_recv, sibling).wait_recv()
    for owner in range(nb):
        for q in range(chips):
            block = w_all.at[owner, 2 * q + 1 - core]
            push(
                block, block, ws_send.at[0, 0], ws_recv.at[owner, 2 * q + 1 - core], seq=sibling
            ).wait_recv()
    own_copy.wait()
    slices.drain()
    whole.drain()
    for copy in sends + z_copies + w_copies:
        copy.wait_send()

    @pl.when(chip == gate_mine)
    def _():
        for c in range(chunks):
            for k in range(half_chips):
                for j in range(1, half_chips):
                    tok_copy(
                        part(xg, me, c), me, c, pass_sem.at[k, j, c], same_recv, sibling
                    ).wait_send()


def gather_tokens(n, nb, tokens, slab, own_w):
    chunks = 4
    chips, half_chips = n // 2, n // 4
    dma = pltpu.SemaphoreType.DMA
    return pl.pallas_call(
        functools.partial(gather_kernel, n, nb, chunks),
        out_shape=(
            jax.ShapeDtypeStruct((n,) + tokens.shape[1:], tokens.dtype),
            jax.ShapeDtypeStruct((nb, n) + slab.shape[1:], slab.dtype),
            jax.ShapeDtypeStruct((nb, n) + own_w.shape, own_w.dtype),
        ),
        in_specs=[pl.BlockSpec(memory_space=pl.ANY)] * 3,
        out_specs=[pl.BlockSpec(memory_space=pl.ANY)] * 3,
        scratch_shapes=[
            dma((chunks,)),
            dma((half_chips, chunks)),
            dma((half_chips, half_chips, chunks)),
            dma((chips, chunks)),
            dma((n, chunks)),
            dma((n, chunks)),
            dma((n,)),
            dma((n,)),
            dma((nb, n)),
            dma((nb, n)),
            dma((chips,)),
            dma((chips,)),
            dma((nb, chips)),
            dma((nb, chips)),
            dma((nb, chips)),
            dma((nb, n)),
            dma((3,)),
        ],
        compiler_params=pltpu.CompilerParams(collective_id=1, has_side_effects=True),
        name="gather_tokens",
    )(tokens, slab, own_w)


def swap_kernel(n, source, target, send_sem, recv_sem, local_sem):
    me = lax.axis_index("seq")
    greet(n, 1)
    copies = []
    for k in range(1, n):
        other = lax.rem(me + k, n)
        copy = push(source.at[other], target.at[me], send_sem.at[k], recv_sem.at[k], seq=other)
        copy.start()
        copies.append(copy)
    own = pltpu.make_async_copy(source.at[me], target.at[me], local_sem)
    own.start()
    own.wait()
    for copy in copies:
        copy.wait()


def swap_blocks(n, blocks, collective_id):
    return pl.pallas_call(
        functools.partial(swap_kernel, n),
        out_shape=jax.ShapeDtypeStruct(blocks.shape, blocks.dtype),
        in_specs=[pl.BlockSpec(memory_space=pl.ANY)],
        out_specs=pl.BlockSpec(memory_space=pl.ANY),
        scratch_shapes=[
            pltpu.SemaphoreType.DMA((n,)),
            pltpu.SemaphoreType.DMA((n,)),
            pltpu.SemaphoreType.DMA,
        ],
        compiler_params=pltpu.CompilerParams(collective_id=collective_id, has_side_effects=True),
        name="swap_blocks",
    )(blocks)


def widen(values):
    rows, width = values.shape
    return jnp.concatenate([values, jnp.zeros((rows, LANES - width), values.dtype)], axis=1)


def project_kernel(heads, size, x_ref, w_ref, gain_ref, coef_ref, h_ref, qkv_ref, q_ref):
    x = x_ref[0].astype(F32)
    normed = x * rms_factor(x)
    h = (normed * gain_ref[...]).astype(LOW)
    h_ref[0] = h
    out = dot(h, w_ref[...])
    for a in range(heads):
        q = widen(out[:, a * size : (a + 1) * size])
        q_ref[a] = q
        qkv_ref[a] = (q * coef_ref[...]).astype(LOW)
    for a in range(heads, 3 * heads):
        qkv_ref[a] = widen(out[:, a * size : (a + 1) * size].astype(LOW))


def project(heads, size, xg, weights, gain, coef):
    n, rows, width = xg.shape
    return pl.pallas_call(
        functools.partial(project_kernel, heads, size),
        grid=(n,),
        out_shape=(
            jax.ShapeDtypeStruct(xg.shape, LOW),
            jax.ShapeDtypeStruct((3 * heads, n * rows, LANES), LOW),
            jax.ShapeDtypeStruct((heads, n * rows, LANES), F32),
        ),
        in_specs=[
            pl.BlockSpec((1, rows, width), lambda i: (i, 0, 0)),
            pl.BlockSpec(weights.shape, lambda i: (0, 0)),
            pl.BlockSpec(gain.shape, lambda i: (0, 0)),
            pl.BlockSpec(coef.shape, lambda i: (0, 0)),
        ],
        out_specs=[
            pl.BlockSpec((1, rows, width), lambda i: (i, 0, 0)),
            pl.BlockSpec((3 * heads, rows, LANES), lambda i: (0, i, 0)),
            pl.BlockSpec((heads, rows, LANES), lambda i: (0, i, 0)),
        ],
        compiler_params=pltpu.CompilerParams(vmem_limit_bytes=48 * MIB),
        name="project",
    )(xg, weights, gain, coef)


def attend_kernel(
    heads, size, fold, len_ref, q_ref, k_ref, v_ref, o_ref, keep_ref, lse_ref, s_ref, m_ref, acc_ref,
    sum_ref,
):
    i = pl.program_id(0)
    block = q_ref.shape[1]
    length = len_ref[0]
    whole = jnp.minimum(i, length // block)
    total = jnp.minimum(i + 1, pl.cdiv(length, block))
    m_ref[...] = jnp.full_like(m_ref, MASKED)
    sum_ref[...] = jnp.zeros_like(sum_ref)
    acc_ref[...] = jnp.zeros_like(acc_ref)

    def score(j, masked):
        keys = pl.ds(pl.multiple_of(j * block, block), block)
        if masked:
            row = i * block + lax.broadcasted_iota(jnp.int32, (block, block), 0)
            col = j * block + lax.broadcasted_iota(jnp.int32, (block, block), 1)
            visible = (col <= row) & (col < length)
        for a in range(heads):
            s = dot(q_ref[a], k_ref[a, keys], 1, 1)
            if masked:
                s = jnp.where(visible, s, MASKED)
            s_ref[a, j] = s
            best = m_ref[a]
            for part in range(block // LANES):
                best = jnp.maximum(best, s[:, part * LANES : (part + 1) * LANES])
            m_ref[a] = best

    pl.loop(0, whole)(lambda j: score(j, False))
    pl.loop(whole, total)(lambda j: score(j, True))
    for a in range(heads):
        m_ref[a] = jnp.broadcast_to(jnp.max(m_ref[a], axis=1, keepdims=True), (block, LANES))

    @pl.loop(0, total)
    def _(j):
        keys = pl.ds(pl.multiple_of(j * block, block), block)
        for a in range(heads):
            best = m_ref[a]
            count = sum_ref[a]
            pieces = []
            for part in range(block // LANES):
                e = jnp.exp(s_ref[a, j, :, part * LANES : (part + 1) * LANES] - best)
                count = count + e
                pieces.append(e.astype(LOW))
            sum_ref[a] = count
            acc_ref[a] += dot(jnp.concatenate(pieces, axis=1), v_ref[a, keys])

    outs = []
    for a in range(heads):
        count = jnp.sum(sum_ref[a], axis=1, keepdims=True)
        out = acc_ref[a] / count
        keep_ref[a] = out
        outs.append(out[:, :size])
        lse = m_ref[a] + jnp.log(count)
        lse_ref[a] = lse.T[:8]
    low = jnp.concatenate(outs, axis=1).astype(LOW)
    piece = block // fold
    o_ref[0] = jnp.concatenate([low[f * piece : (f + 1) * piece] for f in range(fold)], axis=1)


def attend(heads, size, fold, length, qkv, n):
    full = qkv.shape[1]
    block = full // n
    width = heads * size * fold
    return pl.pallas_call(
        functools.partial(attend_kernel, heads, size, fold),
        grid=(n,),
        out_shape=(
            jax.ShapeDtypeStruct((n, block // fold, width), LOW),
            jax.ShapeDtypeStruct((heads, full, LANES), F32),
            jax.ShapeDtypeStruct((heads, 8, full), F32),
        ),
        in_specs=[
            pl.BlockSpec(memory_space=pltpu.SMEM),
            pl.BlockSpec((heads, block, LANES), lambda i: (0, i, 0)),
            pl.BlockSpec((heads, full, LANES), lambda i: (1, 0, 0)),
            pl.BlockSpec((heads, full, LANES), lambda i: (2, 0, 0)),
        ],
        out_specs=[
            pl.BlockSpec((1, block // fold, width), lambda i: (i, 0, 0)),
            pl.BlockSpec((heads, block, LANES), lambda i: (0, i, 0)),
            pl.BlockSpec((heads, 8, block), lambda i: (0, 0, i)),
        ],
        scratch_shapes=[
            pltpu.VMEM((heads, n, block, block), F32),
            pltpu.VMEM((heads, block, LANES), F32),
            pltpu.VMEM((heads, block, LANES), F32),
            pltpu.VMEM((heads, block, LANES), F32),
        ],
        compiler_params=pltpu.CompilerParams(vmem_limit_bytes=48 * MIB),
        name="attend",
    )(length, qkv, qkv, qkv)


def attend_back_kernel(
    heads, size, fold, n, len_ref, coef_ref, q_ref, k_ref, v_ref, go_ref, keep_ref, lse_ref, qf_ref,
    out_ref, scale_ref, kt_ref, gq_ref, gqt_ref, gk_ref, gv_ref, g_ref, delta_ref,
):
    i = pl.program_id(0)
    block = q_ref.shape[1]
    length = len_ref[0]
    whole = jnp.minimum(i, length // block)
    total = jnp.minimum(i + 1, pl.cdiv(length, block))

    @pl.when(i == 0)
    def _():
        gk_ref[...] = jnp.zeros_like(gk_ref)
        gv_ref[...] = jnp.zeros_like(gv_ref)
        scale_ref[...] = jnp.zeros_like(scale_ref)

        @pl.loop(0, n)
        def _(j):
            keys = pl.ds(pl.multiple_of(j * block, block), block)
            for a in range(heads):
                kt_ref[a, j] = k_ref[a, keys].T

    gqt_ref[...] = jnp.zeros_like(gqt_ref)
    for a in range(heads):
        g = widen(
            jnp.concatenate(
                [
                    go_ref[0, :, (f * heads + a) * size : (f * heads + a + 1) * size]
                    for f in range(fold)
                ],
                axis=0,
            )
        )
        g_ref[a] = g
        delta_ref[a] = jnp.broadcast_to(
            jnp.sum((g.astype(F32) * keep_ref[a]).T, axis=0, keepdims=True), (8, block)
        )

    def back(j, masked):
        keys = pl.ds(pl.multiple_of(j * block, block), block)
        if masked:
            col = j * block + lax.broadcasted_iota(jnp.int32, (block, block), 0)
            row = i * block + lax.broadcasted_iota(jnp.int32, (block, block), 1)
            visible = (col <= row) & (col < length)
        for a in range(heads):
            s = dot(k_ref[a, keys], q_ref[a], 1, 1)
            p = jnp.exp(s - lse_ref[a, :1])
            if masked:
                p = jnp.where(visible, p, 0.0)
            dp = dot(v_ref[a, keys], g_ref[a], 1, 1)
            ds = (p * (dp - delta_ref[a, :1])).astype(LOW)
            gk_ref[a, keys] += dot(ds, q_ref[a])
            gv_ref[a, keys] += dot(p.astype(LOW), g_ref[a])
            gqt_ref[a] += dot(kt_ref[a, j], ds)

    pl.loop(0, whole)(lambda j: back(j, False))
    pl.loop(whole, total)(lambda j: back(j, True))

    rows = pl.ds(pl.multiple_of(i * block, block), block)
    for a in range(heads):
        grad = gqt_ref[a].T.astype(LOW).astype(F32)
        scale_ref[...] += jnp.sum((grad * qf_ref[a]).reshape(block // 8, 8, LANES), axis=0)
        gq_ref[a, rows] = (grad * coef_ref[...]).astype(LOW)

    @pl.when(i == n - 1)
    def _():
        @pl.loop(0, n)
        def _(j):
            keys = pl.ds(pl.multiple_of(j * block, block), block)
            pieces = [gq_ref[a, keys][:, :size] for a in range(heads)]
            pieces += [gk_ref[a, keys][:, :size].astype(LOW) for a in range(heads)]
            pieces += [gv_ref[a, keys][:, :size].astype(LOW) for a in range(heads)]
            spare = out_ref.shape[2] - 3 * heads * size
            pieces.append(jnp.zeros((block, spare), LOW))
            out_ref[j] = jnp.concatenate(pieces, axis=1)


def attend_back(heads, size, fold, length, coef, qkv, go, keep, lse, q_full, n, slab_width):
    full = qkv.shape[1]
    block = full // n
    width = heads * size * fold
    return pl.pallas_call(
        functools.partial(attend_back_kernel, heads, size, fold, n),
        grid=(n,),
        out_shape=(
            jax.ShapeDtypeStruct((n, block, slab_width), LOW),
            jax.ShapeDtypeStruct((8, LANES), F32),
        ),
        in_specs=[
            pl.BlockSpec(memory_space=pltpu.SMEM),
            pl.BlockSpec(coef.shape, lambda i: (0, 0)),
            pl.BlockSpec((heads, block, LANES), lambda i: (0, i, 0)),
            pl.BlockSpec((heads, full, LANES), lambda i: (1, 0, 0)),
            pl.BlockSpec((heads, full, LANES), lambda i: (2, 0, 0)),
            pl.BlockSpec((1, block // fold, width), lambda i: (i, 0, 0)),
            pl.BlockSpec((heads, block, LANES), lambda i: (0, i, 0)),
            pl.BlockSpec((heads, 8, block), lambda i: (0, 0, i)),
            pl.BlockSpec((heads, block, LANES), lambda i: (0, i, 0)),
        ],
        out_specs=[
            pl.BlockSpec((n, block, slab_width), lambda i: (0, 0, 0)),
            pl.BlockSpec((8, LANES), lambda i: (0, 0)),
        ],
        scratch_shapes=[
            pltpu.VMEM((heads, n, LANES, block), LOW),
            pltpu.VMEM((heads, full, LANES), LOW),
            pltpu.VMEM((heads, LANES, block), F32),
            pltpu.VMEM((heads, full, LANES), F32),
            pltpu.VMEM((heads, full, LANES), F32),
            pltpu.VMEM((heads, block, LANES), LOW),
            pltpu.VMEM((heads, 8, block), F32),
        ],
        compiler_params=pltpu.CompilerParams(vmem_limit_bytes=56 * MIB),
        name="attend_back",
    )(length, coef, qkv, qkv, qkv, go, keep, lse, q_full)


def fold_rows(values):
    rows, width = values.shape
    return jnp.sum(values.reshape(rows // 8, 8, width), axis=0)


def layer_kernel(
    n, nb, fold, tok, cot, o_in, w_in, gain_ref, y_out, gy_out, go_out, small_out, half_out,
    w, o_s, hidden_s, act_s, gu_s, ga_s, go_s, gw_s, sib_in, w_sem, send_sem, recv_sem, local_sem,
    sib_send, sib_recv,
):
    group_count = n // 2
    me, core, chip, half, base, gate_mine, gate_other = place(n)
    sibling = 2 * chip + 1 - core
    _, rows, width = tok.shape
    group_width = width // group_count
    piece = rows // fold
    barrier = pltpu.get_barrier_semaphore()
    for k in range(1, n):
        pl.semaphore_signal(
            barrier, inc=1, device_id={"seq": lax.rem(me + k, n)}, device_id_type=MESH
        )
    loads = [pltpu.make_async_copy(w_in.at[m], w.at[m], w_sem.at[m]) for m in range(3)]
    for load in loads:
        load.start()
    small_out[...] = jnp.zeros_like(small_out)
    gain = gain_ref[...]

    def go_push(target):
        return push(
            go_s.at[target], go_out.at[me], send_sem.at[target], recv_sem.at[me], seq=target
        )

    own_go = pltpu.make_async_copy(go_s.at[me], go_out.at[me], local_sem)

    for t in range(2):
        parts = [
            jnp.concatenate(
                [
                    o_in[t * group_count + g, :, f * group_width : (f + 1) * group_width]
                    for g in range(group_count)
                ],
                axis=1,
            )
            for f in range(fold)
        ]
        o = jnp.concatenate(parts, axis=0)
        o_s[t] = o
        if t == 0:
            loads[0].wait()
        a = dot(o, w[0])
        small_out[1] += fold_rows(a * a)
        y1 = tok[t].astype(F32) + a
        factor = rms_factor(y1)
        normed = y1 * factor
        hidden = (normed * gain).astype(LOW)
        hidden_s[t] = hidden
        if t == 0:
            loads[1].wait()
        u = dot(hidden, w[1])
        logistic = 1.0 / (1.0 + jnp.exp(-u))
        act = (u * logistic).astype(LOW)
        act_s[t] = act
        if t == 0:
            loads[2].wait()
        f = dot(act, w[2])
        small_out[2] += fold_rows(f * f)
        y = y1 + f
        small_out[3] += fold_rows(y * y)
        y_out[t] = y.astype(LOW)
        gz = dot(cot[t], w[2], 1, 1)
        gu = (gz * (logistic * (1.0 + u * (1.0 - logistic)))).astype(LOW)
        gu_s[t] = gu
        gh = dot(gu, w[1], 1, 1)
        small_out[0] += fold_rows(gh * normed)
        gy = cot[t].astype(F32) + norm_back(gh * gain, normed, factor)
        gy_out[t] = gy
        ga = gy.astype(LOW)
        ga_s[t] = ga
        go = dot(ga, w[0], 1, 1).astype(LOW)
        for g in range(group_count):
            block = go[:, g * group_width : (g + 1) * group_width]
            go_s[t * group_count + g] = jnp.concatenate(
                [block[f * piece : (f + 1) * piece] for f in range(fold)], axis=1
            )
        if t == 0:
            pl.semaphore_wait(barrier, n - 1)
        for g in range(group_count):
            target = t * group_count + g

            @pl.when(target != me)
            def _():
                go_push(target).start()

            @pl.when(target == me)
            def _():
                own_go.start()

    tile = 256
    half_rows = width // nb // 2
    sib_copies = []
    pairs = ((act_s, cot, 2), (hidden_s, gu_s, 1), (o_s, ga_s, 0))
    for left, right, m in pairs:

        @pl.loop(0, width // tile)
        def _(k):
            cols = pl.ds(pl.multiple_of(k * tile, tile), tile)
            total = dot(left[0, :, cols], right[0], 0, 0) + dot(left[1, :, cols], right[1], 0, 0)
            gw_s[m, cols] = total.astype(LOW)

        for b in range(nb):
            start = pl.multiple_of((2 * b + 1 - core) * half_rows, 16)
            copy = push(
                gw_s.at[m, pl.ds(start, half_rows)], sib_in.at[b, m], sib_send.at[b, m],
                sib_recv.at[b, m], seq=sibling,
            )
            copy.start()
            sib_copies.append(copy)
    index = 0
    for _, _, m in pairs:
        for b in range(nb):
            sib_copies[index].wait_recv()
            index += 1
            start = pl.multiple_of((2 * b + core) * half_rows, 16)
            half_out[b, m] = (
                gw_s[m, pl.ds(start, half_rows)].astype(F32) + sib_in[b, m].astype(F32)
            ).astype(LOW)
    for k in range(1, n):
        source = lax.rem(me + k, n)
        push(
            go_s.at[source], go_out.at[source], send_sem.at[source], recv_sem.at[source], seq=source
        ).wait()
    own_go.wait()
    for copy in sib_copies:
        copy.wait_send()


def layer(n, nb, fold, tokens, cotangent, o_recv, w_all, gain):
    _, rows, width = tokens.shape
    half_rows = width // nb // 2
    dma = pltpu.SemaphoreType.DMA
    vmem = pl.BlockSpec(memory_space=pltpu.VMEM)
    anywhere = pl.BlockSpec(memory_space=pl.ANY)
    kept = pltpu.VMEM((2, rows, width), LOW)
    return pl.pallas_call(
        functools.partial(layer_kernel, n, nb, fold),
        out_shape=(
            jax.ShapeDtypeStruct((2, rows, width), LOW),
            jax.ShapeDtypeStruct((2, rows, width), F32),
            jax.ShapeDtypeStruct(o_recv.shape, LOW),
            jax.ShapeDtypeStruct((4, 8, width), F32),
            jax.ShapeDtypeStruct((nb, 3, half_rows, width), LOW),
        ),
        in_specs=[vmem, vmem, vmem, anywhere, vmem],
        out_specs=[vmem, vmem, anywhere, vmem, vmem],
        scratch_shapes=[
            pltpu.VMEM((3, width, width), LOW),
            kept,
            kept,
            kept,
            kept,
            kept,
            pltpu.VMEM(o_recv.shape, LOW),
            pltpu.VMEM((3, width, width), LOW),
            pltpu.VMEM((nb, 3, half_rows, width), LOW),
            dma((3,)),
            dma((n,)),
            dma((n,)),
            dma,
            dma((nb, 3)),
            dma((nb, 3)),
        ],
        compiler_params=pltpu.CompilerParams(
            collective_id=3, has_side_effects=True, vmem_limit_bytes=63 * MIB
        ),
        name="layer",
    )(tokens, cotangent, o_recv, w_all, gain)


def reduce_kernel(
    n, nb, chunks, gh, gw, w_half, out, own_gw, own_w, from_sib, total, gate_in, peer_in, batch_in,
    line_out, line_in, cross_in, cross_out, turn_in, w_line, w_in, sib_send, sib_recv, gate_send,
    gate_recv, peer_send, peer_recv, far_send, far_recv, b_send, b_recv, z_send, z_recv, c_send,
    c_recv, t_send, t_recv, w_send, w_recv,
):
    chips, half_chips = n // 2, n // 4
    me, core, chip, half, base, gate_mine, gate_other = place(n)
    group_count = n // 2
    batch = lax.axis_index("batch")
    rows = gh.shape[1] // chunks
    sibling = 2 * chip + 1 - core
    greet(n, nb)

    split = 2 if nb == 4 else 1
    w_rows = w_half.shape[2] // split
    sides, across = batch_neighbours(batch)

    def w_part(b, h):
        return w_half.at[b, :, pl.ds(h * w_rows, w_rows)]

    w_copies = []
    if nb == 4:
        for h in range(2):
            for j, owner in enumerate((across, sides[h])):
                copy = push(
                    w_part(owner, h), cross_in.at[h, j], c_send.at[h, j], c_recv.at[h, j],
                    batch=sides[h],
                )
                copy.start()
                w_copies.append(copy)
    else:
        for k in range(1, nb):
            target = lax.rem(batch + k, nb)
            copy = push(
                w_half.at[target], cross_in.at[0, k], c_send.at[0, k], c_recv.at[0, k], batch=target
            )
            copy.start()
            w_copies.append(copy)

    b_copies = []
    for k in range(1, nb):
        target = lax.rem(batch + k, nb)
        copy = push(gw.at[target], batch_in.at[k], b_send.at[k], b_recv.at[k], batch=target)
        copy.start()
        b_copies.append(copy)

    order = [far_chip(half_chips - 1 - k, half, half_chips) for k in range(half_chips)]
    order += [base + lax.rem(chip - base + k, half_chips) for k in range(1, half_chips)]
    order += [chip]
    sib_copies = []
    for k, q in enumerate(order):
        copy = push(
            gh.at[2 * q + 1 - core], from_sib.at[q], sib_send.at[q], sib_recv.at[q], seq=sibling
        )
        copy.start()
        sib_copies.append(copy)

    def part(ref, lead, c):
        return ref.at[lead, pl.ds(c * rows, rows)]

    def add_sibling(k):
        q = order[k]
        sib_copies[k].wait_recv()
        total[q] = (gh[2 * q + core].astype(F32) + from_sib[q].astype(F32)).astype(LOW)

    def send_peer(k):
        q = order[half_chips + k - 1]
        copy = push(
            total.at[q], peer_in.at[k], peer_send.at[k], peer_recv.at[k], seq=2 * q + core
        )
        copy.start()
        return copy

    def gate_copy(j, k, c):
        return push(
            part(total, order[k], c), gate_in.at[j, k, pl.ds(c * rows, rows)],
            gate_send.at[k, c], gate_recv.at[j, k, c], seq=2 * gate_mine + core,
        )

    def far_copy(k, c):
        return push(
            part(total, order[k], c), part(out, half, c), far_send.at[k, c], far_recv.at[c],
            seq=2 * order[k] + core,
        )

    @pl.when(chip == gate_mine)
    def _():
        for k in range(1, half_chips):
            add_sibling(half_chips + k - 1)
            send_peer(k)
        for k in range(half_chips):
            add_sibling(k)
        for k in range(half_chips):
            for c in range(chunks):
                span = pl.ds(c * rows, rows)
                value = total[order[k], span].astype(F32)
                for j in range(1, half_chips):
                    gate_copy(j, k, c).wait_recv()
                    value = value + gate_in[j, k, span].astype(F32)
                total[order[k], span] = value.astype(LOW)
                far_copy(k, c).start()

    @pl.when(chip != gate_mine)
    def _():
        after = lax.rem(chip - gate_mine + half_chips, half_chips)
        for k in range(half_chips):
            add_sibling(k)
            for c in range(chunks):
                gate_copy(after, k, c).start()
        for k in range(1, half_chips):
            add_sibling(half_chips + k - 1)
            send_peer(k)

    add_sibling(chips - 1)

    t_copies = []
    if nb == 4:
        for h in range(2):
            w_copies[2 * h].wait_recv()
            span = pl.ds(h * w_rows, w_rows)
            cross_out[h] = (
                w_half[sides[1 - h], :, span].astype(F32) + cross_in[h, 0].astype(F32)
            ).astype(LOW)
            copy = push(
                cross_out.at[h], turn_in.at[h], t_send.at[h], t_recv.at[h], batch=sides[1 - h]
            )
            copy.start()
            t_copies.append(copy)

    for copy in b_copies:
        copy.wait_recv()

    @pl.loop(0, n)
    def _(s):
        value = gw[batch, s].astype(F32)
        for k in range(1, nb):
            value = value + batch_in[k, s].astype(F32)
        line_out[s] = value.astype(LOW)

    z_copies = []
    for k in range(1, n):
        target = lax.rem(me + k, n)
        copy = push(line_out.at[target], line_in.at[me], z_send.at[k], z_recv.at[k], seq=target)
        copy.start()
        z_copies.append(copy)
    line_in[me] = line_out[me]

    shard = own_w.shape[1]
    parts = []
    if nb == 4:
        for h in range(2):
            w_copies[2 * h + 1].wait_recv()
            t_copies[h].wait_recv()
            span = pl.ds(h * w_rows, w_rows)
            parts.append(
                w_half[batch, :, span].astype(F32)
                + cross_in[h, 1].astype(F32)
                + turn_in[h].astype(F32)
            )
    else:
        value = w_half[batch].astype(F32)
        for k in range(1, nb):
            w_copies[k - 1].wait_recv()
            value = value + cross_in[0, k].astype(F32)
        parts.append(value)
    summed = jnp.concatenate(parts, axis=1)
    for i in range(group_count):
        w_line[i] = summed[:, i * shard : (i + 1) * shard].astype(LOW)

    def w_push(i):
        target = core * group_count + i
        return push(w_line.at[i], w_in.at[chip], w_send.at[i], w_recv.at[chip], seq=target)

    for i in range(group_count):
        mine = core * group_count + i == me

        @pl.when(mine)
        def _():
            w_in[chip] = w_line[i]

        @pl.when(jnp.logical_not(mine))
        def _():
            w_push(i).start()

    value = total[chip].astype(F32)
    for k in range(1, half_chips):
        push(
            total.at[chip], peer_in.at[k], peer_send.at[k], peer_recv.at[k], seq=sibling
        ).wait_recv()
        value = value + peer_in[k].astype(F32)
    out[half] = value.astype(LOW)
    for c in range(chunks):
        push(
            part(total, 0, c), part(out, 1 - half, c), far_send.at[0, c], far_recv.at[c], seq=sibling
        ).wait_recv()
    for copy in z_copies:
        copy.wait_recv()
    for g in range(group_count):
        own_gw[g] = line_in[g].astype(F32) + line_in[g + group_count].astype(F32)

    for q in range(chips):

        @pl.when(2 * q + half != me)
        def _():
            push(
                w_line.at[0], w_in.at[q], w_send.at[0], w_recv.at[q], seq=sibling
            ).wait_recv()

    value = w_in[0].astype(F32)
    for q in range(1, chips):
        value = value + w_in[q].astype(F32)
    own_w[...] = value
    for i in range(group_count):

        @pl.when(core * group_count + i != me)
        def _():
            w_push(i).wait_send()

    for copy in b_copies + sib_copies + z_copies + w_copies + t_copies:
        copy.wait_send()
    for k in range(1, half_chips):
        push(
            total.at[chip], peer_in.at[k], peer_send.at[k], peer_recv.at[k], seq=sibling
        ).wait_send()

    @pl.when(chip == gate_mine)
    def _():
        for k in range(half_chips):
            for c in range(chunks):
                far_copy(k, c).wait_send()

    @pl.when(chip != gate_mine)
    def _():
        for k in range(half_chips):
            for c in range(chunks):
                gate_copy(1, k, c).wait_send()


def reduce_grads(n, nb, gh, gw, w_half, shard):
    chunks = 4
    chips, half_chips = n // 2, n // 4
    _, rows, width = gh.shape
    slab = gw.shape[2:]
    half_rows = w_half.shape[2]
    split = 2 if nb == 4 else 1
    steps = 2 if nb == 4 else nb
    dma = pltpu.SemaphoreType.DMA
    return pl.pallas_call(
        functools.partial(reduce_kernel, n, nb, chunks),
        out_shape=(
            jax.ShapeDtypeStruct((2, rows, width), LOW),
            jax.ShapeDtypeStruct((n // 2,) + slab, F32),
            jax.ShapeDtypeStruct((3, shard, width), F32),
        ),
        in_specs=[pl.BlockSpec(memory_space=pltpu.VMEM)] * 3,
        out_specs=[pl.BlockSpec(memory_space=pltpu.VMEM)] * 3,
        scratch_shapes=[
            pltpu.VMEM((chips, rows, width), LOW),
            pltpu.VMEM((chips, rows, width), LOW),
            pltpu.VMEM((half_chips, half_chips, rows, width), LOW),
            pltpu.VMEM((half_chips, rows, width), LOW),
            pltpu.VMEM((nb, n) + slab, LOW),
            pltpu.VMEM((n,) + slab, LOW),
            pltpu.VMEM((n,) + slab, LOW),
            pltpu.VMEM((split, steps, 3, half_rows // split, width), LOW),
            pltpu.VMEM((split, 3, half_rows // split, width), LOW),
            pltpu.VMEM((split, 3, half_rows // split, width), LOW),
            pltpu.VMEM((n // 2, 3, shard, width), LOW),
            pltpu.VMEM((chips, 3, shard, width), LOW),
            dma((chips,)),
            dma((chips,)),
            dma((half_chips, chunks)),
            dma((half_chips, half_chips, chunks)),
            dma((half_chips,)),
            dma((half_chips,)),
            dma((half_chips, chunks)),
            dma((chunks,)),
            dma((nb,)),
            dma((nb,)),
            dma((n,)),
            dma((n,)),
            dma((split, steps)),
            dma((split, steps)),
            dma((split,)),
            dma((split,)),
            dma((n // 2,)),
            dma((chips,)),
        ],
        compiler_params=pltpu.CompilerParams(
            collective_id=4, has_side_effects=True, vmem_limit_bytes=63 * MIB
        ),
        name="reduce_grads",
    )(gh, gw, w_half)


def total_kernel(n, nb, value, out, mine, line_in, batch_in, z_send, z_recv, b_send, b_recv):
    me, batch = lax.axis_index("seq"), lax.axis_index("batch")
    greet(n, nb)
    copies = []
    for k in range(1, n):
        copy = push(
            value, line_in.at[k], z_send.at[k], z_recv.at[k], seq=lax.rem(me + k, n)
        )
        copy.start()
        copies.append(copy)
    line_in[0] = value[...]
    for copy in copies:
        copy.wait_recv()
    part = jnp.zeros_like(value)
    for s in range(n):
        part = part + line_in[lax.rem(me - s + n, n)]
    mine[...] = part
    for k in range(1, nb):
        copy = push(
            mine, batch_in.at[k], b_send.at[k], b_recv.at[k], batch=lax.rem(batch + k, nb)
        )
        copy.start()
        copies.append(copy)
    batch_in[0] = part
    for copy in copies[n - 1 :]:
        copy.wait_recv()
    part = jnp.zeros_like(part)
    for s in range(nb):
        part = part + batch_in[lax.rem(batch - s + nb, nb)]
    out[...] = part
    for copy in copies:
        copy.wait_send()


def total_all(n, nb, value):
    dma = pltpu.SemaphoreType.DMA
    return pl.pallas_call(
        functools.partial(total_kernel, n, nb),
        out_shape=jax.ShapeDtypeStruct(value.shape, F32),
        in_specs=[pl.BlockSpec(memory_space=pltpu.VMEM)],
        out_specs=pl.BlockSpec(memory_space=pltpu.VMEM),
        scratch_shapes=[
            pltpu.VMEM(value.shape, F32),
            pltpu.VMEM((n,) + value.shape, F32),
            pltpu.VMEM((nb,) + value.shape, F32),
            dma((n,)),
            dma((n,)),
            dma((nb,)),
            dma((nb,)),
        ],
        compiler_params=pltpu.CompilerParams(collective_id=5, has_side_effects=True),
        name="total_all",
    )(value)


def body(
    n,
    nb,
    tokens,
    cotangent,
    weights,
    gains,
    query_scale,
    first_weights,
    second_weights,
    first_gains,
    second_gains,
    first_scale,
    second_scale,
    lengths,
):
    series_count, rows, width = tokens.shape
    size = query_scale.shape[0]
    group_count = n // 2
    heads = width // size // group_count
    group_width = heads * size
    fold = 640 // group_width
    shard = weights.shape[1]
    slab_width = (3 * group_width + 2 + LANES - 1) // LANES * LANES
    half = lax.axis_index("seq") // group_count
    length = lax.dynamic_slice(lengths, (half,), (1,))

    low_weights = weights.astype(LOW)
    slab = (
        low_weights[:3]
        .reshape(3, shard, group_count, group_width)
        .transpose(2, 1, 0, 3)
        .reshape(group_count, shard, 3 * group_width)
    )
    low_gains = jnp.broadcast_to(gains.astype(LOW).T[None], (group_count, shard, 2))
    spare = jnp.zeros((group_count, shard, slab_width - 3 * group_width - 2), LOW)
    slab = jnp.concatenate([slab, low_gains, spare], axis=2)

    xg, wout, w_all = gather_tokens(n, nb, tokens, slab, low_weights[3:])
    w_all = w_all.transpose(2, 0, 1, 3, 4).reshape(3, width, width)
    wqkv = wout.reshape(nb * n * shard, slab_width)
    gain_rows = wqkv[:, 3 * group_width : 3 * group_width + 2].astype(F32).T
    gain_one, gain_two = gain_rows[0:1], gain_rows[1:2]

    coef = LOG_TWO_E / math.sqrt(size) * jax.nn.softplus(query_scale)
    coef_row = jnp.concatenate([coef, jnp.zeros((LANES - size,), F32)])[None]
    normed_in, qkv, q_full = project(heads, size, xg, wqkv, gain_one, coef_row)
    o_send, o_keep, lse = attend(heads, size, fold, length, qkv, n)
    o_recv = swap_blocks(n, o_send, 2)
    block_out, grad_middle, go_recv, layer_sums, w_half = layer(
        n, nb, fold, tokens, cotangent, o_recv, w_all, gain_two
    )
    layer_sums = jnp.sum(layer_sums, axis=1)
    grad_gain_two = layer_sums[0]
    stat_terms = jnp.sum(layer_sums[1:], axis=1)
    inputs = tokens.astype(F32)
    factor_one = rms_factor(inputs)
    normed_one = inputs * factor_one

    grad_proj, scale_part = attend_back(
        heads, size, fold, length, coef_row, qkv, go_recv, o_keep, lse, q_full, n, slab_width
    )
    grad_slab = jnp.einsum("nrd,nrc->dc", normed_in, grad_proj, preferred_element_type=F32)
    grad_normed_part = jnp.einsum("nrc,dc->nrd", grad_proj, wqkv, preferred_element_type=F32)
    grad_normed, own_slab, own_three = reduce_grads(
        n, nb, grad_normed_part.astype(LOW),
        grad_slab.astype(LOW).reshape(nb, n, shard, slab_width), w_half, shard,
    )
    grad_normed = grad_normed.astype(F32)
    own_qkv = (
        own_slab[:, :, : 3 * group_width]
        .reshape(group_count, shard, 3, group_width)
        .transpose(2, 1, 0, 3)
        .reshape(3, shard, width)
    )
    own_grads = jnp.concatenate([own_qkv, own_three], axis=0)

    grad_gain_one = jnp.sum(grad_normed * normed_one, axis=(0, 1))
    input_grad = grad_middle + norm_back(grad_normed * gain_one, normed_one, factor_one)
    own_squares = jnp.sum(own_grads * own_grads)
    scale_slope = LOG_TWO_E / math.sqrt(size) * jax.nn.sigmoid(query_scale)
    scale_part = jnp.sum(scale_part, axis=0)[:size] * scale_slope
    small = jnp.concatenate(
        [grad_gain_one, grad_gain_two, scale_part, stat_terms, own_squares[None]]
    )
    small_rows = (small.shape[0] + 8 * LANES - 1) // (8 * LANES) * 8
    small = jnp.pad(small, (0, small_rows * LANES - small.shape[0])).reshape(small_rows, LANES)
    sums = total_all(n, nb, small).reshape(-1)
    gain_sums = sums[: 2 * width].reshape(2, width)
    scale_grad = sums[2 * width : 2 * width + size]
    stat_sums = sums[2 * width + size : 2 * width + size + 3]
    total_squares = (
        sums[2 * width + size + 3] + jnp.sum(gain_sums * gain_sums) + jnp.sum(scale_grad * scale_grad)
    )
    index = lax.axis_index("batch") * n + lax.axis_index("seq")
    own_gain_grads = lax.dynamic_slice(gain_sums, (0, index * shard), (2, shard))

    grad_norm = jnp.sqrt(total_squares)
    clip_factor = CLIP_NORM / jnp.maximum(grad_norm, CLIP_NORM)
    new_weights, new_first_weights, new_second_weights = adam_update(
        weights, own_grads * clip_factor, first_weights, second_weights, MATRIX_RATE, MATRIX_DECAY
    )
    new_gains, new_first_gains, new_second_gains = adam_update(
        gains, own_gain_grads * clip_factor, first_gains, second_gains, GAIN_RATE, 0.0
    )
    new_scale, new_first_scale, new_second_scale = adam_update(
        query_scale, scale_grad * clip_factor, first_scale, second_scale, GAIN_RATE, 0.0
    )
    rms_stats = jnp.sqrt(stat_sums / float(series_count * rows * width * nb * n))
    return (
        block_out,
        input_grad,
        grad_norm,
        new_weights,
        new_first_weights,
        new_second_weights,
        new_gains,
        new_first_gains,
        new_second_gains,
        new_scale,
        new_first_scale,
        new_second_scale,
        rms_stats,
    )


def solution(mesh):
    return jax.shard_map(
        functools.partial(body, mesh.shape["seq"], mesh.shape["batch"]),
        mesh=mesh,
        in_specs=(
            P("batch", "seq", None),
            P("batch", "seq", None),
            P(None, ("batch", "seq"), None),
            P(None, ("batch", "seq")),
            P(),
            P(None, ("batch", "seq"), None),
            P(None, ("batch", "seq"), None),
            P(None, ("batch", "seq")),
            P(None, ("batch", "seq")),
            P(),
            P(),
            P("batch"),
        ),
        out_specs=(
            P("batch", "seq", None),
            P("batch", "seq", None),
            P(),
            P(None, ("batch", "seq"), None),
            P(None, ("batch", "seq"), None),
            P(None, ("batch", "seq"), None),
            P(None, ("batch", "seq")),
            P(None, ("batch", "seq")),
            P(None, ("batch", "seq")),
            P(),
            P(),
            P(),
            P(),
        ),
        check_vma=False,
    )
```

```python
import functools
import math

import jax
import jax.numpy as jnp
from jax import lax
from jax.experimental import pallas as pl
from jax.experimental.pallas import tpu as pltpu
from jax.sharding import PartitionSpec as P

STEP = 10

NORM_EPS = 1e-06
LOG_TWO_E = 1.442695
BETA_FIRST = 0.9
BETA_SECOND = 0.999
ADAM_EPS = 1e-08
MATRIX_RATE = 0.05
GAIN_RATE = 0.5
MATRIX_DECAY = 0.1
CLIP_NORM = 1.0
MASKED = -1e30

MESH = pl.DeviceIdType.MESH
LANES = 128
F32 = jnp.float32
LOW = jnp.bfloat16
MIB = 1024 * 1024


def rms_factor(values):
    return lax.rsqrt(jnp.mean(values * values, axis=-1, keepdims=True) + NORM_EPS)


def norm_back(grad_normed, normed, factor):
    return factor * (grad_normed - normed * jnp.mean(grad_normed * normed, axis=-1, keepdims=True))


def silu_slope(values):
    logistic = jax.nn.sigmoid(values)
    return logistic * (1.0 + values * (1.0 - logistic))


def adam_update(current, gradient, moment_one, moment_two, step_rate, decay_rate):
    new_one = BETA_FIRST * moment_one + (1.0 - BETA_FIRST) * gradient
    new_two = BETA_SECOND * moment_two + (1.0 - BETA_SECOND) * gradient * gradient
    first_hat = new_one / (1.0 - BETA_FIRST**STEP)
    second_hat = new_two / (1.0 - BETA_SECOND**STEP)
    updated = current - step_rate * (
        first_hat / (jnp.sqrt(second_hat) + ADAM_EPS) + decay_rate * current
    )
    return (updated, new_one, new_two)


def dot(left, right, left_axis=1, right_axis=0):
    return lax.dot_general(
        left, right, (((left_axis,), (right_axis,)), ((), ())), preferred_element_type=F32
    )


def greet(seq_count, batch_count):
    barrier = pltpu.get_barrier_semaphore()
    me_seq, me_batch = lax.axis_index("seq"), lax.axis_index("batch")
    for k in range(1, seq_count):
        pl.semaphore_signal(
            barrier,
            inc=1,
            device_id={"seq": lax.rem(me_seq + k, seq_count)},
            device_id_type=MESH,
        )
    for k in range(1, batch_count):
        pl.semaphore_signal(
            barrier,
            inc=1,
            device_id={"batch": lax.rem(me_batch + k, batch_count)},
            device_id_type=MESH,
        )
    pl.semaphore_wait(barrier, seq_count - 1 + batch_count - 1)


def push(source, target, send_sem, recv_sem, **where):
    return pltpu.make_async_remote_copy(
        source, target, send_sem, recv_sem, device_id=where, device_id_type=MESH
    )


def place(seq_count):
    me = lax.axis_index("seq")
    chips = seq_count // 2
    half_chips = chips // 2
    core = lax.rem(me, 2)
    chip = me // 2
    half = chip // half_chips
    base = half * half_chips
    gate_mine = half_chips - 1 + half
    gate_other = half_chips - half
    return me, core, chip, half, base, gate_mine, gate_other


def far_chip(step, half, half_chips):
    return (1 - half) * (half_chips + step) + half * (half_chips - 1 - step)


def batch_neighbours(batch):
    across = lax.rem(batch, 2)
    first = batch + 1 - 2 * across
    second = lax.rem(batch + 2, 4)
    return (first, second), lax.rem(first + 2, 4)


class Spread:
    def __init__(self, nb, ref, send, recv):
        self.nb, self.ref, self.send, self.recv = nb, ref, send, recv
        self.batch = lax.axis_index("batch")
        self.copies = []

    def copy(self, owner, slot, j, lane, target):
        block = self.ref.at[owner, slot]
        return push(block, block, self.send.at[j, lane], self.recv.at[j, lane], batch=target)

    def route(self, lane):
        sides, across = batch_neighbours(self.batch)
        return sides[lane % 2], sides[1 - lane % 2], across

    def begin(self, slot, lane):
        if self.nb == 4:
            first, second, _ = self.route(lane)
            new = [self.copy(self.batch, slot, 0, lane, first), self.copy(self.batch, slot, 1, lane, second)]
        else:
            new = [
                self.copy(self.batch, slot, j - 1, lane, lax.rem(self.batch + j, self.nb))
                for j in range(1, self.nb)
            ]
        for copy in new:
            copy.start()
        self.copies += new

    def relay(self, slot, lane):
        if self.nb == 4:
            first, second, _ = self.route(lane)
            self.copy(first, slot, 0, lane, first).wait_recv()
            copy = self.copy(first, slot, 2, lane, second)
            copy.start()
            self.copies.append(copy)
            return [first]
        return []

    def finish(self, slot, lane):
        if self.nb == 4:
            _, second, across = self.route(lane)
            self.copy(second, slot, 1, lane, second).wait_recv()
            self.copy(across, slot, 2, lane, second).wait_recv()
            return [second, across]
        owners = []
        for j in range(1, self.nb):
            owner = lax.rem(self.batch + self.nb - j, self.nb)
            self.copy(owner, slot, j - 1, lane, owner).wait_recv()
            owners.append(owner)
        return owners

    def drain(self):
        for copy in self.copies:
            copy.wait_send()


def gather_kernel(
    n, nb, chunks, tok, slab, xg, wout, far_sem, own_sem, pass_sem, sib_sem, same_recv, sib_recv,
    z_send, z_recv, b_send, b_recv, local_sem,
):
    chips, half_chips = n // 2, n // 4
    me, core, chip, half, base, gate_mine, gate_other = place(n)
    group_count = n // 2
    batch = lax.axis_index("batch")
    rows = tok.shape[1] // chunks
    sibling = 2 * chip + 1 - core
    greet(n, nb)

    sends = []
    z_copies = []
    for k in range(1, n):
        target = lax.rem(me + k, n)
        copy = push(
            slab.at[lax.rem(target, group_count)], wout.at[batch, me], z_send.at[k],
            z_recv.at[k], seq=target,
        )
        copy.start()
        z_copies.append(copy)

    def part(ref, lead, c):
        return ref.at[lead, pl.ds(c * rows, rows)]

    def tok_copy(source, slot, c, send_sem, recv_sem, target):
        return push(source, part(xg, slot, c), send_sem, recv_sem.at[slot, c], seq=target)

    for c in range(chunks):
        copy = tok_copy(
            part(tok, 1 - half, c), me, c, far_sem.at[c], same_recv, 2 * gate_other + core
        )
        copy.start()
        sends.append(copy)
        for k in range(1, half_chips):
            other = base + lax.rem(chip - base + k, half_chips)
            copy = tok_copy(
                part(tok, half, c), me, c, own_sem.at[k, c], same_recv, 2 * other + core
            )
            copy.start()
            sends.append(copy)
        copy = tok_copy(part(tok, half, c), me, c, sib_sem.at[0, c], sib_recv, sibling)
        copy.start()
        sends.append(copy)
    own_copy = pltpu.make_async_copy(tok.at[half], xg.at[me], local_sem.at[0])
    own_copy.start()
    slab_copy = pltpu.make_async_copy(
        slab.at[lax.rem(me, group_count)], wout.at[batch, me], local_sem.at[1]
    )
    slab_copy.start()
    slab_copy.wait()

    slices = Spread(nb, wout, b_send, b_recv)

    def line_slot(k):
        return lax.rem(me + n - k, n)

    def pass_tokens(c):
        for k in range(1, half_chips):
            slot = 2 * (base + lax.rem(chip - base + half_chips - k, half_chips)) + core
            tok_copy(part(xg, slot, c), slot, c, sib_sem.at[k, c], same_recv, sibling).wait_recv()
            copy = tok_copy(part(xg, slot, c), slot, c, sib_sem.at[k, c], sib_recv, sibling)
            copy.start()
            sends.append(copy)
        for k in range(half_chips):
            slot = 2 * far_chip(k, half, half_chips) + core
            lane = half_chips + k
            tok_copy(part(xg, slot, c), slot, c, sib_sem.at[lane, c], same_recv, sibling).wait_recv()

            @pl.when(chip == gate_mine)
            def _():
                for j in range(1, half_chips):
                    other = base + lax.rem(chip - base + j, half_chips)
                    tok_copy(
                        part(xg, slot, c), slot, c, pass_sem.at[k, j, c], same_recv,
                        2 * other + core,
                    ).start()

            copy = tok_copy(part(xg, slot, c), slot, c, sib_sem.at[lane, c], sib_recv, sibling)
            copy.start()
            sends.append(copy)

    slices.begin(me, 0)
    for k in range(1, n):
        z_copies[k - 1].wait_recv()
        slices.begin(line_slot(k), k)
    pass_tokens(0)
    for k in range(n):
        slices.relay(line_slot(k), k)
    for c in range(1, chunks):
        pass_tokens(c)
    for k in range(n):
        slices.finish(line_slot(k), k)
    for c in range(chunks):
        for q in range(chips):
            slot = 2 * q + 1 - core
            tok_copy(part(xg, slot, c), slot, c, sib_sem.at[0, c], sib_recv, sibling).wait_recv()
    own_copy.wait()
    slices.drain()
    for copy in sends + z_copies:
        copy.wait_send()

    @pl.when(chip == gate_mine)
    def _():
        for c in range(chunks):
            for k in range(half_chips):
                for j in range(1, half_chips):
                    tok_copy(
                        part(xg, me, c), me, c, pass_sem.at[k, j, c], same_recv, sibling
                    ).wait_send()


def gather_tokens(n, nb, tokens, slab):
    chunks = 4
    chips, half_chips = n // 2, n // 4
    dma = pltpu.SemaphoreType.DMA
    return pl.pallas_call(
        functools.partial(gather_kernel, n, nb, chunks),
        out_shape=(
            jax.ShapeDtypeStruct((n,) + tokens.shape[1:], tokens.dtype),
            jax.ShapeDtypeStruct((nb, n) + slab.shape[1:], slab.dtype),
        ),
        in_specs=[pl.BlockSpec(memory_space=pl.ANY)] * 2,
        out_specs=[pl.BlockSpec(memory_space=pl.ANY)] * 2,
        scratch_shapes=[
            dma((chunks,)),
            dma((half_chips, chunks)),
            dma((half_chips, half_chips, chunks)),
            dma((chips, chunks)),
            dma((n, chunks)),
            dma((n, chunks)),
            dma((n,)),
            dma((n,)),
            dma((nb, n)),
            dma((nb, n)),
            dma((2,)),
        ],
        compiler_params=pltpu.CompilerParams(collective_id=1, has_side_effects=True),
        name="gather_tokens",
    )(tokens, slab)


def widen(values):
    rows, width = values.shape
    return jnp.concatenate([values, jnp.zeros((rows, LANES - width), values.dtype)], axis=1)


def attend_kernel(
    n, nb, heads, size, fold, len_ref, x_in, w_ref, gain_ref, coef_ref, own_w, h_out, qkv_out, q_out,
    keep_out, lse_out, o_out, w_all, x_s, qkv_s, q_s, keep_s, o_s, s_s, m_s, acc_s, sum_s, bias_s,
    x_sem, h_sem, qkv_sem, q_sem, keep_sem, local_sem, o_send, o_recv, wz_send, wz_recv, wb_send,
    wb_recv, ws_send, ws_recv,
):
    chips = n // 2
    me, core, chip, *_ = place(n)
    batch = lax.axis_index("batch")
    sibling = 2 * chip + 1 - core
    block = x_in.shape[1]
    group = range(heads)
    greet(n, nb)

    sends = []
    w_copies = []
    for k in range(1, chips):
        target = 2 * lax.rem(chip + k, chips) + core
        copy = push(own_w, w_all.at[batch, me], wz_send.at[k], wz_recv.at[k], seq=target)
        copy.start()
        w_copies.append(copy)
    w_copy = pltpu.make_async_copy(own_w, w_all.at[batch, me], local_sem.at[0])
    w_copy.start()

    def x_load(i):
        return pltpu.make_async_copy(x_in.at[i], x_s.at[i], x_sem.at[i])

    for i in range(n):
        x_load(i).start()
    length = len_ref[0]

    @pl.loop(0, n)
    def _(j):
        col = j * block + lax.broadcasted_iota(jnp.int32, (8, block), 1)
        bias_s[j] = jnp.where(col < length, 0.0, MASKED)

    whole = Spread(nb, w_all, wb_send, wb_recv)

    def chip_slot(k):
        return 2 * lax.rem(chip + chips - k, chips) + core

    def to_sibling(owner, lane, slot, j):
        piece = w_all.at[owner, slot]
        copy = push(piece, piece, ws_send.at[j, lane], ws_recv.at[owner, slot], seq=sibling)
        copy.start()
        sends.append(copy)

    w_copy.wait()
    whole.begin(me, 0)
    to_sibling(batch, 0, me, 0)

    def kept(i):
        return [
            pltpu.make_async_copy(x_s.at[i], h_out.at[i], h_sem.at[i]),
            pltpu.make_async_copy(qkv_s.at[i], qkv_out.at[i], qkv_sem.at[i]),
            pltpu.make_async_copy(q_s.at[i], q_out.at[i], q_sem.at[i]),
            pltpu.make_async_copy(keep_s.at[i], keep_out.at[i], keep_sem.at[i]),
        ]

    def o_push(i):
        return push(o_s.at[i], o_out.at[me], o_send.at[i], o_recv.at[me], seq=i)

    own_o = pltpu.make_async_copy(o_s.at[me], o_out.at[me], local_sem.at[1])

    def project(i):
        x = x_s[i].astype(F32)
        h = (x * rms_factor(x) * gain_ref[...]).astype(LOW)
        x_s[i] = h
        out = dot(h, w_ref[...])
        for a in group:
            q = widen(out[:, a * size : (a + 1) * size])
            q_s[i, a] = q
            qkv_s[i, a] = (q * coef_ref[...]).astype(LOW)
        for a in range(heads, 3 * heads):
            qkv_s[i, a] = widen(out[:, a * size : (a + 1) * size].astype(LOW))

    def score(i, j, diagonal):
        if diagonal:
            row = lax.broadcasted_iota(jnp.int32, (block, block), 0)
            col = lax.broadcasted_iota(jnp.int32, (block, block), 1)
            visible = col <= row
        for a in group:
            s = dot(qkv_s[i, a], qkv_s[j, heads + a], 1, 1) + bias_s[j, :1]
            if diagonal:
                s = jnp.where(visible, s, MASKED)
            s_s[a, j] = s
            best = m_s[a]
            for part in range(block // LANES):
                best = jnp.maximum(best, s[:, part * LANES : (part + 1) * LANES])
            m_s[a] = best

    def mix(j):
        for a in group:
            best = m_s[a]
            count = sum_s[a]
            pieces = []
            for part in range(block // LANES):
                e = jnp.exp(s_s[a, j, :, part * LANES : (part + 1) * LANES] - best)
                count = count + e
                pieces.append(e.astype(LOW))
            sum_s[a] = count
            acc_s[a] += dot(jnp.concatenate(pieces, axis=1), qkv_s[j, 2 * heads + a])

    def query_block(i):
        x_load(i).wait()
        project(i)
        m_s[...] = jnp.full_like(m_s, MASKED)
        sum_s[...] = jnp.zeros_like(sum_s)
        acc_s[...] = jnp.zeros_like(acc_s)
        pl.loop(0, i)(lambda j: score(i, j, False))
        score(i, i, True)
        for a in group:
            m_s[a] = jnp.broadcast_to(jnp.max(m_s[a], axis=1, keepdims=True), (block, LANES))
        pl.loop(0, i + 1)(mix)
        outs = []
        for a in group:
            count = jnp.sum(sum_s[a], axis=1, keepdims=True)
            out = acc_s[a] / count
            keep_s[i, a] = out
            outs.append(out[:, :size])
            lse_out[i, a] = (m_s[a] + jnp.log(count)).T[:8]
        low = jnp.concatenate(outs, axis=1).astype(LOW)
        piece = block // fold
        o_s[i] = jnp.concatenate([low[f * piece : (f + 1) * piece] for f in range(fold)], axis=1)
        for copy in kept(i):
            copy.start()

        @pl.when(i != me)
        def _():
            o_push(i).start()

        @pl.when(i == me)
        def _():
            own_o.start()

    first, second = n // 2 + 1, n - 1
    pl.loop(0, first)(query_block)
    for k in range(1, chips):
        w_copies[k - 1].wait_recv()
        whole.begin(chip_slot(k), k)
        to_sibling(batch, k, chip_slot(k), 0)
    if second > first:
        pl.loop(first, second)(query_block)
    for k in range(chips):
        for j, owner in enumerate(whole.relay(chip_slot(k), k)):
            to_sibling(owner, k, chip_slot(k), 1 + j)
    pl.loop(second, n)(query_block)
    for k in range(chips):
        owners = whole.finish(chip_slot(k), k)
        for j, owner in enumerate(owners):
            to_sibling(owner, k, chip_slot(k), nb - len(owners) + j)

    for k in range(1, n):
        source = lax.rem(me + k, n)
        push(
            o_s.at[source], o_out.at[source], o_send.at[source], o_recv.at[source], seq=source
        ).wait()
    own_o.wait()
    for owner in range(nb):
        for q in range(chips):
            piece = w_all.at[owner, 2 * q + 1 - core]
            push(
                piece, piece, ws_send.at[0, 0], ws_recv.at[owner, 2 * q + 1 - core], seq=sibling
            ).wait_recv()
    whole.drain()
    for copy in sends + w_copies:
        copy.wait_send()

    @pl.loop(0, n)
    def _(i):
        for copy in kept(i):
            copy.wait()


def attend(n, nb, heads, size, fold, length, xg, wqkv, gain, coef, own_w):
    _, rows, width = xg.shape
    chips = n // 2
    folded = (n, rows // fold, heads * size * fold)
    many, one = (n, 3 * heads, rows, LANES), (n, heads, rows, LANES)
    dma = pltpu.SemaphoreType.DMA
    vmem = pl.BlockSpec(memory_space=pltpu.VMEM)
    anywhere = pl.BlockSpec(memory_space=pl.ANY)
    state = pltpu.VMEM((heads, rows, LANES), F32)
    return pl.pallas_call(
        functools.partial(attend_kernel, n, nb, heads, size, fold),
        out_shape=(
            jax.ShapeDtypeStruct(xg.shape, LOW),
            jax.ShapeDtypeStruct(many, LOW),
            jax.ShapeDtypeStruct(one, F32),
            jax.ShapeDtypeStruct(one, F32),
            jax.ShapeDtypeStruct((n, heads, 8, rows), F32),
            jax.ShapeDtypeStruct(folded, LOW),
            jax.ShapeDtypeStruct((nb, n) + own_w.shape, LOW),
        ),
        in_specs=[pl.BlockSpec(memory_space=pltpu.SMEM), anywhere, vmem, vmem, vmem, anywhere],
        out_specs=[anywhere, anywhere, anywhere, anywhere, vmem, anywhere, anywhere],
        scratch_shapes=[
            pltpu.VMEM(xg.shape, LOW),
            pltpu.VMEM(many, LOW),
            pltpu.VMEM(one, F32),
            pltpu.VMEM(one, F32),
            pltpu.VMEM(folded, LOW),
            pltpu.VMEM((heads, n, rows, rows), F32),
            state,
            state,
            state,
            pltpu.VMEM((n, 8, rows), F32),
            dma((n,)),
            dma((n,)),
            dma((n,)),
            dma((n,)),
            dma((n,)),
            dma((2,)),
            dma((n,)),
            dma((n,)),
            dma((chips,)),
            dma((chips,)),
            dma((nb, chips)),
            dma((nb, chips)),
            dma((nb, chips)),
            dma((nb, n)),
        ],
        compiler_params=pltpu.CompilerParams(
            collective_id=2, has_side_effects=True, vmem_limit_bytes=62 * MIB
        ),
        name="attend",
    )(length, xg, wqkv, gain, coef, own_w)


def attend_back_kernel(
    heads, size, fold, n, len_ref, coef_ref, q_ref, k_ref, v_ref, go_ref, keep_ref, lse_ref, qf_ref,
    out_ref, scale_ref, kt_ref, gq_ref, gqt_ref, gk_ref, gv_ref, g_ref, delta_ref,
):
    i = pl.program_id(0)
    block = q_ref.shape[2]
    length = len_ref[0]
    whole = jnp.minimum(i, length // block)
    total = jnp.minimum(i + 1, pl.cdiv(length, block))

    @pl.when(i == 0)
    def _():
        gk_ref[...] = jnp.zeros_like(gk_ref)
        gv_ref[...] = jnp.zeros_like(gv_ref)
        scale_ref[...] = jnp.zeros_like(scale_ref)

        @pl.loop(0, n)
        def _(j):
            keys = pl.ds(pl.multiple_of(j * block, block), block)
            for a in range(heads):
                kt_ref[a, j] = k_ref[j, a].T

    gqt_ref[...] = jnp.zeros_like(gqt_ref)
    for a in range(heads):
        g = widen(
            jnp.concatenate(
                [
                    go_ref[0, :, (f * heads + a) * size : (f * heads + a + 1) * size]
                    for f in range(fold)
                ],
                axis=0,
            )
        )
        g_ref[a] = g
        delta_ref[a] = jnp.broadcast_to(
            jnp.sum((g.astype(F32) * keep_ref[0, a]).T, axis=0, keepdims=True), (8, block)
        )

    def back(j, masked):
        keys = pl.ds(pl.multiple_of(j * block, block), block)
        if masked:
            col = j * block + lax.broadcasted_iota(jnp.int32, (block, block), 0)
            row = i * block + lax.broadcasted_iota(jnp.int32, (block, block), 1)
            visible = (col <= row) & (col < length)
        for a in range(heads):
            s = dot(k_ref[j, a], q_ref[0, a], 1, 1)
            p = jnp.exp(s - lse_ref[0, a, :1])
            if masked:
                p = jnp.where(visible, p, 0.0)
            dp = dot(v_ref[j, a], g_ref[a], 1, 1)
            ds = (p * (dp - delta_ref[a, :1])).astype(LOW)
            gk_ref[a, keys] += dot(ds, q_ref[0, a])
            gv_ref[a, keys] += dot(p.astype(LOW), g_ref[a])
            gqt_ref[a] += dot(kt_ref[a, j], ds)

    pl.loop(0, whole)(lambda j: back(j, False))
    pl.loop(whole, total)(lambda j: back(j, True))

    rows = pl.ds(pl.multiple_of(i * block, block), block)
    for a in range(heads):
        grad = gqt_ref[a].T.astype(LOW).astype(F32)
        scale_ref[...] += jnp.sum((grad * qf_ref[0, a]).reshape(block // 8, 8, LANES), axis=0)
        gq_ref[a, rows] = (grad * coef_ref[...]).astype(LOW)

    @pl.when(i == n - 1)
    def _():
        @pl.loop(0, n)
        def _(j):
            keys = pl.ds(pl.multiple_of(j * block, block), block)
            pieces = [gq_ref[a, keys][:, :size] for a in range(heads)]
            pieces += [gk_ref[a, keys][:, :size].astype(LOW) for a in range(heads)]
            pieces += [gv_ref[a, keys][:, :size].astype(LOW) for a in range(heads)]
            spare = out_ref.shape[2] - 3 * heads * size
            pieces.append(jnp.zeros((block, spare), LOW))
            out_ref[j] = jnp.concatenate(pieces, axis=1)


def attend_back(heads, size, fold, length, coef, qkv, go, keep, lse, q_full, n, slab_width):
    block = qkv.shape[2]
    full = n * block
    width = heads * size * fold
    return pl.pallas_call(
        functools.partial(attend_back_kernel, heads, size, fold, n),
        grid=(n,),
        out_shape=(
            jax.ShapeDtypeStruct((n, block, slab_width), LOW),
            jax.ShapeDtypeStruct((8, LANES), F32),
        ),
        in_specs=[
            pl.BlockSpec(memory_space=pltpu.SMEM),
            pl.BlockSpec(coef.shape, lambda i: (0, 0)),
            pl.BlockSpec((1, heads, block, LANES), lambda i: (i, 0, 0, 0)),
            pl.BlockSpec((n, heads, block, LANES), lambda i: (0, 1, 0, 0)),
            pl.BlockSpec((n, heads, block, LANES), lambda i: (0, 2, 0, 0)),
            pl.BlockSpec((1, block // fold, width), lambda i: (i, 0, 0)),
            pl.BlockSpec((1, heads, block, LANES), lambda i: (i, 0, 0, 0)),
            pl.BlockSpec((1, heads, 8, block), lambda i: (i, 0, 0, 0)),
            pl.BlockSpec((1, heads, block, LANES), lambda i: (i, 0, 0, 0)),
        ],
        out_specs=[
            pl.BlockSpec((n, block, slab_width), lambda i: (0, 0, 0)),
            pl.BlockSpec((8, LANES), lambda i: (0, 0)),
        ],
        scratch_shapes=[
            pltpu.VMEM((heads, n, LANES, block), LOW),
            pltpu.VMEM((heads, full, LANES), LOW),
            pltpu.VMEM((heads, LANES, block), F32),
            pltpu.VMEM((heads, full, LANES), F32),
            pltpu.VMEM((heads, full, LANES), F32),
            pltpu.VMEM((heads, block, LANES), LOW),
            pltpu.VMEM((heads, 8, block), F32),
        ],
        compiler_params=pltpu.CompilerParams(vmem_limit_bytes=56 * MIB),
        name="attend_back",
    )(length, coef, qkv, qkv, qkv, go, keep, lse, q_full)


def fold_rows(values):
    rows, width = values.shape
    return jnp.sum(values.reshape(rows // 8, 8, width), axis=0)


def layer_kernel(
    n, nb, fold, tok, cot, o_in, w_in, gain_ref, y_out, gy_out, go_out, small_out, half_out,
    w, o_s, hidden_s, act_s, gu_s, ga_s, go_s, gw_s, sib_in, w_sem, send_sem, recv_sem, local_sem,
    sib_send, sib_recv,
):
    group_count = n // 2
    me, core, chip, half, base, gate_mine, gate_other = place(n)
    sibling = 2 * chip + 1 - core
    _, rows, width = tok.shape
    group_width = width // group_count
    piece = rows // fold
    barrier = pltpu.get_barrier_semaphore()
    for k in range(1, n):
        pl.semaphore_signal(
            barrier, inc=1, device_id={"seq": lax.rem(me + k, n)}, device_id_type=MESH
        )
    loads = [pltpu.make_async_copy(w_in.at[m], w.at[m], w_sem.at[m]) for m in range(3)]
    for load in loads:
        load.start()
    small_out[...] = jnp.zeros_like(small_out)
    gain = gain_ref[...]

    def go_push(target):
        return push(
            go_s.at[target], go_out.at[me], send_sem.at[target], recv_sem.at[me], seq=target
        )

    own_go = pltpu.make_async_copy(go_s.at[me], go_out.at[me], local_sem)

    for t in range(2):
        parts = [
            jnp.concatenate(
                [
                    o_in[t * group_count + g, :, f * group_width : (f + 1) * group_width]
                    for g in range(group_count)
                ],
                axis=1,
            )
            for f in range(fold)
        ]
        o = jnp.concatenate(parts, axis=0)
        o_s[t] = o
        if t == 0:
            loads[0].wait()
        a = dot(o, w[0])
        small_out[1] += fold_rows(a * a)
        y1 = tok[t].astype(F32) + a
        factor = rms_factor(y1)
        normed = y1 * factor
        hidden = (normed * gain).astype(LOW)
        hidden_s[t] = hidden
        if t == 0:
            loads[1].wait()
        u = dot(hidden, w[1])
        logistic = 1.0 / (1.0 + jnp.exp(-u))
        act = (u * logistic).astype(LOW)
        act_s[t] = act
        if t == 0:
            loads[2].wait()
        f = dot(act, w[2])
        small_out[2] += fold_rows(f * f)
        y = y1 + f
        small_out[3] += fold_rows(y * y)
        y_out[t] = y.astype(LOW)
        gz = dot(cot[t], w[2], 1, 1)
        gu = (gz * (logistic * (1.0 + u * (1.0 - logistic)))).astype(LOW)
        gu_s[t] = gu
        gh = dot(gu, w[1], 1, 1)
        small_out[0] += fold_rows(gh * normed)
        gy = cot[t].astype(F32) + norm_back(gh * gain, normed, factor)
        gy_out[t] = gy
        ga = gy.astype(LOW)
        ga_s[t] = ga
        go = dot(ga, w[0], 1, 1).astype(LOW)
        for g in range(group_count):
            block = go[:, g * group_width : (g + 1) * group_width]
            go_s[t * group_count + g] = jnp.concatenate(
                [block[f * piece : (f + 1) * piece] for f in range(fold)], axis=1
            )
        if t == 0:
            pl.semaphore_wait(barrier, n - 1)
        for g in range(group_count):
            target = t * group_count + g

            @pl.when(target != me)
            def _():
                go_push(target).start()

            @pl.when(target == me)
            def _():
                own_go.start()

    tile = 256
    half_rows = width // nb // 2
    sib_copies = []
    pairs = ((act_s, cot, 2), (hidden_s, gu_s, 1), (o_s, ga_s, 0))
    for left, right, m in pairs:

        @pl.loop(0, width // tile)
        def _(k):
            cols = pl.ds(pl.multiple_of(k * tile, tile), tile)
            total = dot(left[0, :, cols], right[0], 0, 0) + dot(left[1, :, cols], right[1], 0, 0)
            gw_s[m, cols] = total.astype(LOW)

        for b in range(nb):
            start = pl.multiple_of((2 * b + 1 - core) * half_rows, 16)
            copy = push(
                gw_s.at[m, pl.ds(start, half_rows)], sib_in.at[b, m], sib_send.at[b, m],
                sib_recv.at[b, m], seq=sibling,
            )
            copy.start()
            sib_copies.append(copy)
    index = 0
    for _, _, m in pairs:
        for b in range(nb):
            sib_copies[index].wait_recv()
            index += 1
            start = pl.multiple_of((2 * b + core) * half_rows, 16)
            half_out[b, m] = (
                gw_s[m, pl.ds(start, half_rows)].astype(F32) + sib_in[b, m].astype(F32)
            ).astype(LOW)
    for k in range(1, n):
        source = lax.rem(me + k, n)
        push(
            go_s.at[source], go_out.at[source], send_sem.at[source], recv_sem.at[source], seq=source
        ).wait()
    own_go.wait()
    for copy in sib_copies:
        copy.wait_send()


def layer(n, nb, fold, tokens, cotangent, o_recv, w_all, gain):
    _, rows, width = tokens.shape
    half_rows = width // nb // 2
    dma = pltpu.SemaphoreType.DMA
    vmem = pl.BlockSpec(memory_space=pltpu.VMEM)
    anywhere = pl.BlockSpec(memory_space=pl.ANY)
    kept = pltpu.VMEM((2, rows, width), LOW)
    return pl.pallas_call(
        functools.partial(layer_kernel, n, nb, fold),
        out_shape=(
            jax.ShapeDtypeStruct((2, rows, width), LOW),
            jax.ShapeDtypeStruct((2, rows, width), F32),
            jax.ShapeDtypeStruct(o_recv.shape, LOW),
            jax.ShapeDtypeStruct((4, 8, width), F32),
            jax.ShapeDtypeStruct((nb, 3, half_rows, width), LOW),
        ),
        in_specs=[vmem, vmem, vmem, anywhere, vmem],
        out_specs=[vmem, vmem, anywhere, vmem, vmem],
        scratch_shapes=[
            pltpu.VMEM((3, width, width), LOW),
            kept,
            kept,
            kept,
            kept,
            kept,
            pltpu.VMEM(o_recv.shape, LOW),
            pltpu.VMEM((3, width, width), LOW),
            pltpu.VMEM((nb, 3, half_rows, width), LOW),
            dma((3,)),
            dma((n,)),
            dma((n,)),
            dma,
            dma((nb, 3)),
            dma((nb, 3)),
        ],
        compiler_params=pltpu.CompilerParams(
            collective_id=3, has_side_effects=True, vmem_limit_bytes=63 * MIB
        ),
        name="layer",
    )(tokens, cotangent, o_recv, w_all, gain)


def reduce_kernel(
    n, nb, chunks, gh, gw, w_half, out, own_gw, own_w, from_sib, total, gate_in, peer_in, batch_in,
    line_out, line_in, cross_in, cross_out, turn_in, w_line, w_in, sib_send, sib_recv, gate_send,
    gate_recv, peer_send, peer_recv, far_send, far_recv, b_send, b_recv, z_send, z_recv, c_send,
    c_recv, t_send, t_recv, w_send, w_recv,
):
    chips, half_chips = n // 2, n // 4
    me, core, chip, half, base, gate_mine, gate_other = place(n)
    group_count = n // 2
    batch = lax.axis_index("batch")
    rows = gh.shape[1] // chunks
    sibling = 2 * chip + 1 - core
    greet(n, nb)

    split = 2 if nb == 4 else 1
    w_rows = w_half.shape[2] // split
    sides, across = batch_neighbours(batch)

    def w_part(b, h):
        return w_half.at[b, :, pl.ds(h * w_rows, w_rows)]

    w_copies = []
    if nb == 4:
        for h in range(2):
            for j, owner in enumerate((across, sides[h])):
                copy = push(
                    w_part(owner, h), cross_in.at[h, j], c_send.at[h, j], c_recv.at[h, j],
                    batch=sides[h],
                )
                copy.start()
                w_copies.append(copy)
    else:
        for k in range(1, nb):
            target = lax.rem(batch + k, nb)
            copy = push(
                w_half.at[target], cross_in.at[0, k], c_send.at[0, k], c_recv.at[0, k], batch=target
            )
            copy.start()
            w_copies.append(copy)

    b_copies = []
    for k in range(1, nb):
        target = lax.rem(batch + k, nb)
        copy = push(gw.at[target], batch_in.at[k], b_send.at[k], b_recv.at[k], batch=target)
        copy.start()
        b_copies.append(copy)

    order = [far_chip(half_chips - 1 - k, half, half_chips) for k in range(half_chips)]
    order += [base + lax.rem(chip - base + k, half_chips) for k in range(1, half_chips)]
    order += [chip]
    sib_copies = []
    for k, q in enumerate(order):
        copy = push(
            gh.at[2 * q + 1 - core], from_sib.at[q], sib_send.at[q], sib_recv.at[q], seq=sibling
        )
        copy.start()
        sib_copies.append(copy)

    def part(ref, lead, c):
        return ref.at[lead, pl.ds(c * rows, rows)]

    def add_sibling(k):
        q = order[k]
        sib_copies[k].wait_recv()
        total[q] = (gh[2 * q + core].astype(F32) + from_sib[q].astype(F32)).astype(LOW)

    def send_peer(k):
        q = order[half_chips + k - 1]
        copy = push(
            total.at[q], peer_in.at[k], peer_send.at[k], peer_recv.at[k], seq=2 * q + core
        )
        copy.start()
        return copy

    def gate_copy(j, k, c):
        return push(
            part(total, order[k], c), gate_in.at[j, k, pl.ds(c * rows, rows)],
            gate_send.at[k, c], gate_recv.at[j, k, c], seq=2 * gate_mine + core,
        )

    def far_copy(k, c):
        return push(
            part(total, order[k], c), part(out, half, c), far_send.at[k, c], far_recv.at[c],
            seq=2 * order[k] + core,
        )

    @pl.when(chip == gate_mine)
    def _():
        for k in range(1, half_chips):
            add_sibling(half_chips + k - 1)
            send_peer(k)
        for k in range(half_chips):
            add_sibling(k)
        for k in range(half_chips):
            for c in range(chunks):
                span = pl.ds(c * rows, rows)
                value = total[order[k], span].astype(F32)
                for j in range(1, half_chips):
                    gate_copy(j, k, c).wait_recv()
                    value = value + gate_in[j, k, span].astype(F32)
                total[order[k], span] = value.astype(LOW)
                far_copy(k, c).start()

    @pl.when(chip != gate_mine)
    def _():
        after = lax.rem(chip - gate_mine + half_chips, half_chips)
        for k in range(half_chips):
            add_sibling(k)
            for c in range(chunks):
                gate_copy(after, k, c).start()
        for k in range(1, half_chips):
            add_sibling(half_chips + k - 1)
            send_peer(k)

    add_sibling(chips - 1)

    t_copies = []
    if nb == 4:
        for h in range(2):
            w_copies[2 * h].wait_recv()
            span = pl.ds(h * w_rows, w_rows)
            cross_out[h] = (
                w_half[sides[1 - h], :, span].astype(F32) + cross_in[h, 0].astype(F32)
            ).astype(LOW)
            copy = push(
                cross_out.at[h], turn_in.at[h], t_send.at[h], t_recv.at[h], batch=sides[1 - h]
            )
            copy.start()
            t_copies.append(copy)

    for copy in b_copies:
        copy.wait_recv()

    @pl.loop(0, n)
    def _(s):
        value = gw[batch, s].astype(F32)
        for k in range(1, nb):
            value = value + batch_in[k, s].astype(F32)
        line_out[s] = value.astype(LOW)

    z_copies = []
    for k in range(1, n):
        target = lax.rem(me + k, n)
        copy = push(line_out.at[target], line_in.at[me], z_send.at[k], z_recv.at[k], seq=target)
        copy.start()
        z_copies.append(copy)
    line_in[me] = line_out[me]

    shard = own_w.shape[1]
    parts = []
    if nb == 4:
        for h in range(2):
            w_copies[2 * h + 1].wait_recv()
            t_copies[h].wait_recv()
            span = pl.ds(h * w_rows, w_rows)
            parts.append(
                w_half[batch, :, span].astype(F32)
                + cross_in[h, 1].astype(F32)
                + turn_in[h].astype(F32)
            )
    else:
        value = w_half[batch].astype(F32)
        for k in range(1, nb):
            w_copies[k - 1].wait_recv()
            value = value + cross_in[0, k].astype(F32)
        parts.append(value)
    summed = jnp.concatenate(parts, axis=1)
    for i in range(group_count):
        w_line[i] = summed[:, i * shard : (i + 1) * shard].astype(LOW)

    def w_push(i):
        target = core * group_count + i
        return push(w_line.at[i], w_in.at[chip], w_send.at[i], w_recv.at[chip], seq=target)

    for i in range(group_count):
        mine = core * group_count + i == me

        @pl.when(mine)
        def _():
            w_in[chip] = w_line[i]

        @pl.when(jnp.logical_not(mine))
        def _():
            w_push(i).start()

    value = total[chip].astype(F32)
    for k in range(1, half_chips):
        push(
            total.at[chip], peer_in.at[k], peer_send.at[k], peer_recv.at[k], seq=sibling
        ).wait_recv()
        value = value + peer_in[k].astype(F32)
    out[half] = value.astype(LOW)
    for c in range(chunks):
        push(
            part(total, 0, c), part(out, 1 - half, c), far_send.at[0, c], far_recv.at[c], seq=sibling
        ).wait_recv()
    for copy in z_copies:
        copy.wait_recv()
    for g in range(group_count):
        own_gw[g] = line_in[g].astype(F32) + line_in[g + group_count].astype(F32)

    for q in range(chips):

        @pl.when(2 * q + half != me)
        def _():
            push(
                w_line.at[0], w_in.at[q], w_send.at[0], w_recv.at[q], seq=sibling
            ).wait_recv()

    value = w_in[0].astype(F32)
    for q in range(1, chips):
        value = value + w_in[q].astype(F32)
    own_w[...] = value
    for i in range(group_count):

        @pl.when(core * group_count + i != me)
        def _():
            w_push(i).wait_send()

    for copy in b_copies + sib_copies + z_copies + w_copies + t_copies:
        copy.wait_send()
    for k in range(1, half_chips):
        push(
            total.at[chip], peer_in.at[k], peer_send.at[k], peer_recv.at[k], seq=sibling
        ).wait_send()

    @pl.when(chip == gate_mine)
    def _():
        for k in range(half_chips):
            for c in range(chunks):
                far_copy(k, c).wait_send()

    @pl.when(chip != gate_mine)
    def _():
        for k in range(half_chips):
            for c in range(chunks):
                gate_copy(1, k, c).wait_send()


def reduce_grads(n, nb, gh, gw, w_half, shard):
    chunks = 4
    chips, half_chips = n // 2, n // 4
    _, rows, width = gh.shape
    slab = gw.shape[2:]
    half_rows = w_half.shape[2]
    split = 2 if nb == 4 else 1
    steps = 2 if nb == 4 else nb
    dma = pltpu.SemaphoreType.DMA
    return pl.pallas_call(
        functools.partial(reduce_kernel, n, nb, chunks),
        out_shape=(
            jax.ShapeDtypeStruct((2, rows, width), LOW),
            jax.ShapeDtypeStruct((n // 2,) + slab, F32),
            jax.ShapeDtypeStruct((3, shard, width), F32),
        ),
        in_specs=[pl.BlockSpec(memory_space=pltpu.VMEM)] * 3,
        out_specs=[pl.BlockSpec(memory_space=pltpu.VMEM)] * 3,
        scratch_shapes=[
            pltpu.VMEM((chips, rows, width), LOW),
            pltpu.VMEM((chips, rows, width), LOW),
            pltpu.VMEM((half_chips, half_chips, rows, width), LOW),
            pltpu.VMEM((half_chips, rows, width), LOW),
            pltpu.VMEM((nb, n) + slab, LOW),
            pltpu.VMEM((n,) + slab, LOW),
            pltpu.VMEM((n,) + slab, LOW),
            pltpu.VMEM((split, steps, 3, half_rows // split, width), LOW),
            pltpu.VMEM((split, 3, half_rows // split, width), LOW),
            pltpu.VMEM((split, 3, half_rows // split, width), LOW),
            pltpu.VMEM((n // 2, 3, shard, width), LOW),
            pltpu.VMEM((chips, 3, shard, width), LOW),
            dma((chips,)),
            dma((chips,)),
            dma((half_chips, chunks)),
            dma((half_chips, half_chips, chunks)),
            dma((half_chips,)),
            dma((half_chips,)),
            dma((half_chips, chunks)),
            dma((chunks,)),
            dma((nb,)),
            dma((nb,)),
            dma((n,)),
            dma((n,)),
            dma((split, steps)),
            dma((split, steps)),
            dma((split,)),
            dma((split,)),
            dma((n // 2,)),
            dma((chips,)),
        ],
        compiler_params=pltpu.CompilerParams(
            collective_id=4, has_side_effects=True, vmem_limit_bytes=63 * MIB
        ),
        name="reduce_grads",
    )(gh, gw, w_half)


def total_kernel(n, nb, value, out, mine, line_in, batch_in, z_send, z_recv, b_send, b_recv):
    me, batch = lax.axis_index("seq"), lax.axis_index("batch")
    greet(n, nb)
    copies = []
    for k in range(1, n):
        copy = push(
            value, line_in.at[k], z_send.at[k], z_recv.at[k], seq=lax.rem(me + k, n)
        )
        copy.start()
        copies.append(copy)
    line_in[0] = value[...]
    for copy in copies:
        copy.wait_recv()
    part = jnp.zeros_like(value)
    for s in range(n):
        part = part + line_in[lax.rem(me - s + n, n)]
    mine[...] = part
    for k in range(1, nb):
        copy = push(
            mine, batch_in.at[k], b_send.at[k], b_recv.at[k], batch=lax.rem(batch + k, nb)
        )
        copy.start()
        copies.append(copy)
    batch_in[0] = part
    for copy in copies[n - 1 :]:
        copy.wait_recv()
    part = jnp.zeros_like(part)
    for s in range(nb):
        part = part + batch_in[lax.rem(batch - s + nb, nb)]
    out[...] = part
    for copy in copies:
        copy.wait_send()


def total_all(n, nb, value):
    dma = pltpu.SemaphoreType.DMA
    return pl.pallas_call(
        functools.partial(total_kernel, n, nb),
        out_shape=jax.ShapeDtypeStruct(value.shape, F32),
        in_specs=[pl.BlockSpec(memory_space=pltpu.VMEM)],
        out_specs=pl.BlockSpec(memory_space=pltpu.VMEM),
        scratch_shapes=[
            pltpu.VMEM(value.shape, F32),
            pltpu.VMEM((n,) + value.shape, F32),
            pltpu.VMEM((nb,) + value.shape, F32),
            dma((n,)),
            dma((n,)),
            dma((nb,)),
            dma((nb,)),
        ],
        compiler_params=pltpu.CompilerParams(collective_id=5, has_side_effects=True),
        name="total_all",
    )(value)


def body(
    n,
    nb,
    tokens,
    cotangent,
    weights,
    gains,
    query_scale,
    first_weights,
    second_weights,
    first_gains,
    second_gains,
    first_scale,
    second_scale,
    lengths,
):
    series_count, rows, width = tokens.shape
    size = query_scale.shape[0]
    group_count = n // 2
    heads = width // size // group_count
    group_width = heads * size
    fold = 640 // group_width
    shard = weights.shape[1]
    slab_width = (3 * group_width + 2 + LANES - 1) // LANES * LANES
    half = lax.axis_index("seq") // group_count
    length = lax.dynamic_slice(lengths, (half,), (1,))

    low_weights = weights.astype(LOW)
    slab = (
        low_weights[:3]
        .reshape(3, shard, group_count, group_width)
        .transpose(2, 1, 0, 3)
        .reshape(group_count, shard, 3 * group_width)
    )
    low_gains = jnp.broadcast_to(gains.astype(LOW).T[None], (group_count, shard, 2))
    spare = jnp.zeros((group_count, shard, slab_width - 3 * group_width - 2), LOW)
    slab = jnp.concatenate([slab, low_gains, spare], axis=2)

    xg, wout = gather_tokens(n, nb, tokens, slab)
    wqkv = wout.reshape(nb * n * shard, slab_width)
    gain_rows = wqkv[:, 3 * group_width : 3 * group_width + 2].astype(F32).T
    gain_one, gain_two = gain_rows[0:1], gain_rows[1:2]

    coef = LOG_TWO_E / math.sqrt(size) * jax.nn.softplus(query_scale)
    coef_row = jnp.concatenate([coef, jnp.zeros((LANES - size,), F32)])[None]
    normed_in, qkv, q_full, o_keep, lse, o_recv, w_all = attend(
        n, nb, heads, size, fold, length, xg, wqkv, gain_one, coef_row, low_weights[3:]
    )
    w_all = w_all.transpose(2, 0, 1, 3, 4).reshape(3, width, width)
    block_out, grad_middle, go_recv, layer_sums, w_half = layer(
        n, nb, fold, tokens, cotangent, o_recv, w_all, gain_two
    )
    layer_sums = jnp.sum(layer_sums, axis=1)
    grad_gain_two = layer_sums[0]
    stat_terms = jnp.sum(layer_sums[1:], axis=1)
    inputs = tokens.astype(F32)
    factor_one = rms_factor(inputs)
    normed_one = inputs * factor_one

    grad_proj, scale_part = attend_back(
        heads, size, fold, length, coef_row, qkv, go_recv, o_keep, lse, q_full, n, slab_width
    )
    grad_slab = jnp.einsum("nrd,nrc->dc", normed_in, grad_proj, preferred_element_type=F32)
    grad_normed_part = jnp.einsum("nrc,dc->nrd", grad_proj, wqkv, preferred_element_type=F32)
    grad_normed, own_slab, own_three = reduce_grads(
        n, nb, grad_normed_part.astype(LOW),
        grad_slab.astype(LOW).reshape(nb, n, shard, slab_width), w_half, shard,
    )
    grad_normed = grad_normed.astype(F32)
    own_qkv = (
        own_slab[:, :, : 3 * group_width]
        .reshape(group_count, shard, 3, group_width)
        .transpose(2, 1, 0, 3)
        .reshape(3, shard, width)
    )
    own_grads = jnp.concatenate([own_qkv, own_three], axis=0)

    grad_gain_one = jnp.sum(grad_normed * normed_one, axis=(0, 1))
    input_grad = grad_middle + norm_back(grad_normed * gain_one, normed_one, factor_one)
    own_squares = jnp.sum(own_grads * own_grads)
    scale_slope = LOG_TWO_E / math.sqrt(size) * jax.nn.sigmoid(query_scale)
    scale_part = jnp.sum(scale_part, axis=0)[:size] * scale_slope
    small = jnp.concatenate(
        [grad_gain_one, grad_gain_two, scale_part, stat_terms, own_squares[None]]
    )
    small_rows = (small.shape[0] + 8 * LANES - 1) // (8 * LANES) * 8
    small = jnp.pad(small, (0, small_rows * LANES - small.shape[0])).reshape(small_rows, LANES)
    sums = total_all(n, nb, small).reshape(-1)
    gain_sums = sums[: 2 * width].reshape(2, width)
    scale_grad = sums[2 * width : 2 * width + size]
    stat_sums = sums[2 * width + size : 2 * width + size + 3]
    total_squares = (
        sums[2 * width + size + 3] + jnp.sum(gain_sums * gain_sums) + jnp.sum(scale_grad * scale_grad)
    )
    index = lax.axis_index("batch") * n + lax.axis_index("seq")
    own_gain_grads = lax.dynamic_slice(gain_sums, (0, index * shard), (2, shard))

    grad_norm = jnp.sqrt(total_squares)
    clip_factor = CLIP_NORM / jnp.maximum(grad_norm, CLIP_NORM)
    new_weights, new_first_weights, new_second_weights = adam_update(
        weights, own_grads * clip_factor, first_weights, second_weights, MATRIX_RATE, MATRIX_DECAY
    )
    new_gains, new_first_gains, new_second_gains = adam_update(
        gains, own_gain_grads * clip_factor, first_gains, second_gains, GAIN_RATE, 0.0
    )
    new_scale, new_first_scale, new_second_scale = adam_update(
        query_scale, scale_grad * clip_factor, first_scale, second_scale, GAIN_RATE, 0.0
    )
    rms_stats = jnp.sqrt(stat_sums / float(series_count * rows * width * nb * n))
    return (
        block_out,
        input_grad,
        grad_norm,
        new_weights,
        new_first_weights,
        new_second_weights,
        new_gains,
        new_first_gains,
        new_second_gains,
        new_scale,
        new_first_scale,
        new_second_scale,
        rms_stats,
    )


def solution(mesh):
    return jax.shard_map(
        functools.partial(body, mesh.shape["seq"], mesh.shape["batch"]),
        mesh=mesh,
        in_specs=(
            P("batch", "seq", None),
            P("batch", "seq", None),
            P(None, ("batch", "seq"), None),
            P(None, ("batch", "seq")),
            P(),
            P(None, ("batch", "seq"), None),
            P(None, ("batch", "seq"), None),
            P(None, ("batch", "seq")),
            P(None, ("batch", "seq")),
            P(),
            P(),
            P("batch"),
        ),
        out_specs=(
            P("batch", "seq", None),
            P("batch", "seq", None),
            P(),
            P(None, ("batch", "seq"), None),
            P(None, ("batch", "seq"), None),
            P(None, ("batch", "seq"), None),
            P(None, ("batch", "seq")),
            P(None, ("batch", "seq")),
            P(None, ("batch", "seq")),
            P(),
            P(),
            P(),
            P(),
        ),
        check_vma=False,
    )
```

```python
import functools
import math

import jax
import jax.numpy as jnp
from jax import lax
from jax.experimental import pallas as pl
from jax.experimental.pallas import tpu as pltpu
from jax.sharding import PartitionSpec as P

STEP = 10

NORM_EPS = 1e-06
LOG_TWO_E = 1.442695
BETA_FIRST = 0.9
BETA_SECOND = 0.999
ADAM_EPS = 1e-08
MATRIX_RATE = 0.05
GAIN_RATE = 0.5
MATRIX_DECAY = 0.1
CLIP_NORM = 1.0
MASKED = -1e30

MESH = pl.DeviceIdType.MESH
LANES = 128
F32 = jnp.float32
LOW = jnp.bfloat16
MIB = 1024 * 1024


def rms_factor(values):
    return lax.rsqrt(jnp.mean(values * values, axis=-1, keepdims=True) + NORM_EPS)


def norm_back(grad_normed, normed, factor):
    return factor * (grad_normed - normed * jnp.mean(grad_normed * normed, axis=-1, keepdims=True))


def silu_slope(values):
    logistic = jax.nn.sigmoid(values)
    return logistic * (1.0 + values * (1.0 - logistic))


def adam_update(current, gradient, moment_one, moment_two, step_rate, decay_rate):
    new_one = BETA_FIRST * moment_one + (1.0 - BETA_FIRST) * gradient
    new_two = BETA_SECOND * moment_two + (1.0 - BETA_SECOND) * gradient * gradient
    first_hat = new_one / (1.0 - BETA_FIRST**STEP)
    second_hat = new_two / (1.0 - BETA_SECOND**STEP)
    updated = current - step_rate * (
        first_hat / (jnp.sqrt(second_hat) + ADAM_EPS) + decay_rate * current
    )
    return (updated, new_one, new_two)


def dot(left, right, left_axis=1, right_axis=0):
    return lax.dot_general(
        left, right, (((left_axis,), (right_axis,)), ((), ())), preferred_element_type=F32
    )


def greet(seq_count, batch_count):
    barrier = pltpu.get_barrier_semaphore()
    me_seq, me_batch = lax.axis_index("seq"), lax.axis_index("batch")
    for k in range(1, seq_count):
        pl.semaphore_signal(
            barrier,
            inc=1,
            device_id={"seq": lax.rem(me_seq + k, seq_count)},
            device_id_type=MESH,
        )
    for k in range(1, batch_count):
        pl.semaphore_signal(
            barrier,
            inc=1,
            device_id={"batch": lax.rem(me_batch + k, batch_count)},
            device_id_type=MESH,
        )
    pl.semaphore_wait(barrier, seq_count - 1 + batch_count - 1)


def push(source, target, send_sem, recv_sem, **where):
    return pltpu.make_async_remote_copy(
        source, target, send_sem, recv_sem, device_id=where, device_id_type=MESH
    )


def place(seq_count):
    me = lax.axis_index("seq")
    chips = seq_count // 2
    half_chips = chips // 2
    core = lax.rem(me, 2)
    chip = me // 2
    half = chip // half_chips
    base = half * half_chips
    gate_mine = half_chips - 1 + half
    gate_other = half_chips - half
    return me, core, chip, half, base, gate_mine, gate_other


def far_chip(step, half, half_chips):
    return (1 - half) * (half_chips + step) + half * (half_chips - 1 - step)


def batch_neighbours(batch):
    across = lax.rem(batch, 2)
    first = batch + 1 - 2 * across
    second = lax.rem(batch + 2, 4)
    return (first, second), lax.rem(first + 2, 4)


class Spread:
    def __init__(self, nb, ref, send, recv):
        self.nb, self.ref, self.send, self.recv = nb, ref, send, recv
        self.batch = lax.axis_index("batch")
        self.copies = []

    def copy(self, owner, slot, j, lane, target):
        block = self.ref.at[owner, slot]
        return push(block, block, self.send.at[j, lane], self.recv.at[j, lane], batch=target)

    def route(self, lane):
        sides, across = batch_neighbours(self.batch)
        return sides[lane % 2], sides[1 - lane % 2], across

    def begin(self, slot, lane):
        if self.nb == 4:
            first, second, _ = self.route(lane)
            new = [self.copy(self.batch, slot, 0, lane, first), self.copy(self.batch, slot, 1, lane, second)]
        else:
            new = [
                self.copy(self.batch, slot, j - 1, lane, lax.rem(self.batch + j, self.nb))
                for j in range(1, self.nb)
            ]
        for copy in new:
            copy.start()
        self.copies += new

    def relay(self, slot, lane):
        if self.nb == 4:
            first, second, _ = self.route(lane)
            self.copy(first, slot, 0, lane, first).wait_recv()
            copy = self.copy(first, slot, 2, lane, second)
            copy.start()
            self.copies.append(copy)
            return [first]
        return []

    def finish(self, slot, lane):
        if self.nb == 4:
            _, second, across = self.route(lane)
            self.copy(second, slot, 1, lane, second).wait_recv()
            self.copy(across, slot, 2, lane, second).wait_recv()
            return [second, across]
        owners = []
        for j in range(1, self.nb):
            owner = lax.rem(self.batch + self.nb - j, self.nb)
            self.copy(owner, slot, j - 1, lane, owner).wait_recv()
            owners.append(owner)
        return owners

    def drain(self):
        for copy in self.copies:
            copy.wait_send()


def gather_kernel(
    n, nb, chunks, tok, slab, xg, wout, far_sem, own_sem, pass_sem, sib_sem, same_recv, sib_recv,
    z_send, z_recv, b_send, b_recv, local_sem,
):
    chips, half_chips = n // 2, n // 4
    me, core, chip, half, base, gate_mine, gate_other = place(n)
    group_count = n // 2
    batch = lax.axis_index("batch")
    rows = tok.shape[1] // chunks
    sibling = 2 * chip + 1 - core
    greet(n, nb)

    sends = []
    z_copies = []
    for k in range(1, n):
        target = lax.rem(me + k, n)
        copy = push(
            slab.at[lax.rem(target, group_count)], wout.at[batch, me], z_send.at[k],
            z_recv.at[k], seq=target,
        )
        copy.start()
        z_copies.append(copy)

    def part(ref, lead, c):
        return ref.at[lead, pl.ds(c * rows, rows)]

    def tok_copy(source, slot, c, send_sem, recv_sem, target):
        return push(source, part(xg, slot, c), send_sem, recv_sem.at[slot, c], seq=target)

    for c in range(chunks):
        copy = tok_copy(
            part(tok, 1 - half, c), me, c, far_sem.at[c], same_recv, 2 * gate_other + core
        )
        copy.start()
        sends.append(copy)
        for k in range(1, half_chips):
            other = base + lax.rem(chip - base + k, half_chips)
            copy = tok_copy(
                part(tok, half, c), me, c, own_sem.at[k, c], same_recv, 2 * other + core
            )
            copy.start()
            sends.append(copy)
        copy = tok_copy(part(tok, half, c), me, c, sib_sem.at[0, c], sib_recv, sibling)
        copy.start()
        sends.append(copy)
    own_copy = pltpu.make_async_copy(tok.at[half], xg.at[me], local_sem.at[0])
    own_copy.start()
    slab_copy = pltpu.make_async_copy(
        slab.at[lax.rem(me, group_count)], wout.at[batch, me], local_sem.at[1]
    )
    slab_copy.start()
    slab_copy.wait()

    slices = Spread(nb, wout, b_send, b_recv)

    def line_slot(k):
        return lax.rem(me + n - k, n)

    def pass_tokens(c):
        for k in range(1, half_chips):
            slot = 2 * (base + lax.rem(chip - base + half_chips - k, half_chips)) + core
            tok_copy(part(xg, slot, c), slot, c, sib_sem.at[k, c], same_recv, sibling).wait_recv()
            copy = tok_copy(part(xg, slot, c), slot, c, sib_sem.at[k, c], sib_recv, sibling)
            copy.start()
            sends.append(copy)
        for k in range(half_chips):
            slot = 2 * far_chip(k, half, half_chips) + core
            lane = half_chips + k
            tok_copy(part(xg, slot, c), slot, c, sib_sem.at[lane, c], same_recv, sibling).wait_recv()

            @pl.when(chip == gate_mine)
            def _():
                for j in range(1, half_chips):
                    other = base + lax.rem(chip - base + j, half_chips)
                    tok_copy(
                        part(xg, slot, c), slot, c, pass_sem.at[k, j, c], same_recv,
                        2 * other + core,
                    ).start()

            copy = tok_copy(part(xg, slot, c), slot, c, sib_sem.at[lane, c], sib_recv, sibling)
            copy.start()
            sends.append(copy)

    slices.begin(me, 0)
    for k in range(1, n):
        z_copies[k - 1].wait_recv()
        slices.begin(line_slot(k), k)
    pass_tokens(0)
    for k in range(n):
        slices.relay(line_slot(k), k)
    for c in range(1, chunks):
        pass_tokens(c)
    for k in range(n):
        slices.finish(line_slot(k), k)
    for c in range(chunks):
        for q in range(chips):
            slot = 2 * q + 1 - core
            tok_copy(part(xg, slot, c), slot, c, sib_sem.at[0, c], sib_recv, sibling).wait_recv()
    own_copy.wait()
    slices.drain()
    for copy in sends + z_copies:
        copy.wait_send()

    @pl.when(chip == gate_mine)
    def _():
        for c in range(chunks):
            for k in range(half_chips):
                for j in range(1, half_chips):
                    tok_copy(
                        part(xg, me, c), me, c, pass_sem.at[k, j, c], same_recv, sibling
                    ).wait_send()


def gather_tokens(n, nb, tokens, slab):
    chunks = 4
    chips, half_chips = n // 2, n // 4
    dma = pltpu.SemaphoreType.DMA
    return pl.pallas_call(
        functools.partial(gather_kernel, n, nb, chunks),
        out_shape=(
            jax.ShapeDtypeStruct((n,) + tokens.shape[1:], tokens.dtype),
            jax.ShapeDtypeStruct((nb, n) + slab.shape[1:], slab.dtype),
        ),
        in_specs=[pl.BlockSpec(memory_space=pl.ANY)] * 2,
        out_specs=[pl.BlockSpec(memory_space=pl.ANY)] * 2,
        scratch_shapes=[
            dma((chunks,)),
            dma((half_chips, chunks)),
            dma((half_chips, half_chips, chunks)),
            dma((chips, chunks)),
            dma((n, chunks)),
            dma((n, chunks)),
            dma((n,)),
            dma((n,)),
            dma((nb, n)),
            dma((nb, n)),
            dma((2,)),
        ],
        compiler_params=pltpu.CompilerParams(collective_id=1, has_side_effects=True),
        name="gather_tokens",
    )(tokens, slab)


def widen(values):
    rows, width = values.shape
    return jnp.concatenate([values, jnp.zeros((rows, LANES - width), values.dtype)], axis=1)


def attend_kernel(
    n, nb, heads, size, fold, len_ref, x_in, w_ref, gain_ref, coef_ref, own_w, h_out, qkv_out, q_out,
    keep_out, lse_out, o_out, w_all, x_s, qkv_s, q_s, keep_s, o_s, s_s, m_s, acc_s, sum_s,
    x_sem, h_sem, qkv_sem, q_sem, keep_sem, local_sem, o_send, o_recv, wz_send, wz_recv, wb_send,
    wb_recv, ws_send, ws_recv,
):
    chips = n // 2
    me, core, chip, *_ = place(n)
    batch = lax.axis_index("batch")
    sibling = 2 * chip + 1 - core
    block = x_in.shape[1]
    group = range(heads)
    greet(n, nb)

    sends = []
    w_copies = []
    for k in range(1, chips):
        target = 2 * lax.rem(chip + k, chips) + core
        copy = push(own_w, w_all.at[batch, me], wz_send.at[k], wz_recv.at[k], seq=target)
        copy.start()
        w_copies.append(copy)
    w_copy = pltpu.make_async_copy(own_w, w_all.at[batch, me], local_sem.at[0])
    w_copy.start()

    def x_load(i):
        return pltpu.make_async_copy(x_in.at[i], x_s.at[i], x_sem.at[i])

    for i in range(n):
        x_load(i).start()
    length = len_ref[0]

    whole = Spread(nb, w_all, wb_send, wb_recv)

    def chip_slot(k):
        return 2 * lax.rem(chip + chips - k, chips) + core

    def to_sibling(owner, lane, slot, j):
        piece = w_all.at[owner, slot]
        copy = push(piece, piece, ws_send.at[j, lane], ws_recv.at[owner, slot], seq=sibling)
        copy.start()
        sends.append(copy)

    w_copy.wait()
    whole.begin(me, 0)
    to_sibling(batch, 0, me, 0)

    def kept(i):
        return [
            pltpu.make_async_copy(x_s.at[i], h_out.at[i], h_sem.at[i]),
            pltpu.make_async_copy(qkv_s.at[i], qkv_out.at[i], qkv_sem.at[i]),
            pltpu.make_async_copy(q_s.at[i], q_out.at[i], q_sem.at[i]),
            pltpu.make_async_copy(keep_s.at[i], keep_out.at[i], keep_sem.at[i]),
        ]

    def o_push(i):
        return push(o_s.at[i], o_out.at[me], o_send.at[i], o_recv.at[me], seq=i)

    own_o = pltpu.make_async_copy(o_s.at[me], o_out.at[me], local_sem.at[1])

    def project(i):
        x = x_s[i].astype(F32)
        h = (x * rms_factor(x) * gain_ref[...]).astype(LOW)
        x_s[i] = h
        out = dot(h, w_ref[...])
        lane = lax.broadcasted_iota(jnp.int32, (block, LANES), 1)
        row = i * block + lax.broadcasted_iota(jnp.int32, (block, LANES), 0)
        mark = jnp.where(lane == size, 1.0, 0.0)
        hide = jnp.where((lane == size) & (row >= length), MASKED, 0.0)
        for a in group:
            q = widen(out[:, a * size : (a + 1) * size])
            q_s[i, a] = q
            qkv_s[i, a] = (q * coef_ref[...] + mark).astype(LOW)
        for a in range(heads, 2 * heads):
            qkv_s[i, a] = (widen(out[:, a * size : (a + 1) * size]) + hide).astype(LOW)
        for a in range(2 * heads, 3 * heads):
            qkv_s[i, a] = widen(out[:, a * size : (a + 1) * size].astype(LOW))

    def score(i, j, diagonal):
        if diagonal:
            row = lax.broadcasted_iota(jnp.int32, (block, block), 0)
            col = lax.broadcasted_iota(jnp.int32, (block, block), 1)
            visible = col <= row
        for a in group:
            s = dot(qkv_s[i, a], qkv_s[j, heads + a], 1, 1)
            if diagonal:
                s = jnp.where(visible, s, MASKED)
            s_s[a, j] = s
            best = m_s[a]
            for part in range(block // LANES):
                best = jnp.maximum(best, s[:, part * LANES : (part + 1) * LANES])
            m_s[a] = best

    def mix(j):
        for a in group:
            best = m_s[a]
            count = sum_s[a]
            pieces = []
            for part in range(block // LANES):
                e = jnp.exp(s_s[a, j, :, part * LANES : (part + 1) * LANES] - best)
                count = count + e
                pieces.append(e.astype(LOW))
            sum_s[a] = count
            acc_s[a] += dot(jnp.concatenate(pieces, axis=1), qkv_s[j, 2 * heads + a])

    def query_block(i):
        x_load(i).wait()
        project(i)
        m_s[...] = jnp.full_like(m_s, MASKED)
        sum_s[...] = jnp.zeros_like(sum_s)
        acc_s[...] = jnp.zeros_like(acc_s)
        pl.loop(0, i)(lambda j: score(i, j, False))
        score(i, i, True)
        for a in group:
            m_s[a] = jnp.broadcast_to(jnp.max(m_s[a], axis=1, keepdims=True), (block, LANES))
        pl.loop(0, i + 1)(mix)
        outs = []
        for a in group:
            count = jnp.sum(sum_s[a], axis=1, keepdims=True)
            out = acc_s[a] / count
            keep_s[i, a] = out
            outs.append(out[:, :size])
            lse_out[i, a] = (m_s[a] + jnp.log(count)).T[:8]
        low = jnp.concatenate(outs, axis=1).astype(LOW)
        piece = block // fold
        o_s[i] = jnp.concatenate([low[f * piece : (f + 1) * piece] for f in range(fold)], axis=1)
        for copy in kept(i):
            copy.start()

        @pl.when(i != me)
        def _():
            o_push(i).start()

        @pl.when(i == me)
        def _():
            own_o.start()

    first, second = n // 2 + 1, n - 1
    pl.loop(0, first)(query_block)
    for k in range(1, chips):
        w_copies[k - 1].wait_recv()
        whole.begin(chip_slot(k), k)
        to_sibling(batch, k, chip_slot(k), 0)
    if second > first:
        pl.loop(first, second)(query_block)
    for k in range(chips):
        for j, owner in enumerate(whole.relay(chip_slot(k), k)):
            to_sibling(owner, k, chip_slot(k), 1 + j)
    pl.loop(second, n)(query_block)
    for k in range(chips):
        owners = whole.finish(chip_slot(k), k)
        for j, owner in enumerate(owners):
            to_sibling(owner, k, chip_slot(k), nb - len(owners) + j)

    for k in range(1, n):
        source = lax.rem(me + k, n)
        push(
            o_s.at[source], o_out.at[source], o_send.at[source], o_recv.at[source], seq=source
        ).wait()
    own_o.wait()
    for owner in range(nb):
        for q in range(chips):
            piece = w_all.at[owner, 2 * q + 1 - core]
            push(
                piece, piece, ws_send.at[0, 0], ws_recv.at[owner, 2 * q + 1 - core], seq=sibling
            ).wait_recv()
    whole.drain()
    for copy in sends + w_copies:
        copy.wait_send()

    @pl.loop(0, n)
    def _(i):
        for copy in kept(i):
            copy.wait()


def attend(n, nb, heads, size, fold, length, xg, wqkv, gain, coef, own_w):
    _, rows, width = xg.shape
    chips = n // 2
    folded = (n, rows // fold, heads * size * fold)
    many, one = (n, 3 * heads, rows, LANES), (n, heads, rows, LANES)
    dma = pltpu.SemaphoreType.DMA
    vmem = pl.BlockSpec(memory_space=pltpu.VMEM)
    anywhere = pl.BlockSpec(memory_space=pl.ANY)
    state = pltpu.VMEM((heads, rows, LANES), F32)
    return pl.pallas_call(
        functools.partial(attend_kernel, n, nb, heads, size, fold),
        out_shape=(
            jax.ShapeDtypeStruct(xg.shape, LOW),
            jax.ShapeDtypeStruct(many, LOW),
            jax.ShapeDtypeStruct(one, F32),
            jax.ShapeDtypeStruct(one, F32),
            jax.ShapeDtypeStruct((n, heads, 8, rows), F32),
            jax.ShapeDtypeStruct(folded, LOW),
            jax.ShapeDtypeStruct((nb, n) + own_w.shape, LOW),
        ),
        in_specs=[pl.BlockSpec(memory_space=pltpu.SMEM), anywhere, vmem, vmem, vmem, anywhere],
        out_specs=[anywhere, anywhere, anywhere, anywhere, vmem, anywhere, anywhere],
        scratch_shapes=[
            pltpu.VMEM(xg.shape, LOW),
            pltpu.VMEM(many, LOW),
            pltpu.VMEM(one, F32),
            pltpu.VMEM(one, F32),
            pltpu.VMEM(folded, LOW),
            pltpu.VMEM((heads, n, rows, rows), F32),
            state,
            state,
            state,
            dma((n,)),
            dma((n,)),
            dma((n,)),
            dma((n,)),
            dma((n,)),
            dma((2,)),
            dma((n,)),
            dma((n,)),
            dma((chips,)),
            dma((chips,)),
            dma((nb, chips)),
            dma((nb, chips)),
            dma((nb, chips)),
            dma((nb, n)),
        ],
        compiler_params=pltpu.CompilerParams(
            collective_id=2, has_side_effects=True, vmem_limit_bytes=62 * MIB
        ),
        name="attend",
    )(length, xg, wqkv, gain, coef, own_w)


def fold_rows(values):
    rows, width = values.shape
    return jnp.sum(values.reshape(rows // 8, 8, width), axis=0)


def layer_kernel(
    n, nb, fold, tok, cot, o_in, w_in, gain_ref, y_out, gy_out, go_out, small_out, half_out,
    w, o_s, hidden_s, act_s, gu_s, ga_s, go_s, gw_s, sib_in, w_sem, send_sem, recv_sem, local_sem,
    sib_send, sib_recv,
):
    group_count = n // 2
    me, core, chip, half, base, gate_mine, gate_other = place(n)
    sibling = 2 * chip + 1 - core
    _, rows, width = tok.shape
    group_width = width // group_count
    piece = rows // fold
    barrier = pltpu.get_barrier_semaphore()
    for k in range(1, n):
        pl.semaphore_signal(
            barrier, inc=1, device_id={"seq": lax.rem(me + k, n)}, device_id_type=MESH
        )
    loads = [pltpu.make_async_copy(w_in.at[m], w.at[m], w_sem.at[m]) for m in range(3)]
    for load in loads:
        load.start()
    small_out[...] = jnp.zeros_like(small_out)
    gain = gain_ref[...]

    def go_push(target):
        return push(
            go_s.at[target], go_out.at[me], send_sem.at[target], recv_sem.at[me], seq=target
        )

    own_go = pltpu.make_async_copy(go_s.at[me], go_out.at[me], local_sem)

    for t in range(2):
        parts = [
            jnp.concatenate(
                [
                    o_in[t * group_count + g, :, f * group_width : (f + 1) * group_width]
                    for g in range(group_count)
                ],
                axis=1,
            )
            for f in range(fold)
        ]
        o = jnp.concatenate(parts, axis=0)
        o_s[t] = o
        if t == 0:
            loads[0].wait()
        a = dot(o, w[0])
        small_out[1] += fold_rows(a * a)
        y1 = tok[t].astype(F32) + a
        factor = rms_factor(y1)
        normed = y1 * factor
        hidden = (normed * gain).astype(LOW)
        hidden_s[t] = hidden
        if t == 0:
            loads[1].wait()
        u = dot(hidden, w[1])
        logistic = 1.0 / (1.0 + jnp.exp(-u))
        act = (u * logistic).astype(LOW)
        act_s[t] = act
        if t == 0:
            loads[2].wait()
        f = dot(act, w[2])
        small_out[2] += fold_rows(f * f)
        y = y1 + f
        small_out[3] += fold_rows(y * y)
        y_out[t] = y.astype(LOW)
        gz = dot(cot[t], w[2], 1, 1)
        gu = (gz * (logistic * (1.0 + u * (1.0 - logistic)))).astype(LOW)
        gu_s[t] = gu
        gh = dot(gu, w[1], 1, 1)
        small_out[0] += fold_rows(gh * normed)
        gy = cot[t].astype(F32) + norm_back(gh * gain, normed, factor)
        gy_out[t] = gy
        ga = gy.astype(LOW)
        ga_s[t] = ga
        go = dot(ga, w[0], 1, 1).astype(LOW)
        for g in range(group_count):
            block = go[:, g * group_width : (g + 1) * group_width]
            go_s[t * group_count + g] = jnp.concatenate(
                [block[f * piece : (f + 1) * piece] for f in range(fold)], axis=1
            )
        if t == 0:
            pl.semaphore_wait(barrier, n - 1)
        for g in range(group_count):
            target = t * group_count + g

            @pl.when(target != me)
            def _():
                go_push(target).start()

            @pl.when(target == me)
            def _():
                own_go.start()

    tile = 256
    half_rows = width // nb // 2
    sib_copies = []
    pairs = ((act_s, cot, 2), (hidden_s, gu_s, 1), (o_s, ga_s, 0))
    for left, right, m in pairs:

        @pl.loop(0, width // tile)
        def _(k):
            cols = pl.ds(pl.multiple_of(k * tile, tile), tile)
            total = dot(left[0, :, cols], right[0], 0, 0) + dot(left[1, :, cols], right[1], 0, 0)
            gw_s[m, cols] = total.astype(LOW)

        for b in range(nb):
            start = pl.multiple_of((2 * b + 1 - core) * half_rows, 16)
            copy = push(
                gw_s.at[m, pl.ds(start, half_rows)], sib_in.at[b, m], sib_send.at[b, m],
                sib_recv.at[b, m], seq=sibling,
            )
            copy.start()
            sib_copies.append(copy)
    index = 0
    for _, _, m in pairs:
        for b in range(nb):
            sib_copies[index].wait_recv()
            index += 1
            start = pl.multiple_of((2 * b + core) * half_rows, 16)
            half_out[b, m] = (
                gw_s[m, pl.ds(start, half_rows)].astype(F32) + sib_in[b, m].astype(F32)
            ).astype(LOW)
    for k in range(1, n):
        source = lax.rem(me + k, n)
        push(
            go_s.at[source], go_out.at[source], send_sem.at[source], recv_sem.at[source], seq=source
        ).wait()
    own_go.wait()
    for copy in sib_copies:
        copy.wait_send()


def layer(n, nb, fold, tokens, cotangent, o_recv, w_all, gain):
    _, rows, width = tokens.shape
    half_rows = width // nb // 2
    dma = pltpu.SemaphoreType.DMA
    vmem = pl.BlockSpec(memory_space=pltpu.VMEM)
    anywhere = pl.BlockSpec(memory_space=pl.ANY)
    kept = pltpu.VMEM((2, rows, width), LOW)
    return pl.pallas_call(
        functools.partial(layer_kernel, n, nb, fold),
        out_shape=(
            jax.ShapeDtypeStruct((2, rows, width), LOW),
            jax.ShapeDtypeStruct((2, rows, width), F32),
            jax.ShapeDtypeStruct(o_recv.shape, LOW),
            jax.ShapeDtypeStruct((4, 8, width), F32),
            jax.ShapeDtypeStruct((nb, 3, half_rows, width), LOW),
        ),
        in_specs=[vmem, vmem, vmem, anywhere, vmem],
        out_specs=[vmem, vmem, anywhere, vmem, vmem],
        scratch_shapes=[
            pltpu.VMEM((3, width, width), LOW),
            kept,
            kept,
            kept,
            kept,
            kept,
            pltpu.VMEM(o_recv.shape, LOW),
            pltpu.VMEM((3, width, width), LOW),
            pltpu.VMEM((nb, 3, half_rows, width), LOW),
            dma((3,)),
            dma((n,)),
            dma((n,)),
            dma,
            dma((nb, 3)),
            dma((nb, 3)),
        ],
        compiler_params=pltpu.CompilerParams(
            collective_id=3, has_side_effects=True, vmem_limit_bytes=63 * MIB
        ),
        name="layer",
    )(tokens, cotangent, o_recv, w_all, gain)


def back_kernel(
    n, nb, heads, size, fold, len_ref, coef_ref, qkv_in, go_ref, keep_in, lse_ref, q_in, h_in, w_in,
    half_in, out, own_gw, own_w, scale_out, cross_in, turn_in,
    qkv, kt, g_s, delta, gq, gk, gv, q_s, h_s, w_s, gw, gh_own, gh_out, from_sib, gate_in, peer_in,
    stage, cross_out, w_line, w_parts, gw_low, near_in, near_out, near_turn, line_out, line_in,
    load_sem, block_sem, sib_send, sib_recv, gate_send, gate_recv, peer_send, peer_recv, far_send,
    far_recv, c_send, c_recv, t_send, t_recv, w_send, w_recv, b_send, b_recv, bt_send, bt_recv,
    z_send, z_recv, stage_sem,
):
    chips, half_chips = n // 2, n // 4
    me, core, chip, half, base, gate_mine, gate_other = place(n)
    group_count = n // 2
    batch = lax.axis_index("batch")
    sibling = 2 * chip + 1 - core
    block = qkv.shape[2]
    group = range(heads)
    sides, across = batch_neighbours(batch)
    is_gate = chip == gate_mine
    paired = nb == 4
    greet(n, nb)

    w_rows = stage.shape[2]

    def w_piece(owner, h):
        return half_in.at[owner, :, pl.ds(h * w_rows, w_rows)]

    w_copies = []
    if paired:
        for h in range(2):
            for j, owner in enumerate((across, sides[h])):
                w_copies.append(
                    push(
                        w_piece(owner, h), cross_in.at[h, j], c_send.at[h, j], c_recv.at[h, j],
                        batch=sides[h],
                    )
                )
    else:
        for k in range(1, nb):
            target = lax.rem(batch + k, nb)
            w_copies.append(
                push(
                    w_piece(target, 0), cross_in.at[0, k], c_send.at[0, k], c_recv.at[0, k],
                    batch=target,
                )
            )
    for copy in w_copies:
        copy.start()

    keep_load = pltpu.make_async_copy(keep_in, gk, load_sem.at[0])
    qkv_load = pltpu.make_async_copy(qkv_in, qkv, load_sem.at[1])
    w_load = pltpu.make_async_copy(w_in, w_s, load_sem.at[2])
    for load in (keep_load, qkv_load, w_load):
        load.start()
    scale_out[...] = jnp.zeros_like(scale_out)
    gv[...] = jnp.zeros_like(gv)
    gq[...] = jnp.zeros_like(gq)
    keep_load.wait()

    @pl.loop(0, n)
    def _(i):
        for a in group:
            g = widen(
                jnp.concatenate(
                    [
                        go_ref[i, :, (f * heads + a) * size : (f * heads + a + 1) * size]
                        for f in range(fold)
                    ],
                    axis=0,
                )
            )
            g_s[i, a] = g
            delta[i, a] = jnp.broadcast_to(
                jnp.sum((g.astype(F32) * gk[i, a]).T, axis=0, keepdims=True), (8, block)
            )
            gk[i, a] = jnp.zeros_like(gk[i, a])

    qkv_load.wait()

    @pl.loop(0, n)
    def _(j):
        for a in group:
            kt[j, a] = qkv[j, heads + a].T

    w_load.wait()

    def pair_block(i, j, diagonal):
        if diagonal:
            col = lax.broadcasted_iota(jnp.int32, (block, block), 0)
            row = lax.broadcasted_iota(jnp.int32, (block, block), 1)
            visible = col <= row
        for a in group:
            s = dot(qkv[j, heads + a], qkv[i, a], 1, 1)
            p = jnp.exp(s - lse_ref[i, a, :1])
            if diagonal:
                p = jnp.where(visible, p, 0.0)
            dp = dot(qkv[j, 2 * heads + a], g_s[i, a], 1, 1)
            ds = (p * (dp - delta[i, a, :1])).astype(LOW)
            gk[j, a] += dot(ds, qkv[i, a])
            gv[j, a] += dot(p.astype(LOW), g_s[i, a])
            gq[i, a] += dot(kt[j, a], ds)

    def sib_copy(t):
        return push(
            gh_out.at[t % 2], from_sib.at[t], sib_send.at[t], sib_recv.at[t], seq=sibling
        )

    def step(t, u):
        r = half * t + (1 - half) * (n - 1 - t)
        loads = [
            pltpu.make_async_copy(q_in.at[r], q_s, block_sem.at[0]),
            pltpu.make_async_copy(h_in.at[r], h_s, block_sem.at[1]),
        ]
        for load in loads:
            load.start()
        pair_block(r, r, True)
        pl.loop(1, n - t)(lambda v: pair_block(r + half * v, r - (1 - half) * v, False))
        for load in loads:
            load.wait()
        pieces = []
        for a in group:
            grad = gq[r, a].T.astype(LOW).astype(F32)
            scale_out[...] += fold_rows(grad * q_s[a])
            pieces.append((grad * coef_ref[...])[:, :size].astype(LOW))
        pieces += [gk[r, a][:, :size].astype(LOW) for a in group]
        pieces += [gv[r, a][:, :size].astype(LOW) for a in group]
        spare = w_s.shape[1] - 3 * heads * size
        pieces.append(jnp.zeros((block, spare), LOW))
        grads = jnp.concatenate(pieces, axis=1)
        gh = dot(grads, w_s[...], 1, 1).astype(LOW)
        tp = t // 2
        mine = lax.rem(r, 2) == core

        @pl.when(mine)
        def _():
            gh_own[tp] = gh

        @pl.when(jnp.logical_not(mine))
        def _():
            gh_out[tp % 2] = gh
            sib_copy(tp).start()

        part = dot(h_s[...], grads, 0, 0)
        if t == 0:
            gw[...] = part
        else:
            gw[...] += part

    def far_chip_of(tp):
        return half * tp + (1 - half) * (chips - 1 - tp)

    def gate_copy(tp):
        after = lax.rem(chip - gate_mine + half_chips, half_chips)
        return push(
            gh_own.at[tp], gate_in.at[after - 1, tp], gate_send.at[tp],
            gate_recv.at[after - 1, tp], seq=2 * gate_mine + core,
        )

    def far_copy(tp):
        return push(
            gh_own.at[tp], out.at[half], far_send.at[tp], far_recv.at[0],
            seq=2 * far_chip_of(tp) + core,
        )

    def peer_copy(tp):
        q = far_chip_of(tp)
        after = lax.rem(chip - q + half_chips, half_chips)
        return push(
            gh_own.at[tp], peer_in.at[after - 1], peer_send.at[tp], peer_recv.at[after - 1],
            seq=2 * q + core,
        )

    def relay(tp):
        @pl.when(is_gate)
        def _():
            value = gh_own[tp].astype(F32)
            for j in range(half_chips - 1):
                push(
                    gh_own.at[tp], gate_in.at[j, tp], gate_send.at[tp], gate_recv.at[j, tp],
                    seq=sibling,
                ).wait_recv()
                value = value + gate_in[j, tp].astype(F32)
            gh_own[tp] = value.astype(LOW)
            far_copy(tp).start()

    shard = own_w.shape[1]

    def staged(*sources):
        value = None
        for first in range(0, len(sources), 3):
            loads = [
                pltpu.make_async_copy(source, stage.at[j], stage_sem.at[j])
                for j, source in enumerate(sources[first : first + 3])
            ]
            for load in loads:
                load.start()
            for load in loads:
                load.wait()
            for j in range(len(loads)):
                term = stage[j].astype(F32)
                value = term if value is None else value + term
        return value

    t_copies = []

    def turn():
        if paired:
            for h in range(2):
                w_copies[2 * h].wait_recv()
                cross_out[h] = staged(w_piece(sides[1 - h], h), cross_in.at[h, 0]).astype(LOW)
                copy = push(
                    cross_out.at[h], turn_in.at[h], t_send.at[h], t_recv.at[h], batch=sides[1 - h]
                )
                copy.start()
                t_copies.append(copy)

    def w_push(i):
        target = core * group_count + i
        return push(w_line.at[i], w_parts.at[chip], w_send.at[i], w_recv.at[chip], seq=target)

    def to_owners():
        for copy in w_copies[1::2] if paired else w_copies:
            copy.wait_recv()
        for copy in t_copies:
            copy.wait_recv()
        splits = 2 if paired else 1
        each = group_count // splits
        for h in range(splits):
            if paired:
                value = staged(w_piece(batch, h), cross_in.at[h, 1], turn_in.at[h])
            else:
                value = staged(w_piece(batch, 0), *[cross_in.at[0, k] for k in range(1, nb)])
            for i in range(each):
                w_line[h * each + i] = value[:, i * shard : (i + 1) * shard].astype(LOW)
        for i in range(group_count):
            own = core * group_count + i == me

            @pl.when(own)
            def _():
                w_parts[chip] = w_line[i]

            @pl.when(jnp.logical_not(own))
            def _():
                w_push(i).start()

    for tp in range(chips):
        if tp >= 2:
            sib_copy(tp - 2).wait_send()
        step(2 * tp, 0)
        step(2 * tp + 1, 1)
        if tp == 0:
            turn()
        if tp == 1:
            to_owners()
        sib_copy(tp).wait_recv()
        gh_own[tp] = (gh_own[tp].astype(F32) + from_sib[tp].astype(F32)).astype(LOW)
        if tp < half_chips:

            @pl.when(jnp.logical_not(is_gate))
            def _():
                gate_copy(tp).start()

        else:

            @pl.when(far_chip_of(tp) != chip)
            def _():
                peer_copy(tp).start()

        if 1 <= tp <= half_chips:
            relay(tp - 1)

    line_rows = gw.shape[0] // nb
    near_rows = near_in.shape[2]
    for b in range(nb):
        gw_low[b] = gw[b * line_rows : (b + 1) * line_rows].astype(LOW)

    def near_piece(owner, h):
        return gw_low.at[owner, pl.ds(h * near_rows, near_rows)]

    b_copies = []
    if paired:
        for h in range(2):
            for j, owner in enumerate((across, sides[h])):
                b_copies.append(
                    push(
                        near_piece(owner, h), near_in.at[h, j], b_send.at[h, j], b_recv.at[h, j],
                        batch=sides[h],
                    )
                )
    else:
        for k in range(1, nb):
            target = lax.rem(batch + k, nb)
            b_copies.append(
                push(
                    near_piece(target, 0), near_in.at[0, k], b_send.at[0, k], b_recv.at[0, k],
                    batch=target,
                )
            )
    for copy in b_copies:
        copy.start()
    bt_copies = []
    if paired:
        for h in range(2):
            b_copies[2 * h].wait_recv()
            near_out[h] = (
                gw_low[sides[1 - h], pl.ds(h * near_rows, near_rows)].astype(F32)
                + near_in[h, 0].astype(F32)
            ).astype(LOW)
            copy = push(
                near_out.at[h], near_turn.at[h], bt_send.at[h], bt_recv.at[h], batch=sides[1 - h]
            )
            copy.start()
            bt_copies.append(copy)
    z_copies = []

    def z_copy(target):
        return push(
            line_out.at[target], line_in.at[me], z_send.at[target], z_recv.at[me], seq=target
        )

    splits = 2 if paired else 1
    each = n // splits
    for h in range(splits):
        value = gw_low[batch, pl.ds(h * near_rows, near_rows)].astype(F32)
        if paired:
            b_copies[2 * h + 1].wait_recv()
            bt_copies[h].wait_recv()
            value = value + near_in[h, 1].astype(F32) + near_turn[h].astype(F32)
        else:
            for k in range(1, nb):
                b_copies[k - 1].wait_recv()
                value = value + near_in[0, k].astype(F32)
        for i in range(each):
            target = h * each + i
            line_out[target] = value[i * shard : (i + 1) * shard].astype(LOW)

            @pl.when(target != me)
            def _():
                z_copy(target).start()

            @pl.when(target == me)
            def _():
                line_in[me] = line_out[target]

    value = gh_own[half * chip + (1 - half) * (chips - 1 - chip)].astype(F32)
    for j in range(half_chips - 1):
        push(
            gh_own.at[0], peer_in.at[j], peer_send.at[0], peer_recv.at[j], seq=sibling
        ).wait_recv()
        value = value + peer_in[j].astype(F32)
    out[half] = value.astype(LOW)
    push(gh_own.at[0], out.at[1 - half], far_send.at[0], far_recv.at[0], seq=sibling).wait_recv()

    for q in range(chips):

        @pl.when(2 * q + half != me)
        def _():
            push(w_line.at[0], w_parts.at[q], w_send.at[0], w_recv.at[q], seq=sibling).wait_recv()

    value = w_parts[0].astype(F32)
    for q in range(1, chips):
        value = value + w_parts[q].astype(F32)
    own_w[...] = value

    for k in range(1, n):
        source = lax.rem(me + k, n)
        push(
            line_out.at[source], line_in.at[source], z_send.at[source], z_recv.at[source], seq=source
        ).wait()
    for g in range(group_count):
        own_gw[g] = line_in[g].astype(F32) + line_in[g + group_count].astype(F32)

    for i in range(group_count):

        @pl.when(core * group_count + i != me)
        def _():
            w_push(i).wait_send()

    for tp in range(max(chips - 2, 0), chips):
        sib_copy(tp).wait_send()
    for copy in w_copies + t_copies + b_copies + bt_copies:
        copy.wait_send()
    for tp in range(chips):
        if tp < half_chips:

            @pl.when(is_gate)
            def _():
                far_copy(tp).wait_send()

            @pl.when(jnp.logical_not(is_gate))
            def _():
                gate_copy(tp).wait_send()

        else:

            @pl.when(far_chip_of(tp) != chip)
            def _():
                peer_copy(tp).wait_send()


def attend_back(
    n, nb, heads, size, fold, length, coef, qkv, go, keep, lse, q_full, h, wqkv, w_half, shard
):
    _, rows, width = h.shape
    chips, half_chips = n // 2, n // 4
    paired = nb == 4
    split = 2 if paired else 1
    steps = 2 if paired else nb
    w_rows = w_half.shape[2] // split
    line_rows = width // nb
    slab = wqkv.shape[1]
    dma = pltpu.SemaphoreType.DMA
    vmem = pl.BlockSpec(memory_space=pltpu.VMEM)
    anywhere = pl.BlockSpec(memory_space=pl.ANY)
    one = (n, heads, rows, LANES)
    peers = max(half_chips - 1, 1)
    near = (line_rows // split, slab)
    result = pl.pallas_call(
        functools.partial(back_kernel, n, nb, heads, size, fold),
        out_shape=(
            jax.ShapeDtypeStruct((2, rows, width), LOW),
            jax.ShapeDtypeStruct((n // 2, shard, slab), F32),
            jax.ShapeDtypeStruct((3, shard, width), F32),
            jax.ShapeDtypeStruct((8, LANES), F32),
            jax.ShapeDtypeStruct((split, steps, 3, w_rows, width), LOW),
            jax.ShapeDtypeStruct((split, 3, w_rows, width), LOW),
        ),
        in_specs=[pl.BlockSpec(memory_space=pltpu.SMEM), vmem, anywhere, vmem, anywhere, vmem]
        + [anywhere] * 4,
        out_specs=[vmem, vmem, vmem, vmem, anywhere, anywhere],
        scratch_shapes=[
            pltpu.VMEM(qkv.shape, LOW),
            pltpu.VMEM((n, heads, LANES, rows), LOW),
            pltpu.VMEM(one, LOW),
            pltpu.VMEM((n, heads, 8, rows), F32),
            pltpu.VMEM((n, heads, LANES, rows), F32),
            pltpu.VMEM(one, F32),
            pltpu.VMEM(one, F32),
            pltpu.VMEM((heads, rows, LANES), F32),
            pltpu.VMEM((rows, width), LOW),
            pltpu.VMEM(wqkv.shape, LOW),
            pltpu.VMEM(wqkv.shape, F32),
            pltpu.VMEM((chips, rows, width), LOW),
            pltpu.VMEM((2, rows, width), LOW),
            pltpu.VMEM((chips, rows, width), LOW),
            pltpu.VMEM((peers, half_chips, rows, width), LOW),
            pltpu.VMEM((peers, rows, width), LOW),
            pltpu.VMEM((3, 3, w_rows, width), LOW),
            pltpu.VMEM((split, 3, w_rows, width), LOW),
            pltpu.VMEM((n // 2, 3, shard, width), LOW),
            pltpu.VMEM((chips, 3, shard, width), LOW),
            pltpu.VMEM((nb, line_rows, slab), LOW),
            pltpu.VMEM((split, steps) + near, LOW),
            pltpu.VMEM((split,) + near, LOW),
            pltpu.VMEM((split,) + near, LOW),
            pltpu.VMEM((n, shard, slab), LOW),
            pltpu.VMEM((n, shard, slab), LOW),
            dma((3,)),
            dma((2,)),
            dma((chips,)),
            dma((chips,)),
            dma((half_chips,)),
            dma((peers, half_chips)),
            dma((chips,)),
            dma((peers,)),
            dma((half_chips,)),
            dma((1,)),
            dma((split, steps)),
            dma((split, steps)),
            dma((split,)),
            dma((split,)),
            dma((n // 2,)),
            dma((chips,)),
            dma((split, steps)),
            dma((split, steps)),
            dma((split,)),
            dma((split,)),
            dma((n,)),
            dma((n,)),
            dma((3,)),
        ],
        compiler_params=pltpu.CompilerParams(
            collective_id=4, has_side_effects=True, vmem_limit_bytes=63 * MIB
        ),
        name="attend_back",
    )(length, coef, qkv, go, keep, lse, q_full, h, wqkv, w_half)
    return result[:4]


def total_kernel(n, nb, value, out, mine, line_in, batch_in, z_send, z_recv, b_send, b_recv):
    me, batch = lax.axis_index("seq"), lax.axis_index("batch")
    greet(n, nb)
    copies = []
    for k in range(1, n):
        copy = push(
            value, line_in.at[k], z_send.at[k], z_recv.at[k], seq=lax.rem(me + k, n)
        )
        copy.start()
        copies.append(copy)
    line_in[0] = value[...]
    for copy in copies:
        copy.wait_recv()
    part = jnp.zeros_like(value)
    for s in range(n):
        part = part + line_in[lax.rem(me - s + n, n)]
    mine[...] = part
    for k in range(1, nb):
        copy = push(
            mine, batch_in.at[k], b_send.at[k], b_recv.at[k], batch=lax.rem(batch + k, nb)
        )
        copy.start()
        copies.append(copy)
    batch_in[0] = part
    for copy in copies[n - 1 :]:
        copy.wait_recv()
    part = jnp.zeros_like(part)
    for s in range(nb):
        part = part + batch_in[lax.rem(batch - s + nb, nb)]
    out[...] = part
    for copy in copies:
        copy.wait_send()


def total_all(n, nb, value):
    dma = pltpu.SemaphoreType.DMA
    return pl.pallas_call(
        functools.partial(total_kernel, n, nb),
        out_shape=jax.ShapeDtypeStruct(value.shape, F32),
        in_specs=[pl.BlockSpec(memory_space=pltpu.VMEM)],
        out_specs=pl.BlockSpec(memory_space=pltpu.VMEM),
        scratch_shapes=[
            pltpu.VMEM(value.shape, F32),
            pltpu.VMEM((n,) + value.shape, F32),
            pltpu.VMEM((nb,) + value.shape, F32),
            dma((n,)),
            dma((n,)),
            dma((nb,)),
            dma((nb,)),
        ],
        compiler_params=pltpu.CompilerParams(collective_id=5, has_side_effects=True),
        name="total_all",
    )(value)


def body(
    n,
    nb,
    tokens,
    cotangent,
    weights,
    gains,
    query_scale,
    first_weights,
    second_weights,
    first_gains,
    second_gains,
    first_scale,
    second_scale,
    lengths,
):
    series_count, rows, width = tokens.shape
    size = query_scale.shape[0]
    group_count = n // 2
    heads = width // size // group_count
    group_width = heads * size
    fold = 640 // group_width
    shard = weights.shape[1]
    slab_width = (3 * group_width + 2 + LANES - 1) // LANES * LANES
    half = lax.axis_index("seq") // group_count
    length = lax.dynamic_slice(lengths, (half,), (1,))

    low_weights = weights.astype(LOW)
    slab = (
        low_weights[:3]
        .reshape(3, shard, group_count, group_width)
        .transpose(2, 1, 0, 3)
        .reshape(group_count, shard, 3 * group_width)
    )
    low_gains = jnp.broadcast_to(gains.astype(LOW).T[None], (group_count, shard, 2))
    spare = jnp.zeros((group_count, shard, slab_width - 3 * group_width - 2), LOW)
    slab = jnp.concatenate([slab, low_gains, spare], axis=2)

    xg, wout = gather_tokens(n, nb, tokens, slab)
    wqkv = wout.reshape(nb * n * shard, slab_width)
    gain_rows = wqkv[:, 3 * group_width : 3 * group_width + 2].astype(F32).T
    gain_one, gain_two = gain_rows[0:1], gain_rows[1:2]

    coef = LOG_TWO_E / math.sqrt(size) * jax.nn.softplus(query_scale)
    coef_row = jnp.concatenate([coef, jnp.zeros((LANES - size,), F32)])[None]
    normed_in, qkv, q_full, o_keep, lse, o_recv, w_all = attend(
        n, nb, heads, size, fold, length, xg, wqkv, gain_one, coef_row, low_weights[3:]
    )
    w_all = w_all.transpose(2, 0, 1, 3, 4).reshape(3, width, width)
    block_out, grad_middle, go_recv, layer_sums, w_half = layer(
        n, nb, fold, tokens, cotangent, o_recv, w_all, gain_two
    )
    layer_sums = jnp.sum(layer_sums, axis=1)
    grad_gain_two = layer_sums[0]
    stat_terms = jnp.sum(layer_sums[1:], axis=1)
    inputs = tokens.astype(F32)
    factor_one = rms_factor(inputs)
    normed_one = inputs * factor_one

    grad_normed, own_slab, own_three, scale_part = attend_back(
        n, nb, heads, size, fold, length, coef_row, qkv, go_recv, o_keep, lse, q_full, normed_in,
        wqkv, w_half, shard,
    )
    grad_normed = grad_normed.astype(F32)
    own_qkv = (
        own_slab[:, :, : 3 * group_width]
        .reshape(group_count, shard, 3, group_width)
        .transpose(2, 1, 0, 3)
        .reshape(3, shard, width)
    )
    own_grads = jnp.concatenate([own_qkv, own_three], axis=0)

    grad_gain_one = jnp.sum(grad_normed * normed_one, axis=(0, 1))
    input_grad = grad_middle + norm_back(grad_normed * gain_one, normed_one, factor_one)
    own_squares = jnp.sum(own_grads * own_grads)
    scale_slope = LOG_TWO_E / math.sqrt(size) * jax.nn.sigmoid(query_scale)
    scale_part = jnp.sum(scale_part, axis=0)[:size] * scale_slope
    small = jnp.concatenate(
        [grad_gain_one, grad_gain_two, scale_part, stat_terms, own_squares[None]]
    )
    small_rows = (small.shape[0] + 8 * LANES - 1) // (8 * LANES) * 8
    small = jnp.pad(small, (0, small_rows * LANES - small.shape[0])).reshape(small_rows, LANES)
    sums = total_all(n, nb, small).reshape(-1)
    gain_sums = sums[: 2 * width].reshape(2, width)
    scale_grad = sums[2 * width : 2 * width + size]
    stat_sums = sums[2 * width + size : 2 * width + size + 3]
    total_squares = (
        sums[2 * width + size + 3] + jnp.sum(gain_sums * gain_sums) + jnp.sum(scale_grad * scale_grad)
    )
    index = lax.axis_index("batch") * n + lax.axis_index("seq")
    own_gain_grads = lax.dynamic_slice(gain_sums, (0, index * shard), (2, shard))

    grad_norm = jnp.sqrt(total_squares)
    clip_factor = CLIP_NORM / jnp.maximum(grad_norm, CLIP_NORM)
    new_weights, new_first_weights, new_second_weights = adam_update(
        weights, own_grads * clip_factor, first_weights, second_weights, MATRIX_RATE, MATRIX_DECAY
    )
    new_gains, new_first_gains, new_second_gains = adam_update(
        gains, own_gain_grads * clip_factor, first_gains, second_gains, GAIN_RATE, 0.0
    )
    new_scale, new_first_scale, new_second_scale = adam_update(
        query_scale, scale_grad * clip_factor, first_scale, second_scale, GAIN_RATE, 0.0
    )
    rms_stats = jnp.sqrt(stat_sums / float(series_count * rows * width * nb * n))
    return (
        block_out,
        input_grad,
        grad_norm,
        new_weights,
        new_first_weights,
        new_second_weights,
        new_gains,
        new_first_gains,
        new_second_gains,
        new_scale,
        new_first_scale,
        new_second_scale,
        rms_stats,
    )


def solution(mesh):
    return jax.shard_map(
        functools.partial(body, mesh.shape["seq"], mesh.shape["batch"]),
        mesh=mesh,
        in_specs=(
            P("batch", "seq", None),
            P("batch", "seq", None),
            P(None, ("batch", "seq"), None),
            P(None, ("batch", "seq")),
            P(),
            P(None, ("batch", "seq"), None),
            P(None, ("batch", "seq"), None),
            P(None, ("batch", "seq")),
            P(None, ("batch", "seq")),
            P(),
            P(),
            P("batch"),
        ),
        out_specs=(
            P("batch", "seq", None),
            P("batch", "seq", None),
            P(),
            P(None, ("batch", "seq"), None),
            P(None, ("batch", "seq"), None),
            P(None, ("batch", "seq"), None),
            P(None, ("batch", "seq")),
            P(None, ("batch", "seq")),
            P(None, ("batch", "seq")),
            P(),
            P(),
            P(),
            P(),
        ),
        check_vma=False,
    )
```

```python
import functools
import math

import jax
import jax.numpy as jnp
from jax import lax
from jax.experimental import pallas as pl
from jax.experimental.pallas import tpu as pltpu
from jax.sharding import PartitionSpec as P

STEP = 10

NORM_EPS = 1e-06
LOG_TWO_E = 1.442695
BETA_FIRST = 0.9
BETA_SECOND = 0.999
ADAM_EPS = 1e-08
MATRIX_RATE = 0.05
GAIN_RATE = 0.5
MATRIX_DECAY = 0.1
CLIP_NORM = 1.0
MASKED = -1e30

MESH = pl.DeviceIdType.MESH
LANES = 128
F32 = jnp.float32
LOW = jnp.bfloat16
MIB = 1024 * 1024


def rms_factor(values):
    return lax.rsqrt(jnp.mean(values * values, axis=-1, keepdims=True) + NORM_EPS)


def norm_back(grad_normed, normed, factor):
    return factor * (grad_normed - normed * jnp.mean(grad_normed * normed, axis=-1, keepdims=True))


def silu_slope(values):
    logistic = jax.nn.sigmoid(values)
    return logistic * (1.0 + values * (1.0 - logistic))


def adam_update(current, gradient, moment_one, moment_two, step_rate, decay_rate):
    new_one = BETA_FIRST * moment_one + (1.0 - BETA_FIRST) * gradient
    new_two = BETA_SECOND * moment_two + (1.0 - BETA_SECOND) * gradient * gradient
    first_hat = new_one / (1.0 - BETA_FIRST**STEP)
    second_hat = new_two / (1.0 - BETA_SECOND**STEP)
    updated = current - step_rate * (
        first_hat / (jnp.sqrt(second_hat) + ADAM_EPS) + decay_rate * current
    )
    return (updated, new_one, new_two)


def dot(left, right, left_axis=1, right_axis=0):
    return lax.dot_general(
        left, right, (((left_axis,), (right_axis,)), ((), ())), preferred_element_type=F32
    )


def greet(seq_count, batch_count):
    barrier = pltpu.get_barrier_semaphore()
    me_seq, me_batch = lax.axis_index("seq"), lax.axis_index("batch")
    for k in range(1, seq_count):
        pl.semaphore_signal(
            barrier,
            inc=1,
            device_id={"seq": lax.rem(me_seq + k, seq_count)},
            device_id_type=MESH,
        )
    for k in range(1, batch_count):
        pl.semaphore_signal(
            barrier,
            inc=1,
            device_id={"batch": lax.rem(me_batch + k, batch_count)},
            device_id_type=MESH,
        )
    pl.semaphore_wait(barrier, seq_count - 1 + batch_count - 1)


def push(source, target, send_sem, recv_sem, **where):
    return pltpu.make_async_remote_copy(
        source, target, send_sem, recv_sem, device_id=where, device_id_type=MESH
    )


def place(seq_count):
    me = lax.axis_index("seq")
    chips = seq_count // 2
    half_chips = chips // 2
    core = lax.rem(me, 2)
    chip = me // 2
    half = chip // half_chips
    base = half * half_chips
    gate_mine = half_chips - 1 + half
    gate_other = half_chips - half
    return me, core, chip, half, base, gate_mine, gate_other


def far_chip(step, half, half_chips):
    return (1 - half) * (half_chips + step) + half * (half_chips - 1 - step)


def batch_neighbours(batch):
    across = lax.rem(batch, 2)
    first = batch + 1 - 2 * across
    second = lax.rem(batch + 2, 4)
    return (first, second), lax.rem(first + 2, 4)


class Spread:
    def __init__(self, nb, ref, send, recv):
        self.nb, self.ref, self.send, self.recv = nb, ref, send, recv
        self.batch = lax.axis_index("batch")
        self.copies = []

    def copy(self, owner, slot, j, lane, target, source=None):
        block = self.ref.at[owner, slot]
        return push(block if source is None else source, block, self.send.at[j, lane], self.recv.at[j, lane], batch=target)

    def route(self, lane):
        sides, across = batch_neighbours(self.batch)
        return sides[lane % 2], sides[1 - lane % 2], across

    def begin(self, slot, lane, source=None):
        if self.nb == 4:
            first, second, _ = self.route(lane)
            targets = [first, second]
        else:
            targets = [lax.rem(self.batch + j, self.nb) for j in range(1, self.nb)]
        new = [
            self.copy(self.batch, slot, j, lane, target, source) for j, target in enumerate(targets)
        ]
        for copy in new:
            copy.start()
        self.copies += new

    def relay(self, slot, lane):
        if self.nb == 4:
            first, second, _ = self.route(lane)
            self.copy(first, slot, 0, lane, first).wait_recv()
            copy = self.copy(first, slot, 2, lane, second)
            copy.start()
            self.copies.append(copy)
            return [first]
        return []

    def finish(self, slot, lane):
        if self.nb == 4:
            _, second, across = self.route(lane)
            self.copy(second, slot, 1, lane, second).wait_recv()
            self.copy(across, slot, 2, lane, second).wait_recv()
            return [second, across]
        owners = []
        for j in range(1, self.nb):
            owner = lax.rem(self.batch + self.nb - j, self.nb)
            self.copy(owner, slot, j - 1, lane, owner).wait_recv()
            owners.append(owner)
        return owners

    def drain(self):
        for copy in self.copies:
            copy.wait_send()


def gather_kernel(
    n, nb, chunks, tok, slab, xg, wout, far_sem, own_sem, pass_sem, sib_sem, same_recv, sib_recv,
    z_send, z_recv, b_send, b_recv, local_sem,
):
    chips, half_chips = n // 2, n // 4
    me, core, chip, half, base, gate_mine, gate_other = place(n)
    group_count = n // 2
    batch = lax.axis_index("batch")
    rows = tok.shape[1] // chunks
    sibling = 2 * chip + 1 - core
    greet(n, nb)

    sends = []
    z_copies = []
    for k in range(1, n):
        target = lax.rem(me + k, n)
        copy = push(
            slab.at[lax.rem(target, group_count)], wout.at[batch, me], z_send.at[k],
            z_recv.at[k], seq=target,
        )
        copy.start()
        z_copies.append(copy)

    def part(ref, lead, c):
        return ref.at[lead, pl.ds(c * rows, rows)]

    def tok_copy(source, slot, c, send_sem, recv_sem, target):
        return push(source, part(xg, slot, c), send_sem, recv_sem.at[slot, c], seq=target)

    for c in range(chunks):
        copy = tok_copy(
            part(tok, 1 - half, c), me, c, far_sem.at[c], same_recv, 2 * gate_other + core
        )
        copy.start()
        sends.append(copy)
        for k in range(1, half_chips):
            other = base + lax.rem(chip - base + k, half_chips)
            copy = tok_copy(
                part(tok, half, c), me, c, own_sem.at[k, c], same_recv, 2 * other + core
            )
            copy.start()
            sends.append(copy)
        copy = tok_copy(part(tok, half, c), me, c, sib_sem.at[0, c], sib_recv, sibling)
        copy.start()
        sends.append(copy)
    own_slab = slab.at[lax.rem(me, group_count)]
    slab_copy = pltpu.make_async_copy(own_slab, wout.at[batch, me], local_sem)
    slab_copy.start()

    slices = Spread(nb, wout, b_send, b_recv)

    def line_slot(k):
        return lax.rem(me + n - k, n)

    def pass_tokens(c):
        for k in range(1, half_chips):
            slot = 2 * (base + lax.rem(chip - base + half_chips - k, half_chips)) + core
            tok_copy(part(xg, slot, c), slot, c, sib_sem.at[k, c], same_recv, sibling).wait_recv()
            copy = tok_copy(part(xg, slot, c), slot, c, sib_sem.at[k, c], sib_recv, sibling)
            copy.start()
            sends.append(copy)
        for k in range(half_chips):
            slot = 2 * far_chip(k, half, half_chips) + core
            lane = half_chips + k
            tok_copy(part(xg, slot, c), slot, c, sib_sem.at[lane, c], same_recv, sibling).wait_recv()

            @pl.when(chip == gate_mine)
            def _():
                for j in range(1, half_chips):
                    other = base + lax.rem(chip - base + j, half_chips)
                    tok_copy(
                        part(xg, slot, c), slot, c, pass_sem.at[k, j, c], same_recv,
                        2 * other + core,
                    ).start()

            copy = tok_copy(part(xg, slot, c), slot, c, sib_sem.at[lane, c], sib_recv, sibling)
            copy.start()
            sends.append(copy)

    slices.begin(me, 0, own_slab)
    for k in range(1, n):
        z_copies[k - 1].wait_recv()
        slices.begin(line_slot(k), k)
    pass_tokens(0)
    for k in range(n):
        slices.relay(line_slot(k), k)
    for c in range(1, chunks):
        pass_tokens(c)
    for k in range(n):
        slices.finish(line_slot(k), k)
    for c in range(chunks):
        for q in range(chips):
            slot = 2 * q + 1 - core
            tok_copy(part(xg, slot, c), slot, c, sib_sem.at[0, c], sib_recv, sibling).wait_recv()
    slab_copy.wait()
    slices.drain()
    for copy in sends + z_copies:
        copy.wait_send()

    @pl.when(chip == gate_mine)
    def _():
        for c in range(chunks):
            for k in range(half_chips):
                for j in range(1, half_chips):
                    tok_copy(
                        part(xg, me, c), me, c, pass_sem.at[k, j, c], same_recv, sibling
                    ).wait_send()


def gather_tokens(n, nb, tokens, slab):
    chunks = 4
    chips, half_chips = n // 2, n // 4
    dma = pltpu.SemaphoreType.DMA
    return pl.pallas_call(
        functools.partial(gather_kernel, n, nb, chunks),
        out_shape=(
            jax.ShapeDtypeStruct((n,) + tokens.shape[1:], tokens.dtype),
            jax.ShapeDtypeStruct((nb, n) + slab.shape[1:], slab.dtype),
        ),
        in_specs=[pl.BlockSpec(memory_space=pl.ANY)] * 2,
        out_specs=[pl.BlockSpec(memory_space=pl.ANY)] * 2,
        scratch_shapes=[
            dma((chunks,)),
            dma((half_chips, chunks)),
            dma((half_chips, half_chips, chunks)),
            dma((chips, chunks)),
            dma((n, chunks)),
            dma((n, chunks)),
            dma((n,)),
            dma((n,)),
            dma((nb, n)),
            dma((nb, n)),
            dma,
        ],
        compiler_params=pltpu.CompilerParams(collective_id=1, has_side_effects=True),
        name="gather_tokens",
    )(tokens, slab)


def widen(values):
    rows, width = values.shape
    return jnp.concatenate([values, jnp.zeros((rows, LANES - width), values.dtype)], axis=1)


def attend_kernel(
    n, nb, heads, size, fold, len_ref, tok, x_in, w_ref, gain_ref, coef_ref, own_w, h_out, qkv_out, q_out,
    keep_out, lse_out, o_out, w_all, x_s, qkv_s, q_s, keep_s, o_s, s_s, m_s, acc_s, sum_s,
    x_sem, h_sem, qkv_sem, q_sem, keep_sem, local_sem, o_send, o_recv, wz_send, wz_recv, wb_send,
    wb_recv, ws_send, ws_recv,
):
    chips = n // 2
    me, core, chip, half, *_ = place(n)
    batch = lax.axis_index("batch")
    sibling = 2 * chip + 1 - core
    block = x_in.shape[1]
    group = range(heads)
    greet(n, nb)

    sends = []
    w_copies = []
    for k in range(1, chips):
        target = 2 * lax.rem(chip + k, chips) + core
        copy = push(own_w, w_all.at[batch, me], wz_send.at[k], wz_recv.at[k], seq=target)
        copy.start()
        w_copies.append(copy)
    w_copy = pltpu.make_async_copy(own_w, w_all.at[batch, me], local_sem.at[0])
    w_copy.start()

    def x_load(i):
        return pltpu.make_async_copy(x_in.at[i], x_s.at[i], x_sem.at[i])

    for i in range(n):

        @pl.when(i != me)
        def _():
            x_load(i).start()

    pltpu.make_async_copy(tok.at[half], x_s.at[me], x_sem.at[me]).start()
    length = len_ref[0]

    whole = Spread(nb, w_all, wb_send, wb_recv)

    def chip_slot(k):
        return 2 * lax.rem(chip + chips - k, chips) + core

    def to_sibling(owner, lane, slot, j, source=None):
        piece = w_all.at[owner, slot]
        copy = push(piece if source is None else source, piece, ws_send.at[j, lane], ws_recv.at[owner, slot], seq=sibling)
        copy.start()
        sends.append(copy)

    whole.begin(me, 0, own_w)
    to_sibling(batch, 0, me, 0, own_w)

    def kept(i):
        return [
            pltpu.make_async_copy(x_s.at[i], h_out.at[i], h_sem.at[i]),
            pltpu.make_async_copy(qkv_s.at[i], qkv_out.at[i], qkv_sem.at[i]),
            pltpu.make_async_copy(q_s.at[i], q_out.at[i], q_sem.at[i]),
            pltpu.make_async_copy(keep_s.at[i], keep_out.at[i], keep_sem.at[i]),
        ]

    def o_push(i):
        return push(o_s.at[i], o_out.at[me], o_send.at[i], o_recv.at[me], seq=i)

    own_o = pltpu.make_async_copy(o_s.at[me], o_out.at[me], local_sem.at[1])

    def project(i):
        x = x_s[i].astype(F32)
        h = (x * rms_factor(x) * gain_ref[...]).astype(LOW)
        x_s[i] = h
        out = dot(h, w_ref[...])
        lane = lax.broadcasted_iota(jnp.int32, (block, LANES), 1)
        row = i * block + lax.broadcasted_iota(jnp.int32, (block, LANES), 0)
        mark = jnp.where(lane == size, 1.0, 0.0)
        hide = jnp.where((lane == size) & (row >= length), MASKED, 0.0)
        for a in group:
            q = widen(out[:, a * size : (a + 1) * size])
            q_s[i, a] = q
            qkv_s[i, a] = (q * coef_ref[...] + mark).astype(LOW)
        for a in range(heads, 2 * heads):
            qkv_s[i, a] = (widen(out[:, a * size : (a + 1) * size]) + hide).astype(LOW)
        for a in range(2 * heads, 3 * heads):
            qkv_s[i, a] = widen(out[:, a * size : (a + 1) * size].astype(LOW))

    def score(i, j, diagonal):
        if diagonal:
            row = lax.broadcasted_iota(jnp.int32, (block, block), 0)
            col = lax.broadcasted_iota(jnp.int32, (block, block), 1)
            visible = col <= row
        for a in group:
            s = dot(qkv_s[i, a], qkv_s[j, heads + a], 1, 1)
            if diagonal:
                s = jnp.where(visible, s, MASKED)
            s_s[a, j] = s
            best = m_s[a]
            for part in range(block // LANES):
                best = jnp.maximum(best, s[:, part * LANES : (part + 1) * LANES])
            m_s[a] = best

    def mix(j):
        for a in group:
            best = m_s[a]
            count = sum_s[a]
            pieces = []
            for part in range(block // LANES):
                e = jnp.exp(s_s[a, j, :, part * LANES : (part + 1) * LANES] - best)
                count = count + e
                pieces.append(e.astype(LOW))
            sum_s[a] = count
            acc_s[a] += dot(jnp.concatenate(pieces, axis=1), qkv_s[j, 2 * heads + a])

    @pl.loop(0, n)
    def _(i):
        x_load(i).wait()
        project(i)

    def query_block(t):
        i = lax.rem(me + 1 + t, n)
        m_s[...] = jnp.full_like(m_s, MASKED)
        sum_s[...] = jnp.zeros_like(sum_s)
        acc_s[...] = jnp.zeros_like(acc_s)
        pl.loop(0, i)(lambda j: score(i, j, False))
        score(i, i, True)
        for a in group:
            m_s[a] = jnp.broadcast_to(jnp.max(m_s[a], axis=1, keepdims=True), (block, LANES))
        pl.loop(0, i + 1)(mix)
        outs = []
        for a in group:
            count = jnp.sum(sum_s[a], axis=1, keepdims=True)
            out = acc_s[a] / count
            keep_s[i, a] = out
            outs.append(out[:, :size])
            lse_out[i, a] = (m_s[a] + jnp.log(count)).T[:8]
        low = jnp.concatenate(outs, axis=1).astype(LOW)
        piece = block // fold
        o_s[i] = jnp.concatenate([low[f * piece : (f + 1) * piece] for f in range(fold)], axis=1)
        for copy in kept(i):
            copy.start()

        @pl.when(i != me)
        def _():
            o_push(i).start()

        @pl.when(i == me)
        def _():
            own_o.start()

    first, second = n // 2 - 1, n - 2
    pl.loop(0, first)(query_block)
    for k in range(1, chips):
        w_copies[k - 1].wait_recv()
        whole.begin(chip_slot(k), k)
        to_sibling(batch, k, chip_slot(k), 0)
    if second > first:
        pl.loop(first, second)(query_block)
    for k in range(chips):
        for j, owner in enumerate(whole.relay(chip_slot(k), k)):
            to_sibling(owner, k, chip_slot(k), 1 + j)
    pl.loop(second, n)(query_block)
    for k in range(chips):
        owners = whole.finish(chip_slot(k), k)
        for j, owner in enumerate(owners):
            to_sibling(owner, k, chip_slot(k), nb - len(owners) + j)

    for k in range(1, n):
        source = lax.rem(me + k, n)
        push(
            o_s.at[source], o_out.at[source], o_send.at[source], o_recv.at[source], seq=source
        ).wait()
    own_o.wait()
    w_copy.wait()
    for owner in range(nb):
        for q in range(chips):
            piece = w_all.at[owner, 2 * q + 1 - core]
            push(
                piece, piece, ws_send.at[0, 0], ws_recv.at[owner, 2 * q + 1 - core], seq=sibling
            ).wait_recv()
    whole.drain()
    for copy in sends + w_copies:
        copy.wait_send()

    @pl.loop(0, n)
    def _(i):
        for copy in kept(i):
            copy.wait()


def attend(n, nb, heads, size, fold, length, tokens, xg, wqkv, gain, coef, own_w):
    _, rows, width = xg.shape
    chips = n // 2
    folded = (n, rows // fold, heads * size * fold)
    many, one = (n, 3 * heads, rows, LANES), (n, heads, rows, LANES)
    dma = pltpu.SemaphoreType.DMA
    vmem = pl.BlockSpec(memory_space=pltpu.VMEM)
    anywhere = pl.BlockSpec(memory_space=pl.ANY)
    state = pltpu.VMEM((heads, rows, LANES), F32)
    return pl.pallas_call(
        functools.partial(attend_kernel, n, nb, heads, size, fold),
        out_shape=(
            jax.ShapeDtypeStruct(xg.shape, LOW),
            jax.ShapeDtypeStruct(many, LOW),
            jax.ShapeDtypeStruct(one, F32),
            jax.ShapeDtypeStruct(one, F32),
            jax.ShapeDtypeStruct((n, heads, 8, rows), F32),
            jax.ShapeDtypeStruct(folded, LOW),
            jax.ShapeDtypeStruct((nb, n) + own_w.shape, LOW),
        ),
        in_specs=[pl.BlockSpec(memory_space=pltpu.SMEM), anywhere, anywhere, vmem, vmem, vmem]
        + [anywhere],
        out_specs=[anywhere, anywhere, anywhere, anywhere, vmem, anywhere, anywhere],
        scratch_shapes=[
            pltpu.VMEM(xg.shape, LOW),
            pltpu.VMEM(many, LOW),
            pltpu.VMEM(one, F32),
            pltpu.VMEM(one, F32),
            pltpu.VMEM(folded, LOW),
            pltpu.VMEM((heads, n, rows, rows), F32),
            state,
            state,
            state,
            dma((n,)),
            dma((n,)),
            dma((n,)),
            dma((n,)),
            dma((n,)),
            dma((2,)),
            dma((n,)),
            dma((n,)),
            dma((chips,)),
            dma((chips,)),
            dma((nb, chips)),
            dma((nb, chips)),
            dma((nb, chips)),
            dma((nb, n)),
        ],
        compiler_params=pltpu.CompilerParams(
            collective_id=2, has_side_effects=True, vmem_limit_bytes=62 * MIB
        ),
        name="attend",
    )(length, tokens, xg, wqkv, gain, coef, own_w)


def fold_rows(values):
    rows, width = values.shape
    return jnp.sum(values.reshape(rows // 8, 8, width), axis=0)


def layer_kernel(
    n, nb, fold, tok, cot, o_in, w_in, gain_ref, y_out, gy_out, go_out, small_out, half_out,
    w, o_s, hidden_s, act_s, gu_s, ga_s, go_s, gw_s, sib_in, w_sem, send_sem, recv_sem, local_sem,
    sib_send, sib_recv,
):
    group_count = n // 2
    me, core, chip, half, base, gate_mine, gate_other = place(n)
    sibling = 2 * chip + 1 - core
    _, rows, width = tok.shape
    group_width = width // group_count
    piece = rows // fold
    barrier = pltpu.get_barrier_semaphore()
    for k in range(1, n):
        pl.semaphore_signal(
            barrier, inc=1, device_id={"seq": lax.rem(me + k, n)}, device_id_type=MESH
        )
    loads = [pltpu.make_async_copy(w_in.at[m], w.at[m], w_sem.at[m]) for m in range(3)]
    for load in loads:
        load.start()
    small_out[...] = jnp.zeros_like(small_out)
    gain = gain_ref[...]

    def go_push(target):
        return push(
            go_s.at[target], go_out.at[me], send_sem.at[target], recv_sem.at[me], seq=target
        )

    own_go = pltpu.make_async_copy(go_s.at[me], go_out.at[me], local_sem)

    for step in range(2):
        t = half if step else 1 - half
        parts = [
            jnp.concatenate(
                [
                    o_in[t * group_count + g, :, f * group_width : (f + 1) * group_width]
                    for g in range(group_count)
                ],
                axis=1,
            )
            for f in range(fold)
        ]
        o = jnp.concatenate(parts, axis=0)
        o_s[t] = o
        if step == 0:
            loads[0].wait()
        a = dot(o, w[0])
        small_out[1] += fold_rows(a * a)
        y1 = tok[t].astype(F32) + a
        factor = rms_factor(y1)
        normed = y1 * factor
        hidden = (normed * gain).astype(LOW)
        hidden_s[t] = hidden
        if step == 0:
            loads[1].wait()
        u = dot(hidden, w[1])
        logistic = 1.0 / (1.0 + jnp.exp(-u))
        act = (u * logistic).astype(LOW)
        act_s[t] = act
        if step == 0:
            loads[2].wait()
        f = dot(act, w[2])
        small_out[2] += fold_rows(f * f)
        y = y1 + f
        small_out[3] += fold_rows(y * y)
        y_out[t] = y.astype(LOW)
        gz = dot(cot[t], w[2], 1, 1)
        gu = (gz * (logistic * (1.0 + u * (1.0 - logistic)))).astype(LOW)
        gu_s[t] = gu
        gh = dot(gu, w[1], 1, 1)
        small_out[0] += fold_rows(gh * normed)
        gy = cot[t].astype(F32) + norm_back(gh * gain, normed, factor)
        gy_out[t] = gy
        ga = gy.astype(LOW)
        ga_s[t] = ga
        go = dot(ga, w[0], 1, 1).astype(LOW)
        for g in range(group_count):
            block = go[:, g * group_width : (g + 1) * group_width]
            go_s[t * group_count + g] = jnp.concatenate(
                [block[f * piece : (f + 1) * piece] for f in range(fold)], axis=1
            )
        if step == 0:
            pl.semaphore_wait(barrier, n - 1)
        for g in range(group_count):
            target = t * group_count + g

            @pl.when(target != me)
            def _():
                go_push(target).start()

            @pl.when(target == me)
            def _():
                own_go.start()

    tile = 256
    half_rows = width // nb // 2
    sib_copies = []
    pairs = ((act_s, cot, 2), (hidden_s, gu_s, 1), (o_s, ga_s, 0))
    for left, right, m in pairs:

        @pl.loop(0, width // tile)
        def _(k):
            cols = pl.ds(pl.multiple_of(k * tile, tile), tile)
            total = dot(left[0, :, cols], right[0], 0, 0) + dot(left[1, :, cols], right[1], 0, 0)
            gw_s[m, cols] = total.astype(LOW)

        for b in range(nb):
            start = pl.multiple_of((2 * b + 1 - core) * half_rows, 16)
            copy = push(
                gw_s.at[m, pl.ds(start, half_rows)], sib_in.at[b, m], sib_send.at[b, m],
                sib_recv.at[b, m], seq=sibling,
            )
            copy.start()
            sib_copies.append(copy)
    index = 0
    for _, _, m in pairs:
        for b in range(nb):
            sib_copies[index].wait_recv()
            index += 1
            start = pl.multiple_of((2 * b + core) * half_rows, 16)
            half_out[b, m] = (
                gw_s[m, pl.ds(start, half_rows)].astype(F32) + sib_in[b, m].astype(F32)
            ).astype(LOW)
    for k in range(1, n):
        source = lax.rem(me + k, n)
        push(
            go_s.at[source], go_out.at[source], send_sem.at[source], recv_sem.at[source], seq=source
        ).wait()
    own_go.wait()
    for copy in sib_copies:
        copy.wait_send()


def layer(n, nb, fold, tokens, cotangent, o_recv, w_all, gain):
    _, rows, width = tokens.shape
    half_rows = width // nb // 2
    dma = pltpu.SemaphoreType.DMA
    vmem = pl.BlockSpec(memory_space=pltpu.VMEM)
    anywhere = pl.BlockSpec(memory_space=pl.ANY)
    kept = pltpu.VMEM((2, rows, width), LOW)
    return pl.pallas_call(
        functools.partial(layer_kernel, n, nb, fold),
        out_shape=(
            jax.ShapeDtypeStruct((2, rows, width), LOW),
            jax.ShapeDtypeStruct((2, rows, width), F32),
            jax.ShapeDtypeStruct(o_recv.shape, LOW),
            jax.ShapeDtypeStruct((4, 8, width), F32),
            jax.ShapeDtypeStruct((nb, 3, half_rows, width), LOW),
        ),
        in_specs=[vmem, vmem, vmem, anywhere, vmem],
        out_specs=[vmem, vmem, anywhere, vmem, vmem],
        scratch_shapes=[
            pltpu.VMEM((3, width, width), LOW),
            kept,
            kept,
            kept,
            kept,
            kept,
            pltpu.VMEM(o_recv.shape, LOW),
            pltpu.VMEM((3, width, width), LOW),
            pltpu.VMEM((nb, 3, half_rows, width), LOW),
            dma((3,)),
            dma((n,)),
            dma((n,)),
            dma,
            dma((nb, 3)),
            dma((nb, 3)),
        ],
        compiler_params=pltpu.CompilerParams(
            collective_id=3, has_side_effects=True, vmem_limit_bytes=63 * MIB
        ),
        name="layer",
    )(tokens, cotangent, o_recv, w_all, gain)


def back_kernel(
    n, nb, heads, size, fold, len_ref, coef_ref, qkv_in, go_ref, keep_in, lse_ref, q_in, h_in, w_in,
    half_in, out, own_gw, own_w, scale_out, cross_in, turn_in,
    qkv, kt, g_s, delta, gq, gk, gv, q_s, h_s, w_s, gw, gh_own, gh_out, from_sib, gate_in, peer_in,
    stage, cross_out, w_line, w_parts, gw_low, near_in, near_out, near_turn, line_out, line_in,
    load_sem, block_sem, sib_send, sib_recv, gate_send, gate_recv, peer_send, peer_recv, far_send,
    far_recv, c_send, c_recv, t_send, t_recv, w_send, w_recv, b_send, b_recv, bt_send, bt_recv,
    z_send, z_recv, stage_sem,
):
    chips, half_chips = n // 2, n // 4
    me, core, chip, half, base, gate_mine, gate_other = place(n)
    group_count = n // 2
    batch = lax.axis_index("batch")
    sibling = 2 * chip + 1 - core
    block = qkv.shape[2]
    group = range(heads)
    sides, across = batch_neighbours(batch)
    is_gate = chip == gate_mine
    paired = nb == 4
    greet(n, nb)

    w_rows = stage.shape[2]

    def w_piece(owner, h):
        return half_in.at[owner, :, pl.ds(h * w_rows, w_rows)]

    w_copies = []
    if paired:
        for h in range(2):
            for j, owner in enumerate((across, sides[h])):
                w_copies.append(
                    push(
                        w_piece(owner, h), cross_in.at[h, j], c_send.at[h, j], c_recv.at[h, j],
                        batch=sides[h],
                    )
                )
    else:
        for k in range(1, nb):
            target = lax.rem(batch + k, nb)
            w_copies.append(
                push(
                    w_piece(target, 0), cross_in.at[0, k], c_send.at[0, k], c_recv.at[0, k],
                    batch=target,
                )
            )
    for copy in w_copies:
        copy.start()

    keep_load = pltpu.make_async_copy(keep_in, gk, load_sem.at[0])
    qkv_load = pltpu.make_async_copy(qkv_in, qkv, load_sem.at[1])
    w_load = pltpu.make_async_copy(w_in, w_s, load_sem.at[2])
    for load in (keep_load, qkv_load, w_load):
        load.start()
    scale_out[...] = jnp.zeros_like(scale_out)
    gv[...] = jnp.zeros_like(gv)
    gq[...] = jnp.zeros_like(gq)
    keep_load.wait()

    @pl.loop(0, n)
    def _(i):
        for a in group:
            g = widen(
                jnp.concatenate(
                    [
                        go_ref[i, :, (f * heads + a) * size : (f * heads + a + 1) * size]
                        for f in range(fold)
                    ],
                    axis=0,
                )
            )
            g_s[i, a] = g
            delta[i, a] = jnp.broadcast_to(
                jnp.sum((g.astype(F32) * gk[i, a]).T, axis=0, keepdims=True), (8, block)
            )
            gk[i, a] = jnp.zeros_like(gk[i, a])

    qkv_load.wait()

    @pl.loop(0, n)
    def _(j):
        for a in group:
            kt[j, a] = qkv[j, heads + a].T

    w_load.wait()

    def pair_block(i, j, diagonal):
        if diagonal:
            col = lax.broadcasted_iota(jnp.int32, (block, block), 0)
            row = lax.broadcasted_iota(jnp.int32, (block, block), 1)
            visible = col <= row
        for a in group:
            s = dot(qkv[j, heads + a], qkv[i, a], 1, 1)
            p = jnp.exp(s - lse_ref[i, a, :1])
            if diagonal:
                p = jnp.where(visible, p, 0.0)
            dp = dot(qkv[j, 2 * heads + a], g_s[i, a], 1, 1)
            ds = (p * (dp - delta[i, a, :1])).astype(LOW)
            gk[j, a] += dot(ds, qkv[i, a])
            gv[j, a] += dot(p.astype(LOW), g_s[i, a])
            gq[i, a] += dot(kt[j, a], ds)

    def sib_copy(t):
        return push(
            gh_out.at[t % 2], from_sib.at[t], sib_send.at[t], sib_recv.at[t], seq=sibling
        )

    def step(t, u):
        r = half * t + (1 - half) * (n - 1 - t)
        loads = [
            pltpu.make_async_copy(q_in.at[r], q_s, block_sem.at[0]),
            pltpu.make_async_copy(h_in.at[r], h_s, block_sem.at[1]),
        ]
        for load in loads:
            load.start()
        pair_block(r, r, True)
        pl.loop(1, n - t)(lambda v: pair_block(r + half * v, r - (1 - half) * v, False))
        for load in loads:
            load.wait()
        pieces = []
        for a in group:
            grad = gq[r, a].T.astype(LOW).astype(F32)
            scale_out[...] += fold_rows(grad * q_s[a])
            pieces.append((grad * coef_ref[...])[:, :size].astype(LOW))
        pieces += [gk[r, a][:, :size].astype(LOW) for a in group]
        pieces += [gv[r, a][:, :size].astype(LOW) for a in group]
        spare = w_s.shape[1] - 3 * heads * size
        pieces.append(jnp.zeros((block, spare), LOW))
        grads = jnp.concatenate(pieces, axis=1)
        gh = dot(grads, w_s[...], 1, 1).astype(LOW)
        tp = t // 2
        mine = lax.rem(r, 2) == core

        @pl.when(mine)
        def _():
            gh_own[tp] = gh

        @pl.when(jnp.logical_not(mine))
        def _():
            gh_out[tp % 2] = gh
            sib_copy(tp).start()

        part = dot(h_s[...], grads, 0, 0)
        if t == 0:
            gw[...] = part
        else:
            gw[...] += part

    def far_chip_of(tp):
        return half * tp + (1 - half) * (chips - 1 - tp)

    def gate_copy(tp):
        after = lax.rem(chip - gate_mine + half_chips, half_chips)
        return push(
            gh_own.at[tp], gate_in.at[after - 1, tp], gate_send.at[tp],
            gate_recv.at[after - 1, tp], seq=2 * gate_mine + core,
        )

    def far_copy(tp):
        return push(
            gh_own.at[tp], out.at[half], far_send.at[tp], far_recv.at[0],
            seq=2 * far_chip_of(tp) + core,
        )

    def peer_copy(tp):
        q = far_chip_of(tp)
        after = lax.rem(chip - q + half_chips, half_chips)
        return push(
            gh_own.at[tp], peer_in.at[after - 1], peer_send.at[tp], peer_recv.at[after - 1],
            seq=2 * q + core,
        )

    def relay(tp):
        @pl.when(is_gate)
        def _():
            value = gh_own[tp].astype(F32)
            for j in range(half_chips - 1):
                push(
                    gh_own.at[tp], gate_in.at[j, tp], gate_send.at[tp], gate_recv.at[j, tp],
                    seq=sibling,
                ).wait_recv()
                value = value + gate_in[j, tp].astype(F32)
            gh_own[tp] = value.astype(LOW)
            far_copy(tp).start()

    shard = own_w.shape[1]

    def staged(*sources):
        value = None
        for first in range(0, len(sources), 3):
            loads = [
                pltpu.make_async_copy(source, stage.at[j], stage_sem.at[j])
                for j, source in enumerate(sources[first : first + 3])
            ]
            for load in loads:
                load.start()
            for load in loads:
                load.wait()
            for j in range(len(loads)):
                term = stage[j].astype(F32)
                value = term if value is None else value + term
        return value

    t_copies = []

    def turn():
        if paired:
            for h in range(2):
                w_copies[2 * h].wait_recv()
                cross_out[h] = staged(w_piece(sides[1 - h], h), cross_in.at[h, 0]).astype(LOW)
                copy = push(
                    cross_out.at[h], turn_in.at[h], t_send.at[h], t_recv.at[h], batch=sides[1 - h]
                )
                copy.start()
                t_copies.append(copy)

    def w_push(i):
        target = core * group_count + i
        return push(w_line.at[i], w_parts.at[chip], w_send.at[i], w_recv.at[chip], seq=target)

    def to_owners():
        for copy in w_copies[1::2] if paired else w_copies:
            copy.wait_recv()
        for copy in t_copies:
            copy.wait_recv()
        splits = 2 if paired else 1
        each = group_count // splits
        for h in range(splits):
            if paired:
                value = staged(w_piece(batch, h), cross_in.at[h, 1], turn_in.at[h])
            else:
                value = staged(w_piece(batch, 0), *[cross_in.at[0, k] for k in range(1, nb)])
            for i in range(each):
                w_line[h * each + i] = value[:, i * shard : (i + 1) * shard].astype(LOW)
        for i in range(group_count):
            own = core * group_count + i == me

            @pl.when(own)
            def _():
                w_parts[chip] = w_line[i]

            @pl.when(jnp.logical_not(own))
            def _():
                w_push(i).start()

    for tp in range(chips):
        if tp >= 2:
            sib_copy(tp - 2).wait_send()
        step(2 * tp, 0)
        step(2 * tp + 1, 1)
        if tp == 0:
            turn()
        if tp == 1:
            to_owners()
        sib_copy(tp).wait_recv()
        gh_own[tp] = (gh_own[tp].astype(F32) + from_sib[tp].astype(F32)).astype(LOW)
        if tp < half_chips:

            @pl.when(jnp.logical_not(is_gate))
            def _():
                gate_copy(tp).start()

        else:

            @pl.when(far_chip_of(tp) != chip)
            def _():
                peer_copy(tp).start()

        if 1 <= tp < half_chips:
            relay(tp - 1)

    line_rows = gw.shape[0] // nb
    near_rows = near_in.shape[2]
    for b in range(nb):
        gw_low[b] = gw[b * line_rows : (b + 1) * line_rows].astype(LOW)

    def near_piece(owner, h):
        return gw_low.at[owner, pl.ds(h * near_rows, near_rows)]

    b_copies = []
    if paired:
        for h in range(2):
            for j, owner in enumerate((across, sides[h])):
                b_copies.append(
                    push(
                        near_piece(owner, h), near_in.at[h, j], b_send.at[h, j], b_recv.at[h, j],
                        batch=sides[h],
                    )
                )
    else:
        for k in range(1, nb):
            target = lax.rem(batch + k, nb)
            b_copies.append(
                push(
                    near_piece(target, 0), near_in.at[0, k], b_send.at[0, k], b_recv.at[0, k],
                    batch=target,
                )
            )
    for copy in b_copies:
        copy.start()
    relay(half_chips - 1)
    bt_copies = []
    if paired:
        for h in range(2):
            b_copies[2 * h].wait_recv()
            near_out[h] = (
                gw_low[sides[1 - h], pl.ds(h * near_rows, near_rows)].astype(F32)
                + near_in[h, 0].astype(F32)
            ).astype(LOW)
            copy = push(
                near_out.at[h], near_turn.at[h], bt_send.at[h], bt_recv.at[h], batch=sides[1 - h]
            )
            copy.start()
            bt_copies.append(copy)
    z_copies = []

    def z_copy(target):
        return push(
            line_out.at[target], line_in.at[me], z_send.at[target], z_recv.at[me], seq=target
        )

    splits = 2 if paired else 1
    each = n // splits
    for h in range(splits):
        value = gw_low[batch, pl.ds(h * near_rows, near_rows)].astype(F32)
        if paired:
            b_copies[2 * h + 1].wait_recv()
            bt_copies[h].wait_recv()
            value = value + near_in[h, 1].astype(F32) + near_turn[h].astype(F32)
        else:
            for k in range(1, nb):
                b_copies[k - 1].wait_recv()
                value = value + near_in[0, k].astype(F32)
        for i in range(each):
            target = h * each + i
            line_out[target] = value[i * shard : (i + 1) * shard].astype(LOW)

            @pl.when(target != me)
            def _():
                z_copy(target).start()

            @pl.when(target == me)
            def _():
                line_in[me] = line_out[target]

    value = gh_own[half * chip + (1 - half) * (chips - 1 - chip)].astype(F32)
    for j in range(half_chips - 1):
        push(
            gh_own.at[0], peer_in.at[j], peer_send.at[0], peer_recv.at[j], seq=sibling
        ).wait_recv()
        value = value + peer_in[j].astype(F32)
    out[half] = value.astype(LOW)
    push(gh_own.at[0], out.at[1 - half], far_send.at[0], far_recv.at[0], seq=sibling).wait_recv()

    for q in range(chips):

        @pl.when(2 * q + half != me)
        def _():
            push(w_line.at[0], w_parts.at[q], w_send.at[0], w_recv.at[q], seq=sibling).wait_recv()

    value = w_parts[0].astype(F32)
    for q in range(1, chips):
        value = value + w_parts[q].astype(F32)
    own_w[...] = value

    for k in range(1, n):
        source = lax.rem(me + k, n)
        push(
            line_out.at[source], line_in.at[source], z_send.at[source], z_recv.at[source], seq=source
        ).wait()
    for g in range(group_count):
        own_gw[g] = line_in[g].astype(F32) + line_in[g + group_count].astype(F32)

    for i in range(group_count):

        @pl.when(core * group_count + i != me)
        def _():
            w_push(i).wait_send()

    for tp in range(max(chips - 2, 0), chips):
        sib_copy(tp).wait_send()
    for copy in w_copies + t_copies + b_copies + bt_copies:
        copy.wait_send()
    for tp in range(chips):
        if tp < half_chips:

            @pl.when(is_gate)
            def _():
                far_copy(tp).wait_send()

            @pl.when(jnp.logical_not(is_gate))
            def _():
                gate_copy(tp).wait_send()

        else:

            @pl.when(far_chip_of(tp) != chip)
            def _():
                peer_copy(tp).wait_send()


def attend_back(
    n, nb, heads, size, fold, length, coef, qkv, go, keep, lse, q_full, h, wqkv, w_half, shard
):
    _, rows, width = h.shape
    chips, half_chips = n // 2, n // 4
    paired = nb == 4
    split = 2 if paired else 1
    steps = 2 if paired else nb
    w_rows = w_half.shape[2] // split
    line_rows = width // nb
    slab = wqkv.shape[1]
    dma = pltpu.SemaphoreType.DMA
    vmem = pl.BlockSpec(memory_space=pltpu.VMEM)
    anywhere = pl.BlockSpec(memory_space=pl.ANY)
    one = (n, heads, rows, LANES)
    peers = max(half_chips - 1, 1)
    near = (line_rows // split, slab)
    result = pl.pallas_call(
        functools.partial(back_kernel, n, nb, heads, size, fold),
        out_shape=(
            jax.ShapeDtypeStruct((2, rows, width), LOW),
            jax.ShapeDtypeStruct((n // 2, shard, slab), F32),
            jax.ShapeDtypeStruct((3, shard, width), F32),
            jax.ShapeDtypeStruct((8, LANES), F32),
            jax.ShapeDtypeStruct((split, steps, 3, w_rows, width), LOW),
            jax.ShapeDtypeStruct((split, 3, w_rows, width), LOW),
        ),
        in_specs=[pl.BlockSpec(memory_space=pltpu.SMEM), vmem, anywhere, vmem, anywhere, vmem]
        + [anywhere] * 4,
        out_specs=[vmem, vmem, vmem, vmem, anywhere, anywhere],
        scratch_shapes=[
            pltpu.VMEM(qkv.shape, LOW),
            pltpu.VMEM((n, heads, LANES, rows), LOW),
            pltpu.VMEM(one, LOW),
            pltpu.VMEM((n, heads, 8, rows), F32),
            pltpu.VMEM((n, heads, LANES, rows), F32),
            pltpu.VMEM(one, F32),
            pltpu.VMEM(one, F32),
            pltpu.VMEM((heads, rows, LANES), F32),
            pltpu.VMEM((rows, width), LOW),
            pltpu.VMEM(wqkv.shape, LOW),
            pltpu.VMEM(wqkv.shape, F32),
            pltpu.VMEM((chips, rows, width), LOW),
            pltpu.VMEM((2, rows, width), LOW),
            pltpu.VMEM((chips, rows, width), LOW),
            pltpu.VMEM((peers, half_chips, rows, width), LOW),
            pltpu.VMEM((peers, rows, width), LOW),
            pltpu.VMEM((3, 3, w_rows, width), LOW),
            pltpu.VMEM((split, 3, w_rows, width), LOW),
            pltpu.VMEM((n // 2, 3, shard, width), LOW),
            pltpu.VMEM((chips, 3, shard, width), LOW),
            pltpu.VMEM((nb, line_rows, slab), LOW),
            pltpu.VMEM((split, steps) + near, LOW),
            pltpu.VMEM((split,) + near, LOW),
            pltpu.VMEM((split,) + near, LOW),
            pltpu.VMEM((n, shard, slab), LOW),
            pltpu.VMEM((n, shard, slab), LOW),
            dma((3,)),
            dma((2,)),
            dma((chips,)),
            dma((chips,)),
            dma((half_chips,)),
            dma((peers, half_chips)),
            dma((chips,)),
            dma((peers,)),
            dma((half_chips,)),
            dma((1,)),
            dma((split, steps)),
            dma((split, steps)),
            dma((split,)),
            dma((split,)),
            dma((n // 2,)),
            dma((chips,)),
            dma((split, steps)),
            dma((split, steps)),
            dma((split,)),
            dma((split,)),
            dma((n,)),
            dma((n,)),
            dma((3,)),
        ],
        compiler_params=pltpu.CompilerParams(
            collective_id=4, has_side_effects=True, vmem_limit_bytes=63 * MIB
        ),
        name="attend_back",
    )(length, coef, qkv, go, keep, lse, q_full, h, wqkv, w_half)
    return result[:4]


def total_kernel(n, nb, value, out, mine, line_in, batch_in, z_send, z_recv, b_send, b_recv):
    me, batch = lax.axis_index("seq"), lax.axis_index("batch")
    greet(n, nb)
    copies = []
    for k in range(1, n):
        copy = push(
            value, line_in.at[k], z_send.at[k], z_recv.at[k], seq=lax.rem(me + k, n)
        )
        copy.start()
        copies.append(copy)
    line_in[0] = value[...]
    for copy in copies:
        copy.wait_recv()
    part = jnp.zeros_like(value)
    for s in range(n):
        part = part + line_in[lax.rem(me - s + n, n)]
    mine[...] = part
    for k in range(1, nb):
        copy = push(
            mine, batch_in.at[k], b_send.at[k], b_recv.at[k], batch=lax.rem(batch + k, nb)
        )
        copy.start()
        copies.append(copy)
    batch_in[0] = part
    for copy in copies[n - 1 :]:
        copy.wait_recv()
    part = jnp.zeros_like(part)
    for s in range(nb):
        part = part + batch_in[lax.rem(batch - s + nb, nb)]
    out[...] = part
    for copy in copies:
        copy.wait_send()


def total_all(n, nb, value):
    dma = pltpu.SemaphoreType.DMA
    return pl.pallas_call(
        functools.partial(total_kernel, n, nb),
        out_shape=jax.ShapeDtypeStruct(value.shape, F32),
        in_specs=[pl.BlockSpec(memory_space=pltpu.VMEM)],
        out_specs=pl.BlockSpec(memory_space=pltpu.VMEM),
        scratch_shapes=[
            pltpu.VMEM(value.shape, F32),
            pltpu.VMEM((n,) + value.shape, F32),
            pltpu.VMEM((nb,) + value.shape, F32),
            dma((n,)),
            dma((n,)),
            dma((nb,)),
            dma((nb,)),
        ],
        compiler_params=pltpu.CompilerParams(collective_id=5, has_side_effects=True),
        name="total_all",
    )(value)


def body(
    n,
    nb,
    tokens,
    cotangent,
    weights,
    gains,
    query_scale,
    first_weights,
    second_weights,
    first_gains,
    second_gains,
    first_scale,
    second_scale,
    lengths,
):
    series_count, rows, width = tokens.shape
    size = query_scale.shape[0]
    group_count = n // 2
    heads = width // size // group_count
    group_width = heads * size
    fold = 640 // group_width
    shard = weights.shape[1]
    slab_width = (3 * group_width + 2 + LANES - 1) // LANES * LANES
    half = lax.axis_index("seq") // group_count
    length = lax.dynamic_slice(lengths, (half,), (1,))

    low_weights = weights.astype(LOW)
    slab = (
        low_weights[:3]
        .reshape(3, shard, group_count, group_width)
        .transpose(2, 1, 0, 3)
        .reshape(group_count, shard, 3 * group_width)
    )
    low_gains = jnp.broadcast_to(gains.astype(LOW).T[None], (group_count, shard, 2))
    spare = jnp.zeros((group_count, shard, slab_width - 3 * group_width - 2), LOW)
    slab = jnp.concatenate([slab, low_gains, spare], axis=2)

    xg, wout = gather_tokens(n, nb, tokens, slab)
    wqkv = wout.reshape(nb * n * shard, slab_width)
    gain_rows = wqkv[:, 3 * group_width : 3 * group_width + 2].astype(F32).T
    gain_one, gain_two = gain_rows[0:1], gain_rows[1:2]

    coef = LOG_TWO_E / math.sqrt(size) * jax.nn.softplus(query_scale)
    coef_row = jnp.concatenate([coef, jnp.zeros((LANES - size,), F32)])[None]
    normed_in, qkv, q_full, o_keep, lse, o_recv, w_all = attend(
        n, nb, heads, size, fold, length, tokens, xg, wqkv, gain_one, coef_row, low_weights[3:]
    )
    w_all = w_all.transpose(2, 0, 1, 3, 4).reshape(3, width, width)
    block_out, grad_middle, go_recv, layer_sums, w_half = layer(
        n, nb, fold, tokens, cotangent, o_recv, w_all, gain_two
    )
    layer_sums = jnp.sum(layer_sums, axis=1)
    grad_gain_two = layer_sums[0]
    stat_terms = jnp.sum(layer_sums[1:], axis=1)
    inputs = tokens.astype(F32)
    factor_one = rms_factor(inputs)
    normed_one = inputs * factor_one

    grad_normed, own_slab, own_three, scale_part = attend_back(
        n, nb, heads, size, fold, length, coef_row, qkv, go_recv, o_keep, lse, q_full, normed_in,
        wqkv, w_half, shard,
    )
    grad_normed = grad_normed.astype(F32)
    own_qkv = (
        own_slab[:, :, : 3 * group_width]
        .reshape(group_count, shard, 3, group_width)
        .transpose(2, 1, 0, 3)
        .reshape(3, shard, width)
    )
    own_grads = jnp.concatenate([own_qkv, own_three], axis=0)

    grad_gain_one = jnp.sum(grad_normed * normed_one, axis=(0, 1))
    input_grad = grad_middle + norm_back(grad_normed * gain_one, normed_one, factor_one)
    own_squares = jnp.sum(own_grads * own_grads)
    scale_slope = LOG_TWO_E / math.sqrt(size) * jax.nn.sigmoid(query_scale)
    scale_part = jnp.sum(scale_part, axis=0)[:size] * scale_slope
    small = jnp.concatenate(
        [grad_gain_one, grad_gain_two, scale_part, stat_terms, own_squares[None]]
    )
    small_rows = (small.shape[0] + 8 * LANES - 1) // (8 * LANES) * 8
    small = jnp.pad(small, (0, small_rows * LANES - small.shape[0])).reshape(small_rows, LANES)
    sums = total_all(n, nb, small).reshape(-1)
    gain_sums = sums[: 2 * width].reshape(2, width)
    scale_grad = sums[2 * width : 2 * width + size]
    stat_sums = sums[2 * width + size : 2 * width + size + 3]
    total_squares = (
        sums[2 * width + size + 3] + jnp.sum(gain_sums * gain_sums) + jnp.sum(scale_grad * scale_grad)
    )
    index = lax.axis_index("batch") * n + lax.axis_index("seq")
    own_gain_grads = lax.dynamic_slice(gain_sums, (0, index * shard), (2, shard))

    grad_norm = jnp.sqrt(total_squares)
    clip_factor = CLIP_NORM / jnp.maximum(grad_norm, CLIP_NORM)
    new_weights, new_first_weights, new_second_weights = adam_update(
        weights, own_grads * clip_factor, first_weights, second_weights, MATRIX_RATE, MATRIX_DECAY
    )
    new_gains, new_first_gains, new_second_gains = adam_update(
        gains, own_gain_grads * clip_factor, first_gains, second_gains, GAIN_RATE, 0.0
    )
    new_scale, new_first_scale, new_second_scale = adam_update(
        query_scale, scale_grad * clip_factor, first_scale, second_scale, GAIN_RATE, 0.0
    )
    rms_stats = jnp.sqrt(stat_sums / float(series_count * rows * width * nb * n))
    return (
        block_out,
        input_grad,
        grad_norm,
        new_weights,
        new_first_weights,
        new_second_weights,
        new_gains,
        new_first_gains,
        new_second_gains,
        new_scale,
        new_first_scale,
        new_second_scale,
        rms_stats,
    )


def solution(mesh):
    return jax.shard_map(
        functools.partial(body, mesh.shape["seq"], mesh.shape["batch"]),
        mesh=mesh,
        in_specs=(
            P("batch", "seq", None),
            P("batch", "seq", None),
            P(None, ("batch", "seq"), None),
            P(None, ("batch", "seq")),
            P(),
            P(None, ("batch", "seq"), None),
            P(None, ("batch", "seq"), None),
            P(None, ("batch", "seq")),
            P(None, ("batch", "seq")),
            P(),
            P(),
            P("batch"),
        ),
        out_specs=(
            P("batch", "seq", None),
            P("batch", "seq", None),
            P(),
            P(None, ("batch", "seq"), None),
            P(None, ("batch", "seq"), None),
            P(None, ("batch", "seq"), None),
            P(None, ("batch", "seq")),
            P(None, ("batch", "seq")),
            P(None, ("batch", "seq")),
            P(),
            P(),
            P(),
            P(),
        ),
        check_vma=False,
    )
```

```python
import functools
import math

import jax
import jax.numpy as jnp
from jax import lax
from jax.experimental import pallas as pl
from jax.experimental.pallas import tpu as pltpu
from jax.sharding import PartitionSpec as P

STEP = 10

NORM_EPS = 1e-06
LOG_TWO_E = 1.442695
BETA_FIRST = 0.9
BETA_SECOND = 0.999
ADAM_EPS = 1e-08
MATRIX_RATE = 0.05
GAIN_RATE = 0.5
MATRIX_DECAY = 0.1
CLIP_NORM = 1.0
MASKED = -1e30

MESH = pl.DeviceIdType.MESH
LANES = 128
F32 = jnp.float32
LOW = jnp.bfloat16
MIB = 1024 * 1024


def rms_factor(values):
    return lax.rsqrt(jnp.mean(values * values, axis=-1, keepdims=True) + NORM_EPS)


def norm_back(grad_normed, normed, factor):
    return factor * (grad_normed - normed * jnp.mean(grad_normed * normed, axis=-1, keepdims=True))


def silu_slope(values):
    logistic = jax.nn.sigmoid(values)
    return logistic * (1.0 + values * (1.0 - logistic))


def adam_update(current, gradient, moment_one, moment_two, step_rate, decay_rate):
    new_one = BETA_FIRST * moment_one + (1.0 - BETA_FIRST) * gradient
    new_two = BETA_SECOND * moment_two + (1.0 - BETA_SECOND) * gradient * gradient
    first_hat = new_one / (1.0 - BETA_FIRST**STEP)
    second_hat = new_two / (1.0 - BETA_SECOND**STEP)
    updated = current - step_rate * (
        first_hat / (jnp.sqrt(second_hat) + ADAM_EPS) + decay_rate * current
    )
    return (updated, new_one, new_two)


def dot(left, right, left_axis=1, right_axis=0):
    return lax.dot_general(
        left, right, (((left_axis,), (right_axis,)), ((), ())), preferred_element_type=F32
    )


def greet(seq_count, batch_count):
    barrier = pltpu.get_barrier_semaphore()
    me_seq, me_batch = lax.axis_index("seq"), lax.axis_index("batch")
    for k in range(1, seq_count):
        pl.semaphore_signal(
            barrier,
            inc=1,
            device_id={"seq": lax.rem(me_seq + k, seq_count)},
            device_id_type=MESH,
        )
    for k in range(1, batch_count):
        pl.semaphore_signal(
            barrier,
            inc=1,
            device_id={"batch": lax.rem(me_batch + k, batch_count)},
            device_id_type=MESH,
        )
    pl.semaphore_wait(barrier, seq_count - 1 + batch_count - 1)


def push(source, target, send_sem, recv_sem, **where):
    return pltpu.make_async_remote_copy(
        source, target, send_sem, recv_sem, device_id=where, device_id_type=MESH
    )


def place(seq_count):
    me = lax.axis_index("seq")
    chips = seq_count // 2
    half_chips = chips // 2
    core = lax.rem(me, 2)
    chip = me // 2
    half = chip // half_chips
    base = half * half_chips
    gate_mine = half_chips - 1 + half
    gate_other = half_chips - half
    return me, core, chip, half, base, gate_mine, gate_other


def far_chip(step, half, half_chips):
    return (1 - half) * (half_chips + step) + half * (half_chips - 1 - step)


def batch_neighbours(batch):
    across = lax.rem(batch, 2)
    first = batch + 1 - 2 * across
    second = lax.rem(batch + 2, 4)
    return (first, second), lax.rem(first + 2, 4)


class Spread:
    def __init__(self, nb, ref, send, recv):
        self.nb, self.ref, self.send, self.recv = nb, ref, send, recv
        self.batch = lax.axis_index("batch")
        self.copies = []

    def copy(self, owner, slot, j, lane, target, source=None):
        block = self.ref.at[owner, slot]
        return push(block if source is None else source, block, self.send.at[j, lane], self.recv.at[j, lane], batch=target)

    def route(self, lane):
        sides, across = batch_neighbours(self.batch)
        return sides[lane % 2], sides[1 - lane % 2], across

    def begin(self, slot, lane, source=None):
        if self.nb == 4:
            first, second, _ = self.route(lane)
            targets = [first, second]
        else:
            targets = [lax.rem(self.batch + j, self.nb) for j in range(1, self.nb)]
        new = [
            self.copy(self.batch, slot, j, lane, target, source) for j, target in enumerate(targets)
        ]
        for copy in new:
            copy.start()
        self.copies += new

    def relay(self, slot, lane):
        if self.nb == 4:
            first, second, _ = self.route(lane)
            self.copy(first, slot, 0, lane, first).wait_recv()
            copy = self.copy(first, slot, 2, lane, second)
            copy.start()
            self.copies.append(copy)
            return [first]
        return []

    def finish(self, slot, lane):
        if self.nb == 4:
            _, second, across = self.route(lane)
            self.copy(second, slot, 1, lane, second).wait_recv()
            self.copy(across, slot, 2, lane, second).wait_recv()
            return [second, across]
        owners = []
        for j in range(1, self.nb):
            owner = lax.rem(self.batch + self.nb - j, self.nb)
            self.copy(owner, slot, j - 1, lane, owner).wait_recv()
            owners.append(owner)
        return owners

    def drain(self):
        for copy in self.copies:
            copy.wait_send()


def gather_kernel(
    n, nb, chunks, tok, slab, xg, wout, far_sem, own_sem, pass_sem, sib_sem, same_recv, sib_recv,
    z_send, z_recv, b_send, b_recv, local_sem,
):
    chips, half_chips = n // 2, n // 4
    me, core, chip, half, base, gate_mine, gate_other = place(n)
    group_count = n // 2
    batch = lax.axis_index("batch")
    rows = tok.shape[1] // chunks
    sibling = 2 * chip + 1 - core
    greet(n, nb)

    sends = []
    z_copies = []
    for k in range(1, n):
        target = lax.rem(me + k, n)
        copy = push(
            slab.at[lax.rem(target, group_count)], wout.at[batch, me], z_send.at[k],
            z_recv.at[k], seq=target,
        )
        copy.start()
        z_copies.append(copy)

    def part(ref, lead, c):
        return ref.at[lead, pl.ds(c * rows, rows)]

    def tok_copy(source, slot, c, send_sem, recv_sem, target):
        return push(source, part(xg, slot, c), send_sem, recv_sem.at[slot, c], seq=target)

    for c in range(chunks):
        copy = tok_copy(
            part(tok, 1 - half, c), me, c, far_sem.at[c], same_recv, 2 * gate_other + core
        )
        copy.start()
        sends.append(copy)
        for k in range(1, half_chips):
            other = base + lax.rem(chip - base + k, half_chips)
            copy = tok_copy(
                part(tok, half, c), me, c, own_sem.at[k, c], same_recv, 2 * other + core
            )
            copy.start()
            sends.append(copy)
        copy = tok_copy(part(tok, half, c), me, c, sib_sem.at[0, c], sib_recv, sibling)
        copy.start()
        sends.append(copy)
    own_slab = slab.at[lax.rem(me, group_count)]
    slab_copy = pltpu.make_async_copy(own_slab, wout.at[batch, me], local_sem)
    slab_copy.start()

    slices = Spread(nb, wout, b_send, b_recv)

    def line_slot(k):
        return lax.rem(me + n - k, n)

    def pass_tokens(c):
        for k in range(1, half_chips):
            slot = 2 * (base + lax.rem(chip - base + half_chips - k, half_chips)) + core
            tok_copy(part(xg, slot, c), slot, c, sib_sem.at[k, c], same_recv, sibling).wait_recv()
            copy = tok_copy(part(xg, slot, c), slot, c, sib_sem.at[k, c], sib_recv, sibling)
            copy.start()
            sends.append(copy)
        for k in range(half_chips):
            slot = 2 * far_chip(k, half, half_chips) + core
            lane = half_chips + k
            tok_copy(part(xg, slot, c), slot, c, sib_sem.at[lane, c], same_recv, sibling).wait_recv()

            @pl.when(chip == gate_mine)
            def _():
                for j in range(1, half_chips):
                    other = base + lax.rem(chip - base + j, half_chips)
                    tok_copy(
                        part(xg, slot, c), slot, c, pass_sem.at[k, j, c], same_recv,
                        2 * other + core,
                    ).start()

            copy = tok_copy(part(xg, slot, c), slot, c, sib_sem.at[lane, c], sib_recv, sibling)
            copy.start()
            sends.append(copy)

    slices.begin(me, 0, own_slab)
    for k in range(1, n):
        z_copies[k - 1].wait_recv()
        slices.begin(line_slot(k), k)
    pass_tokens(0)
    for k in range(n):
        slices.relay(line_slot(k), k)
    for c in range(1, chunks):
        pass_tokens(c)
    for k in range(n):
        slices.finish(line_slot(k), k)
    for c in range(chunks):
        for q in range(chips):
            slot = 2 * q + 1 - core
            tok_copy(part(xg, slot, c), slot, c, sib_sem.at[0, c], sib_recv, sibling).wait_recv()
    slab_copy.wait()
    slices.drain()
    for copy in sends + z_copies:
        copy.wait_send()

    @pl.when(chip == gate_mine)
    def _():
        for c in range(chunks):
            for k in range(half_chips):
                for j in range(1, half_chips):
                    tok_copy(
                        part(xg, me, c), me, c, pass_sem.at[k, j, c], same_recv, sibling
                    ).wait_send()


def gather_tokens(n, nb, tokens, slab):
    chunks = 4
    chips, half_chips = n // 2, n // 4
    dma = pltpu.SemaphoreType.DMA
    return pl.pallas_call(
        functools.partial(gather_kernel, n, nb, chunks),
        out_shape=(
            jax.ShapeDtypeStruct((n,) + tokens.shape[1:], tokens.dtype),
            jax.ShapeDtypeStruct((nb, n) + slab.shape[1:], slab.dtype),
        ),
        in_specs=[pl.BlockSpec(memory_space=pl.ANY)] * 2,
        out_specs=[pl.BlockSpec(memory_space=pl.ANY)] * 2,
        scratch_shapes=[
            dma((chunks,)),
            dma((half_chips, chunks)),
            dma((half_chips, half_chips, chunks)),
            dma((chips, chunks)),
            dma((n, chunks)),
            dma((n, chunks)),
            dma((n,)),
            dma((n,)),
            dma((nb, n)),
            dma((nb, n)),
            dma,
        ],
        compiler_params=pltpu.CompilerParams(collective_id=1, has_side_effects=True),
        name="gather_tokens",
    )(tokens, slab)


def widen(values):
    rows, width = values.shape
    return jnp.concatenate([values, jnp.zeros((rows, LANES - width), values.dtype)], axis=1)


def attend_kernel(
    n, nb, heads, size, fold, len_ref, tok, x_in, w_ref, gain_ref, coef_ref, own_w, h_out, qkv_out, q_out,
    keep_out, lse_out, o_out, w_all, x_s, qkv_s, q_s, keep_s, o_s, s_s, m_s, acc_s, sum_s,
    x_sem, h_sem, qkv_sem, q_sem, keep_sem, local_sem, o_send, o_recv, wz_send, wz_recv, wb_send,
    wb_recv, ws_send, ws_recv,
):
    chips = n // 2
    me, core, chip, half, *_ = place(n)
    batch = lax.axis_index("batch")
    sibling = 2 * chip + 1 - core
    block = x_in.shape[1]
    group = range(heads)
    greet(n, nb)

    sends = []
    w_copies = []
    for k in range(1, chips):
        target = 2 * lax.rem(chip + k, chips) + core
        copy = push(own_w, w_all.at[batch, me], wz_send.at[k], wz_recv.at[k], seq=target)
        copy.start()
        w_copies.append(copy)
    w_copy = pltpu.make_async_copy(own_w, w_all.at[batch, me], local_sem.at[0])
    w_copy.start()

    def x_load(i):
        return pltpu.make_async_copy(x_in.at[i], x_s.at[i], x_sem.at[i])

    for i in range(n):

        @pl.when(i != me)
        def _():
            x_load(i).start()

    pltpu.make_async_copy(tok.at[half], x_s.at[me], x_sem.at[me]).start()
    length = len_ref[0]

    whole = Spread(nb, w_all, wb_send, wb_recv)

    def chip_slot(k):
        return 2 * lax.rem(chip + chips - k, chips) + core

    def to_sibling(owner, lane, slot, j, source=None):
        piece = w_all.at[owner, slot]
        copy = push(piece if source is None else source, piece, ws_send.at[j, lane], ws_recv.at[owner, slot], seq=sibling)
        copy.start()
        sends.append(copy)

    whole.begin(me, 0, own_w)
    to_sibling(batch, 0, me, 0, own_w)

    def kept(i):
        return [
            pltpu.make_async_copy(x_s.at[i], h_out.at[i], h_sem.at[i]),
            pltpu.make_async_copy(qkv_s.at[i], qkv_out.at[i], qkv_sem.at[i]),
            pltpu.make_async_copy(q_s.at[i], q_out.at[i], q_sem.at[i]),
            pltpu.make_async_copy(keep_s.at[i], keep_out.at[i], keep_sem.at[i]),
        ]

    def o_push(i):
        return push(o_s.at[i], o_out.at[me], o_send.at[i], o_recv.at[me], seq=i)

    own_o = pltpu.make_async_copy(o_s.at[me], o_out.at[me], local_sem.at[1])

    def project(i):
        x = x_s[i].astype(F32)
        h = (x * rms_factor(x) * gain_ref[...]).astype(LOW)
        x_s[i] = h
        out = dot(h, w_ref[...])
        lane = lax.broadcasted_iota(jnp.int32, (block, LANES), 1)
        row = i * block + lax.broadcasted_iota(jnp.int32, (block, LANES), 0)
        mark = jnp.where(lane == size, 1.0, 0.0)
        hide = jnp.where((lane == size) & (row >= length), MASKED, 0.0)
        for a in group:
            q = widen(out[:, a * size : (a + 1) * size])
            q_s[i, a] = q
            qkv_s[i, a] = (q * coef_ref[...] + mark).astype(LOW)
        for a in range(heads, 2 * heads):
            qkv_s[i, a] = (widen(out[:, a * size : (a + 1) * size]) + hide).astype(LOW)
        for a in range(2 * heads, 3 * heads):
            qkv_s[i, a] = widen(out[:, a * size : (a + 1) * size].astype(LOW))

    def score(i, j, diagonal):
        if diagonal:
            row = lax.broadcasted_iota(jnp.int32, (block, block), 0)
            col = lax.broadcasted_iota(jnp.int32, (block, block), 1)
            visible = col <= row
        for a in group:
            s = dot(qkv_s[i, a], qkv_s[j, heads + a], 1, 1)
            if diagonal:
                s = jnp.where(visible, s, MASKED)
            s_s[a, j] = s
            best = m_s[a]
            for part in range(block // LANES):
                best = jnp.maximum(best, s[:, part * LANES : (part + 1) * LANES])
            m_s[a] = best

    def mix(j):
        for a in group:
            best = m_s[a]
            count = sum_s[a]
            pieces = []
            for part in range(block // LANES):
                e = jnp.exp(s_s[a, j, :, part * LANES : (part + 1) * LANES] - best)
                count = count + e
                pieces.append(e.astype(LOW))
            sum_s[a] = count
            acc_s[a] += dot(jnp.concatenate(pieces, axis=1), qkv_s[j, 2 * heads + a])

    @pl.loop(0, n)
    def _(i):
        x_load(i).wait()
        project(i)

    def query_block(t):
        i = lax.rem(me + 1 + t, n)
        m_s[...] = jnp.full_like(m_s, MASKED)
        sum_s[...] = jnp.zeros_like(sum_s)
        acc_s[...] = jnp.zeros_like(acc_s)
        pl.loop(0, i)(lambda j: score(i, j, False))
        score(i, i, True)
        for a in group:
            m_s[a] = jnp.broadcast_to(jnp.max(m_s[a], axis=1, keepdims=True), (block, LANES))
        pl.loop(0, i + 1)(mix)
        outs = []
        for a in group:
            count = jnp.sum(sum_s[a], axis=1, keepdims=True)
            out = acc_s[a] / count
            keep_s[i, a] = out
            outs.append(out[:, :size])
            lse_out[i, a] = (m_s[a] + jnp.log(count)).T[:8]
        low = jnp.concatenate(outs, axis=1).astype(LOW)
        piece = block // fold
        o_s[i] = jnp.concatenate([low[f * piece : (f + 1) * piece] for f in range(fold)], axis=1)
        for copy in kept(i):
            copy.start()

        @pl.when(i != me)
        def _():
            o_push(i).start()

        @pl.when(i == me)
        def _():
            own_o.start()

    first, second = n // 2 - 1, n - 2
    pl.loop(0, first)(query_block)
    for k in range(1, chips):
        w_copies[k - 1].wait_recv()
        whole.begin(chip_slot(k), k)
        to_sibling(batch, k, chip_slot(k), 0)
    if second > first:
        pl.loop(first, second)(query_block)
    for k in range(chips):
        for j, owner in enumerate(whole.relay(chip_slot(k), k)):
            to_sibling(owner, k, chip_slot(k), 1 + j)
    pl.loop(second, n)(query_block)
    for k in range(chips):
        owners = whole.finish(chip_slot(k), k)
        for j, owner in enumerate(owners):
            to_sibling(owner, k, chip_slot(k), nb - len(owners) + j)

    for k in range(1, n):
        source = lax.rem(me + k, n)
        push(
            o_s.at[source], o_out.at[source], o_send.at[source], o_recv.at[source], seq=source
        ).wait()
    own_o.wait()
    w_copy.wait()
    for owner in range(nb):
        for q in range(chips):
            piece = w_all.at[owner, 2 * q + 1 - core]
            push(
                piece, piece, ws_send.at[0, 0], ws_recv.at[owner, 2 * q + 1 - core], seq=sibling
            ).wait_recv()
    whole.drain()
    for copy in sends + w_copies:
        copy.wait_send()

    @pl.loop(0, n)
    def _(i):
        for copy in kept(i):
            copy.wait()


def attend(n, nb, heads, size, fold, length, tokens, xg, wqkv, gain, coef, own_w):
    _, rows, width = xg.shape
    chips = n // 2
    folded = (n, rows // fold, heads * size * fold)
    many, one = (n, 3 * heads, rows, LANES), (n, heads, rows, LANES)
    dma = pltpu.SemaphoreType.DMA
    vmem = pl.BlockSpec(memory_space=pltpu.VMEM)
    anywhere = pl.BlockSpec(memory_space=pl.ANY)
    state = pltpu.VMEM((heads, rows, LANES), F32)
    return pl.pallas_call(
        functools.partial(attend_kernel, n, nb, heads, size, fold),
        out_shape=(
            jax.ShapeDtypeStruct(xg.shape, LOW),
            jax.ShapeDtypeStruct(many, LOW),
            jax.ShapeDtypeStruct(one, F32),
            jax.ShapeDtypeStruct(one, F32),
            jax.ShapeDtypeStruct((n, heads, 8, rows), F32),
            jax.ShapeDtypeStruct(folded, LOW),
            jax.ShapeDtypeStruct((nb, n) + own_w.shape, LOW),
        ),
        in_specs=[pl.BlockSpec(memory_space=pltpu.SMEM), anywhere, anywhere, vmem, vmem, vmem]
        + [anywhere],
        out_specs=[anywhere, anywhere, anywhere, anywhere, vmem, anywhere, anywhere],
        scratch_shapes=[
            pltpu.VMEM(xg.shape, LOW),
            pltpu.VMEM(many, LOW),
            pltpu.VMEM(one, F32),
            pltpu.VMEM(one, F32),
            pltpu.VMEM(folded, LOW),
            pltpu.VMEM((heads, n, rows, rows), F32),
            state,
            state,
            state,
            dma((n,)),
            dma((n,)),
            dma((n,)),
            dma((n,)),
            dma((n,)),
            dma((2,)),
            dma((n,)),
            dma((n,)),
            dma((chips,)),
            dma((chips,)),
            dma((nb, chips)),
            dma((nb, chips)),
            dma((nb, chips)),
            dma((nb, n)),
        ],
        compiler_params=pltpu.CompilerParams(
            collective_id=2, has_side_effects=True, vmem_limit_bytes=62 * MIB
        ),
        name="attend",
    )(length, tokens, xg, wqkv, gain, coef, own_w)


def fold_rows(values):
    rows, width = values.shape
    return jnp.sum(values.reshape(rows // 8, 8, width), axis=0)


def layer_kernel(
    n, nb, fold, tok, cot, o_in, w_in, gain_ref, y_out, gy_out, go_out, small_out, half_out,
    w, o_s, hidden_s, act_s, gu_s, ga_s, go_s, gw_s, sib_in, w_sem, send_sem, recv_sem, local_sem,
    sib_send, sib_recv,
):
    group_count = n // 2
    me, core, chip, half, base, gate_mine, gate_other = place(n)
    sibling = 2 * chip + 1 - core
    _, rows, width = tok.shape
    group_width = width // group_count
    piece = rows // fold
    barrier = pltpu.get_barrier_semaphore()
    for k in range(1, n):
        pl.semaphore_signal(
            barrier, inc=1, device_id={"seq": lax.rem(me + k, n)}, device_id_type=MESH
        )
    loads = [pltpu.make_async_copy(w_in.at[m], w.at[m], w_sem.at[m]) for m in range(3)]
    for load in loads:
        load.start()
    small_out[...] = jnp.zeros_like(small_out)
    gain = gain_ref[...]

    def go_push(target):
        return push(
            go_s.at[target], go_out.at[me], send_sem.at[target], recv_sem.at[me], seq=target
        )

    own_go = pltpu.make_async_copy(go_s.at[me], go_out.at[me], local_sem)

    for step in range(2):
        t = half if step else 1 - half
        parts = [
            jnp.concatenate(
                [
                    o_in[t * group_count + g, :, f * group_width : (f + 1) * group_width]
                    for g in range(group_count)
                ],
                axis=1,
            )
            for f in range(fold)
        ]
        o = jnp.concatenate(parts, axis=0)
        o_s[t] = o
        if step == 0:
            loads[0].wait()
        a = dot(o, w[0])
        small_out[1] += fold_rows(a * a)
        y1 = tok[t].astype(F32) + a
        factor = rms_factor(y1)
        normed = y1 * factor
        hidden = (normed * gain).astype(LOW)
        hidden_s[t] = hidden
        if step == 0:
            loads[1].wait()
        u = dot(hidden, w[1])
        logistic = 1.0 / (1.0 + jnp.exp(-u))
        act = (u * logistic).astype(LOW)
        act_s[t] = act
        if step == 0:
            loads[2].wait()
        f = dot(act, w[2])
        small_out[2] += fold_rows(f * f)
        y = y1 + f
        small_out[3] += fold_rows(y * y)
        y_out[t] = y.astype(LOW)
        gz = dot(cot[t], w[2], 1, 1)
        gu = (gz * (logistic * (1.0 + u * (1.0 - logistic)))).astype(LOW)
        gu_s[t] = gu
        gh = dot(gu, w[1], 1, 1)
        small_out[0] += fold_rows(gh * normed)
        gy = cot[t].astype(F32) + norm_back(gh * gain, normed, factor)
        gy_out[t] = gy
        ga = gy.astype(LOW)
        ga_s[t] = ga
        go = dot(ga, w[0], 1, 1).astype(LOW)
        for g in range(group_count):
            block = go[:, g * group_width : (g + 1) * group_width]
            go_s[t * group_count + g] = jnp.concatenate(
                [block[f * piece : (f + 1) * piece] for f in range(fold)], axis=1
            )
        if step == 0:
            pl.semaphore_wait(barrier, n - 1)
        for g in range(group_count):
            target = t * group_count + g

            @pl.when(target != me)
            def _():
                go_push(target).start()

            @pl.when(target == me)
            def _():
                own_go.start()

    tile = 256
    half_rows = width // nb // 2
    sib_copies = []
    pairs = ((act_s, cot, 2), (hidden_s, gu_s, 1), (o_s, ga_s, 0))
    for left, right, m in pairs:

        @pl.loop(0, width // tile)
        def _(k):
            cols = pl.ds(pl.multiple_of(k * tile, tile), tile)
            total = dot(left[0, :, cols], right[0], 0, 0) + dot(left[1, :, cols], right[1], 0, 0)
            gw_s[m, cols] = total.astype(LOW)

        for b in range(nb):
            start = pl.multiple_of((2 * b + 1 - core) * half_rows, 16)
            copy = push(
                gw_s.at[m, pl.ds(start, half_rows)], sib_in.at[b, m], sib_send.at[b, m],
                sib_recv.at[b, m], seq=sibling,
            )
            copy.start()
            sib_copies.append(copy)
    index = 0
    for _, _, m in pairs:
        for b in range(nb):
            sib_copies[index].wait_recv()
            index += 1
            start = pl.multiple_of((2 * b + core) * half_rows, 16)
            half_out[b, m] = (
                gw_s[m, pl.ds(start, half_rows)].astype(F32) + sib_in[b, m].astype(F32)
            ).astype(LOW)
    for k in range(1, n):
        source = lax.rem(me + k, n)
        push(
            go_s.at[source], go_out.at[source], send_sem.at[source], recv_sem.at[source], seq=source
        ).wait()
    own_go.wait()
    for copy in sib_copies:
        copy.wait_send()


def layer(n, nb, fold, tokens, cotangent, o_recv, w_all, gain):
    _, rows, width = tokens.shape
    half_rows = width // nb // 2
    dma = pltpu.SemaphoreType.DMA
    vmem = pl.BlockSpec(memory_space=pltpu.VMEM)
    anywhere = pl.BlockSpec(memory_space=pl.ANY)
    kept = pltpu.VMEM((2, rows, width), LOW)
    return pl.pallas_call(
        functools.partial(layer_kernel, n, nb, fold),
        out_shape=(
            jax.ShapeDtypeStruct((2, rows, width), LOW),
            jax.ShapeDtypeStruct((2, rows, width), F32),
            jax.ShapeDtypeStruct(o_recv.shape, LOW),
            jax.ShapeDtypeStruct((4, 8, width), F32),
            jax.ShapeDtypeStruct((nb, 3, half_rows, width), LOW),
        ),
        in_specs=[vmem, vmem, vmem, anywhere, vmem],
        out_specs=[vmem, vmem, anywhere, vmem, vmem],
        scratch_shapes=[
            pltpu.VMEM((3, width, width), LOW),
            kept,
            kept,
            kept,
            kept,
            kept,
            pltpu.VMEM(o_recv.shape, LOW),
            pltpu.VMEM((3, width, width), LOW),
            pltpu.VMEM((nb, 3, half_rows, width), LOW),
            dma((3,)),
            dma((n,)),
            dma((n,)),
            dma,
            dma((nb, 3)),
            dma((nb, 3)),
        ],
        compiler_params=pltpu.CompilerParams(
            collective_id=3, has_side_effects=True, vmem_limit_bytes=63 * MIB
        ),
        name="layer",
    )(tokens, cotangent, o_recv, w_all, gain)


def back_kernel(
    n, nb, heads, size, fold, len_ref, coef_ref, qkv_in, go_ref, keep_in, lse_ref, q_in, h_in, w_in,
    half_in, tok, sums_ref, out, own_gw, own_w, sums_out, cross_in, turn_in,
    qkv, kt, g_s, delta, gq, gk, gv, q_s, h_s, w_s, gw, gh_own, gh_out, from_sib, gate_in, peer_in,
    stage, cross_out, w_line, w_parts, gw_low, near_in, near_out, near_turn, line_out, line_in,
    load_sem, block_sem, sib_send, sib_recv, gate_send, gate_recv, peer_send, peer_recv, far_send,
    far_recv, c_send, c_recv, t_send, t_recv, w_send, w_recv, b_send, b_recv, bt_send, bt_recv,
    z_send, z_recv, stage_sem, scale_sum, sum_mine, sum_line, sum_batch, s_send, s_recv, u_send,
    u_recv,
):
    chips, half_chips = n // 2, n // 4
    me, core, chip, half, base, gate_mine, gate_other = place(n)
    group_count = n // 2
    batch = lax.axis_index("batch")
    sibling = 2 * chip + 1 - core
    block = qkv.shape[2]
    group = range(heads)
    sides, across = batch_neighbours(batch)
    is_gate = chip == gate_mine
    paired = nb == 4
    greet(n, nb)

    w_rows = stage.shape[2]

    def w_piece(owner, h):
        return half_in.at[owner, :, pl.ds(h * w_rows, w_rows)]

    w_copies = []
    if paired:
        for h in range(2):
            for j, owner in enumerate((across, sides[h])):
                w_copies.append(
                    push(
                        w_piece(owner, h), cross_in.at[h, j], c_send.at[h, j], c_recv.at[h, j],
                        batch=sides[h],
                    )
                )
    else:
        for k in range(1, nb):
            target = lax.rem(batch + k, nb)
            w_copies.append(
                push(
                    w_piece(target, 0), cross_in.at[0, k], c_send.at[0, k], c_recv.at[0, k],
                    batch=target,
                )
            )
    for copy in w_copies:
        copy.start()

    keep_load = pltpu.make_async_copy(keep_in, gk, load_sem.at[0])
    qkv_load = pltpu.make_async_copy(qkv_in, qkv, load_sem.at[1])
    w_load = pltpu.make_async_copy(w_in, w_s, load_sem.at[2])
    for load in (keep_load, qkv_load, w_load):
        load.start()
    scale_sum[...] = jnp.zeros_like(scale_sum)
    gv[...] = jnp.zeros_like(gv)
    gq[...] = jnp.zeros_like(gq)
    keep_load.wait()

    @pl.loop(0, n)
    def _(i):
        for a in group:
            g = widen(
                jnp.concatenate(
                    [
                        go_ref[i, :, (f * heads + a) * size : (f * heads + a + 1) * size]
                        for f in range(fold)
                    ],
                    axis=0,
                )
            )
            g_s[i, a] = g
            delta[i, a] = jnp.broadcast_to(
                jnp.sum((g.astype(F32) * gk[i, a]).T, axis=0, keepdims=True), (8, block)
            )
            gk[i, a] = jnp.zeros_like(gk[i, a])

    qkv_load.wait()

    @pl.loop(0, n)
    def _(j):
        for a in group:
            kt[j, a] = qkv[j, heads + a].T

    w_load.wait()

    def pair_block(i, j, diagonal):
        if diagonal:
            col = lax.broadcasted_iota(jnp.int32, (block, block), 0)
            row = lax.broadcasted_iota(jnp.int32, (block, block), 1)
            visible = col <= row
        for a in group:
            s = dot(qkv[j, heads + a], qkv[i, a], 1, 1)
            p = jnp.exp(s - lse_ref[i, a, :1])
            if diagonal:
                p = jnp.where(visible, p, 0.0)
            dp = dot(qkv[j, 2 * heads + a], g_s[i, a], 1, 1)
            ds = (p * (dp - delta[i, a, :1])).astype(LOW)
            gk[j, a] += dot(ds, qkv[i, a])
            gv[j, a] += dot(p.astype(LOW), g_s[i, a])
            gq[i, a] += dot(kt[j, a], ds)

    def sib_copy(t):
        return push(
            gh_out.at[t % 2], from_sib.at[t], sib_send.at[t], sib_recv.at[t], seq=sibling
        )

    def step(t, u):
        r = half * t + (1 - half) * (n - 1 - t)
        loads = [
            pltpu.make_async_copy(q_in.at[r], q_s, block_sem.at[0]),
            pltpu.make_async_copy(h_in.at[r], h_s, block_sem.at[1]),
        ]
        for load in loads:
            load.start()
        pair_block(r, r, True)
        pl.loop(1, n - t)(lambda v: pair_block(r + half * v, r - (1 - half) * v, False))
        for load in loads:
            load.wait()
        pieces = []
        for a in group:
            grad = gq[r, a].T.astype(LOW).astype(F32)
            scale_sum[...] += fold_rows(grad * q_s[a])
            pieces.append((grad * coef_ref[...])[:, :size].astype(LOW))
        pieces += [gk[r, a][:, :size].astype(LOW) for a in group]
        pieces += [gv[r, a][:, :size].astype(LOW) for a in group]
        spare = w_s.shape[1] - 3 * heads * size
        pieces.append(jnp.zeros((block, spare), LOW))
        grads = jnp.concatenate(pieces, axis=1)
        gh = dot(grads, w_s[...], 1, 1).astype(LOW)
        tp = t // 2
        mine = lax.rem(r, 2) == core

        @pl.when(mine)
        def _():
            gh_own[tp] = gh

        @pl.when(jnp.logical_not(mine))
        def _():
            gh_out[tp % 2] = gh
            sib_copy(tp).start()

        part = dot(h_s[...], grads, 0, 0)
        if t == 0:
            gw[...] = part
        else:
            gw[...] += part

    def far_chip_of(tp):
        return half * tp + (1 - half) * (chips - 1 - tp)

    def gate_copy(tp):
        after = lax.rem(chip - gate_mine + half_chips, half_chips)
        return push(
            gh_own.at[tp], gate_in.at[after - 1, tp], gate_send.at[tp],
            gate_recv.at[after - 1, tp], seq=2 * gate_mine + core,
        )

    def far_copy(tp):
        return push(
            gh_own.at[tp], out.at[half], far_send.at[tp], far_recv.at[0],
            seq=2 * far_chip_of(tp) + core,
        )

    def peer_copy(tp):
        q = far_chip_of(tp)
        after = lax.rem(chip - q + half_chips, half_chips)
        return push(
            gh_own.at[tp], peer_in.at[after - 1], peer_send.at[tp], peer_recv.at[after - 1],
            seq=2 * q + core,
        )

    def relay(tp):
        @pl.when(is_gate)
        def _():
            value = gh_own[tp].astype(F32)
            for j in range(half_chips - 1):
                push(
                    gh_own.at[tp], gate_in.at[j, tp], gate_send.at[tp], gate_recv.at[j, tp],
                    seq=sibling,
                ).wait_recv()
                value = value + gate_in[j, tp].astype(F32)
            gh_own[tp] = value.astype(LOW)
            far_copy(tp).start()

    shard = own_w.shape[1]

    def staged(*sources):
        value = None
        for first in range(0, len(sources), 3):
            loads = [
                pltpu.make_async_copy(source, stage.at[j], stage_sem.at[j])
                for j, source in enumerate(sources[first : first + 3])
            ]
            for load in loads:
                load.start()
            for load in loads:
                load.wait()
            for j in range(len(loads)):
                term = stage[j].astype(F32)
                value = term if value is None else value + term
        return value

    t_copies = []

    def turn():
        if paired:
            for h in range(2):
                w_copies[2 * h].wait_recv()
                cross_out[h] = staged(w_piece(sides[1 - h], h), cross_in.at[h, 0]).astype(LOW)
                copy = push(
                    cross_out.at[h], turn_in.at[h], t_send.at[h], t_recv.at[h], batch=sides[1 - h]
                )
                copy.start()
                t_copies.append(copy)

    def w_push(i):
        target = core * group_count + i
        return push(w_line.at[i], w_parts.at[chip], w_send.at[i], w_recv.at[chip], seq=target)

    def to_owners():
        for copy in w_copies[1::2] if paired else w_copies:
            copy.wait_recv()
        for copy in t_copies:
            copy.wait_recv()
        splits = 2 if paired else 1
        each = group_count // splits
        for h in range(splits):
            if paired:
                value = staged(w_piece(batch, h), cross_in.at[h, 1], turn_in.at[h])
            else:
                value = staged(w_piece(batch, 0), *[cross_in.at[0, k] for k in range(1, nb)])
            for i in range(each):
                w_line[h * each + i] = value[:, i * shard : (i + 1) * shard].astype(LOW)
        for i in range(group_count):
            own = core * group_count + i == me

            @pl.when(own)
            def _():
                w_parts[chip] = w_line[i]

            @pl.when(jnp.logical_not(own))
            def _():
                w_push(i).start()

    for tp in range(chips):
        if tp >= 2:
            sib_copy(tp - 2).wait_send()
        step(2 * tp, 0)
        step(2 * tp + 1, 1)
        if tp == 0:
            turn()
        if tp == 1:
            to_owners()
        sib_copy(tp).wait_recv()
        gh_own[tp] = (gh_own[tp].astype(F32) + from_sib[tp].astype(F32)).astype(LOW)
        if tp < half_chips:

            @pl.when(jnp.logical_not(is_gate))
            def _():
                gate_copy(tp).start()

        else:

            @pl.when(far_chip_of(tp) != chip)
            def _():
                peer_copy(tp).start()

        if 1 <= tp < half_chips:
            relay(tp - 1)

    line_rows = gw.shape[0] // nb
    near_rows = near_in.shape[2]
    for b in range(nb):
        gw_low[b] = gw[b * line_rows : (b + 1) * line_rows].astype(LOW)

    def near_piece(owner, h):
        return gw_low.at[owner, pl.ds(h * near_rows, near_rows)]

    b_copies = []
    if paired:
        for h in range(2):
            for j, owner in enumerate((across, sides[h])):
                b_copies.append(
                    push(
                        near_piece(owner, h), near_in.at[h, j], b_send.at[h, j], b_recv.at[h, j],
                        batch=sides[h],
                    )
                )
    else:
        for k in range(1, nb):
            target = lax.rem(batch + k, nb)
            b_copies.append(
                push(
                    near_piece(target, 0), near_in.at[0, k], b_send.at[0, k], b_recv.at[0, k],
                    batch=target,
                )
            )
    for copy in b_copies:
        copy.start()
    relay(half_chips - 1)
    bt_copies = []
    if paired:
        for h in range(2):
            b_copies[2 * h].wait_recv()
            near_out[h] = (
                gw_low[sides[1 - h], pl.ds(h * near_rows, near_rows)].astype(F32)
                + near_in[h, 0].astype(F32)
            ).astype(LOW)
            copy = push(
                near_out.at[h], near_turn.at[h], bt_send.at[h], bt_recv.at[h], batch=sides[1 - h]
            )
            copy.start()
            bt_copies.append(copy)
    z_copies = []

    def z_copy(target):
        return push(
            line_out.at[target], line_in.at[me], z_send.at[target], z_recv.at[me], seq=target
        )

    splits = 2 if paired else 1
    each = n // splits
    for h in range(splits):
        value = gw_low[batch, pl.ds(h * near_rows, near_rows)].astype(F32)
        if paired:
            b_copies[2 * h + 1].wait_recv()
            bt_copies[h].wait_recv()
            value = value + near_in[h, 1].astype(F32) + near_turn[h].astype(F32)
        else:
            for k in range(1, nb):
                b_copies[k - 1].wait_recv()
                value = value + near_in[0, k].astype(F32)
        for i in range(each):
            target = h * each + i
            line_out[target] = value[i * shard : (i + 1) * shard].astype(LOW)

            @pl.when(target != me)
            def _():
                z_copy(target).start()

            @pl.when(target == me)
            def _():
                line_in[me] = line_out[target]

    value = gh_own[half * chip + (1 - half) * (chips - 1 - chip)].astype(F32)
    for j in range(half_chips - 1):
        push(
            gh_own.at[0], peer_in.at[j], peer_send.at[0], peer_recv.at[j], seq=sibling
        ).wait_recv()
        value = value + peer_in[j].astype(F32)
    out[half] = value.astype(LOW)
    push(gh_own.at[0], out.at[1 - half], far_send.at[0], far_recv.at[0], seq=sibling).wait_recv()

    tiles = out.shape[2] // LANES
    gain_sum = None
    for t in range(2):
        load = pltpu.make_async_copy(tok.at[t], h_s, block_sem.at[1])
        load.start()
        load.wait()
        x = h_s[...].astype(F32)
        term = fold_rows(out[t].astype(F32) * (x * rms_factor(x)))
        gain_sum = term if gain_sum is None else gain_sum + term

    def lanes(row):
        return [row[:, k * LANES : (k + 1) * LANES] for k in range(row.shape[1] // LANES)]

    def squeeze(row):
        total = None
        for piece in lanes(row):
            total = piece if total is None else total + piece
        return total

    rows_out = lanes(jnp.sum(gain_sum, axis=0, keepdims=True))
    rows_out += lanes(jnp.sum(sums_ref[0], axis=0, keepdims=True))
    rows_out.append(jnp.sum(scale_sum[...], axis=0, keepdims=True))
    for k in range(1, 4):
        rows_out.append(squeeze(jnp.sum(sums_ref[k], axis=0, keepdims=True)))

    for q in range(chips):

        @pl.when(2 * q + half != me)
        def _():
            push(w_line.at[0], w_parts.at[q], w_send.at[0], w_recv.at[q], seq=sibling).wait_recv()

    value = w_parts[0].astype(F32)
    for q in range(1, chips):
        value = value + w_parts[q].astype(F32)
    own_w[...] = value

    for k in range(1, n):
        source = lax.rem(me + k, n)
        push(
            line_out.at[source], line_in.at[source], z_send.at[source], z_recv.at[source], seq=source
        ).wait()
    for g in range(group_count):
        own_gw[g] = line_in[g].astype(F32) + line_in[g + group_count].astype(F32)

    squares = None
    for value in [own_gw[g] for g in range(group_count)] + [own_w[m] for m in range(3)]:
        term = squeeze(jnp.sum(value * value, axis=0, keepdims=True))
        squares = term if squares is None else squares + term
    rows_out.append(squares)
    sum_mine[0] = jnp.zeros_like(sum_mine[0])
    for k, row in enumerate(rows_out):
        sum_mine[0, k : k + 1, :] = row
    s_copies = []
    for k in range(1, n):
        copy = push(
            sum_mine.at[0], sum_line.at[k], s_send.at[k], s_recv.at[k], seq=lax.rem(me + k, n)
        )
        copy.start()
        s_copies.append(copy)
    sum_line[0] = sum_mine[0]
    for copy in s_copies:
        copy.wait_recv()
    value = jnp.zeros_like(sum_mine[0])
    for k in range(n):
        value = value + sum_line[lax.rem(me - k + n, n)]
    sum_mine[1] = value
    for k in range(1, nb):
        copy = push(
            sum_mine.at[1], sum_batch.at[k], u_send.at[k], u_recv.at[k],
            batch=lax.rem(batch + k, nb),
        )
        copy.start()
        s_copies.append(copy)
    sum_batch[0] = value
    for copy in s_copies[n - 1 :]:
        copy.wait_recv()
    value = jnp.zeros_like(value)
    for k in range(nb):
        value = value + sum_batch[lax.rem(batch - k + nb, nb)]
    sums_out[...] = value

    for i in range(group_count):

        @pl.when(core * group_count + i != me)
        def _():
            w_push(i).wait_send()

    for tp in range(max(chips - 2, 0), chips):
        sib_copy(tp).wait_send()
    for copy in w_copies + t_copies + b_copies + bt_copies + s_copies:
        copy.wait_send()
    for tp in range(chips):
        if tp < half_chips:

            @pl.when(is_gate)
            def _():
                far_copy(tp).wait_send()

            @pl.when(jnp.logical_not(is_gate))
            def _():
                gate_copy(tp).wait_send()

        else:

            @pl.when(far_chip_of(tp) != chip)
            def _():
                peer_copy(tp).wait_send()


def attend_back(
    n, nb, heads, size, fold, length, coef, qkv, go, keep, lse, q_full, h, wqkv, w_half, tokens,
    layer_sums, shard,
):
    _, rows, width = h.shape
    chips, half_chips = n // 2, n // 4
    paired = nb == 4
    split = 2 if paired else 1
    steps = 2 if paired else nb
    w_rows = w_half.shape[2] // split
    line_rows = width // nb
    slab = wqkv.shape[1]
    dma = pltpu.SemaphoreType.DMA
    vmem = pl.BlockSpec(memory_space=pltpu.VMEM)
    anywhere = pl.BlockSpec(memory_space=pl.ANY)
    one = (n, heads, rows, LANES)
    peers = max(half_chips - 1, 1)
    near = (line_rows // split, slab)
    small_rows = (2 * (width // LANES) + 5 + 7) // 8 * 8
    result = pl.pallas_call(
        functools.partial(back_kernel, n, nb, heads, size, fold),
        out_shape=(
            jax.ShapeDtypeStruct((2, rows, width), LOW),
            jax.ShapeDtypeStruct((n // 2, shard, slab), F32),
            jax.ShapeDtypeStruct((3, shard, width), F32),
            jax.ShapeDtypeStruct((small_rows, LANES), F32),
            jax.ShapeDtypeStruct((split, steps, 3, w_rows, width), LOW),
            jax.ShapeDtypeStruct((split, 3, w_rows, width), LOW),
        ),
        in_specs=[pl.BlockSpec(memory_space=pltpu.SMEM), vmem, anywhere, vmem, anywhere, vmem]
        + [anywhere] * 5
        + [vmem],
        out_specs=[vmem, vmem, vmem, vmem, anywhere, anywhere],
        scratch_shapes=[
            pltpu.VMEM(qkv.shape, LOW),
            pltpu.VMEM((n, heads, LANES, rows), LOW),
            pltpu.VMEM(one, LOW),
            pltpu.VMEM((n, heads, 8, rows), F32),
            pltpu.VMEM((n, heads, LANES, rows), F32),
            pltpu.VMEM(one, F32),
            pltpu.VMEM(one, F32),
            pltpu.VMEM((heads, rows, LANES), F32),
            pltpu.VMEM((rows, width), LOW),
            pltpu.VMEM(wqkv.shape, LOW),
            pltpu.VMEM(wqkv.shape, F32),
            pltpu.VMEM((chips, rows, width), LOW),
            pltpu.VMEM((2, rows, width), LOW),
            pltpu.VMEM((chips, rows, width), LOW),
            pltpu.VMEM((peers, half_chips, rows, width), LOW),
            pltpu.VMEM((peers, rows, width), LOW),
            pltpu.VMEM((3, 3, w_rows, width), LOW),
            pltpu.VMEM((split, 3, w_rows, width), LOW),
            pltpu.VMEM((n // 2, 3, shard, width), LOW),
            pltpu.VMEM((chips, 3, shard, width), LOW),
            pltpu.VMEM((nb, line_rows, slab), LOW),
            pltpu.VMEM((split, steps) + near, LOW),
            pltpu.VMEM((split,) + near, LOW),
            pltpu.VMEM((split,) + near, LOW),
            pltpu.VMEM((n, shard, slab), LOW),
            pltpu.VMEM((n, shard, slab), LOW),
            dma((3,)),
            dma((2,)),
            dma((chips,)),
            dma((chips,)),
            dma((half_chips,)),
            dma((peers, half_chips)),
            dma((chips,)),
            dma((peers,)),
            dma((half_chips,)),
            dma((1,)),
            dma((split, steps)),
            dma((split, steps)),
            dma((split,)),
            dma((split,)),
            dma((n // 2,)),
            dma((chips,)),
            dma((split, steps)),
            dma((split, steps)),
            dma((split,)),
            dma((split,)),
            dma((n,)),
            dma((n,)),
            dma((3,)),
            pltpu.VMEM((8, LANES), F32),
            pltpu.VMEM((2, small_rows, LANES), F32),
            pltpu.VMEM((n, small_rows, LANES), F32),
            pltpu.VMEM((nb, small_rows, LANES), F32),
            dma((n,)),
            dma((n,)),
            dma((nb,)),
            dma((nb,)),
        ],
        compiler_params=pltpu.CompilerParams(
            collective_id=4, has_side_effects=True, vmem_limit_bytes=63 * MIB
        ),
        name="attend_back",
    )(length, coef, qkv, go, keep, lse, q_full, h, wqkv, w_half, tokens, layer_sums)
    return result[:4]


def update_kernel(
    group_count, group_width, count, sums, gw, gw3, gain_ref, scale, first_s, second_s, gains, first_g,
    second_g, tok_in, gy_in, gh_in, w_in, m_in, s_in, norm_out, scale_out, first_s_out, second_s_out,
    gains_out, first_g_out, second_g_out, rms_out, grad_out, w_out, m_out, s_out,
    tok, gy, gh, w, m, v, sems,
):
    pairs = [(tok_in, tok), (gh_in, gh), (gy_in, gy), (w_in, w), (m_in, m), (s_in, v)]
    loads = [pltpu.make_async_copy(a, b, sems.at[k]) for k, (a, b) in enumerate(pairs)]
    for load in loads:
        load.start()
    width = tok.shape[2]
    tiles = width // LANES
    size = scale.shape[1]
    shard = gains.shape[1]
    gain_sums = [
        jnp.concatenate([sums[k * tiles + j : k * tiles + j + 1] for j in range(tiles)], axis=1)
        for k in range(2)
    ]
    slope = LOG_TWO_E / math.sqrt(size) / (1.0 + jnp.exp(-scale[...]))
    scale_grad = sums[2 * tiles : 2 * tiles + 1, :size] * slope

    def add_up(row):
        return jnp.sum(row, axis=1, keepdims=True)

    stats = [add_up(sums[2 * tiles + 1 + k : 2 * tiles + 2 + k]) for k in range(4)]
    for k in range(3):
        rms_out[:, k : k + 1] = jnp.sqrt(stats[k] / count)
    norm = jnp.sqrt(
        stats[3]
        + add_up(gain_sums[0] * gain_sums[0])
        + add_up(gain_sums[1] * gain_sums[1])
        + add_up(scale_grad * scale_grad)
    )
    norm_out[...] = norm
    clip = CLIP_NORM / jnp.maximum(norm, CLIP_NORM)

    def adam(outs, current, gradient, one, two, rate, decay):
        for out, value in zip(outs, adam_update(current, gradient * clip, one, two, rate, decay)):
            out[...] = value

    adam(
        (scale_out, first_s_out, second_s_out), scale[...], scale_grad, first_s[...], second_s[...],
        GAIN_RATE, 0.0,
    )
    index = lax.axis_index("batch") * lax.axis_size("seq") + lax.axis_index("seq")
    own = jnp.concatenate(gain_sums + [jnp.zeros((6, width), F32)], axis=0)
    own = pltpu.roll(own, lax.rem(width - index * shard, width), 1)[:2, :shard]
    adam(
        (gains_out, first_g_out, second_g_out), gains[...], own, first_g[...], second_g[...],
        GAIN_RATE, 0.0,
    )

    for load in loads[:3]:
        load.wait()
    for t in range(2):
        x = tok[t].astype(F32)
        factor = rms_factor(x)
        grad = gh[t].astype(F32) * gain_ref[...]
        gy[t] = gy[t] + norm_back(grad, x * factor, factor)
    stores = [pltpu.make_async_copy(gy, grad_out, sems.at[0])]
    stores[0].start()
    for load in loads[3:]:
        load.wait()
    for k in range(6):
        if k < 3:
            span = slice(k * group_width, (k + 1) * group_width)
            gradient = jnp.concatenate([gw[g][:, span] for g in range(group_count)], axis=1)
        else:
            gradient = gw3[k - 3]
        w[k], m[k], v[k] = adam_update(w[k], gradient * clip, m[k], v[k], MATRIX_RATE, MATRIX_DECAY)
        for j, (a, b) in enumerate(((w, w_out), (m, m_out), (v, s_out))):
            copy = pltpu.make_async_copy(a.at[k], b.at[k], sems.at[6 + 3 * k + j])
            copy.start()
            stores.append(copy)
    for copy in stores:
        copy.wait()


def update(
    group_count, group_width, count, sums, gw, gw3, gain, scale, first_s, second_s, gains, first_g,
    second_g, tokens, gy, gh, weights, first_w, second_w,
):
    vmem = pl.BlockSpec(memory_space=pltpu.VMEM)
    anywhere = pl.BlockSpec(memory_space=pl.ANY)

    def like(value):
        return jax.ShapeDtypeStruct(value.shape, F32)

    kept = pltpu.VMEM(weights.shape, F32)
    return pl.pallas_call(
        functools.partial(update_kernel, group_count, group_width, count),
        out_shape=(
            jax.ShapeDtypeStruct((1, 1), F32), like(scale), like(scale), like(scale), like(gains),
            like(gains), like(gains), jax.ShapeDtypeStruct((1, 3), F32), like(gy), like(weights),
            like(weights), like(weights),
        ),
        in_specs=[vmem] * 10 + [anywhere] * 6,
        out_specs=[vmem] * 8 + [anywhere] * 4,
        scratch_shapes=[
            pltpu.VMEM(tokens.shape, LOW),
            pltpu.VMEM(gy.shape, F32),
            pltpu.VMEM(gh.shape, LOW),
            kept,
            kept,
            kept,
            pltpu.SemaphoreType.DMA((24,)),
        ],
        compiler_params=pltpu.CompilerParams(vmem_limit_bytes=62 * MIB),
        name="update",
    )(
        sums, gw, gw3, gain, scale, first_s, second_s, gains, first_g, second_g, tokens, gy, gh,
        weights, first_w, second_w,
    )


def body(
    n,
    nb,
    tokens,
    cotangent,
    weights,
    gains,
    query_scale,
    first_weights,
    second_weights,
    first_gains,
    second_gains,
    first_scale,
    second_scale,
    lengths,
):
    series_count, rows, width = tokens.shape
    size = query_scale.shape[0]
    group_count = n // 2
    heads = width // size // group_count
    group_width = heads * size
    fold = 640 // group_width
    shard = weights.shape[1]
    slab_width = (3 * group_width + 2 + LANES - 1) // LANES * LANES
    half = lax.axis_index("seq") // group_count
    length = lax.dynamic_slice(lengths, (half,), (1,))

    low_weights = weights.astype(LOW)
    slab = (
        low_weights[:3]
        .reshape(3, shard, group_count, group_width)
        .transpose(2, 1, 0, 3)
        .reshape(group_count, shard, 3 * group_width)
    )
    low_gains = jnp.broadcast_to(gains.astype(LOW).T[None], (group_count, shard, 2))
    spare = jnp.zeros((group_count, shard, slab_width - 3 * group_width - 2), LOW)
    slab = jnp.concatenate([slab, low_gains, spare], axis=2)

    xg, wout = gather_tokens(n, nb, tokens, slab)
    wqkv = wout.reshape(nb * n * shard, slab_width)
    gain_rows = wqkv[:, 3 * group_width : 3 * group_width + 2].astype(F32).T
    gain_one, gain_two = gain_rows[0:1], gain_rows[1:2]

    coef = LOG_TWO_E / math.sqrt(size) * jax.nn.softplus(query_scale)
    coef_row = jnp.concatenate([coef, jnp.zeros((LANES - size,), F32)])[None]
    normed_in, qkv, q_full, o_keep, lse, o_recv, w_all = attend(
        n, nb, heads, size, fold, length, tokens, xg, wqkv, gain_one, coef_row, low_weights[3:]
    )
    w_all = w_all.transpose(2, 0, 1, 3, 4).reshape(3, width, width)
    block_out, grad_middle, go_recv, layer_sums, w_half = layer(
        n, nb, fold, tokens, cotangent, o_recv, w_all, gain_two
    )
    grad_normed, own_slab, own_three, sums = attend_back(
        n, nb, heads, size, fold, length, coef_row, qkv, go_recv, o_keep, lse, q_full, normed_in,
        wqkv, w_half, tokens, layer_sums, shard,
    )
    count = float(series_count * rows * width * nb * n)
    (
        grad_norm, new_scale, new_first_scale, new_second_scale, new_gains, new_first_gains,
        new_second_gains, rms_stats, input_grad, new_weights, new_first_weights, new_second_weights,
    ) = update(
        group_count, group_width, count, sums, own_slab, own_three, gain_one, query_scale[None],
        first_scale[None], second_scale[None], gains, first_gains, second_gains, tokens, grad_middle,
        grad_normed, weights, first_weights, second_weights,
    )
    grad_norm = grad_norm.reshape(())
    new_scale, new_first_scale, new_second_scale = (
        new_scale.reshape(size), new_first_scale.reshape(size), new_second_scale.reshape(size)
    )
    rms_stats = rms_stats.reshape(3)
    return (
        block_out,
        input_grad,
        grad_norm,
        new_weights,
        new_first_weights,
        new_second_weights,
        new_gains,
        new_first_gains,
        new_second_gains,
        new_scale,
        new_first_scale,
        new_second_scale,
        rms_stats,
    )


def solution(mesh):
    return jax.shard_map(
        functools.partial(body, mesh.shape["seq"], mesh.shape["batch"]),
        mesh=mesh,
        in_specs=(
            P("batch", "seq", None),
            P("batch", "seq", None),
            P(None, ("batch", "seq"), None),
            P(None, ("batch", "seq")),
            P(),
            P(None, ("batch", "seq"), None),
            P(None, ("batch", "seq"), None),
            P(None, ("batch", "seq")),
            P(None, ("batch", "seq")),
            P(),
            P(),
            P("batch"),
        ),
        out_specs=(
            P("batch", "seq", None),
            P("batch", "seq", None),
            P(),
            P(None, ("batch", "seq"), None),
            P(None, ("batch", "seq"), None),
            P(None, ("batch", "seq"), None),
            P(None, ("batch", "seq")),
            P(None, ("batch", "seq")),
            P(None, ("batch", "seq")),
            P(),
            P(),
            P(),
            P(),
        ),
        check_vma=False,
    )
```

```python
import functools
import math

import jax
import jax.numpy as jnp
from jax import lax
from jax.experimental import pallas as pl
from jax.experimental.pallas import tpu as pltpu
from jax.sharding import PartitionSpec as P

STEP = 10

NORM_EPS = 1e-06
LOG_TWO_E = 1.442695
BETA_FIRST = 0.9
BETA_SECOND = 0.999
ADAM_EPS = 1e-08
MATRIX_RATE = 0.05
GAIN_RATE = 0.5
MATRIX_DECAY = 0.1
CLIP_NORM = 1.0
MASKED = -1e30

MESH = pl.DeviceIdType.MESH
LANES = 128
F32 = jnp.float32
LOW = jnp.bfloat16
MIB = 1024 * 1024


def rms_factor(values):
    return lax.rsqrt(jnp.mean(values * values, axis=-1, keepdims=True) + NORM_EPS)


def norm_back(grad_normed, normed, factor):
    return factor * (grad_normed - normed * jnp.mean(grad_normed * normed, axis=-1, keepdims=True))


def silu_slope(values):
    logistic = jax.nn.sigmoid(values)
    return logistic * (1.0 + values * (1.0 - logistic))


def adam_update(current, gradient, moment_one, moment_two, step_rate, decay_rate):
    new_one = BETA_FIRST * moment_one + (1.0 - BETA_FIRST) * gradient
    new_two = BETA_SECOND * moment_two + (1.0 - BETA_SECOND) * gradient * gradient
    first_hat = new_one / (1.0 - BETA_FIRST**STEP)
    second_hat = new_two / (1.0 - BETA_SECOND**STEP)
    updated = current - step_rate * (
        first_hat / (jnp.sqrt(second_hat) + ADAM_EPS) + decay_rate * current
    )
    return (updated, new_one, new_two)


def dot(left, right, left_axis=1, right_axis=0):
    return lax.dot_general(
        left, right, (((left_axis,), (right_axis,)), ((), ())), preferred_element_type=F32
    )


def greet(seq_count, batch_count):
    barrier = pltpu.get_barrier_semaphore()
    me_seq, me_batch = lax.axis_index("seq"), lax.axis_index("batch")
    for k in range(1, seq_count):
        pl.semaphore_signal(
            barrier,
            inc=1,
            device_id={"seq": lax.rem(me_seq + k, seq_count)},
            device_id_type=MESH,
        )
    for k in range(1, batch_count):
        pl.semaphore_signal(
            barrier,
            inc=1,
            device_id={"batch": lax.rem(me_batch + k, batch_count)},
            device_id_type=MESH,
        )
    pl.semaphore_wait(barrier, seq_count - 1 + batch_count - 1)


def push(source, target, send_sem, recv_sem, **where):
    return pltpu.make_async_remote_copy(
        source, target, send_sem, recv_sem, device_id=where, device_id_type=MESH
    )


def place(seq_count):
    me = lax.axis_index("seq")
    chips = seq_count // 2
    half_chips = chips // 2
    core = lax.rem(me, 2)
    chip = me // 2
    half = chip // half_chips
    base = half * half_chips
    gate_mine = half_chips - 1 + half
    gate_other = half_chips - half
    return me, core, chip, half, base, gate_mine, gate_other


def far_chip(step, half, half_chips):
    return (1 - half) * (half_chips + step) + half * (half_chips - 1 - step)


def batch_neighbours(batch):
    across = lax.rem(batch, 2)
    first = batch + 1 - 2 * across
    second = lax.rem(batch + 2, 4)
    return (first, second), lax.rem(first + 2, 4)


class Spread:
    def __init__(self, nb, block, send, recv):
        self.nb, self.block, self.send, self.recv = nb, block, send, recv
        self.batch = lax.axis_index("batch")
        self.copies = []

    def copy(self, owner, slot, j, lane, target, source=None):
        block = self.block(owner, slot)
        return push(
            block if source is None else source, block, self.send.at[j, lane],
            self.recv.at[j, lane], batch=target,
        )

    def route(self, lane):
        sides, across = batch_neighbours(self.batch)
        return sides[lane % 2], sides[1 - lane % 2], across

    def begin(self, slot, lane, source=None):
        if self.nb == 4:
            first, second, _ = self.route(lane)
            targets = [first, second]
        else:
            targets = [lax.rem(self.batch + j, self.nb) for j in range(1, self.nb)]
        new = [
            self.copy(self.batch, slot, j, lane, target, source) for j, target in enumerate(targets)
        ]
        for copy in new:
            copy.start()
        self.copies += new

    def relay(self, slot, lane):
        if self.nb == 4:
            first, second, _ = self.route(lane)
            self.copy(first, slot, 0, lane, first).wait_recv()
            copy = self.copy(first, slot, 2, lane, second)
            copy.start()
            self.copies.append(copy)
            return [first]
        return []

    def finish(self, slot, lane):
        if self.nb == 4:
            _, second, across = self.route(lane)
            self.copy(second, slot, 1, lane, second).wait_recv()
            self.copy(across, slot, 2, lane, second).wait_recv()
            return [second, across]
        owners = []
        for j in range(1, self.nb):
            owner = lax.rem(self.batch + self.nb - j, self.nb)
            self.copy(owner, slot, j - 1, lane, owner).wait_recv()
            owners.append(owner)
        return owners

    def drain(self):
        for copy in self.copies:
            copy.wait_send()


def widen(values):
    rows, width = values.shape
    return jnp.concatenate([values, jnp.zeros((rows, LANES - width), values.dtype)], axis=1)


def front_kernel(
    n, nb, heads, size, fold, chunks, joined, len_ref, scale_ref, tok, slab, own_w, h_out, qkv_out,
    q_out, keep_out, lse_out, o_out, w_all, wq_out, gain_out, coef_out,
    x_s, h_s, zin, wq, chip_w, sib_w, qkv_s, q_s, keep_s, o_s, s_s, m_s, acc_s, sum_s,
    far_sem, own_sem, pass_sem, sib_sem, same_recv, sib_recv, z_send, z_recv, b_send, b_recv,
    h_sem, qkv_sem, q_sem, keep_sem, local_sem, o_send, o_recv, wz_send, wz_recv, wb_send, wb_recv,
    ws_send, ws_recv, wx_send, wx_recv,
):
    chips, half_chips = n // 2, n // 4
    me, core, chip, half, base, gate_mine, gate_other = place(n)
    group_count = n // 2
    batch = lax.axis_index("batch")
    sibling = 2 * chip + 1 - core
    block = tok.shape[1]
    width = tok.shape[2]
    rows = block // chunks
    group = range(heads)
    shard = own_w.shape[1]
    line = n * shard
    half_width = width // 2
    greet(n, nb)

    sends = []
    z_copies = []
    for k in range(1, n):
        target = lax.rem(me + k, n)
        copy = push(
            slab.at[lax.rem(target, group_count)], zin.at[me], z_send.at[k], z_recv.at[k], seq=target
        )
        copy.start()
        z_copies.append(copy)
    slab_copy = pltpu.make_async_copy(
        slab.at[lax.rem(me, group_count)], zin.at[me], local_sem.at[0]
    )
    slab_copy.start()

    x_copy = None
    if joined:
        theirs = pl.ds(pl.multiple_of((1 - core) * half_width, LANES), half_width)
        ours = pl.ds(pl.multiple_of(core * half_width, LANES), half_width)
        x_copy = push(own_w.at[:, :, theirs], sib_w.at[0], wx_send, wx_recv, seq=sibling)
        x_copy.start()
        own_half = pltpu.make_async_copy(own_w.at[:, :, ours], sib_w.at[1], local_sem.at[1])
        own_half.start()

    def part(ref, lead, c):
        return ref.at[lead, pl.ds(c * rows, rows)]

    def tok_copy(source, slot, c, send_sem, recv_sem, target):
        return push(source, part(x_s, slot, c), send_sem, recv_sem.at[slot, c], seq=target)

    def send_tokens(c):
        copy = tok_copy(
            part(tok, 1 - half, c), me, c, far_sem.at[c], same_recv, 2 * gate_other + core
        )
        copy.start()
        sends.append(copy)
        for k in range(1, half_chips):
            other = base + lax.rem(chip - base + k, half_chips)
            copy = tok_copy(
                part(tok, half, c), me, c, own_sem.at[k, c], same_recv, 2 * other + core
            )
            copy.start()
            sends.append(copy)
        copy = tok_copy(part(tok, half, c), me, c, sib_sem.at[0, c], sib_recv, sibling)
        copy.start()
        sends.append(copy)

    for c in range(chunks):
        send_tokens(c)
    own_tok = pltpu.make_async_copy(tok.at[half], x_s.at[me], local_sem.at[2])
    own_tok.start()
    length = len_ref[half]
    scale = jnp.concatenate([scale_ref[...], jnp.zeros((1, LANES - size), F32)], axis=1)
    spot = lax.broadcasted_iota(jnp.int32, (1, LANES), 1)
    coef = jnp.where(
        spot < size,
        LOG_TWO_E / math.sqrt(size) * (jnp.maximum(scale, 0.0) + jnp.log1p(jnp.exp(-jnp.abs(scale)))),
        0.0,
    )
    coef_out[...] = coef

    def w_block(m, owner, p, c):
        if joined:
            start = pl.multiple_of((owner * chips + p) * 2 * shard, 16)
            return w_all.at[
                m, pl.ds(start, 2 * shard),
                pl.ds(pl.multiple_of(c * half_width, LANES), half_width),
            ]
        return w_all.at[owner, 2 * p + c, m]

    def w_source(m):
        return chip_w.at[m] if joined else own_w.at[m]

    matrices = [
        Spread(
            nb, lambda owner, p, m=m: w_block(m, owner, p, core), wb_send.at[m], wb_recv.at[m]
        )
        for m in range(3)
    ]
    w_line = []
    w_own = [
        pltpu.make_async_copy(w_source(m), w_block(m, batch, chip, core), local_sem.at[3 + m])
        for m in range(3)
    ]

    def chip_slot(k):
        return lax.rem(chip + chips - k, chips)

    def to_sibling(m, owner, k, j, source=None):
        piece = w_block(m, owner, chip_slot(k), core)
        copy = push(
            piece if source is None else source, piece, ws_send.at[m, j, k],
            ws_recv.at[m, owner, chip_slot(k)], seq=sibling,
        )
        copy.start()
        sends.append(copy)

    def w_send_line(m):
        for k in range(1, chips):
            target = 2 * lax.rem(chip + k, chips) + core
            copy = push(
                w_source(m), w_block(m, batch, chip, core), wz_send.at[m, k], wz_recv.at[m, k],
                seq=target,
            )
            copy.start()
            w_line.append(copy)
        w_own[m].start()
        matrices[m].begin(chip, 0, w_source(m))
        to_sibling(m, batch, 0, 0, w_source(m))

    def w_begin(m):
        for k in range(1, chips):
            slot = chip_slot(k)
            push(
                w_source(m), w_block(m, batch, slot, core), wz_send.at[m, k], wz_recv.at[m, k],
                seq=sibling,
            ).wait_recv()
            matrices[m].begin(slot, k)
            to_sibling(m, batch, k, 0)

    def w_relay(m):
        for k in range(chips):
            for j, owner in enumerate(matrices[m].relay(chip_slot(k), k)):
                to_sibling(m, owner, k, 1 + j)

    def w_finish(m):
        for k in range(chips):
            owners = matrices[m].finish(chip_slot(k), k)
            for j, owner in enumerate(owners):
                to_sibling(m, owner, k, nb - len(owners) + j)

    if joined:
        x_copy.wait_recv()
        own_half.wait()
        for m in range(3):
            other, mine = sib_w[0, m].astype(F32), sib_w[1, m].astype(F32)
            upper = jnp.where(core == 0, mine, other)
            lower = jnp.where(core == 0, other, mine)
            chip_w[m] = jnp.concatenate([upper, lower], axis=0).astype(LOW)
    w_send_line(0)

    slab_copy.wait()
    for copy in z_copies:
        copy.wait_recv()
    parts = [zin[k].astype(F32) for k in range(n)]
    line_start = pl.multiple_of(batch * line, 16)
    wq[pl.ds(line_start, line)] = jnp.concatenate(parts, axis=0).astype(LOW)
    pieces = 2 if nb == 4 else 1
    piece_rows = line // pieces

    def wq_block(owner, slot):
        return wq.at[pl.ds(pl.multiple_of(owner * line + slot * piece_rows, 16), piece_rows)]

    slices = Spread(nb, wq_block, b_send, b_recv)
    for k in range(pieces):
        slices.begin(k, k)

    def pass_tokens(c):
        for k in range(1, half_chips):
            slot = 2 * (base + lax.rem(chip - base + half_chips - k, half_chips)) + core
            tok_copy(part(x_s, slot, c), slot, c, sib_sem.at[k, c], same_recv, sibling).wait_recv()
            copy = tok_copy(part(x_s, slot, c), slot, c, sib_sem.at[k, c], sib_recv, sibling)
            copy.start()
            sends.append(copy)
        for k in range(half_chips):
            slot = 2 * far_chip(k, half, half_chips) + core
            lane = half_chips + k
            tok_copy(part(x_s, slot, c), slot, c, sib_sem.at[lane, c], same_recv, sibling).wait_recv()

            @pl.when(chip == gate_mine)
            def _():
                for j in range(1, half_chips):
                    other = base + lax.rem(chip - base + j, half_chips)
                    tok_copy(
                        part(x_s, slot, c), slot, c, pass_sem.at[k, j, c], same_recv,
                        2 * other + core,
                    ).start()

            copy = tok_copy(part(x_s, slot, c), slot, c, sib_sem.at[lane, c], sib_recv, sibling)
            copy.start()
            sends.append(copy)

    pass_tokens(0)
    for k in range(pieces):
        slices.relay(k, k)
    pass_tokens(1)
    w_begin(0)
    pass_tokens(2)
    for k in range(pieces):
        slices.finish(k, k)
    w_relay(0)
    wq_copy = pltpu.make_async_copy(wq, wq_out, local_sem.at[6])
    wq_copy.start()
    columns = 3 * heads * size
    tile = columns // LANES * LANES
    turned = wq[:, tile : tile + LANES].astype(F32).T
    gains = jnp.concatenate(
        [turned[columns - tile + k : columns - tile + k + 1] for k in range(2)], axis=0
    )
    gain_out[...] = gains
    gain = gains[:1]

    def kept(i):
        return [
            pltpu.make_async_copy(qkv_s.at[i], qkv_out.at[i], qkv_sem.at[i]),
            pltpu.make_async_copy(q_s.at[i], q_out.at[i], q_sem.at[i]),
        ]

    def h_copy(i, lane):
        return pltpu.make_async_copy(h_s.at[lane], h_out.at[i], h_sem.at[lane])

    def keep_copy(i):
        return pltpu.make_async_copy(keep_s.at[i], keep_out.at[i], keep_sem.at[i])

    def o_push(i):
        return push(o_s.at[i], o_out.at[me], o_send.at[i], o_recv.at[me], seq=i)

    own_o = pltpu.make_async_copy(o_s.at[me], o_out.at[me], local_sem.at[7])

    def project(i, lane):
        x = x_s[i].astype(F32)
        h = (x * rms_factor(x) * gain).astype(LOW)
        h_s[lane] = h
        h_copy(i, lane).start()
        out = dot(h, wq[...])
        place_in = lax.broadcasted_iota(jnp.int32, (block, LANES), 1)
        row = i * block + lax.broadcasted_iota(jnp.int32, (block, LANES), 0)
        mark = jnp.where(place_in == size, 1.0, 0.0)
        hide = jnp.where((place_in == size) & (row >= length), MASKED, 0.0)
        for a in group:
            q = widen(out[:, a * size : (a + 1) * size])
            q_s[i, a] = q
            qkv_s[i, a] = (q * coef + mark).astype(LOW)
        for a in range(heads, 2 * heads):
            qkv_s[i, a] = (widen(out[:, a * size : (a + 1) * size]) + hide).astype(LOW)
        for a in range(2 * heads, 3 * heads):
            qkv_s[i, a] = widen(out[:, a * size : (a + 1) * size].astype(LOW))
        for copy in kept(i):
            copy.start()

    own_tok.wait()
    project(me, 0)
    pass_tokens(3)
    w_send_line(1)
    w_send_line(2)
    for c in range(chunks):
        tok_copy(part(x_s, sibling, c), sibling, c, sib_sem.at[0, c], sib_recv, sibling).wait_recv()
    project(sibling, 1)
    w_finish(0)
    h_copy(me, 0).wait()
    h_copy(sibling, 1).wait()

    @pl.loop(1, chips)
    def _(k):
        q = lax.rem(chip + k, chips)
        for lane in range(2):
            slot = 2 * q + (core if lane == 0 else 1 - core)
            if lane == 1:
                for c in range(chunks):
                    tok_copy(
                        part(x_s, slot, c), slot, c, sib_sem.at[0, c], sib_recv, sibling
                    ).wait_recv()

            @pl.when(k > 1)
            def _():
                h_copy(slot, lane).wait()

            project(slot, lane)

    for lane in range(2):
        h_copy(me, lane).wait()

    def score(i, j, diagonal):
        if diagonal:
            row = lax.broadcasted_iota(jnp.int32, (block, block), 0)
            col = lax.broadcasted_iota(jnp.int32, (block, block), 1)
            visible = col <= row
        for a in group:
            s = dot(qkv_s[i, a], qkv_s[j, heads + a], 1, 1)
            if diagonal:
                s = jnp.where(visible, s, MASKED)
            s_s[a, j] = s
            best = m_s[a]
            for lane in range(block // LANES):
                best = jnp.maximum(best, s[:, lane * LANES : (lane + 1) * LANES])
            m_s[a] = best

    def mix(j):
        for a in group:
            best = m_s[a]
            count = sum_s[a]
            terms = []
            for lane in range(block // LANES):
                e = jnp.exp(s_s[a, j, :, lane * LANES : (lane + 1) * LANES] - best)
                count = count + e
                terms.append(e.astype(LOW))
            sum_s[a] = count
            acc_s[a] += dot(jnp.concatenate(terms, axis=1), qkv_s[j, 2 * heads + a])

    def query_block(t):
        i = lax.rem(me + 1 + t, n)
        m_s[...] = jnp.full_like(m_s, MASKED)
        sum_s[...] = jnp.zeros_like(sum_s)
        acc_s[...] = jnp.zeros_like(acc_s)
        pl.loop(0, i)(lambda j: score(i, j, False))
        score(i, i, True)
        for a in group:
            m_s[a] = jnp.broadcast_to(jnp.max(m_s[a], axis=1, keepdims=True), (block, LANES))
        pl.loop(0, i + 1)(mix)
        outs = []
        for a in group:
            count = jnp.sum(sum_s[a], axis=1, keepdims=True)
            out = acc_s[a] / count
            keep_s[i, a] = out
            outs.append(out[:, :size])
            lse_out[i, a] = (m_s[a] + jnp.log(count)).T[:8]
        low = jnp.concatenate(outs, axis=1).astype(LOW)
        piece = block // fold
        o_s[i] = jnp.concatenate([low[f * piece : (f + 1) * piece] for f in range(fold)], axis=1)
        keep_copy(i).start()

        @pl.when(i != me)
        def _():
            o_push(i).start()

        @pl.when(i == me)
        def _():
            own_o.start()

    bounds = [0, 2, 3, n - 3, n - 2, n] if n > 4 else [0, 1, 1, 2, 2, n]
    events = [lambda: w_begin(1), lambda: w_begin(2), lambda: w_relay(1), lambda: w_relay(2), None]
    for first, last, event in zip(bounds[:-1], bounds[1:], events):
        if last > first:
            pl.loop(first, last)(query_block)
        if event is not None:
            event()
    w_finish(1)
    w_finish(2)

    for k in range(1, n):
        source = lax.rem(me + k, n)
        push(
            o_s.at[source], o_out.at[source], o_send.at[source], o_recv.at[source], seq=source
        ).wait()
    own_o.wait()
    for m in range(3):
        for owner in range(nb):
            for q in range(chips):
                piece = w_block(m, owner, q, 1 - core)
                push(
                    piece, piece, ws_send.at[0, 0, 0], ws_recv.at[m, owner, q], seq=sibling
                ).wait_recv()
        matrices[m].drain()
        w_own[m].wait()
    slices.drain()
    if joined:
        x_copy.wait_send()
    wq_copy.wait()
    for copy in sends + z_copies + w_line:
        copy.wait_send()

    @pl.when(chip == gate_mine)
    def _():
        for c in range(chunks):
            for k in range(half_chips):
                for j in range(1, half_chips):
                    tok_copy(
                        part(x_s, me, c), me, c, pass_sem.at[k, j, c], same_recv, sibling
                    ).wait_send()

    @pl.loop(0, n)
    def _(i):
        keep_copy(i).wait()
        for copy in kept(i):
            copy.wait()


def front(n, nb, heads, size, fold, lengths, scale, tokens, slab, own_w):
    chunks = 4
    _, rows, width = tokens.shape
    chips, half_chips = n // 2, n // 4
    shard = own_w.shape[1]
    joined = 2 * shard % 16 == 0
    folded = (n, rows // fold, heads * size * fold)
    many, one = (n, 3 * heads, rows, LANES), (n, heads, rows, LANES)
    slab_width = slab.shape[2]
    pieces = 2 if nb == 4 else 1
    all_shape = (3, width, width) if joined else (nb, n) + own_w.shape
    pair = (3, 2 * shard, width // 2) if joined else (3, 16, LANES)
    single = (2, 3, shard, width // 2) if joined else (2, 3, 16, LANES)
    dma = pltpu.SemaphoreType.DMA
    vmem = pl.BlockSpec(memory_space=pltpu.VMEM)
    smem = pl.BlockSpec(memory_space=pltpu.SMEM)
    anywhere = pl.BlockSpec(memory_space=pl.ANY)
    state = pltpu.VMEM((heads, rows, LANES), F32)
    return pl.pallas_call(
        functools.partial(front_kernel, n, nb, heads, size, fold, chunks, joined),
        out_shape=(
            jax.ShapeDtypeStruct((n, rows, width), LOW),
            jax.ShapeDtypeStruct(many, LOW),
            jax.ShapeDtypeStruct(one, F32),
            jax.ShapeDtypeStruct(one, F32),
            jax.ShapeDtypeStruct((n, heads, 8, rows), F32),
            jax.ShapeDtypeStruct(folded, LOW),
            jax.ShapeDtypeStruct(all_shape, LOW),
            jax.ShapeDtypeStruct((width, slab_width), LOW),
            jax.ShapeDtypeStruct((2, width), F32),
            jax.ShapeDtypeStruct((1, LANES), F32),
        ),
        in_specs=[smem, vmem, anywhere, anywhere, anywhere],
        out_specs=[anywhere] * 4 + [vmem] + [anywhere] * 3 + [vmem, vmem],
        scratch_shapes=[
            pltpu.VMEM((n, rows, width), LOW),
            pltpu.VMEM((2, rows, width), LOW),
            pltpu.VMEM((n, shard, slab_width), LOW),
            pltpu.VMEM((width, slab_width), LOW),
            pltpu.VMEM(pair, LOW),
            pltpu.VMEM(single, LOW),
            pltpu.VMEM(many, LOW),
            pltpu.VMEM(one, F32),
            pltpu.VMEM(one, F32),
            pltpu.VMEM(folded, LOW),
            pltpu.VMEM((heads, n, rows, rows), F32),
            state,
            state,
            state,
            dma((chunks,)),
            dma((half_chips, chunks)),
            dma((half_chips, half_chips, chunks)),
            dma((chips, chunks)),
            dma((n, chunks)),
            dma((n, chunks)),
            dma((n,)),
            dma((n,)),
            dma((nb, pieces)),
            dma((nb, pieces)),
            dma((2,)),
            dma((n,)),
            dma((n,)),
            dma((n,)),
            dma((8,)),
            dma((n,)),
            dma((n,)),
            dma((3, chips)),
            dma((3, chips)),
            dma((3, nb, chips)),
            dma((3, nb, chips)),
            dma((3, nb, chips)),
            dma((3, nb, chips)),
            dma,
            dma,
        ],
        compiler_params=pltpu.CompilerParams(
            collective_id=2, has_side_effects=True, vmem_limit_bytes=62 * MIB
        ),
        name="front",
    )(lengths, scale, tokens, slab, own_w)


def fold_rows(values):
    rows, width = values.shape
    return jnp.sum(values.reshape(rows // 8, 8, width), axis=0)


def layer_kernel(
    n, nb, fold, tok, cot, o_in, w_in, gain_ref, y_out, gy_out, go_out, small_out, half_out,
    w, o_s, hidden_s, act_s, gu_s, ga_s, go_s, gw_s, sib_in, w_sem, send_sem, recv_sem, local_sem,
    sib_send, sib_recv,
):
    group_count = n // 2
    me, core, chip, half, base, gate_mine, gate_other = place(n)
    sibling = 2 * chip + 1 - core
    _, rows, width = tok.shape
    group_width = width // group_count
    piece = rows // fold
    barrier = pltpu.get_barrier_semaphore()
    for k in range(1, n):
        pl.semaphore_signal(
            barrier, inc=1, device_id={"seq": lax.rem(me + k, n)}, device_id_type=MESH
        )
    loads = [pltpu.make_async_copy(w_in.at[m], w.at[m], w_sem.at[m]) for m in range(3)]
    for load in loads:
        load.start()
    small_out[...] = jnp.zeros_like(small_out)
    gain = gain_ref[1:2]

    def go_push(target):
        return push(
            go_s.at[target], go_out.at[me], send_sem.at[target], recv_sem.at[me], seq=target
        )

    own_go = pltpu.make_async_copy(go_s.at[me], go_out.at[me], local_sem)

    for step in range(2):
        t = half if step else 1 - half
        parts = [
            jnp.concatenate(
                [
                    o_in[t * group_count + g, :, f * group_width : (f + 1) * group_width]
                    for g in range(group_count)
                ],
                axis=1,
            )
            for f in range(fold)
        ]
        o = jnp.concatenate(parts, axis=0)
        o_s[t] = o
        if step == 0:
            loads[0].wait()
        a = dot(o, w[0])
        small_out[1] += fold_rows(a * a)
        y1 = tok[t].astype(F32) + a
        factor = rms_factor(y1)
        normed = y1 * factor
        hidden = (normed * gain).astype(LOW)
        hidden_s[t] = hidden
        if step == 0:
            loads[1].wait()
        u = dot(hidden, w[1])
        logistic = 1.0 / (1.0 + jnp.exp(-u))
        act = (u * logistic).astype(LOW)
        act_s[t] = act
        if step == 0:
            loads[2].wait()
        f = dot(act, w[2])
        small_out[2] += fold_rows(f * f)
        y = y1 + f
        small_out[3] += fold_rows(y * y)
        y_out[t] = y.astype(LOW)
        gz = dot(cot[t], w[2], 1, 1)
        gu = (gz * (logistic * (1.0 + u * (1.0 - logistic)))).astype(LOW)
        gu_s[t] = gu
        gh = dot(gu, w[1], 1, 1)
        small_out[0] += fold_rows(gh * normed)
        gy = cot[t].astype(F32) + norm_back(gh * gain, normed, factor)
        gy_out[t] = gy
        ga = gy.astype(LOW)
        ga_s[t] = ga
        go = dot(ga, w[0], 1, 1).astype(LOW)
        for g in range(group_count):
            block = go[:, g * group_width : (g + 1) * group_width]
            go_s[t * group_count + g] = jnp.concatenate(
                [block[f * piece : (f + 1) * piece] for f in range(fold)], axis=1
            )
        if step == 0:
            pl.semaphore_wait(barrier, n - 1)
        for g in range(group_count):
            target = t * group_count + g

            @pl.when(target != me)
            def _():
                go_push(target).start()

            @pl.when(target == me)
            def _():
                own_go.start()

    tile = 256
    half_rows = width // nb // 2
    sib_copies = []
    pairs = ((act_s, cot, 2), (hidden_s, gu_s, 1), (o_s, ga_s, 0))
    for left, right, m in pairs:

        @pl.loop(0, width // tile)
        def _(k):
            cols = pl.ds(pl.multiple_of(k * tile, tile), tile)
            total = dot(left[0, :, cols], right[0], 0, 0) + dot(left[1, :, cols], right[1], 0, 0)
            gw_s[m, cols] = total.astype(LOW)

        for b in range(nb):
            start = pl.multiple_of((2 * b + 1 - core) * half_rows, 16)
            copy = push(
                gw_s.at[m, pl.ds(start, half_rows)], sib_in.at[b, m], sib_send.at[b, m],
                sib_recv.at[b, m], seq=sibling,
            )
            copy.start()
            sib_copies.append(copy)
    index = 0
    for _, _, m in pairs:
        for b in range(nb):
            sib_copies[index].wait_recv()
            index += 1
            start = pl.multiple_of((2 * b + core) * half_rows, 16)
            half_out[b, m] = (
                gw_s[m, pl.ds(start, half_rows)].astype(F32) + sib_in[b, m].astype(F32)
            ).astype(LOW)
    for k in range(1, n):
        source = lax.rem(me + k, n)
        push(
            go_s.at[source], go_out.at[source], send_sem.at[source], recv_sem.at[source], seq=source
        ).wait()
    own_go.wait()
    for copy in sib_copies:
        copy.wait_send()


def layer(n, nb, fold, tokens, cotangent, o_recv, w_all, gain):
    _, rows, width = tokens.shape
    half_rows = width // nb // 2
    dma = pltpu.SemaphoreType.DMA
    vmem = pl.BlockSpec(memory_space=pltpu.VMEM)
    anywhere = pl.BlockSpec(memory_space=pl.ANY)
    kept = pltpu.VMEM((2, rows, width), LOW)
    return pl.pallas_call(
        functools.partial(layer_kernel, n, nb, fold),
        out_shape=(
            jax.ShapeDtypeStruct((2, rows, width), LOW),
            jax.ShapeDtypeStruct((2, rows, width), F32),
            jax.ShapeDtypeStruct(o_recv.shape, LOW),
            jax.ShapeDtypeStruct((4, 8, width), F32),
            jax.ShapeDtypeStruct((nb, 3, half_rows, width), LOW),
        ),
        in_specs=[vmem, vmem, vmem, anywhere, vmem],
        out_specs=[vmem, vmem, anywhere, vmem, vmem],
        scratch_shapes=[
            pltpu.VMEM((3, width, width), LOW),
            kept,
            kept,
            kept,
            kept,
            kept,
            pltpu.VMEM(o_recv.shape, LOW),
            pltpu.VMEM((3, width, width), LOW),
            pltpu.VMEM((nb, 3, half_rows, width), LOW),
            dma((3,)),
            dma((n,)),
            dma((n,)),
            dma,
            dma((nb, 3)),
            dma((nb, 3)),
        ],
        compiler_params=pltpu.CompilerParams(
            collective_id=3, has_side_effects=True, vmem_limit_bytes=63 * MIB
        ),
        name="layer",
    )(tokens, cotangent, o_recv, w_all, gain)


def back_kernel(
    n, nb, heads, size, fold, coef_ref, qkv_in, go_ref, keep_in, lse_ref, q_in, h_in, w_in,
    half_in, tok, sums_ref, out, own_gw, own_w, sums_out, cross_in, turn_in,
    qkv, kt, g_s, delta, gq, gk, gv, q_s, h_s, w_s, gw, gh_own, gh_out, from_sib, gate_in, peer_in,
    stage, cross_out, w_line, w_parts, gw_low, near_in, near_out, near_turn, line_out, line_in,
    load_sem, block_sem, sib_send, sib_recv, gate_send, gate_recv, peer_send, peer_recv, far_send,
    far_recv, c_send, c_recv, t_send, t_recv, w_send, w_recv, b_send, b_recv, bt_send, bt_recv,
    z_send, z_recv, stage_sem, scale_sum, sum_mine, sum_line, sum_batch, s_send, s_recv, u_send,
    u_recv,
):
    chips, half_chips = n // 2, n // 4
    me, core, chip, half, base, gate_mine, gate_other = place(n)
    group_count = n // 2
    batch = lax.axis_index("batch")
    sibling = 2 * chip + 1 - core
    block = qkv.shape[2]
    group = range(heads)
    sides, across = batch_neighbours(batch)
    is_gate = chip == gate_mine
    paired = nb == 4
    greet(n, nb)

    w_rows = stage.shape[2]

    def w_piece(owner, h):
        return half_in.at[owner, :, pl.ds(h * w_rows, w_rows)]

    w_copies = []
    if paired:
        for h in range(2):
            for j, owner in enumerate((across, sides[h])):
                w_copies.append(
                    push(
                        w_piece(owner, h), cross_in.at[h, j], c_send.at[h, j], c_recv.at[h, j],
                        batch=sides[h],
                    )
                )
    else:
        for k in range(1, nb):
            target = lax.rem(batch + k, nb)
            w_copies.append(
                push(
                    w_piece(target, 0), cross_in.at[0, k], c_send.at[0, k], c_recv.at[0, k],
                    batch=target,
                )
            )
    for copy in w_copies:
        copy.start()

    keep_load = pltpu.make_async_copy(keep_in, gk, load_sem.at[0])
    qkv_load = pltpu.make_async_copy(qkv_in, qkv, load_sem.at[1])
    w_load = pltpu.make_async_copy(w_in, w_s, load_sem.at[2])
    for load in (keep_load, qkv_load, w_load):
        load.start()
    scale_sum[...] = jnp.zeros_like(scale_sum)
    gv[...] = jnp.zeros_like(gv)
    gq[...] = jnp.zeros_like(gq)
    keep_load.wait()

    @pl.loop(0, n)
    def _(i):
        for a in group:
            g = widen(
                jnp.concatenate(
                    [
                        go_ref[i, :, (f * heads + a) * size : (f * heads + a + 1) * size]
                        for f in range(fold)
                    ],
                    axis=0,
                )
            )
            g_s[i, a] = g
            delta[i, a] = jnp.broadcast_to(
                jnp.sum((g.astype(F32) * gk[i, a]).T, axis=0, keepdims=True), (8, block)
            )
            gk[i, a] = jnp.zeros_like(gk[i, a])

    qkv_load.wait()

    @pl.loop(0, n)
    def _(j):
        for a in group:
            kt[j, a] = qkv[j, heads + a].T

    w_load.wait()

    def pair_block(i, j, diagonal):
        if diagonal:
            col = lax.broadcasted_iota(jnp.int32, (block, block), 0)
            row = lax.broadcasted_iota(jnp.int32, (block, block), 1)
            visible = col <= row
        for a in group:
            s = dot(qkv[j, heads + a], qkv[i, a], 1, 1)
            p = jnp.exp(s - lse_ref[i, a, :1])
            if diagonal:
                p = jnp.where(visible, p, 0.0)
            dp = dot(qkv[j, 2 * heads + a], g_s[i, a], 1, 1)
            ds = (p * (dp - delta[i, a, :1])).astype(LOW)
            gk[j, a] += dot(ds, qkv[i, a])
            gv[j, a] += dot(p.astype(LOW), g_s[i, a])
            gq[i, a] += dot(kt[j, a], ds)

    def sib_copy(t):
        return push(
            gh_out.at[t % 2], from_sib.at[t], sib_send.at[t], sib_recv.at[t], seq=sibling
        )

    def step(t, u):
        r = half * t + (1 - half) * (n - 1 - t)
        loads = [
            pltpu.make_async_copy(q_in.at[r], q_s, block_sem.at[0]),
            pltpu.make_async_copy(h_in.at[r], h_s, block_sem.at[1]),
        ]
        for load in loads:
            load.start()
        pair_block(r, r, True)
        pl.loop(1, n - t)(lambda v: pair_block(r + half * v, r - (1 - half) * v, False))
        for load in loads:
            load.wait()
        pieces = []
        for a in group:
            grad = gq[r, a].T.astype(LOW).astype(F32)
            scale_sum[...] += fold_rows(grad * q_s[a])
            pieces.append((grad * coef_ref[...])[:, :size].astype(LOW))
        pieces += [gk[r, a][:, :size].astype(LOW) for a in group]
        pieces += [gv[r, a][:, :size].astype(LOW) for a in group]
        spare = w_s.shape[1] - 3 * heads * size
        pieces.append(jnp.zeros((block, spare), LOW))
        grads = jnp.concatenate(pieces, axis=1)
        gh = dot(grads, w_s[...], 1, 1).astype(LOW)
        tp = t // 2
        mine = lax.rem(r, 2) == core

        @pl.when(mine)
        def _():
            gh_own[tp] = gh

        @pl.when(jnp.logical_not(mine))
        def _():
            gh_out[tp % 2] = gh
            sib_copy(tp).start()

        part = dot(h_s[...], grads, 0, 0)
        if t == 0:
            gw[...] = part
        else:
            gw[...] += part

    def far_chip_of(tp):
        return half * tp + (1 - half) * (chips - 1 - tp)

    def gate_copy(tp):
        after = lax.rem(chip - gate_mine + half_chips, half_chips)
        return push(
            gh_own.at[tp], gate_in.at[after - 1, tp], gate_send.at[tp],
            gate_recv.at[after - 1, tp], seq=2 * gate_mine + core,
        )

    def far_copy(tp):
        return push(
            gh_own.at[tp], out.at[half], far_send.at[tp], far_recv.at[0],
            seq=2 * far_chip_of(tp) + core,
        )

    def peer_copy(tp):
        q = far_chip_of(tp)
        after = lax.rem(chip - q + half_chips, half_chips)
        return push(
            gh_own.at[tp], peer_in.at[after - 1], peer_send.at[tp], peer_recv.at[after - 1],
            seq=2 * q + core,
        )

    def relay(tp):
        @pl.when(is_gate)
        def _():
            value = gh_own[tp].astype(F32)
            for j in range(half_chips - 1):
                push(
                    gh_own.at[tp], gate_in.at[j, tp], gate_send.at[tp], gate_recv.at[j, tp],
                    seq=sibling,
                ).wait_recv()
                value = value + gate_in[j, tp].astype(F32)
            gh_own[tp] = value.astype(LOW)
            far_copy(tp).start()

    shard = own_w.shape[1]

    def staged(*sources):
        value = None
        for first in range(0, len(sources), 3):
            loads = [
                pltpu.make_async_copy(source, stage.at[j], stage_sem.at[j])
                for j, source in enumerate(sources[first : first + 3])
            ]
            for load in loads:
                load.start()
            for load in loads:
                load.wait()
            for j in range(len(loads)):
                term = stage[j].astype(F32)
                value = term if value is None else value + term
        return value

    t_copies = []

    def turn():
        if paired:
            for h in range(2):
                w_copies[2 * h].wait_recv()
                cross_out[h] = staged(w_piece(sides[1 - h], h), cross_in.at[h, 0]).astype(LOW)
                copy = push(
                    cross_out.at[h], turn_in.at[h], t_send.at[h], t_recv.at[h], batch=sides[1 - h]
                )
                copy.start()
                t_copies.append(copy)

    def w_push(i):
        target = core * group_count + i
        return push(w_line.at[i], w_parts.at[chip], w_send.at[i], w_recv.at[chip], seq=target)

    def to_owners():
        for copy in w_copies[1::2] if paired else w_copies:
            copy.wait_recv()
        for copy in t_copies:
            copy.wait_recv()
        splits = 2 if paired else 1
        each = group_count // splits
        for h in range(splits):
            if paired:
                value = staged(w_piece(batch, h), cross_in.at[h, 1], turn_in.at[h])
            else:
                value = staged(w_piece(batch, 0), *[cross_in.at[0, k] for k in range(1, nb)])
            for i in range(each):
                w_line[h * each + i] = value[:, i * shard : (i + 1) * shard].astype(LOW)
        for i in range(group_count):
            own = core * group_count + i == me

            @pl.when(own)
            def _():
                w_parts[chip] = w_line[i]

            @pl.when(jnp.logical_not(own))
            def _():
                w_push(i).start()

    for tp in range(chips):
        if tp >= 2:
            sib_copy(tp - 2).wait_send()
        step(2 * tp, 0)
        step(2 * tp + 1, 1)
        if tp == 0:
            turn()
        if tp == 1:
            to_owners()
        sib_copy(tp).wait_recv()
        gh_own[tp] = (gh_own[tp].astype(F32) + from_sib[tp].astype(F32)).astype(LOW)
        if tp < half_chips:

            @pl.when(jnp.logical_not(is_gate))
            def _():
                gate_copy(tp).start()

        else:

            @pl.when(far_chip_of(tp) != chip)
            def _():
                peer_copy(tp).start()

        if 1 <= tp < half_chips:
            relay(tp - 1)

    line_rows = gw.shape[0] // nb
    near_rows = near_in.shape[2]
    for b in range(nb):
        gw_low[b] = gw[b * line_rows : (b + 1) * line_rows].astype(LOW)

    def near_piece(owner, h):
        return gw_low.at[owner, pl.ds(h * near_rows, near_rows)]

    b_copies = []
    if paired:
        for h in range(2):
            for j, owner in enumerate((across, sides[h])):
                b_copies.append(
                    push(
                        near_piece(owner, h), near_in.at[h, j], b_send.at[h, j], b_recv.at[h, j],
                        batch=sides[h],
                    )
                )
    else:
        for k in range(1, nb):
            target = lax.rem(batch + k, nb)
            b_copies.append(
                push(
                    near_piece(target, 0), near_in.at[0, k], b_send.at[0, k], b_recv.at[0, k],
                    batch=target,
                )
            )
    for copy in b_copies:
        copy.start()
    relay(half_chips - 1)
    bt_copies = []
    if paired:
        for h in range(2):
            b_copies[2 * h].wait_recv()
            near_out[h] = (
                gw_low[sides[1 - h], pl.ds(h * near_rows, near_rows)].astype(F32)
                + near_in[h, 0].astype(F32)
            ).astype(LOW)
            copy = push(
                near_out.at[h], near_turn.at[h], bt_send.at[h], bt_recv.at[h], batch=sides[1 - h]
            )
            copy.start()
            bt_copies.append(copy)
    z_copies = []

    def z_copy(target):
        return push(
            line_out.at[target], line_in.at[me], z_send.at[target], z_recv.at[me], seq=target
        )

    splits = 2 if paired else 1
    each = n // splits
    for h in range(splits):
        value = gw_low[batch, pl.ds(h * near_rows, near_rows)].astype(F32)
        if paired:
            b_copies[2 * h + 1].wait_recv()
            bt_copies[h].wait_recv()
            value = value + near_in[h, 1].astype(F32) + near_turn[h].astype(F32)
        else:
            for k in range(1, nb):
                b_copies[k - 1].wait_recv()
                value = value + near_in[0, k].astype(F32)
        for i in range(each):
            target = h * each + i
            line_out[target] = value[i * shard : (i + 1) * shard].astype(LOW)

            @pl.when(target != me)
            def _():
                z_copy(target).start()

            @pl.when(target == me)
            def _():
                line_in[me] = line_out[target]

    value = gh_own[half * chip + (1 - half) * (chips - 1 - chip)].astype(F32)
    for j in range(half_chips - 1):
        push(
            gh_own.at[0], peer_in.at[j], peer_send.at[0], peer_recv.at[j], seq=sibling
        ).wait_recv()
        value = value + peer_in[j].astype(F32)
    out[half] = value.astype(LOW)
    push(gh_own.at[0], out.at[1 - half], far_send.at[0], far_recv.at[0], seq=sibling).wait_recv()

    tiles = out.shape[2] // LANES
    gain_sum = None
    for t in range(2):
        load = pltpu.make_async_copy(tok.at[t], h_s, block_sem.at[1])
        load.start()
        load.wait()
        x = h_s[...].astype(F32)
        term = fold_rows(out[t].astype(F32) * (x * rms_factor(x)))
        gain_sum = term if gain_sum is None else gain_sum + term

    def lanes(row):
        return [row[:, k * LANES : (k + 1) * LANES] for k in range(row.shape[1] // LANES)]

    def squeeze(row):
        total = None
        for piece in lanes(row):
            total = piece if total is None else total + piece
        return total

    rows_out = lanes(jnp.sum(gain_sum, axis=0, keepdims=True))
    rows_out += lanes(jnp.sum(sums_ref[0], axis=0, keepdims=True))
    rows_out.append(jnp.sum(scale_sum[...], axis=0, keepdims=True))
    for k in range(1, 4):
        rows_out.append(squeeze(jnp.sum(sums_ref[k], axis=0, keepdims=True)))

    for q in range(chips):

        @pl.when(2 * q + half != me)
        def _():
            push(w_line.at[0], w_parts.at[q], w_send.at[0], w_recv.at[q], seq=sibling).wait_recv()

    value = w_parts[0].astype(F32)
    for q in range(1, chips):
        value = value + w_parts[q].astype(F32)
    own_w[...] = value

    for k in range(1, n):
        source = lax.rem(me + k, n)
        push(
            line_out.at[source], line_in.at[source], z_send.at[source], z_recv.at[source], seq=source
        ).wait()
    for g in range(group_count):
        own_gw[g] = line_in[g].astype(F32) + line_in[g + group_count].astype(F32)

    squares = None
    for value in [own_gw[g] for g in range(group_count)] + [own_w[m] for m in range(3)]:
        term = squeeze(jnp.sum(value * value, axis=0, keepdims=True))
        squares = term if squares is None else squares + term
    rows_out.append(squares)
    sum_mine[0] = jnp.zeros_like(sum_mine[0])
    for k, row in enumerate(rows_out):
        sum_mine[0, k : k + 1, :] = row
    s_copies = []
    for k in range(1, n):
        copy = push(
            sum_mine.at[0], sum_line.at[k], s_send.at[k], s_recv.at[k], seq=lax.rem(me + k, n)
        )
        copy.start()
        s_copies.append(copy)
    sum_line[0] = sum_mine[0]
    for copy in s_copies:
        copy.wait_recv()
    value = jnp.zeros_like(sum_mine[0])
    for k in range(n):
        value = value + sum_line[lax.rem(me - k + n, n)]
    sum_mine[1] = value
    for k in range(1, nb):
        copy = push(
            sum_mine.at[1], sum_batch.at[k], u_send.at[k], u_recv.at[k],
            batch=lax.rem(batch + k, nb),
        )
        copy.start()
        s_copies.append(copy)
    sum_batch[0] = value
    for copy in s_copies[n - 1 :]:
        copy.wait_recv()
    value = jnp.zeros_like(value)
    for k in range(nb):
        value = value + sum_batch[lax.rem(batch - k + nb, nb)]
    sums_out[...] = value

    for i in range(group_count):

        @pl.when(core * group_count + i != me)
        def _():
            w_push(i).wait_send()

    for tp in range(max(chips - 2, 0), chips):
        sib_copy(tp).wait_send()
    for copy in w_copies + t_copies + b_copies + bt_copies + s_copies:
        copy.wait_send()
    for tp in range(chips):
        if tp < half_chips:

            @pl.when(is_gate)
            def _():
                far_copy(tp).wait_send()

            @pl.when(jnp.logical_not(is_gate))
            def _():
                gate_copy(tp).wait_send()

        else:

            @pl.when(far_chip_of(tp) != chip)
            def _():
                peer_copy(tp).wait_send()


def attend_back(
    n, nb, heads, size, fold, coef, qkv, go, keep, lse, q_full, h, wqkv, w_half, tokens,
    layer_sums, shard,
):
    _, rows, width = h.shape
    chips, half_chips = n // 2, n // 4
    paired = nb == 4
    split = 2 if paired else 1
    steps = 2 if paired else nb
    w_rows = w_half.shape[2] // split
    line_rows = width // nb
    slab = wqkv.shape[1]
    dma = pltpu.SemaphoreType.DMA
    vmem = pl.BlockSpec(memory_space=pltpu.VMEM)
    anywhere = pl.BlockSpec(memory_space=pl.ANY)
    one = (n, heads, rows, LANES)
    peers = max(half_chips - 1, 1)
    near = (line_rows // split, slab)
    small_rows = (2 * (width // LANES) + 5 + 7) // 8 * 8
    result = pl.pallas_call(
        functools.partial(back_kernel, n, nb, heads, size, fold),
        out_shape=(
            jax.ShapeDtypeStruct((2, rows, width), LOW),
            jax.ShapeDtypeStruct((n // 2, shard, slab), F32),
            jax.ShapeDtypeStruct((3, shard, width), F32),
            jax.ShapeDtypeStruct((small_rows, LANES), F32),
            jax.ShapeDtypeStruct((split, steps, 3, w_rows, width), LOW),
            jax.ShapeDtypeStruct((split, 3, w_rows, width), LOW),
        ),
        in_specs=[vmem, anywhere, vmem, anywhere, vmem]
        + [anywhere] * 5
        + [vmem],
        out_specs=[vmem, vmem, vmem, vmem, anywhere, anywhere],
        scratch_shapes=[
            pltpu.VMEM(qkv.shape, LOW),
            pltpu.VMEM((n, heads, LANES, rows), LOW),
            pltpu.VMEM(one, LOW),
            pltpu.VMEM((n, heads, 8, rows), F32),
            pltpu.VMEM((n, heads, LANES, rows), F32),
            pltpu.VMEM(one, F32),
            pltpu.VMEM(one, F32),
            pltpu.VMEM((heads, rows, LANES), F32),
            pltpu.VMEM((rows, width), LOW),
            pltpu.VMEM(wqkv.shape, LOW),
            pltpu.VMEM(wqkv.shape, F32),
            pltpu.VMEM((chips, rows, width), LOW),
            pltpu.VMEM((2, rows, width), LOW),
            pltpu.VMEM((chips, rows, width), LOW),
            pltpu.VMEM((peers, half_chips, rows, width), LOW),
            pltpu.VMEM((peers, rows, width), LOW),
            pltpu.VMEM((3, 3, w_rows, width), LOW),
            pltpu.VMEM((split, 3, w_rows, width), LOW),
            pltpu.VMEM((n // 2, 3, shard, width), LOW),
            pltpu.VMEM((chips, 3, shard, width), LOW),
            pltpu.VMEM((nb, line_rows, slab), LOW),
            pltpu.VMEM((split, steps) + near, LOW),
            pltpu.VMEM((split,) + near, LOW),
            pltpu.VMEM((split,) + near, LOW),
            pltpu.VMEM((n, shard, slab), LOW),
            pltpu.VMEM((n, shard, slab), LOW),
            dma((3,)),
            dma((2,)),
            dma((chips,)),
            dma((chips,)),
            dma((half_chips,)),
            dma((peers, half_chips)),
            dma((chips,)),
            dma((peers,)),
            dma((half_chips,)),
            dma((1,)),
            dma((split, steps)),
            dma((split, steps)),
            dma((split,)),
            dma((split,)),
            dma((n // 2,)),
            dma((chips,)),
            dma((split, steps)),
            dma((split, steps)),
            dma((split,)),
            dma((split,)),
            dma((n,)),
            dma((n,)),
            dma((3,)),
            pltpu.VMEM((8, LANES), F32),
            pltpu.VMEM((2, small_rows, LANES), F32),
            pltpu.VMEM((n, small_rows, LANES), F32),
            pltpu.VMEM((nb, small_rows, LANES), F32),
            dma((n,)),
            dma((n,)),
            dma((nb,)),
            dma((nb,)),
        ],
        compiler_params=pltpu.CompilerParams(
            collective_id=4, has_side_effects=True, vmem_limit_bytes=63 * MIB
        ),
        name="attend_back",
    )(coef, qkv, go, keep, lse, q_full, h, wqkv, w_half, tokens, layer_sums)
    return result[:4]


def update_kernel(
    group_count, group_width, count, sums, gw, gw3, gain_ref, scale, first_s, second_s, gains, first_g,
    second_g, tok_in, gy_in, gh_in, w_in, m_in, s_in, norm_out, scale_out, first_s_out, second_s_out,
    gains_out, first_g_out, second_g_out, rms_out, grad_out, w_out, m_out, s_out,
    tok, gy, gh, w, m, v, sems,
):
    pairs = [(tok_in, tok), (gh_in, gh), (gy_in, gy), (w_in, w), (m_in, m), (s_in, v)]
    loads = [pltpu.make_async_copy(a, b, sems.at[k]) for k, (a, b) in enumerate(pairs)]
    for load in loads:
        load.start()
    width = tok.shape[2]
    tiles = width // LANES
    size = scale.shape[1]
    shard = gains.shape[1]
    gain_sums = [
        jnp.concatenate([sums[k * tiles + j : k * tiles + j + 1] for j in range(tiles)], axis=1)
        for k in range(2)
    ]
    slope = LOG_TWO_E / math.sqrt(size) / (1.0 + jnp.exp(-scale[...]))
    scale_grad = sums[2 * tiles : 2 * tiles + 1, :size] * slope

    def add_up(row):
        return jnp.sum(row, axis=1, keepdims=True)

    stats = [add_up(sums[2 * tiles + 1 + k : 2 * tiles + 2 + k]) for k in range(4)]
    for k in range(3):
        rms_out[:, k : k + 1] = jnp.sqrt(stats[k] / count)
    norm = jnp.sqrt(
        stats[3]
        + add_up(gain_sums[0] * gain_sums[0])
        + add_up(gain_sums[1] * gain_sums[1])
        + add_up(scale_grad * scale_grad)
    )
    norm_out[...] = norm
    clip = CLIP_NORM / jnp.maximum(norm, CLIP_NORM)

    def adam(outs, current, gradient, one, two, rate, decay):
        for out, value in zip(outs, adam_update(current, gradient * clip, one, two, rate, decay)):
            out[...] = value

    adam(
        (scale_out, first_s_out, second_s_out), scale[...], scale_grad, first_s[...], second_s[...],
        GAIN_RATE, 0.0,
    )
    index = lax.axis_index("batch") * lax.axis_size("seq") + lax.axis_index("seq")
    own = jnp.concatenate(gain_sums + [jnp.zeros((6, width), F32)], axis=0)
    own = pltpu.roll(own, lax.rem(width - index * shard, width), 1)[:2, :shard]
    adam(
        (gains_out, first_g_out, second_g_out), gains[...], own, first_g[...], second_g[...],
        GAIN_RATE, 0.0,
    )

    for load in loads[:3]:
        load.wait()
    for t in range(2):
        x = tok[t].astype(F32)
        factor = rms_factor(x)
        grad = gh[t].astype(F32) * gain_ref[:1]
        gy[t] = gy[t] + norm_back(grad, x * factor, factor)
    stores = [pltpu.make_async_copy(gy, grad_out, sems.at[0])]
    stores[0].start()
    for load in loads[3:]:
        load.wait()
    for k in range(6):
        if k < 3:
            span = slice(k * group_width, (k + 1) * group_width)
            gradient = jnp.concatenate([gw[g][:, span] for g in range(group_count)], axis=1)
        else:
            gradient = gw3[k - 3]
        w[k], m[k], v[k] = adam_update(w[k], gradient * clip, m[k], v[k], MATRIX_RATE, MATRIX_DECAY)
        for j, (a, b) in enumerate(((w, w_out), (m, m_out), (v, s_out))):
            copy = pltpu.make_async_copy(a.at[k], b.at[k], sems.at[6 + 3 * k + j])
            copy.start()
            stores.append(copy)
    for copy in stores:
        copy.wait()


def update(
    group_count, group_width, count, sums, gw, gw3, gain, scale, first_s, second_s, gains, first_g,
    second_g, tokens, gy, gh, weights, first_w, second_w,
):
    vmem = pl.BlockSpec(memory_space=pltpu.VMEM)
    anywhere = pl.BlockSpec(memory_space=pl.ANY)

    def like(value):
        return jax.ShapeDtypeStruct(value.shape, F32)

    kept = pltpu.VMEM(weights.shape, F32)
    return pl.pallas_call(
        functools.partial(update_kernel, group_count, group_width, count),
        out_shape=(
            jax.ShapeDtypeStruct((1, 1), F32), like(scale), like(scale), like(scale), like(gains),
            like(gains), like(gains), jax.ShapeDtypeStruct((1, 3), F32), like(gy), like(weights),
            like(weights), like(weights),
        ),
        in_specs=[vmem] * 10 + [anywhere] * 6,
        out_specs=[vmem] * 8 + [anywhere] * 4,
        scratch_shapes=[
            pltpu.VMEM(tokens.shape, LOW),
            pltpu.VMEM(gy.shape, F32),
            pltpu.VMEM(gh.shape, LOW),
            kept,
            kept,
            kept,
            pltpu.SemaphoreType.DMA((24,)),
        ],
        compiler_params=pltpu.CompilerParams(vmem_limit_bytes=62 * MIB),
        name="update",
    )(
        sums, gw, gw3, gain, scale, first_s, second_s, gains, first_g, second_g, tokens, gy, gh,
        weights, first_w, second_w,
    )


def body(
    n,
    nb,
    tokens,
    cotangent,
    weights,
    gains,
    query_scale,
    first_weights,
    second_weights,
    first_gains,
    second_gains,
    first_scale,
    second_scale,
    lengths,
):
    series_count, rows, width = tokens.shape
    size = query_scale.shape[0]
    group_count = n // 2
    heads = width // size // group_count
    group_width = heads * size
    fold = 640 // group_width
    shard = weights.shape[1]
    slab_width = (3 * group_width + 2 + LANES - 1) // LANES * LANES
    low_weights = weights.astype(LOW)
    slab = (
        low_weights[:3]
        .reshape(3, shard, group_count, group_width)
        .transpose(2, 1, 0, 3)
        .reshape(group_count, shard, 3 * group_width)
    )
    low_gains = jnp.broadcast_to(gains.astype(LOW).T[None], (group_count, shard, 2))
    spare = jnp.zeros((group_count, shard, slab_width - 3 * group_width - 2), LOW)
    slab = jnp.concatenate([slab, low_gains, spare], axis=2)

    (
        normed_in, qkv, q_full, o_keep, lse, o_recv, w_all, wqkv, gain_rows, coef_row,
    ) = front(n, nb, heads, size, fold, lengths, query_scale[None], tokens, slab, low_weights[3:])
    if w_all.ndim == 5:
        w_all = w_all.transpose(2, 0, 1, 3, 4).reshape(3, width, width)
    block_out, grad_middle, go_recv, layer_sums, w_half = layer(
        n, nb, fold, tokens, cotangent, o_recv, w_all, gain_rows
    )
    grad_normed, own_slab, own_three, sums = attend_back(
        n, nb, heads, size, fold, coef_row, qkv, go_recv, o_keep, lse, q_full, normed_in,
        wqkv, w_half, tokens, layer_sums, shard,
    )
    count = float(series_count * rows * width * nb * n)
    (
        grad_norm, new_scale, new_first_scale, new_second_scale, new_gains, new_first_gains,
        new_second_gains, rms_stats, input_grad, new_weights, new_first_weights, new_second_weights,
    ) = update(
        group_count, group_width, count, sums, own_slab, own_three, gain_rows, query_scale[None],
        first_scale[None], second_scale[None], gains, first_gains, second_gains, tokens, grad_middle,
        grad_normed, weights, first_weights, second_weights,
    )
    grad_norm = grad_norm.reshape(())
    new_scale, new_first_scale, new_second_scale = (
        new_scale.reshape(size), new_first_scale.reshape(size), new_second_scale.reshape(size)
    )
    rms_stats = rms_stats.reshape(3)
    return (
        block_out,
        input_grad,
        grad_norm,
        new_weights,
        new_first_weights,
        new_second_weights,
        new_gains,
        new_first_gains,
        new_second_gains,
        new_scale,
        new_first_scale,
        new_second_scale,
        rms_stats,
    )


def solution(mesh):
    return jax.shard_map(
        functools.partial(body, mesh.shape["seq"], mesh.shape["batch"]),
        mesh=mesh,
        in_specs=(
            P("batch", "seq", None),
            P("batch", "seq", None),
            P(None, ("batch", "seq"), None),
            P(None, ("batch", "seq")),
            P(),
            P(None, ("batch", "seq"), None),
            P(None, ("batch", "seq"), None),
            P(None, ("batch", "seq")),
            P(None, ("batch", "seq")),
            P(),
            P(),
            P("batch"),
        ),
        out_specs=(
            P("batch", "seq", None),
            P("batch", "seq", None),
            P(),
            P(None, ("batch", "seq"), None),
            P(None, ("batch", "seq"), None),
            P(None, ("batch", "seq"), None),
            P(None, ("batch", "seq")),
            P(None, ("batch", "seq")),
            P(None, ("batch", "seq")),
            P(),
            P(),
            P(),
            P(),
        ),
        check_vma=False,
    )
```

```python
import functools
import math

import jax
import jax.numpy as jnp
from jax import lax
from jax.experimental import pallas as pl
from jax.experimental.pallas import tpu as pltpu
from jax.sharding import PartitionSpec as P

STEP = 10

NORM_EPS = 1e-06
LOG_TWO_E = 1.442695
BETA_FIRST = 0.9
BETA_SECOND = 0.999
ADAM_EPS = 1e-08
MATRIX_RATE = 0.05
GAIN_RATE = 0.5
MATRIX_DECAY = 0.1
CLIP_NORM = 1.0
MASKED = -1e30

MESH = pl.DeviceIdType.MESH
LANES = 128
F32 = jnp.float32
LOW = jnp.bfloat16
MIB = 1024 * 1024


def rms_factor(values):
    return lax.rsqrt(jnp.mean(values * values, axis=-1, keepdims=True) + NORM_EPS)


def norm_back(grad_normed, normed, factor):
    return factor * (grad_normed - normed * jnp.mean(grad_normed * normed, axis=-1, keepdims=True))


def silu_slope(values):
    logistic = jax.nn.sigmoid(values)
    return logistic * (1.0 + values * (1.0 - logistic))


def adam_update(current, gradient, moment_one, moment_two, step_rate, decay_rate):
    new_one = BETA_FIRST * moment_one + (1.0 - BETA_FIRST) * gradient
    new_two = BETA_SECOND * moment_two + (1.0 - BETA_SECOND) * gradient * gradient
    first_hat = new_one / (1.0 - BETA_FIRST**STEP)
    second_hat = new_two / (1.0 - BETA_SECOND**STEP)
    updated = current - step_rate * (
        first_hat / (jnp.sqrt(second_hat) + ADAM_EPS) + decay_rate * current
    )
    return (updated, new_one, new_two)


def dot(left, right, left_axis=1, right_axis=0):
    return lax.dot_general(
        left, right, (((left_axis,), (right_axis,)), ((), ())), preferred_element_type=F32
    )


def greet(seq_count, batch_count):
    barrier = pltpu.get_barrier_semaphore()
    me_seq, me_batch = lax.axis_index("seq"), lax.axis_index("batch")
    for k in range(1, seq_count):
        pl.semaphore_signal(
            barrier,
            inc=1,
            device_id={"seq": lax.rem(me_seq + k, seq_count)},
            device_id_type=MESH,
        )
    for k in range(1, batch_count):
        pl.semaphore_signal(
            barrier,
            inc=1,
            device_id={"batch": lax.rem(me_batch + k, batch_count)},
            device_id_type=MESH,
        )
    pl.semaphore_wait(barrier, seq_count - 1 + batch_count - 1)


def push(source, target, send_sem, recv_sem, **where):
    return pltpu.make_async_remote_copy(
        source, target, send_sem, recv_sem, device_id=where, device_id_type=MESH
    )


def place(seq_count):
    me = lax.axis_index("seq")
    chips = seq_count // 2
    half_chips = chips // 2
    core = lax.rem(me, 2)
    chip = me // 2
    half = chip // half_chips
    base = half * half_chips
    gate_mine = half_chips - 1 + half
    gate_other = half_chips - half
    return me, core, chip, half, base, gate_mine, gate_other


def far_chip(step, half, half_chips):
    return (1 - half) * (half_chips + step) + half * (half_chips - 1 - step)


def batch_neighbours(batch):
    across = lax.rem(batch, 2)
    first = batch + 1 - 2 * across
    second = lax.rem(batch + 2, 4)
    return (first, second), lax.rem(first + 2, 4)


class Spread:
    def __init__(self, nb, block, send, recv):
        self.nb, self.block, self.send, self.recv = nb, block, send, recv
        self.batch = lax.axis_index("batch")
        self.copies = []

    def copy(self, owner, slot, j, lane, target, source=None):
        block = self.block(owner, slot)
        return push(
            block if source is None else source, block, self.send.at[j, lane],
            self.recv.at[j, lane], batch=target,
        )

    def route(self, lane):
        sides, across = batch_neighbours(self.batch)
        return sides[lane % 2], sides[1 - lane % 2], across

    def begin(self, slot, lane, source=None):
        if self.nb == 4:
            first, second, _ = self.route(lane)
            targets = [first, second]
        else:
            targets = [lax.rem(self.batch + j, self.nb) for j in range(1, self.nb)]
        new = [
            self.copy(self.batch, slot, j, lane, target, source) for j, target in enumerate(targets)
        ]
        for copy in new:
            copy.start()
        self.copies += new

    def relay(self, slot, lane):
        if self.nb == 4:
            first, second, _ = self.route(lane)
            self.copy(first, slot, 0, lane, first).wait_recv()
            copy = self.copy(first, slot, 2, lane, second)
            copy.start()
            self.copies.append(copy)
            return [first]
        return []

    def finish(self, slot, lane):
        if self.nb == 4:
            _, second, across = self.route(lane)
            self.copy(second, slot, 1, lane, second).wait_recv()
            self.copy(across, slot, 2, lane, second).wait_recv()
            return [second, across]
        owners = []
        for j in range(1, self.nb):
            owner = lax.rem(self.batch + self.nb - j, self.nb)
            self.copy(owner, slot, j - 1, lane, owner).wait_recv()
            owners.append(owner)
        return owners

    def drain(self):
        for copy in self.copies:
            copy.wait_send()


def widen(values):
    rows, width = values.shape
    return jnp.concatenate([values, jnp.zeros((rows, LANES - width), values.dtype)], axis=1)


def front_kernel(
    n, nb, heads, size, fold, chunks, joined, len_ref, scale_ref, gain_in, tok, w_in, h_out, qkv_out,
    q_out, keep_out, lse_out, o_out, w_all, wq_out, gain_out, coef_out,
    w_f, own_w, slab, x_s, h_s, zin, wq, chip_w, sib_w, qkv_s, q_s, keep_s, o_s, s_s, m_s, acc_s, sum_s,
    far_sem, own_sem, pass_sem, sib_sem, same_recv, sib_recv, z_send, z_recv, b_send, b_recv,
    h_sem, qkv_sem, q_sem, keep_sem, local_sem, o_send, o_recv, wz_send, wz_recv, wb_send, wb_recv,
    ws_send, ws_recv, wx_send, wx_recv,
):
    chips, half_chips = n // 2, n // 4
    me, core, chip, half, base, gate_mine, gate_other = place(n)
    group_count = n // 2
    batch = lax.axis_index("batch")
    sibling = 2 * chip + 1 - core
    block = tok.shape[1]
    width = tok.shape[2]
    rows = block // chunks
    group = range(heads)
    shard = own_w.shape[1]
    line = n * shard
    half_width = width // 2
    w_load = pltpu.make_async_copy(w_in, w_f, local_sem.at[8])
    w_load.start()
    greet(n, nb)
    w_load.wait()
    for m in range(3):
        own_w[m] = w_f[3 + m].astype(LOW)
    span = heads * size
    turned_gains = jnp.concatenate(
        [
            jnp.concatenate([gain_in[...], jnp.zeros((6, shard), F32)], axis=0),
            jnp.zeros((8, LANES - shard), F32),
        ],
        axis=1,
    ).T[:shard, :2]
    behind = jnp.zeros((shard, slab.shape[2] - 3 * span - 2), F32)
    for g in range(group_count):
        columns = [w_f[m, :, g * span : (g + 1) * span] for m in range(3)]
        slab[g] = jnp.concatenate(columns + [turned_gains, behind], axis=1).astype(LOW)

    sends = []
    z_copies = []
    for k in range(1, n):
        target = lax.rem(me + k, n)
        copy = push(
            slab.at[lax.rem(target, group_count)], zin.at[me], z_send.at[k], z_recv.at[k], seq=target
        )
        copy.start()
        z_copies.append(copy)
    slab_copy = pltpu.make_async_copy(
        slab.at[lax.rem(me, group_count)], zin.at[me], local_sem.at[0]
    )
    slab_copy.start()

    x_copy = None
    if joined:
        theirs = pl.ds(pl.multiple_of((1 - core) * half_width, LANES), half_width)
        ours = pl.ds(pl.multiple_of(core * half_width, LANES), half_width)
        x_copy = push(own_w.at[:, :, theirs], sib_w.at[0], wx_send, wx_recv, seq=sibling)
        x_copy.start()
        own_half = pltpu.make_async_copy(own_w.at[:, :, ours], sib_w.at[1], local_sem.at[1])
        own_half.start()

    def part(ref, lead, c):
        return ref.at[lead, pl.ds(c * rows, rows)]

    def tok_copy(source, slot, c, send_sem, recv_sem, target):
        return push(source, part(x_s, slot, c), send_sem, recv_sem.at[slot, c], seq=target)

    def send_tokens(c):
        copy = tok_copy(
            part(tok, 1 - half, c), me, c, far_sem.at[c], same_recv, 2 * gate_other + core
        )
        copy.start()
        sends.append(copy)
        for k in range(1, half_chips):
            other = base + lax.rem(chip - base + k, half_chips)
            copy = tok_copy(
                part(tok, half, c), me, c, own_sem.at[k, c], same_recv, 2 * other + core
            )
            copy.start()
            sends.append(copy)
        copy = tok_copy(part(tok, half, c), me, c, sib_sem.at[0, c], sib_recv, sibling)
        copy.start()
        sends.append(copy)

    for c in range(chunks):
        send_tokens(c)
    own_tok = pltpu.make_async_copy(tok.at[half], x_s.at[me], local_sem.at[2])
    own_tok.start()
    length = len_ref[half]
    scale = jnp.concatenate([scale_ref[...], jnp.zeros((1, LANES - size), F32)], axis=1)
    spot = lax.broadcasted_iota(jnp.int32, (1, LANES), 1)
    coef = jnp.where(
        spot < size,
        LOG_TWO_E / math.sqrt(size) * (jnp.maximum(scale, 0.0) + jnp.log1p(jnp.exp(-jnp.abs(scale)))),
        0.0,
    )
    coef_out[...] = coef

    def w_block(m, owner, p, c):
        if joined:
            start = pl.multiple_of((owner * chips + p) * 2 * shard, 16)
            return w_all.at[
                m, pl.ds(start, 2 * shard),
                pl.ds(pl.multiple_of(c * half_width, LANES), half_width),
            ]
        return w_all.at[owner, 2 * p + c, m]

    def w_source(m):
        return chip_w.at[m] if joined else own_w.at[m]

    matrices = [
        Spread(
            nb, lambda owner, p, m=m: w_block(m, owner, p, core), wb_send.at[m], wb_recv.at[m]
        )
        for m in range(3)
    ]
    w_line = []
    w_own = [
        pltpu.make_async_copy(w_source(m), w_block(m, batch, chip, core), local_sem.at[3 + m])
        for m in range(3)
    ]

    def chip_slot(k):
        return lax.rem(chip + chips - k, chips)

    def to_sibling(m, owner, k, j, source=None):
        piece = w_block(m, owner, chip_slot(k), core)
        copy = push(
            piece if source is None else source, piece, ws_send.at[m, j, k],
            ws_recv.at[m, owner, chip_slot(k)], seq=sibling,
        )
        copy.start()
        sends.append(copy)

    def w_send_line(m):
        for k in range(1, chips):
            target = 2 * lax.rem(chip + k, chips) + core
            copy = push(
                w_source(m), w_block(m, batch, chip, core), wz_send.at[m, k], wz_recv.at[m, k],
                seq=target,
            )
            copy.start()
            w_line.append(copy)
        w_own[m].start()
        matrices[m].begin(chip, 0, w_source(m))
        to_sibling(m, batch, 0, 0, w_source(m))

    def w_begin(m):
        for k in range(1, chips):
            slot = chip_slot(k)
            push(
                w_source(m), w_block(m, batch, slot, core), wz_send.at[m, k], wz_recv.at[m, k],
                seq=sibling,
            ).wait_recv()
            matrices[m].begin(slot, k)
            to_sibling(m, batch, k, 0)

    def w_relay(m):
        for k in range(chips):
            for j, owner in enumerate(matrices[m].relay(chip_slot(k), k)):
                to_sibling(m, owner, k, 1 + j)

    def w_finish(m):
        for k in range(chips):
            owners = matrices[m].finish(chip_slot(k), k)
            for j, owner in enumerate(owners):
                to_sibling(m, owner, k, nb - len(owners) + j)

    if joined:
        x_copy.wait_recv()
        own_half.wait()
        for m in range(3):
            other, mine = sib_w[0, m].astype(F32), sib_w[1, m].astype(F32)
            upper = jnp.where(core == 0, mine, other)
            lower = jnp.where(core == 0, other, mine)
            chip_w[m] = jnp.concatenate([upper, lower], axis=0).astype(LOW)
    w_send_line(0)

    slab_copy.wait()
    for copy in z_copies:
        copy.wait_recv()
    parts = [zin[k].astype(F32) for k in range(n)]
    line_start = pl.multiple_of(batch * line, 16)
    wq[pl.ds(line_start, line)] = jnp.concatenate(parts, axis=0).astype(LOW)
    pieces = 2 if nb == 4 else 1
    piece_rows = line // pieces

    def wq_block(owner, slot):
        return wq.at[pl.ds(pl.multiple_of(owner * line + slot * piece_rows, 16), piece_rows)]

    slices = Spread(nb, wq_block, b_send, b_recv)
    for k in range(pieces):
        slices.begin(k, k)

    def pass_near(c):
        for k in range(1, half_chips):
            slot = 2 * (base + lax.rem(chip - base + half_chips - k, half_chips)) + core
            tok_copy(part(x_s, slot, c), slot, c, sib_sem.at[k, c], same_recv, sibling).wait_recv()
            copy = tok_copy(part(x_s, slot, c), slot, c, sib_sem.at[k, c], sib_recv, sibling)
            copy.start()
            sends.append(copy)

    def pass_far(c):
        for k in range(half_chips):
            slot = 2 * far_chip(k, half, half_chips) + core
            lane = half_chips + k
            tok_copy(part(x_s, slot, c), slot, c, sib_sem.at[lane, c], same_recv, sibling).wait_recv()

            @pl.when(chip == gate_mine)
            def _():
                for j in range(1, half_chips):
                    other = base + lax.rem(chip - base + j, half_chips)
                    tok_copy(
                        part(x_s, slot, c), slot, c, pass_sem.at[k, j, c], same_recv,
                        2 * other + core,
                    ).start()

            copy = tok_copy(part(x_s, slot, c), slot, c, sib_sem.at[lane, c], sib_recv, sibling)
            copy.start()
            sends.append(copy)

    pass_near(0)
    pass_near(1)
    pass_far(0)
    for k in range(pieces):
        slices.relay(k, k)
    pass_near(2)
    pass_near(3)
    pass_far(1)
    w_begin(0)
    pass_far(2)
    for k in range(pieces):
        slices.finish(k, k)
    w_relay(0)
    wq_copy = pltpu.make_async_copy(wq, wq_out, local_sem.at[6])
    wq_copy.start()
    columns = 3 * heads * size
    tile = columns // LANES * LANES
    turned = wq[:, tile : tile + LANES].astype(F32).T
    gains = jnp.concatenate(
        [turned[columns - tile + k : columns - tile + k + 1] for k in range(2)], axis=0
    )
    gain_out[...] = gains
    gain = gains[:1]

    def kept(i):
        return [
            pltpu.make_async_copy(qkv_s.at[i], qkv_out.at[i], qkv_sem.at[i]),
            pltpu.make_async_copy(q_s.at[i], q_out.at[i], q_sem.at[i]),
        ]

    def h_copy(i, lane):
        return pltpu.make_async_copy(h_s.at[lane], h_out.at[i], h_sem.at[lane])

    def keep_copy(i):
        return pltpu.make_async_copy(keep_s.at[i], keep_out.at[i], keep_sem.at[i])

    def o_push(i):
        return push(o_s.at[i], o_out.at[me], o_send.at[i], o_recv.at[me], seq=i)

    own_o = pltpu.make_async_copy(o_s.at[me], o_out.at[me], local_sem.at[7])

    def project(i, lane):
        x = x_s[i].astype(F32)
        h = (x * rms_factor(x) * gain).astype(LOW)
        h_s[lane] = h
        h_copy(i, lane).start()
        out = dot(h, wq[...])
        place_in = lax.broadcasted_iota(jnp.int32, (block, LANES), 1)
        row = i * block + lax.broadcasted_iota(jnp.int32, (block, LANES), 0)
        mark = jnp.where(place_in == size, 1.0, 0.0)
        hide = jnp.where((place_in == size) & (row >= length), MASKED, 0.0)
        for a in group:
            q = widen(out[:, a * size : (a + 1) * size])
            q_s[i, a] = q
            qkv_s[i, a] = (q * coef + mark).astype(LOW)
        for a in range(heads, 2 * heads):
            qkv_s[i, a] = (widen(out[:, a * size : (a + 1) * size]) + hide).astype(LOW)
        for a in range(2 * heads, 3 * heads):
            qkv_s[i, a] = widen(out[:, a * size : (a + 1) * size].astype(LOW))
        for copy in kept(i):
            copy.start()

    own_tok.wait()

    def project_chips(first, last):
        @pl.loop(first, last)
        def _(k):
            q = half * (chips - 1 - k) + (1 - half) * k
            for lane in range(2):
                slot = 2 * q + (core if lane == 0 else 1 - core)
                if lane == 1:
                    for c in range(chunks):
                        tok_copy(
                            part(x_s, slot, c), slot, c, sib_sem.at[0, c], sib_recv, sibling
                        ).wait_recv()

                @pl.when(k > 0)
                def _():
                    h_copy(slot, lane).wait()

                project(slot, lane)

    @pl.when(chip != gate_mine)
    def _():
        project_chips(0, half_chips)

    pass_far(3)
    w_send_line(1)
    w_send_line(2)

    @pl.when(chip == gate_mine)
    def _():
        project_chips(0, half_chips)

    w_finish(0)
    project_chips(half_chips, chips)
    for lane in range(2):
        h_copy(me, lane).wait()

    def score(i, j, diagonal):
        if diagonal:
            row = lax.broadcasted_iota(jnp.int32, (block, block), 0)
            col = lax.broadcasted_iota(jnp.int32, (block, block), 1)
            visible = col <= row
        for a in group:
            s = dot(qkv_s[i, a], qkv_s[j, heads + a], 1, 1)
            if diagonal:
                s = jnp.where(visible, s, MASKED)
            s_s[a, j] = s
            best = m_s[a]
            for lane in range(block // LANES):
                best = jnp.maximum(best, s[:, lane * LANES : (lane + 1) * LANES])
            m_s[a] = best

    def mix(j):
        for a in group:
            best = m_s[a]
            count = sum_s[a]
            terms = []
            for lane in range(block // LANES):
                e = jnp.exp(s_s[a, j, :, lane * LANES : (lane + 1) * LANES] - best)
                count = count + e
                terms.append(e.astype(LOW))
            sum_s[a] = count
            acc_s[a] += dot(jnp.concatenate(terms, axis=1), qkv_s[j, 2 * heads + a])

    def query_block(t):
        i = lax.rem(me + 1 + t, n)
        m_s[...] = jnp.full_like(m_s, MASKED)
        sum_s[...] = jnp.zeros_like(sum_s)
        acc_s[...] = jnp.zeros_like(acc_s)
        pl.loop(0, i)(lambda j: score(i, j, False))
        score(i, i, True)
        for a in group:
            m_s[a] = jnp.broadcast_to(jnp.max(m_s[a], axis=1, keepdims=True), (block, LANES))
        pl.loop(0, i + 1)(mix)
        outs = []
        for a in group:
            count = jnp.sum(sum_s[a], axis=1, keepdims=True)
            out = acc_s[a] / count
            keep_s[i, a] = out
            outs.append(out[:, :size])
            lse_out[i, a] = (m_s[a] + jnp.log(count)).T[:8]
        low = jnp.concatenate(outs, axis=1).astype(LOW)
        piece = block // fold
        o_s[i] = jnp.concatenate([low[f * piece : (f + 1) * piece] for f in range(fold)], axis=1)
        keep_copy(i).start()

        @pl.when(i != me)
        def _():
            o_push(i).start()

        @pl.when(i == me)
        def _():
            own_o.start()

    bounds = [0, 2, 3, n - 3, n - 2, n] if n > 4 else [0, 1, 1, 2, 2, n]
    events = [lambda: w_begin(1), lambda: w_begin(2), lambda: w_relay(1), lambda: w_relay(2), None]
    for first, last, event in zip(bounds[:-1], bounds[1:], events):
        if last > first:
            pl.loop(first, last)(query_block)
        if event is not None:
            event()
    w_finish(1)
    w_finish(2)

    for k in range(1, n):
        source = lax.rem(me + k, n)
        push(
            o_s.at[source], o_out.at[source], o_send.at[source], o_recv.at[source], seq=source
        ).wait()
    own_o.wait()
    for m in range(3):
        for owner in range(nb):
            for q in range(chips):
                piece = w_block(m, owner, q, 1 - core)
                push(
                    piece, piece, ws_send.at[0, 0, 0], ws_recv.at[m, owner, q], seq=sibling
                ).wait_recv()
        matrices[m].drain()
        w_own[m].wait()
    slices.drain()
    if joined:
        x_copy.wait_send()
    wq_copy.wait()
    for copy in sends + z_copies + w_line:
        copy.wait_send()

    @pl.when(chip == gate_mine)
    def _():
        for c in range(chunks):
            for k in range(half_chips):
                for j in range(1, half_chips):
                    tok_copy(
                        part(x_s, me, c), me, c, pass_sem.at[k, j, c], same_recv, sibling
                    ).wait_send()

    @pl.loop(0, n)
    def _(i):
        keep_copy(i).wait()
        for copy in kept(i):
            copy.wait()


def front(n, nb, heads, size, fold, lengths, scale, gains, tokens, weights):
    chunks = 4
    _, rows, width = tokens.shape
    chips, half_chips = n // 2, n // 4
    shard = weights.shape[1]
    joined = 2 * shard % 16 == 0
    folded = (n, rows // fold, heads * size * fold)
    many, one = (n, 3 * heads, rows, LANES), (n, heads, rows, LANES)
    slab_width = (3 * heads * size + 2 + LANES - 1) // LANES * LANES
    pieces = 2 if nb == 4 else 1
    all_shape = (3, width, width) if joined else (nb, n, 3, shard, width)
    pair = (3, 2 * shard, width // 2) if joined else (3, 16, LANES)
    single = (2, 3, shard, width // 2) if joined else (2, 3, 16, LANES)
    dma = pltpu.SemaphoreType.DMA
    vmem = pl.BlockSpec(memory_space=pltpu.VMEM)
    smem = pl.BlockSpec(memory_space=pltpu.SMEM)
    anywhere = pl.BlockSpec(memory_space=pl.ANY)
    state = pltpu.VMEM((heads, rows, LANES), F32)
    return pl.pallas_call(
        functools.partial(front_kernel, n, nb, heads, size, fold, chunks, joined),
        out_shape=(
            jax.ShapeDtypeStruct((n, rows, width), LOW),
            jax.ShapeDtypeStruct(many, LOW),
            jax.ShapeDtypeStruct(one, F32),
            jax.ShapeDtypeStruct(one, F32),
            jax.ShapeDtypeStruct((n, heads, 8, rows), F32),
            jax.ShapeDtypeStruct(folded, LOW),
            jax.ShapeDtypeStruct(all_shape, LOW),
            jax.ShapeDtypeStruct((width, slab_width), LOW),
            jax.ShapeDtypeStruct((2, width), F32),
            jax.ShapeDtypeStruct((1, LANES), F32),
        ),
        in_specs=[smem, vmem, vmem, anywhere, anywhere],
        out_specs=[anywhere] * 4 + [vmem] + [anywhere] * 3 + [vmem, vmem],
        scratch_shapes=[
            pltpu.VMEM(weights.shape, F32),
            pltpu.VMEM((3, shard, width), LOW),
            pltpu.VMEM((n // 2, shard, slab_width), LOW),
            pltpu.VMEM((n, rows, width), LOW),
            pltpu.VMEM((2, rows, width), LOW),
            pltpu.VMEM((n, shard, slab_width), LOW),
            pltpu.VMEM((width, slab_width), LOW),
            pltpu.VMEM(pair, LOW),
            pltpu.VMEM(single, LOW),
            pltpu.VMEM(many, LOW),
            pltpu.VMEM(one, F32),
            pltpu.VMEM(one, F32),
            pltpu.VMEM(folded, LOW),
            pltpu.VMEM((heads, n, rows, rows), F32),
            state,
            state,
            state,
            dma((chunks,)),
            dma((half_chips, chunks)),
            dma((half_chips, half_chips, chunks)),
            dma((chips, chunks)),
            dma((n, chunks)),
            dma((n, chunks)),
            dma((n,)),
            dma((n,)),
            dma((nb, pieces)),
            dma((nb, pieces)),
            dma((2,)),
            dma((n,)),
            dma((n,)),
            dma((n,)),
            dma((9,)),
            dma((n,)),
            dma((n,)),
            dma((3, chips)),
            dma((3, chips)),
            dma((3, nb, chips)),
            dma((3, nb, chips)),
            dma((3, nb, chips)),
            dma((3, nb, chips)),
            dma,
            dma,
        ],
        compiler_params=pltpu.CompilerParams(
            collective_id=2, has_side_effects=True, vmem_limit_bytes=62 * MIB
        ),
        name="front",
    )(lengths, scale, gains, tokens, weights)


def fold_rows(values):
    rows, width = values.shape
    return jnp.sum(values.reshape(rows // 8, 8, width), axis=0)


def layer_kernel(
    n, nb, fold, tok, cot, o_in, w_in, gain_ref, y_out, gy_out, go_out, small_out, half_out,
    w, o_s, hidden_s, act_s, gu_s, ga_s, go_s, gw_s, sib_in, w_sem, send_sem, recv_sem, local_sem,
    sib_send, sib_recv,
):
    group_count = n // 2
    me, core, chip, half, base, gate_mine, gate_other = place(n)
    sibling = 2 * chip + 1 - core
    _, rows, width = tok.shape
    group_width = width // group_count
    piece = rows // fold
    barrier = pltpu.get_barrier_semaphore()
    for k in range(1, n):
        pl.semaphore_signal(
            barrier, inc=1, device_id={"seq": lax.rem(me + k, n)}, device_id_type=MESH
        )
    loads = [pltpu.make_async_copy(w_in.at[m], w.at[m], w_sem.at[m]) for m in range(3)]
    for load in loads:
        load.start()
    small_out[...] = jnp.zeros_like(small_out)
    gain = gain_ref[1:2]

    def go_push(target):
        return push(
            go_s.at[target], go_out.at[me], send_sem.at[target], recv_sem.at[me], seq=target
        )

    own_go = pltpu.make_async_copy(go_s.at[me], go_out.at[me], local_sem)

    for step in range(2):
        t = half if step else 1 - half
        parts = [
            jnp.concatenate(
                [
                    o_in[t * group_count + g, :, f * group_width : (f + 1) * group_width]
                    for g in range(group_count)
                ],
                axis=1,
            )
            for f in range(fold)
        ]
        o = jnp.concatenate(parts, axis=0)
        o_s[t] = o
        if step == 0:
            loads[0].wait()
        a = dot(o, w[0])
        small_out[1] += fold_rows(a * a)
        y1 = tok[t].astype(F32) + a
        factor = rms_factor(y1)
        normed = y1 * factor
        hidden = (normed * gain).astype(LOW)
        hidden_s[t] = hidden
        if step == 0:
            loads[1].wait()
        u = dot(hidden, w[1])
        logistic = 1.0 / (1.0 + jnp.exp(-u))
        act = (u * logistic).astype(LOW)
        act_s[t] = act
        if step == 0:
            loads[2].wait()
        f = dot(act, w[2])
        small_out[2] += fold_rows(f * f)
        y = y1 + f
        small_out[3] += fold_rows(y * y)
        y_out[t] = y.astype(LOW)
        gz = dot(cot[t], w[2], 1, 1)
        gu = (gz * (logistic * (1.0 + u * (1.0 - logistic)))).astype(LOW)
        gu_s[t] = gu
        gh = dot(gu, w[1], 1, 1)
        small_out[0] += fold_rows(gh * normed)
        gy = cot[t].astype(F32) + norm_back(gh * gain, normed, factor)
        gy_out[t] = gy
        ga = gy.astype(LOW)
        ga_s[t] = ga
        go = dot(ga, w[0], 1, 1).astype(LOW)
        for g in range(group_count):
            block = go[:, g * group_width : (g + 1) * group_width]
            go_s[t * group_count + g] = jnp.concatenate(
                [block[f * piece : (f + 1) * piece] for f in range(fold)], axis=1
            )
        if step == 0:
            pl.semaphore_wait(barrier, n - 1)
        for g in range(group_count):
            target = t * group_count + g

            @pl.when(target != me)
            def _():
                go_push(target).start()

            @pl.when(target == me)
            def _():
                own_go.start()

    tile = 256
    half_rows = width // nb // 2
    sib_copies = []
    pairs = ((act_s, cot, 2), (hidden_s, gu_s, 1), (o_s, ga_s, 0))
    for left, right, m in pairs:

        @pl.loop(0, width // tile)
        def _(k):
            cols = pl.ds(pl.multiple_of(k * tile, tile), tile)
            total = dot(left[0, :, cols], right[0], 0, 0) + dot(left[1, :, cols], right[1], 0, 0)
            gw_s[m, cols] = total.astype(LOW)

        for b in range(nb):
            start = pl.multiple_of((2 * b + 1 - core) * half_rows, 16)
            copy = push(
                gw_s.at[m, pl.ds(start, half_rows)], sib_in.at[b, m], sib_send.at[b, m],
                sib_recv.at[b, m], seq=sibling,
            )
            copy.start()
            sib_copies.append(copy)
    index = 0
    for _, _, m in pairs:
        for b in range(nb):
            sib_copies[index].wait_recv()
            index += 1
            start = pl.multiple_of((2 * b + core) * half_rows, 16)
            half_out[b, m] = (
                gw_s[m, pl.ds(start, half_rows)].astype(F32) + sib_in[b, m].astype(F32)
            ).astype(LOW)
    for k in range(1, n):
        source = lax.rem(me + k, n)
        push(
            go_s.at[source], go_out.at[source], send_sem.at[source], recv_sem.at[source], seq=source
        ).wait()
    own_go.wait()
    for copy in sib_copies:
        copy.wait_send()


def layer(n, nb, fold, tokens, cotangent, o_recv, w_all, gain):
    _, rows, width = tokens.shape
    half_rows = width // nb // 2
    dma = pltpu.SemaphoreType.DMA
    vmem = pl.BlockSpec(memory_space=pltpu.VMEM)
    anywhere = pl.BlockSpec(memory_space=pl.ANY)
    kept = pltpu.VMEM((2, rows, width), LOW)
    return pl.pallas_call(
        functools.partial(layer_kernel, n, nb, fold),
        out_shape=(
            jax.ShapeDtypeStruct((2, rows, width), LOW),
            jax.ShapeDtypeStruct((2, rows, width), F32),
            jax.ShapeDtypeStruct(o_recv.shape, LOW),
            jax.ShapeDtypeStruct((4, 8, width), F32),
            jax.ShapeDtypeStruct((nb, 3, half_rows, width), LOW),
        ),
        in_specs=[vmem, vmem, vmem, anywhere, vmem],
        out_specs=[vmem, vmem, anywhere, vmem, vmem],
        scratch_shapes=[
            pltpu.VMEM((3, width, width), LOW),
            kept,
            kept,
            kept,
            kept,
            kept,
            pltpu.VMEM(o_recv.shape, LOW),
            pltpu.VMEM((3, width, width), LOW),
            pltpu.VMEM((nb, 3, half_rows, width), LOW),
            dma((3,)),
            dma((n,)),
            dma((n,)),
            dma,
            dma((nb, 3)),
            dma((nb, 3)),
        ],
        compiler_params=pltpu.CompilerParams(
            collective_id=3, has_side_effects=True, vmem_limit_bytes=63 * MIB
        ),
        name="layer",
    )(tokens, cotangent, o_recv, w_all, gain)


def back_kernel(
    n, nb, heads, size, fold, coef_ref, qkv_in, go_ref, keep_in, lse_ref, q_in, h_in, w_in,
    half_in, tok, sums_ref, out, own_gw, own_w, sums_out, cross_in, turn_in,
    qkv, kt, g_s, delta, gq, gk, gv, q_s, h_s, w_s, gw, gh_own, gh_out, from_sib, gate_in, peer_in,
    stage, cross_out, w_line, w_parts, gw_low, near_in, near_out, near_turn, line_out, line_in,
    load_sem, block_sem, sib_send, sib_recv, gate_send, gate_recv, peer_send, peer_recv, far_send,
    far_recv, c_send, c_recv, t_send, t_recv, w_send, w_recv, b_send, b_recv, bt_send, bt_recv,
    z_send, z_recv, stage_sem, scale_sum, sum_mine, sum_line, sum_batch, s_send, s_recv, u_send,
    u_recv,
):
    chips, half_chips = n // 2, n // 4
    me, core, chip, half, base, gate_mine, gate_other = place(n)
    group_count = n // 2
    batch = lax.axis_index("batch")
    sibling = 2 * chip + 1 - core
    block = qkv.shape[2]
    group = range(heads)
    sides, across = batch_neighbours(batch)
    is_gate = chip == gate_mine
    paired = nb == 4
    greet(n, nb)

    w_rows = stage.shape[2]

    def w_piece(owner, h):
        return half_in.at[owner, :, pl.ds(h * w_rows, w_rows)]

    w_copies = []
    if paired:
        for h in range(2):
            for j, owner in enumerate((across, sides[h])):
                w_copies.append(
                    push(
                        w_piece(owner, h), cross_in.at[h, j], c_send.at[h, j], c_recv.at[h, j],
                        batch=sides[h],
                    )
                )
    else:
        for k in range(1, nb):
            target = lax.rem(batch + k, nb)
            w_copies.append(
                push(
                    w_piece(target, 0), cross_in.at[0, k], c_send.at[0, k], c_recv.at[0, k],
                    batch=target,
                )
            )
    for copy in w_copies:
        copy.start()

    own_terms = []
    if paired:
        for slot, (owner, h) in enumerate(((sides[1], 0), (sides[0], 1), (batch, 0), (batch, 1))):
            load = pltpu.make_async_copy(w_piece(owner, h), stage.at[slot], stage_sem.at[slot])
            own_terms.append(load)

    keep_load = pltpu.make_async_copy(keep_in, gk, load_sem.at[0])
    qkv_load = pltpu.make_async_copy(qkv_in, qkv, load_sem.at[1])
    w_load = pltpu.make_async_copy(w_in, w_s, load_sem.at[2])
    for load in (keep_load, qkv_load, w_load):
        load.start()
    for load in own_terms:
        load.start()
    scale_sum[...] = jnp.zeros_like(scale_sum)
    gv[...] = jnp.zeros_like(gv)
    gq[...] = jnp.zeros_like(gq)
    keep_load.wait()

    @pl.loop(0, n)
    def _(i):
        for a in group:
            g = widen(
                jnp.concatenate(
                    [
                        go_ref[i, :, (f * heads + a) * size : (f * heads + a + 1) * size]
                        for f in range(fold)
                    ],
                    axis=0,
                )
            )
            g_s[i, a] = g
            delta[i, a] = jnp.broadcast_to(
                jnp.sum((g.astype(F32) * gk[i, a]).T, axis=0, keepdims=True), (8, block)
            )
            gk[i, a] = jnp.zeros_like(gk[i, a])

    qkv_load.wait()

    @pl.loop(0, n)
    def _(j):
        for a in group:
            kt[j, a] = qkv[j, heads + a].T

    w_load.wait()

    def pair_block(i, j, diagonal):
        if diagonal:
            col = lax.broadcasted_iota(jnp.int32, (block, block), 0)
            row = lax.broadcasted_iota(jnp.int32, (block, block), 1)
            visible = col <= row
        for a in group:
            s = dot(qkv[j, heads + a], qkv[i, a], 1, 1)
            p = jnp.exp(s - lse_ref[i, a, :1])
            if diagonal:
                p = jnp.where(visible, p, 0.0)
            dp = dot(qkv[j, 2 * heads + a], g_s[i, a], 1, 1)
            ds = (p * (dp - delta[i, a, :1])).astype(LOW)
            gk[j, a] += dot(ds, qkv[i, a])
            gv[j, a] += dot(p.astype(LOW), g_s[i, a])
            gq[i, a] += dot(kt[j, a], ds)

    def sib_copy(t):
        return push(
            gh_out.at[t % 2], from_sib.at[t], sib_send.at[t], sib_recv.at[t], seq=sibling
        )

    def step(t, u):
        r = half * t + (1 - half) * (n - 1 - t)
        loads = [
            pltpu.make_async_copy(q_in.at[r], q_s, block_sem.at[0]),
            pltpu.make_async_copy(h_in.at[r], h_s, block_sem.at[1]),
        ]
        for load in loads:
            load.start()
        pair_block(r, r, True)
        pl.loop(1, n - t)(lambda v: pair_block(r + half * v, r - (1 - half) * v, False))
        for load in loads:
            load.wait()
        pieces = []
        for a in group:
            grad = gq[r, a].T.astype(LOW).astype(F32)
            scale_sum[...] += fold_rows(grad * q_s[a])
            pieces.append((grad * coef_ref[...])[:, :size].astype(LOW))
        pieces += [gk[r, a][:, :size].astype(LOW) for a in group]
        pieces += [gv[r, a][:, :size].astype(LOW) for a in group]
        spare = w_s.shape[1] - 3 * heads * size
        pieces.append(jnp.zeros((block, spare), LOW))
        grads = jnp.concatenate(pieces, axis=1)
        gh = dot(grads, w_s[...], 1, 1).astype(LOW)
        tp = t // 2
        mine = lax.rem(r, 2) == core

        @pl.when(mine)
        def _():
            gh_own[tp] = gh

        @pl.when(jnp.logical_not(mine))
        def _():
            gh_out[tp % 2] = gh
            sib_copy(tp).start()

        part = dot(h_s[...], grads, 0, 0)
        if t == 0:
            gw[...] = part
        else:
            gw[...] += part

    def far_chip_of(tp):
        return half * tp + (1 - half) * (chips - 1 - tp)

    def gate_copy(tp):
        after = lax.rem(chip - gate_mine + half_chips, half_chips)
        return push(
            gh_own.at[tp], gate_in.at[after - 1, tp], gate_send.at[tp],
            gate_recv.at[after - 1, tp], seq=2 * gate_mine + core,
        )

    def far_copy(tp):
        return push(
            gh_own.at[tp], out.at[half], far_send.at[tp], far_recv.at[0],
            seq=2 * far_chip_of(tp) + core,
        )

    def peer_copy(tp):
        q = far_chip_of(tp)
        after = lax.rem(chip - q + half_chips, half_chips)
        return push(
            gh_own.at[tp], peer_in.at[after - 1], peer_send.at[tp], peer_recv.at[after - 1],
            seq=2 * q + core,
        )

    def relay(tp):
        @pl.when(is_gate)
        def _():
            value = gh_own[tp].astype(F32)
            for j in range(half_chips - 1):
                push(
                    gh_own.at[tp], gate_in.at[j, tp], gate_send.at[tp], gate_recv.at[j, tp],
                    seq=sibling,
                ).wait_recv()
                value = value + gate_in[j, tp].astype(F32)
            gh_own[tp] = value.astype(LOW)
            far_copy(tp).start()

    shard = own_w.shape[1]

    def staged(*sources):
        value = None
        for first in range(0, len(sources), 3):
            loads = [
                pltpu.make_async_copy(source, stage.at[j], stage_sem.at[j])
                for j, source in enumerate(sources[first : first + 3])
            ]
            for load in loads:
                load.start()
            for load in loads:
                load.wait()
            for j in range(len(loads)):
                term = stage[j].astype(F32)
                value = term if value is None else value + term
        return value

    t_copies = []

    def turn():
        if paired:
            for h in range(2):
                w_copies[2 * h].wait_recv()
                own_terms[h].wait()
                cross_out[h] = (stage[h].astype(F32) + cross_in[h, 0].astype(F32)).astype(LOW)
                copy = push(
                    cross_out.at[h], turn_in.at[h], t_send.at[h], t_recv.at[h], batch=sides[1 - h]
                )
                copy.start()
                t_copies.append(copy)

    def w_push(i):
        target = core * group_count + i
        return push(w_line.at[i], w_parts.at[chip], w_send.at[i], w_recv.at[chip], seq=target)

    def to_owners():
        for copy in w_copies[1::2] if paired else w_copies:
            copy.wait_recv()
        for copy in t_copies:
            copy.wait_recv()
        splits = 2 if paired else 1
        each = group_count // splits
        for h in range(splits):
            if paired:
                own_terms[2 + h].wait()
                value = stage[2 + h].astype(F32) + cross_in[h, 1].astype(F32) + turn_in[h].astype(F32)
            else:
                value = staged(w_piece(batch, 0), *[cross_in.at[0, k] for k in range(1, nb)])
            for i in range(each):
                w_line[h * each + i] = value[:, i * shard : (i + 1) * shard].astype(LOW)
        for i in range(group_count):
            own = core * group_count + i == me

            @pl.when(own)
            def _():
                w_parts[chip] = w_line[i]

            @pl.when(jnp.logical_not(own))
            def _():
                w_push(i).start()

    for tp in range(chips):
        if tp >= 2:
            sib_copy(tp - 2).wait_send()
        step(2 * tp, 0)
        if tp == 1:
            to_owners()
        step(2 * tp + 1, 1)
        if tp == 0:
            turn()
        sib_copy(tp).wait_recv()
        gh_own[tp] = (gh_own[tp].astype(F32) + from_sib[tp].astype(F32)).astype(LOW)
        if tp < half_chips:

            @pl.when(jnp.logical_not(is_gate))
            def _():
                gate_copy(tp).start()

        else:

            @pl.when(far_chip_of(tp) != chip)
            def _():
                peer_copy(tp).start()

        if 1 <= tp < half_chips:
            relay(tp - 1)

    line_rows = gw.shape[0] // nb
    near_rows = near_in.shape[2]
    for b in range(nb):
        gw_low[b] = gw[b * line_rows : (b + 1) * line_rows].astype(LOW)

    def near_piece(owner, h):
        return gw_low.at[owner, pl.ds(h * near_rows, near_rows)]

    b_copies = []
    if paired:
        for h in range(2):
            for j, owner in enumerate((across, sides[h])):
                b_copies.append(
                    push(
                        near_piece(owner, h), near_in.at[h, j], b_send.at[h, j], b_recv.at[h, j],
                        batch=sides[h],
                    )
                )
    else:
        for k in range(1, nb):
            target = lax.rem(batch + k, nb)
            b_copies.append(
                push(
                    near_piece(target, 0), near_in.at[0, k], b_send.at[0, k], b_recv.at[0, k],
                    batch=target,
                )
            )
    for copy in b_copies:
        copy.start()
    relay(half_chips - 1)
    bt_copies = []
    if paired:
        for h in range(2):
            b_copies[2 * h].wait_recv()
            near_out[h] = (
                gw_low[sides[1 - h], pl.ds(h * near_rows, near_rows)].astype(F32)
                + near_in[h, 0].astype(F32)
            ).astype(LOW)
            copy = push(
                near_out.at[h], near_turn.at[h], bt_send.at[h], bt_recv.at[h], batch=sides[1 - h]
            )
            copy.start()
            bt_copies.append(copy)
    z_copies = []

    def z_copy(target):
        return push(
            line_out.at[target], line_in.at[me], z_send.at[target], z_recv.at[me], seq=target
        )

    splits = 2 if paired else 1
    each = n // splits
    for h in range(splits):
        value = gw_low[batch, pl.ds(h * near_rows, near_rows)].astype(F32)
        if paired:
            b_copies[2 * h + 1].wait_recv()
            bt_copies[h].wait_recv()
            value = value + near_in[h, 1].astype(F32) + near_turn[h].astype(F32)
        else:
            for k in range(1, nb):
                b_copies[k - 1].wait_recv()
                value = value + near_in[0, k].astype(F32)
        for i in range(each):
            target = h * each + i
            line_out[target] = value[i * shard : (i + 1) * shard].astype(LOW)

            @pl.when(target != me)
            def _():
                z_copy(target).start()

            @pl.when(target == me)
            def _():
                line_in[me] = line_out[target]

    value = gh_own[half * chip + (1 - half) * (chips - 1 - chip)].astype(F32)
    for j in range(half_chips - 1):
        push(
            gh_own.at[0], peer_in.at[j], peer_send.at[0], peer_recv.at[j], seq=sibling
        ).wait_recv()
        value = value + peer_in[j].astype(F32)
    out[half] = value.astype(LOW)
    push(gh_own.at[0], out.at[1 - half], far_send.at[0], far_recv.at[0], seq=sibling).wait_recv()

    tiles = out.shape[2] // LANES
    gain_sum = None
    for t in range(2):
        load = pltpu.make_async_copy(tok.at[t], h_s, block_sem.at[1])
        load.start()
        load.wait()
        x = h_s[...].astype(F32)
        term = fold_rows(out[t].astype(F32) * (x * rms_factor(x)))
        gain_sum = term if gain_sum is None else gain_sum + term

    def lanes(row):
        return [row[:, k * LANES : (k + 1) * LANES] for k in range(row.shape[1] // LANES)]

    def squeeze(row):
        total = None
        for piece in lanes(row):
            total = piece if total is None else total + piece
        return total

    rows_out = lanes(jnp.sum(gain_sum, axis=0, keepdims=True))
    rows_out += lanes(jnp.sum(sums_ref[0], axis=0, keepdims=True))
    rows_out.append(jnp.sum(scale_sum[...], axis=0, keepdims=True))
    for k in range(1, 4):
        rows_out.append(squeeze(jnp.sum(sums_ref[k], axis=0, keepdims=True)))

    for q in range(chips):

        @pl.when(2 * q + half != me)
        def _():
            push(w_line.at[0], w_parts.at[q], w_send.at[0], w_recv.at[q], seq=sibling).wait_recv()

    value = w_parts[0].astype(F32)
    for q in range(1, chips):
        value = value + w_parts[q].astype(F32)
    own_w[...] = value

    for k in range(1, n):
        source = lax.rem(me + k, n)
        push(
            line_out.at[source], line_in.at[source], z_send.at[source], z_recv.at[source], seq=source
        ).wait()
    for g in range(group_count):
        own_gw[g] = line_in[g].astype(F32) + line_in[g + group_count].astype(F32)

    squares = None
    for value in [own_gw[g] for g in range(group_count)] + [own_w[m] for m in range(3)]:
        term = squeeze(jnp.sum(value * value, axis=0, keepdims=True))
        squares = term if squares is None else squares + term
    rows_out.append(squares)
    sum_mine[0] = jnp.zeros_like(sum_mine[0])
    for k, row in enumerate(rows_out):
        sum_mine[0, k : k + 1, :] = row
    s_copies = []
    for k in range(1, n):
        copy = push(
            sum_mine.at[0], sum_line.at[k], s_send.at[k], s_recv.at[k], seq=lax.rem(me + k, n)
        )
        copy.start()
        s_copies.append(copy)
    sum_line[0] = sum_mine[0]
    for copy in s_copies:
        copy.wait_recv()
    value = jnp.zeros_like(sum_mine[0])
    for k in range(n):
        value = value + sum_line[lax.rem(me - k + n, n)]
    sum_mine[1] = value
    for k in range(1, nb):
        copy = push(
            sum_mine.at[1], sum_batch.at[k], u_send.at[k], u_recv.at[k],
            batch=lax.rem(batch + k, nb),
        )
        copy.start()
        s_copies.append(copy)
    sum_batch[0] = value
    for copy in s_copies[n - 1 :]:
        copy.wait_recv()
    value = jnp.zeros_like(value)
    for k in range(nb):
        value = value + sum_batch[lax.rem(batch - k + nb, nb)]
    sums_out[...] = value

    for i in range(group_count):

        @pl.when(core * group_count + i != me)
        def _():
            w_push(i).wait_send()

    for tp in range(max(chips - 2, 0), chips):
        sib_copy(tp).wait_send()
    for copy in w_copies + t_copies + b_copies + bt_copies + s_copies:
        copy.wait_send()
    for tp in range(chips):
        if tp < half_chips:

            @pl.when(is_gate)
            def _():
                far_copy(tp).wait_send()

            @pl.when(jnp.logical_not(is_gate))
            def _():
                gate_copy(tp).wait_send()

        else:

            @pl.when(far_chip_of(tp) != chip)
            def _():
                peer_copy(tp).wait_send()


def attend_back(
    n, nb, heads, size, fold, coef, qkv, go, keep, lse, q_full, h, wqkv, w_half, tokens,
    layer_sums, shard,
):
    _, rows, width = h.shape
    chips, half_chips = n // 2, n // 4
    paired = nb == 4
    split = 2 if paired else 1
    steps = 2 if paired else nb
    w_rows = w_half.shape[2] // split
    line_rows = width // nb
    slab = wqkv.shape[1]
    dma = pltpu.SemaphoreType.DMA
    vmem = pl.BlockSpec(memory_space=pltpu.VMEM)
    anywhere = pl.BlockSpec(memory_space=pl.ANY)
    one = (n, heads, rows, LANES)
    peers = max(half_chips - 1, 1)
    near = (line_rows // split, slab)
    landing = ((split, steps, 3, w_rows, width), (split, 3, w_rows, width))
    small_rows = (2 * (width // LANES) + 5 + 7) // 8 * 8
    result = pl.pallas_call(
        functools.partial(back_kernel, n, nb, heads, size, fold),
        out_shape=(
            jax.ShapeDtypeStruct((2, rows, width), LOW),
            jax.ShapeDtypeStruct((n // 2, shard, slab), F32),
            jax.ShapeDtypeStruct((3, shard, width), F32),
            jax.ShapeDtypeStruct((small_rows, LANES), F32),
        )
        + (() if paired else tuple(jax.ShapeDtypeStruct(shape, LOW) for shape in landing)),
        in_specs=[vmem, anywhere, vmem, anywhere, vmem]
        + [anywhere] * 5
        + [vmem],
        out_specs=[vmem] * 4 + ([] if paired else [anywhere] * 2),
        scratch_shapes=([pltpu.VMEM(shape, LOW) for shape in landing] if paired else [])
        + [
            pltpu.VMEM(qkv.shape, LOW),
            pltpu.VMEM((n, heads, LANES, rows), LOW),
            pltpu.VMEM(one, LOW),
            pltpu.VMEM((n, heads, 8, rows), F32),
            pltpu.VMEM((n, heads, LANES, rows), F32),
            pltpu.VMEM(one, F32),
            pltpu.VMEM(one, F32),
            pltpu.VMEM((heads, rows, LANES), F32),
            pltpu.VMEM((rows, width), LOW),
            pltpu.VMEM(wqkv.shape, LOW),
            pltpu.VMEM(wqkv.shape, F32),
            pltpu.VMEM((chips, rows, width), LOW),
            pltpu.VMEM((2, rows, width), LOW),
            pltpu.VMEM((chips, rows, width), LOW),
            pltpu.VMEM((peers, half_chips, rows, width), LOW),
            pltpu.VMEM((peers, rows, width), LOW),
            pltpu.VMEM((4 if paired else 3, 3, w_rows, width), LOW),
            pltpu.VMEM((split, 3, w_rows, width), LOW),
            pltpu.VMEM((n // 2, 3, shard, width), LOW),
            pltpu.VMEM((chips, 3, shard, width), LOW),
            pltpu.VMEM((nb, line_rows, slab), LOW),
            pltpu.VMEM((split, steps) + near, LOW),
            pltpu.VMEM((split,) + near, LOW),
            pltpu.VMEM((split,) + near, LOW),
            pltpu.VMEM((n, shard, slab), LOW),
            pltpu.VMEM((n, shard, slab), LOW),
            dma((3,)),
            dma((2,)),
            dma((chips,)),
            dma((chips,)),
            dma((half_chips,)),
            dma((peers, half_chips)),
            dma((chips,)),
            dma((peers,)),
            dma((half_chips,)),
            dma((1,)),
            dma((split, steps)),
            dma((split, steps)),
            dma((split,)),
            dma((split,)),
            dma((n // 2,)),
            dma((chips,)),
            dma((split, steps)),
            dma((split, steps)),
            dma((split,)),
            dma((split,)),
            dma((n,)),
            dma((n,)),
            dma((4,)),
            pltpu.VMEM((8, LANES), F32),
            pltpu.VMEM((2, small_rows, LANES), F32),
            pltpu.VMEM((n, small_rows, LANES), F32),
            pltpu.VMEM((nb, small_rows, LANES), F32),
            dma((n,)),
            dma((n,)),
            dma((nb,)),
            dma((nb,)),
        ],
        compiler_params=pltpu.CompilerParams(
            collective_id=4, has_side_effects=True, vmem_limit_bytes=63 * MIB
        ),
        name="attend_back",
    )(coef, qkv, go, keep, lse, q_full, h, wqkv, w_half, tokens, layer_sums)
    return result[:4]


def update_kernel(
    group_count, group_width, count, sums, gw, gw3, gain_ref, scale, first_s, second_s, gains, first_g,
    second_g, tok_in, gy_in, gh_in, w_in, m_in, s_in, norm_out, scale_out, first_s_out, second_s_out,
    gains_out, first_g_out, second_g_out, rms_out, grad_out, w_out, m_out, s_out,
    tok, gy, gh, w, m, v, sems,
):
    pairs = [(tok_in, tok), (gh_in, gh), (gy_in, gy), (w_in, w), (m_in, m), (s_in, v)]
    loads = [pltpu.make_async_copy(a, b, sems.at[k]) for k, (a, b) in enumerate(pairs)]
    for load in loads:
        load.start()
    width = tok.shape[2]
    tiles = width // LANES
    size = scale.shape[1]
    shard = gains.shape[1]
    gain_sums = [
        jnp.concatenate([sums[k * tiles + j : k * tiles + j + 1] for j in range(tiles)], axis=1)
        for k in range(2)
    ]
    slope = LOG_TWO_E / math.sqrt(size) / (1.0 + jnp.exp(-scale[...]))
    scale_grad = sums[2 * tiles : 2 * tiles + 1, :size] * slope

    def add_up(row):
        return jnp.sum(row, axis=1, keepdims=True)

    stats = [add_up(sums[2 * tiles + 1 + k : 2 * tiles + 2 + k]) for k in range(4)]
    for k in range(3):
        rms_out[:, k : k + 1] = jnp.sqrt(stats[k] / count)
    norm = jnp.sqrt(
        stats[3]
        + add_up(gain_sums[0] * gain_sums[0])
        + add_up(gain_sums[1] * gain_sums[1])
        + add_up(scale_grad * scale_grad)
    )
    norm_out[...] = norm
    clip = CLIP_NORM / jnp.maximum(norm, CLIP_NORM)

    def adam(outs, current, gradient, one, two, rate, decay):
        for out, value in zip(outs, adam_update(current, gradient * clip, one, two, rate, decay)):
            out[...] = value

    adam(
        (scale_out, first_s_out, second_s_out), scale[...], scale_grad, first_s[...], second_s[...],
        GAIN_RATE, 0.0,
    )
    index = lax.axis_index("batch") * lax.axis_size("seq") + lax.axis_index("seq")
    own = jnp.concatenate(gain_sums + [jnp.zeros((6, width), F32)], axis=0)
    own = pltpu.roll(own, lax.rem(width - index * shard, width), 1)[:2, :shard]
    adam(
        (gains_out, first_g_out, second_g_out), gains[...], own, first_g[...], second_g[...],
        GAIN_RATE, 0.0,
    )

    for load in loads[:3]:
        load.wait()
    for t in range(2):
        x = tok[t].astype(F32)
        factor = rms_factor(x)
        grad = gh[t].astype(F32) * gain_ref[:1]
        gy[t] = gy[t] + norm_back(grad, x * factor, factor)
    stores = [pltpu.make_async_copy(gy, grad_out, sems.at[0])]
    stores[0].start()
    for load in loads[3:]:
        load.wait()
    for k in range(6):
        if k < 3:
            span = slice(k * group_width, (k + 1) * group_width)
            gradient = jnp.concatenate([gw[g][:, span] for g in range(group_count)], axis=1)
        else:
            gradient = gw3[k - 3]
        w[k], m[k], v[k] = adam_update(w[k], gradient * clip, m[k], v[k], MATRIX_RATE, MATRIX_DECAY)
        for j, (a, b) in enumerate(((w, w_out), (m, m_out), (v, s_out))):
            copy = pltpu.make_async_copy(a.at[k], b.at[k], sems.at[6 + 3 * k + j])
            copy.start()
            stores.append(copy)
    for copy in stores:
        copy.wait()


def update(
    group_count, group_width, count, sums, gw, gw3, gain, scale, first_s, second_s, gains, first_g,
    second_g, tokens, gy, gh, weights, first_w, second_w,
):
    vmem = pl.BlockSpec(memory_space=pltpu.VMEM)
    anywhere = pl.BlockSpec(memory_space=pl.ANY)

    def like(value):
        return jax.ShapeDtypeStruct(value.shape, F32)

    kept = pltpu.VMEM(weights.shape, F32)
    return pl.pallas_call(
        functools.partial(update_kernel, group_count, group_width, count),
        out_shape=(
            jax.ShapeDtypeStruct((1, 1), F32), like(scale), like(scale), like(scale), like(gains),
            like(gains), like(gains), jax.ShapeDtypeStruct((1, 3), F32), like(gy), like(weights),
            like(weights), like(weights),
        ),
        in_specs=[vmem] * 10 + [anywhere] * 6,
        out_specs=[vmem] * 8 + [anywhere] * 4,
        scratch_shapes=[
            pltpu.VMEM(tokens.shape, LOW),
            pltpu.VMEM(gy.shape, F32),
            pltpu.VMEM(gh.shape, LOW),
            kept,
            kept,
            kept,
            pltpu.SemaphoreType.DMA((24,)),
        ],
        compiler_params=pltpu.CompilerParams(vmem_limit_bytes=62 * MIB),
        name="update",
    )(
        sums, gw, gw3, gain, scale, first_s, second_s, gains, first_g, second_g, tokens, gy, gh,
        weights, first_w, second_w,
    )


def body(
    n,
    nb,
    tokens,
    cotangent,
    weights,
    gains,
    query_scale,
    first_weights,
    second_weights,
    first_gains,
    second_gains,
    first_scale,
    second_scale,
    lengths,
):
    series_count, rows, width = tokens.shape
    size = query_scale.shape[0]
    group_count = n // 2
    heads = width // size // group_count
    group_width = heads * size
    fold = 640 // group_width
    shard = weights.shape[1]
    slab_width = (3 * group_width + 2 + LANES - 1) // LANES * LANES
    (
        normed_in, qkv, q_full, o_keep, lse, o_recv, w_all, wqkv, gain_rows, coef_row,
    ) = front(n, nb, heads, size, fold, lengths, query_scale[None], gains, tokens, weights)
    if w_all.ndim == 5:
        w_all = w_all.transpose(2, 0, 1, 3, 4).reshape(3, width, width)
    block_out, grad_middle, go_recv, layer_sums, w_half = layer(
        n, nb, fold, tokens, cotangent, o_recv, w_all, gain_rows
    )
    grad_normed, own_slab, own_three, sums = attend_back(
        n, nb, heads, size, fold, coef_row, qkv, go_recv, o_keep, lse, q_full, normed_in,
        wqkv, w_half, tokens, layer_sums, shard,
    )
    count = float(series_count * rows * width * nb * n)
    (
        grad_norm, new_scale, new_first_scale, new_second_scale, new_gains, new_first_gains,
        new_second_gains, rms_stats, input_grad, new_weights, new_first_weights, new_second_weights,
    ) = update(
        group_count, group_width, count, sums, own_slab, own_three, gain_rows, query_scale[None],
        first_scale[None], second_scale[None], gains, first_gains, second_gains, tokens, grad_middle,
        grad_normed, weights, first_weights, second_weights,
    )
    grad_norm = grad_norm.reshape(())
    new_scale, new_first_scale, new_second_scale = (
        new_scale.reshape(size), new_first_scale.reshape(size), new_second_scale.reshape(size)
    )
    rms_stats = rms_stats.reshape(3)
    return (
        block_out,
        input_grad,
        grad_norm,
        new_weights,
        new_first_weights,
        new_second_weights,
        new_gains,
        new_first_gains,
        new_second_gains,
        new_scale,
        new_first_scale,
        new_second_scale,
        rms_stats,
    )


def solution(mesh):
    return jax.shard_map(
        functools.partial(body, mesh.shape["seq"], mesh.shape["batch"]),
        mesh=mesh,
        in_specs=(
            P("batch", "seq", None),
            P("batch", "seq", None),
            P(None, ("batch", "seq"), None),
            P(None, ("batch", "seq")),
            P(),
            P(None, ("batch", "seq"), None),
            P(None, ("batch", "seq"), None),
            P(None, ("batch", "seq")),
            P(None, ("batch", "seq")),
            P(),
            P(),
            P("batch"),
        ),
        out_specs=(
            P("batch", "seq", None),
            P("batch", "seq", None),
            P(),
            P(None, ("batch", "seq"), None),
            P(None, ("batch", "seq"), None),
            P(None, ("batch", "seq"), None),
            P(None, ("batch", "seq")),
            P(None, ("batch", "seq")),
            P(None, ("batch", "seq")),
            P(),
            P(),
            P(),
            P(),
        ),
        check_vma=False,
    )
```

```python
import functools
import math

import jax
import jax.numpy as jnp
from jax import lax
from jax.experimental import pallas as pl
from jax.experimental.pallas import tpu as pltpu
from jax.sharding import PartitionSpec as P

STEP = 10

NORM_EPS = 1e-06
LOG_TWO_E = 1.442695
BETA_FIRST = 0.9
BETA_SECOND = 0.999
ADAM_EPS = 1e-08
MATRIX_RATE = 0.05
GAIN_RATE = 0.5
MATRIX_DECAY = 0.1
CLIP_NORM = 1.0
MASKED = -1e30

MESH = pl.DeviceIdType.MESH
LANES = 128
F32 = jnp.float32
LOW = jnp.bfloat16
MIB = 1024 * 1024


def rms_factor(values):
    return lax.rsqrt(jnp.mean(values * values, axis=-1, keepdims=True) + NORM_EPS)


def norm_back(grad_normed, normed, factor):
    return factor * (grad_normed - normed * jnp.mean(grad_normed * normed, axis=-1, keepdims=True))


def silu_slope(values):
    logistic = jax.nn.sigmoid(values)
    return logistic * (1.0 + values * (1.0 - logistic))


def adam_update(current, gradient, moment_one, moment_two, step_rate, decay_rate):
    new_one = BETA_FIRST * moment_one + (1.0 - BETA_FIRST) * gradient
    new_two = BETA_SECOND * moment_two + (1.0 - BETA_SECOND) * gradient * gradient
    first_hat = new_one / (1.0 - BETA_FIRST**STEP)
    second_hat = new_two / (1.0 - BETA_SECOND**STEP)
    updated = current - step_rate * (
        first_hat / (jnp.sqrt(second_hat) + ADAM_EPS) + decay_rate * current
    )
    return (updated, new_one, new_two)


def dot(left, right, left_axis=1, right_axis=0):
    return lax.dot_general(
        left, right, (((left_axis,), (right_axis,)), ((), ())), preferred_element_type=F32
    )


def greet(seq_count, batch_count):
    barrier = pltpu.get_barrier_semaphore()
    me_seq, me_batch = lax.axis_index("seq"), lax.axis_index("batch")
    for k in range(1, seq_count):
        pl.semaphore_signal(
            barrier,
            inc=1,
            device_id={"seq": lax.rem(me_seq + k, seq_count)},
            device_id_type=MESH,
        )
    for k in range(1, batch_count):
        pl.semaphore_signal(
            barrier,
            inc=1,
            device_id={"batch": lax.rem(me_batch + k, batch_count)},
            device_id_type=MESH,
        )
    pl.semaphore_wait(barrier, seq_count - 1 + batch_count - 1)


def push(source, target, send_sem, recv_sem, **where):
    return pltpu.make_async_remote_copy(
        source, target, send_sem, recv_sem, device_id=where, device_id_type=MESH
    )


def place(seq_count):
    me = lax.axis_index("seq")
    chips = seq_count // 2
    half_chips = chips // 2
    core = lax.rem(me, 2)
    chip = me // 2
    half = chip // half_chips
    base = half * half_chips
    gate_mine = half_chips - 1 + half
    gate_other = half_chips - half
    return me, core, chip, half, base, gate_mine, gate_other


def far_chip(step, half, half_chips):
    return (1 - half) * (half_chips + step) + half * (half_chips - 1 - step)


def batch_neighbours(batch):
    across = lax.rem(batch, 2)
    first = batch + 1 - 2 * across
    second = lax.rem(batch + 2, 4)
    return (first, second), lax.rem(first + 2, 4)


class Spread:
    def __init__(self, nb, block, send, recv):
        self.nb, self.block, self.send, self.recv = nb, block, send, recv
        self.batch = lax.axis_index("batch")
        self.copies = []

    def copy(self, owner, slot, j, lane, target, source=None):
        block = self.block(owner, slot)
        return push(
            block if source is None else source, block, self.send.at[j, lane],
            self.recv.at[j, lane], batch=target,
        )

    def route(self, lane):
        sides, across = batch_neighbours(self.batch)
        return sides[lane % 2], sides[1 - lane % 2], across

    def begin(self, slot, lane, source=None):
        if self.nb == 4:
            first, second, _ = self.route(lane)
            targets = [first, second]
        else:
            targets = [lax.rem(self.batch + j, self.nb) for j in range(1, self.nb)]
        new = [
            self.copy(self.batch, slot, j, lane, target, source) for j, target in enumerate(targets)
        ]
        for copy in new:
            copy.start()
        self.copies += new

    def relay(self, slot, lane):
        if self.nb == 4:
            first, second, _ = self.route(lane)
            self.copy(first, slot, 0, lane, first).wait_recv()
            copy = self.copy(first, slot, 2, lane, second)
            copy.start()
            self.copies.append(copy)
            return [first]
        return []

    def finish(self, slot, lane):
        if self.nb == 4:
            _, second, across = self.route(lane)
            self.copy(second, slot, 1, lane, second).wait_recv()
            self.copy(across, slot, 2, lane, second).wait_recv()
            return [second, across]
        owners = []
        for j in range(1, self.nb):
            owner = lax.rem(self.batch + self.nb - j, self.nb)
            self.copy(owner, slot, j - 1, lane, owner).wait_recv()
            owners.append(owner)
        return owners

    def drain(self):
        for copy in self.copies:
            copy.wait_send()


def widen(values):
    rows, width = values.shape
    return jnp.concatenate([values, jnp.zeros((rows, LANES - width), values.dtype)], axis=1)


def front_kernel(
    n, nb, heads, size, fold, chunks, joined, len_ref, scale_ref, gain_in, tok, w_in, h_out, qkv_out,
    q_out, keep_out, lse_out, o_out, w_all, wq_out, gain_out, coef_out,
    w_f, own_w, slab, x_s, h_s, zin, wq, chip_w, sib_w, qkv_s, q_s, keep_s, o_s, s_s, m_s, acc_s, sum_s,
    far_sem, own_sem, pass_sem, sib_sem, same_recv, sib_recv, z_send, z_recv, b_send, b_recv,
    h_sem, qkv_sem, q_sem, keep_sem, local_sem, o_send, o_recv, wz_send, wz_recv, wb_send, wb_recv,
    ws_send, ws_recv, wx_send, wx_recv,
):
    chips, half_chips = n // 2, n // 4
    me, core, chip, half, base, gate_mine, gate_other = place(n)
    group_count = n // 2
    batch = lax.axis_index("batch")
    sibling = 2 * chip + 1 - core
    block = tok.shape[1]
    width = tok.shape[2]
    rows = block // chunks
    group = range(heads)
    shard = own_w.shape[1]
    line = n * shard
    half_width = width // 2
    w_load = pltpu.make_async_copy(w_in, w_f, local_sem.at[8])
    w_load.start()
    greet(n, nb)
    w_load.wait()
    for m in range(3):
        own_w[m] = w_f[3 + m].astype(LOW)
    span = heads * size
    turned_gains = jnp.concatenate(
        [
            jnp.concatenate([gain_in[...], jnp.zeros((6, shard), F32)], axis=0),
            jnp.zeros((8, LANES - shard), F32),
        ],
        axis=1,
    ).T[:shard, :2]
    behind = jnp.zeros((shard, slab.shape[2] - 3 * span - 2), F32)
    for g in range(group_count):
        columns = [w_f[m, :, g * span : (g + 1) * span] for m in range(3)]
        slab[g] = jnp.concatenate(columns + [turned_gains, behind], axis=1).astype(LOW)

    sends = []
    z_copies = []
    for k in range(1, n):
        target = lax.rem(me + k, n)
        copy = push(
            slab.at[lax.rem(target, group_count)], zin.at[me], z_send.at[k], z_recv.at[k], seq=target
        )
        copy.start()
        z_copies.append(copy)
    slab_copy = pltpu.make_async_copy(
        slab.at[lax.rem(me, group_count)], zin.at[me], local_sem.at[0]
    )
    slab_copy.start()

    x_copy = None
    if joined:
        theirs = pl.ds(pl.multiple_of((1 - core) * half_width, LANES), half_width)
        ours = pl.ds(pl.multiple_of(core * half_width, LANES), half_width)
        x_copy = push(own_w.at[:, :, theirs], sib_w.at[0], wx_send, wx_recv, seq=sibling)
        x_copy.start()
        own_half = pltpu.make_async_copy(own_w.at[:, :, ours], sib_w.at[1], local_sem.at[1])
        own_half.start()

    def part(ref, lead, c):
        return ref.at[lead, pl.ds(c * rows, rows)]

    def tok_copy(source, slot, c, send_sem, recv_sem, target):
        return push(source, part(x_s, slot, c), send_sem, recv_sem.at[slot, c], seq=target)

    def send_tokens(c):
        copy = tok_copy(
            part(tok, 1 - half, c), me, c, far_sem.at[c], same_recv, 2 * gate_other + core
        )
        copy.start()
        sends.append(copy)
        for k in range(1, half_chips):
            other = base + lax.rem(chip - base + k, half_chips)
            copy = tok_copy(
                part(tok, half, c), me, c, own_sem.at[k, c], same_recv, 2 * other + core
            )
            copy.start()
            sends.append(copy)
        copy = tok_copy(part(tok, half, c), me, c, sib_sem.at[0, c], sib_recv, sibling)
        copy.start()
        sends.append(copy)

    for c in range(chunks):
        send_tokens(c)
    own_tok = pltpu.make_async_copy(tok.at[half], x_s.at[me], local_sem.at[2])
    own_tok.start()
    length = len_ref[half]
    scale = jnp.concatenate([scale_ref[...], jnp.zeros((1, LANES - size), F32)], axis=1)
    spot = lax.broadcasted_iota(jnp.int32, (1, LANES), 1)
    coef = jnp.where(
        spot < size,
        LOG_TWO_E / math.sqrt(size) * (jnp.maximum(scale, 0.0) + jnp.log1p(jnp.exp(-jnp.abs(scale)))),
        0.0,
    )
    coef_out[...] = coef

    def w_block(m, owner, p, c):
        if joined:
            start = pl.multiple_of((owner * chips + p) * 2 * shard, 16)
            return w_all.at[
                m, pl.ds(start, 2 * shard),
                pl.ds(pl.multiple_of(c * half_width, LANES), half_width),
            ]
        return w_all.at[owner, 2 * p + c, m]

    def w_source(m):
        return chip_w.at[m] if joined else own_w.at[m]

    matrices = [
        Spread(
            nb, lambda owner, p, m=m: w_block(m, owner, p, core), wb_send.at[m], wb_recv.at[m]
        )
        for m in range(3)
    ]
    w_line = []
    w_own = [
        pltpu.make_async_copy(w_source(m), w_block(m, batch, chip, core), local_sem.at[3 + m])
        for m in range(3)
    ]

    def chip_slot(k):
        return lax.rem(chip + chips - k, chips)

    def to_sibling(m, owner, k, j, source=None):
        piece = w_block(m, owner, chip_slot(k), core)
        copy = push(
            piece if source is None else source, piece, ws_send.at[m, j, k],
            ws_recv.at[m, owner, chip_slot(k)], seq=sibling,
        )
        copy.start()
        sends.append(copy)

    def w_send_line(m):
        for k in range(1, chips):
            target = 2 * lax.rem(chip + k, chips) + core
            copy = push(
                w_source(m), w_block(m, batch, chip, core), wz_send.at[m, k], wz_recv.at[m, k],
                seq=target,
            )
            copy.start()
            w_line.append(copy)
        w_own[m].start()
        matrices[m].begin(chip, 0, w_source(m))
        to_sibling(m, batch, 0, 0, w_source(m))

    def w_begin(m):
        for k in range(1, chips):
            slot = chip_slot(k)
            push(
                w_source(m), w_block(m, batch, slot, core), wz_send.at[m, k], wz_recv.at[m, k],
                seq=sibling,
            ).wait_recv()
            matrices[m].begin(slot, k)
            to_sibling(m, batch, k, 0)

    def w_relay(m):
        for k in range(chips):
            for j, owner in enumerate(matrices[m].relay(chip_slot(k), k)):
                to_sibling(m, owner, k, 1 + j)

    def w_finish(m):
        for k in range(chips):
            owners = matrices[m].finish(chip_slot(k), k)
            for j, owner in enumerate(owners):
                to_sibling(m, owner, k, nb - len(owners) + j)

    if joined:
        x_copy.wait_recv()
        own_half.wait()
        for m in range(3):
            other, mine = sib_w[0, m].astype(F32), sib_w[1, m].astype(F32)
            upper = jnp.where(core == 0, mine, other)
            lower = jnp.where(core == 0, other, mine)
            chip_w[m] = jnp.concatenate([upper, lower], axis=0).astype(LOW)
    w_send_line(0)

    slab_copy.wait()
    for copy in z_copies:
        copy.wait_recv()
    parts = [zin[k].astype(F32) for k in range(n)]
    line_start = pl.multiple_of(batch * line, 16)
    wq[pl.ds(line_start, line)] = jnp.concatenate(parts, axis=0).astype(LOW)
    pieces = 2 if nb == 4 else 1
    piece_rows = line // pieces

    def wq_block(owner, slot):
        return wq.at[pl.ds(pl.multiple_of(owner * line + slot * piece_rows, 16), piece_rows)]

    slices = Spread(nb, wq_block, b_send, b_recv)
    for k in range(pieces):
        slices.begin(k, k)

    def pass_near(c):
        for k in range(1, half_chips):
            slot = 2 * (base + lax.rem(chip - base + half_chips - k, half_chips)) + core
            tok_copy(part(x_s, slot, c), slot, c, sib_sem.at[k, c], same_recv, sibling).wait_recv()
            copy = tok_copy(part(x_s, slot, c), slot, c, sib_sem.at[k, c], sib_recv, sibling)
            copy.start()
            sends.append(copy)

    def pass_far(c):
        for k in range(half_chips):
            slot = 2 * far_chip(k, half, half_chips) + core
            lane = half_chips + k
            tok_copy(part(x_s, slot, c), slot, c, sib_sem.at[lane, c], same_recv, sibling).wait_recv()

            @pl.when(chip == gate_mine)
            def _():
                for j in range(1, half_chips):
                    other = base + lax.rem(chip - base + j, half_chips)
                    tok_copy(
                        part(x_s, slot, c), slot, c, pass_sem.at[k, j, c], same_recv,
                        2 * other + core,
                    ).start()

            copy = tok_copy(part(x_s, slot, c), slot, c, sib_sem.at[lane, c], sib_recv, sibling)
            copy.start()
            sends.append(copy)

    pass_near(0)
    pass_near(1)
    pass_far(0)
    for k in range(pieces):
        slices.relay(k, k)
    pass_near(2)
    pass_near(3)
    pass_far(1)
    w_begin(0)
    pass_far(2)
    for k in range(pieces):
        slices.finish(k, k)
    w_relay(0)
    wq_copy = pltpu.make_async_copy(wq, wq_out, local_sem.at[6])
    wq_copy.start()
    columns = 3 * heads * size
    tile = columns // LANES * LANES
    turned = wq[:, tile : tile + LANES].astype(F32).T
    gains = jnp.concatenate(
        [turned[columns - tile + k : columns - tile + k + 1] for k in range(2)], axis=0
    )
    gain_out[...] = gains
    gain = gains[:1]

    def kept(i):
        return [
            pltpu.make_async_copy(qkv_s.at[i], qkv_out.at[i], qkv_sem.at[i]),
            pltpu.make_async_copy(q_s.at[i], q_out.at[i], q_sem.at[i]),
        ]

    def h_copy(i, lane):
        return pltpu.make_async_copy(h_s.at[lane], h_out.at[i], h_sem.at[lane])

    def keep_copy(i):
        return pltpu.make_async_copy(keep_s.at[i], keep_out.at[i], keep_sem.at[i])

    def o_push(i):
        return push(o_s.at[i], o_out.at[me], o_send.at[i], o_recv.at[me], seq=i)

    own_o = pltpu.make_async_copy(o_s.at[me], o_out.at[me], local_sem.at[7])

    def project(i, lane):
        x = x_s[i].astype(F32)
        h = (x * rms_factor(x) * gain).astype(LOW)
        h_s[lane] = h
        h_copy(i, lane).start()
        out = dot(h, wq[...])
        place_in = lax.broadcasted_iota(jnp.int32, (block, LANES), 1)
        row = i * block + lax.broadcasted_iota(jnp.int32, (block, LANES), 0)
        mark = jnp.where(place_in == size, 1.0, 0.0)
        hide = jnp.where((place_in == size) & (row >= length), MASKED, 0.0)
        for a in group:
            q = widen(out[:, a * size : (a + 1) * size])
            q_s[i, a] = q
            qkv_s[i, a] = (q * coef + mark).astype(LOW)
        for a in range(heads, 2 * heads):
            qkv_s[i, a] = (widen(out[:, a * size : (a + 1) * size]) + hide).astype(LOW)
        for a in range(2 * heads, 3 * heads):
            qkv_s[i, a] = widen(out[:, a * size : (a + 1) * size].astype(LOW))
        for copy in kept(i):
            copy.start()

    own_tok.wait()

    def project_chips(first, last):
        @pl.loop(first, last)
        def _(k):
            q = half * (chips - 1 - k) + (1 - half) * k
            for lane in range(2):
                slot = 2 * q + (core if lane == 0 else 1 - core)
                if lane == 1:
                    for c in range(chunks):
                        tok_copy(
                            part(x_s, slot, c), slot, c, sib_sem.at[0, c], sib_recv, sibling
                        ).wait_recv()

                @pl.when(k > 0)
                def _():
                    h_copy(slot, lane).wait()

                project(slot, lane)

    @pl.when(chip != gate_mine)
    def _():
        project_chips(0, half_chips)

    pass_far(3)
    w_send_line(1)
    w_send_line(2)

    @pl.when(chip == gate_mine)
    def _():
        project_chips(0, half_chips)

    w_finish(0)
    project_chips(half_chips, chips)
    for lane in range(2):
        h_copy(me, lane).wait()

    def score(i, j, diagonal):
        if diagonal:
            row = lax.broadcasted_iota(jnp.int32, (block, block), 0)
            col = lax.broadcasted_iota(jnp.int32, (block, block), 1)
            visible = col <= row
        for a in group:
            s = dot(qkv_s[i, a], qkv_s[j, heads + a], 1, 1)
            if diagonal:
                s = jnp.where(visible, s, MASKED)
            s_s[a, j] = s
            best = m_s[a]
            for lane in range(block // LANES):
                best = jnp.maximum(best, s[:, lane * LANES : (lane + 1) * LANES])
            m_s[a] = best

    def mix(j):
        for a in group:
            best = m_s[a]
            count = sum_s[a]
            terms = []
            for lane in range(block // LANES):
                e = jnp.exp(s_s[a, j, :, lane * LANES : (lane + 1) * LANES] - best)
                count = count + e
                terms.append(e.astype(LOW))
            sum_s[a] = count
            acc_s[a] += dot(jnp.concatenate(terms, axis=1), qkv_s[j, 2 * heads + a])

    def query_block(t):
        i = lax.rem(me + 1 + t, n)
        m_s[...] = jnp.full_like(m_s, MASKED)
        sum_s[...] = jnp.zeros_like(sum_s)
        acc_s[...] = jnp.zeros_like(acc_s)
        pl.loop(0, i)(lambda j: score(i, j, False))
        score(i, i, True)
        for a in group:
            m_s[a] = jnp.broadcast_to(jnp.max(m_s[a], axis=1, keepdims=True), (block, LANES))
        pl.loop(0, i + 1)(mix)
        outs = []
        for a in group:
            count = jnp.sum(sum_s[a], axis=1, keepdims=True)
            out = acc_s[a] / count
            keep_s[i, a] = out
            outs.append(out[:, :size])
            lse_out[i, a] = (m_s[a] + jnp.log(count)).T[:8]
        low = jnp.concatenate(outs, axis=1).astype(LOW)
        piece = block // fold
        o_s[i] = jnp.concatenate([low[f * piece : (f + 1) * piece] for f in range(fold)], axis=1)
        keep_copy(i).start()

        @pl.when(i != me)
        def _():
            o_push(i).start()

        @pl.when(i == me)
        def _():
            own_o.start()

    bounds = [0, 2, 3, n - 3, n - 2, n] if n > 4 else [0, 1, 1, 2, 2, n]
    events = [lambda: w_begin(1), lambda: w_begin(2), lambda: w_relay(1), lambda: w_relay(2), None]
    for first, last, event in zip(bounds[:-1], bounds[1:], events):
        if last > first:
            pl.loop(first, last)(query_block)
        if event is not None:
            event()
    w_finish(1)
    w_finish(2)

    for k in range(1, n):
        source = lax.rem(me + k, n)
        push(
            o_s.at[source], o_out.at[source], o_send.at[source], o_recv.at[source], seq=source
        ).wait()
    own_o.wait()
    for m in range(3):
        for owner in range(nb):
            for q in range(chips):
                piece = w_block(m, owner, q, 1 - core)
                push(
                    piece, piece, ws_send.at[0, 0, 0], ws_recv.at[m, owner, q], seq=sibling
                ).wait_recv()
        matrices[m].drain()
        w_own[m].wait()
    slices.drain()
    if joined:
        x_copy.wait_send()
    wq_copy.wait()
    for copy in sends + z_copies + w_line:
        copy.wait_send()

    @pl.when(chip == gate_mine)
    def _():
        for c in range(chunks):
            for k in range(half_chips):
                for j in range(1, half_chips):
                    tok_copy(
                        part(x_s, me, c), me, c, pass_sem.at[k, j, c], same_recv, sibling
                    ).wait_send()

    @pl.loop(0, n)
    def _(i):
        keep_copy(i).wait()
        for copy in kept(i):
            copy.wait()


def front(n, nb, heads, size, fold, lengths, scale, gains, tokens, weights):
    chunks = 4
    _, rows, width = tokens.shape
    chips, half_chips = n // 2, n // 4
    shard = weights.shape[1]
    joined = 2 * shard % 16 == 0
    folded = (n, rows // fold, heads * size * fold)
    many, one = (n, 3 * heads, rows, LANES), (n, heads, rows, LANES)
    slab_width = (3 * heads * size + 2 + LANES - 1) // LANES * LANES
    pieces = 2 if nb == 4 else 1
    all_shape = (3, width, width) if joined else (nb, n, 3, shard, width)
    pair = (3, 2 * shard, width // 2) if joined else (3, 16, LANES)
    single = (2, 3, shard, width // 2) if joined else (2, 3, 16, LANES)
    dma = pltpu.SemaphoreType.DMA
    vmem = pl.BlockSpec(memory_space=pltpu.VMEM)
    smem = pl.BlockSpec(memory_space=pltpu.SMEM)
    anywhere = pl.BlockSpec(memory_space=pl.ANY)
    state = pltpu.VMEM((heads, rows, LANES), F32)
    return pl.pallas_call(
        functools.partial(front_kernel, n, nb, heads, size, fold, chunks, joined),
        out_shape=(
            jax.ShapeDtypeStruct((n, rows, width), LOW),
            jax.ShapeDtypeStruct(many, LOW),
            jax.ShapeDtypeStruct(one, F32),
            jax.ShapeDtypeStruct(one, F32),
            jax.ShapeDtypeStruct((n, heads, 8, rows), F32),
            jax.ShapeDtypeStruct(folded, LOW),
            jax.ShapeDtypeStruct(all_shape, LOW),
            jax.ShapeDtypeStruct((width, slab_width), LOW),
            jax.ShapeDtypeStruct((2, width), F32),
            jax.ShapeDtypeStruct((1, LANES), F32),
        ),
        in_specs=[smem, vmem, vmem, anywhere, anywhere],
        out_specs=[anywhere] * 4 + [vmem] + [anywhere] * 3 + [vmem, vmem],
        scratch_shapes=[
            pltpu.VMEM(weights.shape, F32),
            pltpu.VMEM((3, shard, width), LOW),
            pltpu.VMEM((n // 2, shard, slab_width), LOW),
            pltpu.VMEM((n, rows, width), LOW),
            pltpu.VMEM((2, rows, width), LOW),
            pltpu.VMEM((n, shard, slab_width), LOW),
            pltpu.VMEM((width, slab_width), LOW),
            pltpu.VMEM(pair, LOW),
            pltpu.VMEM(single, LOW),
            pltpu.VMEM(many, LOW),
            pltpu.VMEM(one, F32),
            pltpu.VMEM(one, F32),
            pltpu.VMEM(folded, LOW),
            pltpu.VMEM((heads, n, rows, rows), F32),
            state,
            state,
            state,
            dma((chunks,)),
            dma((half_chips, chunks)),
            dma((half_chips, half_chips, chunks)),
            dma((chips, chunks)),
            dma((n, chunks)),
            dma((n, chunks)),
            dma((n,)),
            dma((n,)),
            dma((nb, pieces)),
            dma((nb, pieces)),
            dma((2,)),
            dma((n,)),
            dma((n,)),
            dma((n,)),
            dma((9,)),
            dma((n,)),
            dma((n,)),
            dma((3, chips)),
            dma((3, chips)),
            dma((3, nb, chips)),
            dma((3, nb, chips)),
            dma((3, nb, chips)),
            dma((3, nb, chips)),
            dma,
            dma,
        ],
        compiler_params=pltpu.CompilerParams(
            collective_id=2, has_side_effects=True, vmem_limit_bytes=62 * MIB
        ),
        name="front",
    )(lengths, scale, gains, tokens, weights)


def fold_rows(values):
    rows, width = values.shape
    return jnp.sum(values.reshape(rows // 8, 8, width), axis=0)


def layer_kernel(
    n, nb, fold, tok, cot, o_in, w_in, gain_ref, y_out, gy_out, go_out, small_out, half_out,
    w, y_s, o_s, hidden_s, act_s, gu_s, ga_s, go_s, gw_s, sib_in, w_sem, send_sem, recv_sem, local_sem,
    sib_send, sib_recv,
):
    group_count = n // 2
    me, core, chip, half, base, gate_mine, gate_other = place(n)
    sibling = 2 * chip + 1 - core
    _, rows, width = tok.shape
    group_width = width // group_count
    piece = rows // fold
    barrier = pltpu.get_barrier_semaphore()
    for k in range(1, n):
        pl.semaphore_signal(
            barrier, inc=1, device_id={"seq": lax.rem(me + k, n)}, device_id_type=MESH
        )
    loads = [pltpu.make_async_copy(w_in.at[m], w.at[m], w_sem.at[m]) for m in range(3)]
    for load in loads:
        load.start()
    small_out[...] = jnp.zeros_like(small_out)
    gain = gain_ref[1:2]

    def go_push(target):
        return push(
            go_s.at[target], go_out.at[me], send_sem.at[target], recv_sem.at[me], seq=target
        )

    own_go = pltpu.make_async_copy(go_s.at[me], go_out.at[me], local_sem)

    for step in range(2):
        t = half if step else 1 - half
        parts = [
            jnp.concatenate(
                [
                    o_in[t * group_count + g, :, f * group_width : (f + 1) * group_width]
                    for g in range(group_count)
                ],
                axis=1,
            )
            for f in range(fold)
        ]
        o = jnp.concatenate(parts, axis=0)
        o_s[t] = o
        if step == 0:
            loads[0].wait()
        a = dot(o, w[0])
        small_out[1] += fold_rows(a * a)
        y1 = tok[t].astype(F32) + a
        factor = rms_factor(y1)
        normed = y1 * factor
        hidden = (normed * gain).astype(LOW)
        hidden_s[t] = hidden
        if step == 0:
            loads[1].wait()
        u = dot(hidden, w[1])
        logistic = 1.0 / (1.0 + jnp.exp(-u))
        act = (u * logistic).astype(LOW)
        act_s[t] = act
        y_s[t] = y1
        if step == 0:
            loads[2].wait()
        gz = dot(cot[t], w[2], 1, 1)
        gu = (gz * (logistic * (1.0 + u * (1.0 - logistic)))).astype(LOW)
        gu_s[t] = gu
        gh = dot(gu, w[1], 1, 1)
        small_out[0] += fold_rows(gh * normed)
        gy = cot[t].astype(F32) + norm_back(gh * gain, normed, factor)
        gy_out[t] = gy
        ga = gy.astype(LOW)
        ga_s[t] = ga
        go = dot(ga, w[0], 1, 1).astype(LOW)
        for g in range(group_count):
            block = go[:, g * group_width : (g + 1) * group_width]
            go_s[t * group_count + g] = jnp.concatenate(
                [block[f * piece : (f + 1) * piece] for f in range(fold)], axis=1
            )
        if step == 0:
            pl.semaphore_wait(barrier, n - 1)
        for g in range(group_count):
            target = t * group_count + g

            @pl.when(target != me)
            def _():
                go_push(target).start()

            @pl.when(target == me)
            def _():
                own_go.start()

    @pl.loop(0, 2)
    def _(t):
        f = dot(act_s[t], w[2])
        small_out[2] += fold_rows(f * f)
        y = y_s[t] + f
        small_out[3] += fold_rows(y * y)
        y_out[t] = y.astype(LOW)

    tile = 256
    half_rows = width // nb // 2
    sib_copies = []
    pairs = ((act_s, cot, 2), (hidden_s, gu_s, 1), (o_s, ga_s, 0))
    for left, right, m in pairs:

        @pl.loop(0, width // tile)
        def _(k):
            cols = pl.ds(pl.multiple_of(k * tile, tile), tile)
            total = dot(left[0, :, cols], right[0], 0, 0) + dot(left[1, :, cols], right[1], 0, 0)
            gw_s[m, cols] = total.astype(LOW)

        for b in range(nb):
            start = pl.multiple_of((2 * b + 1 - core) * half_rows, 16)
            copy = push(
                gw_s.at[m, pl.ds(start, half_rows)], sib_in.at[b, m], sib_send.at[b, m],
                sib_recv.at[b, m], seq=sibling,
            )
            copy.start()
            sib_copies.append(copy)
    index = 0
    for _, _, m in pairs:
        for b in range(nb):
            sib_copies[index].wait_recv()
            index += 1
            start = pl.multiple_of((2 * b + core) * half_rows, 16)
            half_out[b, m] = (
                gw_s[m, pl.ds(start, half_rows)].astype(F32) + sib_in[b, m].astype(F32)
            ).astype(LOW)
    for k in range(1, n):
        source = lax.rem(me + k, n)
        push(
            go_s.at[source], go_out.at[source], send_sem.at[source], recv_sem.at[source], seq=source
        ).wait()
    own_go.wait()
    for copy in sib_copies:
        copy.wait_send()


def layer(n, nb, fold, tokens, cotangent, o_recv, w_all, gain):
    _, rows, width = tokens.shape
    half_rows = width // nb // 2
    dma = pltpu.SemaphoreType.DMA
    vmem = pl.BlockSpec(memory_space=pltpu.VMEM)
    anywhere = pl.BlockSpec(memory_space=pl.ANY)
    kept = pltpu.VMEM((2, rows, width), LOW)
    return pl.pallas_call(
        functools.partial(layer_kernel, n, nb, fold),
        out_shape=(
            jax.ShapeDtypeStruct((2, rows, width), LOW),
            jax.ShapeDtypeStruct((2, rows, width), F32),
            jax.ShapeDtypeStruct(o_recv.shape, LOW),
            jax.ShapeDtypeStruct((4, 8, width), F32),
            jax.ShapeDtypeStruct((nb, 3, half_rows, width), LOW),
        ),
        in_specs=[vmem, vmem, vmem, anywhere, vmem],
        out_specs=[vmem, vmem, anywhere, vmem, vmem],
        scratch_shapes=[
            pltpu.VMEM((3, width, width), LOW),
            pltpu.VMEM((2, rows, width), F32),
            kept,
            kept,
            kept,
            kept,
            kept,
            pltpu.VMEM(o_recv.shape, LOW),
            pltpu.VMEM((3, width, width), LOW),
            pltpu.VMEM((nb, 3, half_rows, width), LOW),
            dma((3,)),
            dma((n,)),
            dma((n,)),
            dma,
            dma((nb, 3)),
            dma((nb, 3)),
        ],
        compiler_params=pltpu.CompilerParams(
            collective_id=3, has_side_effects=True, vmem_limit_bytes=63 * MIB
        ),
        name="layer",
    )(tokens, cotangent, o_recv, w_all, gain)


def back_kernel(
    n, nb, heads, size, fold, coef_ref, qkv_in, go_ref, keep_in, lse_ref, q_in, h_in, w_in,
    half_in, tok, sums_ref, out, own_gw, own_w, sums_out, cross_in, turn_in,
    qkv, kt, g_s, delta, gq, gk, gv, q_s, h_s, w_s, gw, gh_own, gh_out, from_sib, gate_in, peer_in,
    stage, cross_out, w_line, w_parts, gw_low, near_in, near_out, near_turn, line_out, line_in,
    load_sem, block_sem, sib_send, sib_recv, gate_send, gate_recv, peer_send, peer_recv, far_send,
    far_recv, c_send, c_recv, t_send, t_recv, w_send, w_recv, b_send, b_recv, bt_send, bt_recv,
    z_send, z_recv, stage_sem, scale_sum, sum_mine, sum_line, sum_batch, s_send, s_recv, u_send,
    u_recv,
):
    chips, half_chips = n // 2, n // 4
    me, core, chip, half, base, gate_mine, gate_other = place(n)
    group_count = n // 2
    batch = lax.axis_index("batch")
    sibling = 2 * chip + 1 - core
    block = qkv.shape[2]
    group = range(heads)
    sides, across = batch_neighbours(batch)
    is_gate = chip == gate_mine
    paired = nb == 4
    keep_load = pltpu.make_async_copy(keep_in, gk, load_sem.at[0])
    qkv_load = pltpu.make_async_copy(qkv_in, qkv, load_sem.at[1])
    w_load = pltpu.make_async_copy(w_in, w_s, load_sem.at[2])
    for load in (keep_load, qkv_load, w_load):
        load.start()
    greet(n, nb)

    w_rows = stage.shape[2]

    def w_piece(owner, h):
        return half_in.at[owner, :, pl.ds(h * w_rows, w_rows)]

    w_copies = []
    if paired:
        for h in range(2):
            for j, owner in enumerate((across, sides[h])):
                w_copies.append(
                    push(
                        w_piece(owner, h), cross_in.at[h, j], c_send.at[h, j], c_recv.at[h, j],
                        batch=sides[h],
                    )
                )
    else:
        for k in range(1, nb):
            target = lax.rem(batch + k, nb)
            w_copies.append(
                push(
                    w_piece(target, 0), cross_in.at[0, k], c_send.at[0, k], c_recv.at[0, k],
                    batch=target,
                )
            )
    for copy in w_copies:
        copy.start()

    own_terms = []
    if paired:
        for slot, (owner, h) in enumerate(((sides[1], 0), (sides[0], 1), (batch, 0), (batch, 1))):
            load = pltpu.make_async_copy(w_piece(owner, h), stage.at[slot], stage_sem.at[slot])
            own_terms.append(load)

    for load in own_terms:
        load.start()
    scale_sum[...] = jnp.zeros_like(scale_sum)
    gv[...] = jnp.zeros_like(gv)
    gq[...] = jnp.zeros_like(gq)
    keep_load.wait()

    @pl.loop(0, n)
    def _(i):
        for a in group:
            g = widen(
                jnp.concatenate(
                    [
                        go_ref[i, :, (f * heads + a) * size : (f * heads + a + 1) * size]
                        for f in range(fold)
                    ],
                    axis=0,
                )
            )
            g_s[i, a] = g
            delta[i, a] = jnp.broadcast_to(
                jnp.sum((g.astype(F32) * gk[i, a]).T, axis=0, keepdims=True), (8, block)
            )
            gk[i, a] = jnp.zeros_like(gk[i, a])

    qkv_load.wait()

    @pl.loop(0, n)
    def _(j):
        for a in group:
            kt[j, a] = qkv[j, heads + a].T

    w_load.wait()

    def pair_block(i, j, diagonal):
        if diagonal:
            col = lax.broadcasted_iota(jnp.int32, (block, block), 0)
            row = lax.broadcasted_iota(jnp.int32, (block, block), 1)
            visible = col <= row
        for a in group:
            s = dot(qkv[j, heads + a], qkv[i, a], 1, 1)
            p = jnp.exp(s - lse_ref[i, a, :1])
            if diagonal:
                p = jnp.where(visible, p, 0.0)
            dp = dot(qkv[j, 2 * heads + a], g_s[i, a], 1, 1)
            ds = (p * (dp - delta[i, a, :1])).astype(LOW)
            gk[j, a] += dot(ds, qkv[i, a])
            gv[j, a] += dot(p.astype(LOW), g_s[i, a])
            gq[i, a] += dot(kt[j, a], ds)

    def sib_copy(t):
        return push(
            gh_out.at[t % 2], from_sib.at[t], sib_send.at[t], sib_recv.at[t], seq=sibling
        )

    def step(t, u):
        r = half * t + (1 - half) * (n - 1 - t)
        loads = [
            pltpu.make_async_copy(q_in.at[r], q_s, block_sem.at[0]),
            pltpu.make_async_copy(h_in.at[r], h_s, block_sem.at[1]),
        ]
        for load in loads:
            load.start()
        pair_block(r, r, True)
        pl.loop(1, n - t)(lambda v: pair_block(r + half * v, r - (1 - half) * v, False))
        for load in loads:
            load.wait()
        pieces = []
        for a in group:
            grad = gq[r, a].T.astype(LOW).astype(F32)
            scale_sum[...] += fold_rows(grad * q_s[a])
            pieces.append((grad * coef_ref[...])[:, :size].astype(LOW))
        pieces += [gk[r, a][:, :size].astype(LOW) for a in group]
        pieces += [gv[r, a][:, :size].astype(LOW) for a in group]
        spare = w_s.shape[1] - 3 * heads * size
        pieces.append(jnp.zeros((block, spare), LOW))
        grads = jnp.concatenate(pieces, axis=1)
        gh = dot(grads, w_s[...], 1, 1).astype(LOW)
        tp = t // 2
        mine = lax.rem(r, 2) == core

        @pl.when(mine)
        def _():
            gh_own[tp] = gh

        @pl.when(jnp.logical_not(mine))
        def _():
            gh_out[tp % 2] = gh
            sib_copy(tp).start()

        part = dot(h_s[...], grads, 0, 0)
        if t == 0:
            gw[...] = part
        else:
            gw[...] += part

    def far_chip_of(tp):
        return half * tp + (1 - half) * (chips - 1 - tp)

    def gate_copy(tp):
        after = lax.rem(chip - gate_mine + half_chips, half_chips)
        return push(
            gh_own.at[tp], gate_in.at[after - 1, tp], gate_send.at[tp],
            gate_recv.at[after - 1, tp], seq=2 * gate_mine + core,
        )

    def far_copy(tp):
        return push(
            gh_own.at[tp], out.at[half], far_send.at[tp], far_recv.at[0],
            seq=2 * far_chip_of(tp) + core,
        )

    def peer_copy(tp):
        q = far_chip_of(tp)
        after = lax.rem(chip - q + half_chips, half_chips)
        return push(
            gh_own.at[tp], peer_in.at[after - 1], peer_send.at[tp], peer_recv.at[after - 1],
            seq=2 * q + core,
        )

    def relay(tp):
        @pl.when(is_gate)
        def _():
            value = gh_own[tp].astype(F32)
            for j in range(half_chips - 1):
                push(
                    gh_own.at[tp], gate_in.at[j, tp], gate_send.at[tp], gate_recv.at[j, tp],
                    seq=sibling,
                ).wait_recv()
                value = value + gate_in[j, tp].astype(F32)
            gh_own[tp] = value.astype(LOW)
            far_copy(tp).start()

    shard = own_w.shape[1]

    def staged(*sources):
        value = None
        for first in range(0, len(sources), 3):
            loads = [
                pltpu.make_async_copy(source, stage.at[j], stage_sem.at[j])
                for j, source in enumerate(sources[first : first + 3])
            ]
            for load in loads:
                load.start()
            for load in loads:
                load.wait()
            for j in range(len(loads)):
                term = stage[j].astype(F32)
                value = term if value is None else value + term
        return value

    t_copies = []

    def turn():
        if paired:
            for h in range(2):
                w_copies[2 * h].wait_recv()
                own_terms[h].wait()
                cross_out[h] = (stage[h].astype(F32) + cross_in[h, 0].astype(F32)).astype(LOW)
                copy = push(
                    cross_out.at[h], turn_in.at[h], t_send.at[h], t_recv.at[h], batch=sides[1 - h]
                )
                copy.start()
                t_copies.append(copy)

    def w_push(i):
        target = core * group_count + i
        return push(w_line.at[i], w_parts.at[chip], w_send.at[i], w_recv.at[chip], seq=target)

    def to_owners():
        for copy in w_copies[1::2] if paired else w_copies:
            copy.wait_recv()
        for copy in t_copies:
            copy.wait_recv()
        splits = 2 if paired else 1
        each = group_count // splits
        for h in range(splits):
            if paired:
                own_terms[2 + h].wait()
                value = stage[2 + h].astype(F32) + cross_in[h, 1].astype(F32) + turn_in[h].astype(F32)
            else:
                value = staged(w_piece(batch, 0), *[cross_in.at[0, k] for k in range(1, nb)])
            for i in range(each):
                w_line[h * each + i] = value[:, i * shard : (i + 1) * shard].astype(LOW)
        for i in range(group_count):
            own = core * group_count + i == me

            @pl.when(own)
            def _():
                w_parts[chip] = w_line[i]

            @pl.when(jnp.logical_not(own))
            def _():
                w_push(i).start()

    line_rows = gw.shape[0] // nb
    near_rows = near_in.shape[2]

    def near_piece(owner, h):
        return gw_low.at[owner, pl.ds(h * near_rows, near_rows)]

    b_copies = []

    def begin_slices():
        for b in range(nb):
            gw_low[b] = gw[b * line_rows : (b + 1) * line_rows].astype(LOW)
        if paired:
            for h in range(2):
                for j, owner in enumerate((across, sides[h])):
                    b_copies.append(
                        push(
                            near_piece(owner, h), near_in.at[h, j], b_send.at[h, j], b_recv.at[h, j],
                            batch=sides[h],
                        )
                    )
        else:
            for k in range(1, nb):
                target = lax.rem(batch + k, nb)
                b_copies.append(
                    push(
                        near_piece(target, 0), near_in.at[0, k], b_send.at[0, k], b_recv.at[0, k],
                        batch=target,
                    )
                )
        for copy in b_copies:
            copy.start()

    for tp in range(chips):
        if tp >= 2:
            sib_copy(tp - 2).wait_send()
        step(2 * tp, 0)
        if tp == 1:
            to_owners()
        step(2 * tp + 1, 1)
        if tp == 0:
            turn()
        if tp == chips - 1:
            begin_slices()
        sib_copy(tp).wait_recv()
        gh_own[tp] = (gh_own[tp].astype(F32) + from_sib[tp].astype(F32)).astype(LOW)
        if tp < half_chips:

            @pl.when(jnp.logical_not(is_gate))
            def _():
                gate_copy(tp).start()

        else:

            @pl.when(far_chip_of(tp) != chip)
            def _():
                peer_copy(tp).start()

        if 1 <= tp < half_chips:
            relay(tp - 1)

    relay(half_chips - 1)
    bt_copies = []
    if paired:
        for h in range(2):
            b_copies[2 * h].wait_recv()
            near_out[h] = (
                gw_low[sides[1 - h], pl.ds(h * near_rows, near_rows)].astype(F32)
                + near_in[h, 0].astype(F32)
            ).astype(LOW)
            copy = push(
                near_out.at[h], near_turn.at[h], bt_send.at[h], bt_recv.at[h], batch=sides[1 - h]
            )
            copy.start()
            bt_copies.append(copy)
    z_copies = []

    def z_copy(target):
        return push(
            line_out.at[target], line_in.at[me], z_send.at[target], z_recv.at[me], seq=target
        )

    splits = 2 if paired else 1
    each = n // splits
    for h in range(splits):
        value = gw_low[batch, pl.ds(h * near_rows, near_rows)].astype(F32)
        if paired:
            b_copies[2 * h + 1].wait_recv()
            bt_copies[h].wait_recv()
            value = value + near_in[h, 1].astype(F32) + near_turn[h].astype(F32)
        else:
            for k in range(1, nb):
                b_copies[k - 1].wait_recv()
                value = value + near_in[0, k].astype(F32)
        for i in range(each):
            target = h * each + i
            line_out[target] = value[i * shard : (i + 1) * shard].astype(LOW)

            @pl.when(target != me)
            def _():
                z_copy(target).start()

            @pl.when(target == me)
            def _():
                line_in[me] = line_out[target]

    value = gh_own[half * chip + (1 - half) * (chips - 1 - chip)].astype(F32)
    for j in range(half_chips - 1):
        push(
            gh_own.at[0], peer_in.at[j], peer_send.at[0], peer_recv.at[j], seq=sibling
        ).wait_recv()
        value = value + peer_in[j].astype(F32)
    out[half] = value.astype(LOW)
    push(gh_own.at[0], out.at[1 - half], far_send.at[0], far_recv.at[0], seq=sibling).wait_recv()

    tiles = out.shape[2] // LANES
    gain_sum = None
    for t in range(2):
        load = pltpu.make_async_copy(tok.at[t], h_s, block_sem.at[1])
        load.start()
        load.wait()
        x = h_s[...].astype(F32)
        term = fold_rows(out[t].astype(F32) * (x * rms_factor(x)))
        gain_sum = term if gain_sum is None else gain_sum + term

    def lanes(row):
        return [row[:, k * LANES : (k + 1) * LANES] for k in range(row.shape[1] // LANES)]

    def squeeze(row):
        total = None
        for piece in lanes(row):
            total = piece if total is None else total + piece
        return total

    rows_out = lanes(jnp.sum(gain_sum, axis=0, keepdims=True))
    rows_out += lanes(jnp.sum(sums_ref[0], axis=0, keepdims=True))
    rows_out.append(jnp.sum(scale_sum[...], axis=0, keepdims=True))
    for k in range(1, 4):
        rows_out.append(squeeze(jnp.sum(sums_ref[k], axis=0, keepdims=True)))

    for q in range(chips):

        @pl.when(2 * q + half != me)
        def _():
            push(w_line.at[0], w_parts.at[q], w_send.at[0], w_recv.at[q], seq=sibling).wait_recv()

    value = w_parts[0].astype(F32)
    for q in range(1, chips):
        value = value + w_parts[q].astype(F32)
    own_w[...] = value

    for k in range(1, n):
        source = lax.rem(me + k, n)
        push(
            line_out.at[source], line_in.at[source], z_send.at[source], z_recv.at[source], seq=source
        ).wait()
    for g in range(group_count):
        own_gw[g] = line_in[g].astype(F32) + line_in[g + group_count].astype(F32)

    squares = None
    for value in [own_gw[g] for g in range(group_count)] + [own_w[m] for m in range(3)]:
        term = squeeze(jnp.sum(value * value, axis=0, keepdims=True))
        squares = term if squares is None else squares + term
    rows_out.append(squares)
    sum_mine[0] = jnp.zeros_like(sum_mine[0])
    for k, row in enumerate(rows_out):
        sum_mine[0, k : k + 1, :] = row
    s_copies = []
    for k in range(1, n):
        copy = push(
            sum_mine.at[0], sum_line.at[k], s_send.at[k], s_recv.at[k], seq=lax.rem(me + k, n)
        )
        copy.start()
        s_copies.append(copy)
    sum_line[0] = sum_mine[0]
    for copy in s_copies:
        copy.wait_recv()
    value = jnp.zeros_like(sum_mine[0])
    for k in range(n):
        value = value + sum_line[lax.rem(me - k + n, n)]
    sum_mine[1] = value
    for k in range(1, nb):
        copy = push(
            sum_mine.at[1], sum_batch.at[k], u_send.at[k], u_recv.at[k],
            batch=lax.rem(batch + k, nb),
        )
        copy.start()
        s_copies.append(copy)
    sum_batch[0] = value
    for copy in s_copies[n - 1 :]:
        copy.wait_recv()
    value = jnp.zeros_like(value)
    for k in range(nb):
        value = value + sum_batch[lax.rem(batch - k + nb, nb)]
    sums_out[...] = value

    for i in range(group_count):

        @pl.when(core * group_count + i != me)
        def _():
            w_push(i).wait_send()

    for tp in range(max(chips - 2, 0), chips):
        sib_copy(tp).wait_send()
    for copy in w_copies + t_copies + b_copies + bt_copies + s_copies:
        copy.wait_send()
    for tp in range(chips):
        if tp < half_chips:

            @pl.when(is_gate)
            def _():
                far_copy(tp).wait_send()

            @pl.when(jnp.logical_not(is_gate))
            def _():
                gate_copy(tp).wait_send()

        else:

            @pl.when(far_chip_of(tp) != chip)
            def _():
                peer_copy(tp).wait_send()


def attend_back(
    n, nb, heads, size, fold, coef, qkv, go, keep, lse, q_full, h, wqkv, w_half, tokens,
    layer_sums, shard,
):
    _, rows, width = h.shape
    chips, half_chips = n // 2, n // 4
    paired = nb == 4
    split = 2 if paired else 1
    steps = 2 if paired else nb
    w_rows = w_half.shape[2] // split
    line_rows = width // nb
    slab = wqkv.shape[1]
    dma = pltpu.SemaphoreType.DMA
    vmem = pl.BlockSpec(memory_space=pltpu.VMEM)
    anywhere = pl.BlockSpec(memory_space=pl.ANY)
    one = (n, heads, rows, LANES)
    peers = max(half_chips - 1, 1)
    near = (line_rows // split, slab)
    landing = ((split, steps, 3, w_rows, width), (split, 3, w_rows, width))
    small_rows = (2 * (width // LANES) + 5 + 7) // 8 * 8
    result = pl.pallas_call(
        functools.partial(back_kernel, n, nb, heads, size, fold),
        out_shape=(
            jax.ShapeDtypeStruct((2, rows, width), LOW),
            jax.ShapeDtypeStruct((n // 2, shard, slab), F32),
            jax.ShapeDtypeStruct((3, shard, width), F32),
            jax.ShapeDtypeStruct((small_rows, LANES), F32),
        )
        + (() if paired else tuple(jax.ShapeDtypeStruct(shape, LOW) for shape in landing)),
        in_specs=[vmem, anywhere, vmem, anywhere, vmem]
        + [anywhere] * 5
        + [vmem],
        out_specs=[vmem] * 4 + ([] if paired else [anywhere] * 2),
        scratch_shapes=([pltpu.VMEM(shape, LOW) for shape in landing] if paired else [])
        + [
            pltpu.VMEM(qkv.shape, LOW),
            pltpu.VMEM((n, heads, LANES, rows), LOW),
            pltpu.VMEM(one, LOW),
            pltpu.VMEM((n, heads, 8, rows), F32),
            pltpu.VMEM((n, heads, LANES, rows), F32),
            pltpu.VMEM(one, F32),
            pltpu.VMEM(one, F32),
            pltpu.VMEM((heads, rows, LANES), F32),
            pltpu.VMEM((rows, width), LOW),
            pltpu.VMEM(wqkv.shape, LOW),
            pltpu.VMEM(wqkv.shape, F32),
            pltpu.VMEM((chips, rows, width), LOW),
            pltpu.VMEM((2, rows, width), LOW),
            pltpu.VMEM((chips, rows, width), LOW),
            pltpu.VMEM((peers, half_chips, rows, width), LOW),
            pltpu.VMEM((peers, rows, width), LOW),
            pltpu.VMEM((4 if paired else 3, 3, w_rows, width), LOW),
            pltpu.VMEM((split, 3, w_rows, width), LOW),
            pltpu.VMEM((n // 2, 3, shard, width), LOW),
            pltpu.VMEM((chips, 3, shard, width), LOW),
            pltpu.VMEM((nb, line_rows, slab), LOW),
            pltpu.VMEM((split, steps) + near, LOW),
            pltpu.VMEM((split,) + near, LOW),
            pltpu.VMEM((split,) + near, LOW),
            pltpu.VMEM((n, shard, slab), LOW),
            pltpu.VMEM((n, shard, slab), LOW),
            dma((3,)),
            dma((2,)),
            dma((chips,)),
            dma((chips,)),
            dma((half_chips,)),
            dma((peers, half_chips)),
            dma((chips,)),
            dma((peers,)),
            dma((half_chips,)),
            dma((1,)),
            dma((split, steps)),
            dma((split, steps)),
            dma((split,)),
            dma((split,)),
            dma((n // 2,)),
            dma((chips,)),
            dma((split, steps)),
            dma((split, steps)),
            dma((split,)),
            dma((split,)),
            dma((n,)),
            dma((n,)),
            dma((4,)),
            pltpu.VMEM((8, LANES), F32),
            pltpu.VMEM((2, small_rows, LANES), F32),
            pltpu.VMEM((n, small_rows, LANES), F32),
            pltpu.VMEM((nb, small_rows, LANES), F32),
            dma((n,)),
            dma((n,)),
            dma((nb,)),
            dma((nb,)),
        ],
        compiler_params=pltpu.CompilerParams(
            collective_id=4, has_side_effects=True, vmem_limit_bytes=63 * MIB
        ),
        name="attend_back",
    )(coef, qkv, go, keep, lse, q_full, h, wqkv, w_half, tokens, layer_sums)
    return result[:4]


def update_kernel(
    group_count, group_width, count, sums, gw, gw3, gain_ref, scale, first_s, second_s, gains, first_g,
    second_g, tok_in, gy_in, gh_in, w_in, m_in, s_in, norm_out, scale_out, first_s_out, second_s_out,
    gains_out, first_g_out, second_g_out, rms_out, grad_out, w_out, m_out, s_out,
    tok, gy, gh, w, m, v, sems,
):
    pairs = [(tok_in, tok), (gh_in, gh), (gy_in, gy), (w_in, w), (m_in, m), (s_in, v)]
    loads = [pltpu.make_async_copy(a, b, sems.at[k]) for k, (a, b) in enumerate(pairs)]
    for load in loads:
        load.start()
    width = tok.shape[2]
    tiles = width // LANES
    size = scale.shape[1]
    shard = gains.shape[1]
    gain_sums = [
        jnp.concatenate([sums[k * tiles + j : k * tiles + j + 1] for j in range(tiles)], axis=1)
        for k in range(2)
    ]
    slope = LOG_TWO_E / math.sqrt(size) / (1.0 + jnp.exp(-scale[...]))
    scale_grad = sums[2 * tiles : 2 * tiles + 1, :size] * slope

    def add_up(row):
        return jnp.sum(row, axis=1, keepdims=True)

    stats = [add_up(sums[2 * tiles + 1 + k : 2 * tiles + 2 + k]) for k in range(4)]
    for k in range(3):
        rms_out[:, k : k + 1] = jnp.sqrt(stats[k] / count)
    norm = jnp.sqrt(
        stats[3]
        + add_up(gain_sums[0] * gain_sums[0])
        + add_up(gain_sums[1] * gain_sums[1])
        + add_up(scale_grad * scale_grad)
    )
    norm_out[...] = norm
    clip = CLIP_NORM / jnp.maximum(norm, CLIP_NORM)

    def adam(outs, current, gradient, one, two, rate, decay):
        for out, value in zip(outs, adam_update(current, gradient * clip, one, two, rate, decay)):
            out[...] = value

    adam(
        (scale_out, first_s_out, second_s_out), scale[...], scale_grad, first_s[...], second_s[...],
        GAIN_RATE, 0.0,
    )
    index = lax.axis_index("batch") * lax.axis_size("seq") + lax.axis_index("seq")
    own = jnp.concatenate(gain_sums + [jnp.zeros((6, width), F32)], axis=0)
    own = pltpu.roll(own, lax.rem(width - index * shard, width), 1)[:2, :shard]
    adam(
        (gains_out, first_g_out, second_g_out), gains[...], own, first_g[...], second_g[...],
        GAIN_RATE, 0.0,
    )

    for load in loads[:3]:
        load.wait()
    for t in range(2):
        x = tok[t].astype(F32)
        factor = rms_factor(x)
        grad = gh[t].astype(F32) * gain_ref[:1]
        gy[t] = gy[t] + norm_back(grad, x * factor, factor)
    stores = [pltpu.make_async_copy(gy, grad_out, sems.at[0])]
    stores[0].start()
    for load in loads[3:]:
        load.wait()
    for k in range(6):
        if k < 3:
            span = slice(k * group_width, (k + 1) * group_width)
            gradient = jnp.concatenate([gw[g][:, span] for g in range(group_count)], axis=1)
        else:
            gradient = gw3[k - 3]
        w[k], m[k], v[k] = adam_update(w[k], gradient * clip, m[k], v[k], MATRIX_RATE, MATRIX_DECAY)
        for j, (a, b) in enumerate(((w, w_out), (m, m_out), (v, s_out))):
            copy = pltpu.make_async_copy(a.at[k], b.at[k], sems.at[6 + 3 * k + j])
            copy.start()
            stores.append(copy)
    for copy in stores:
        copy.wait()


def update(
    group_count, group_width, count, sums, gw, gw3, gain, scale, first_s, second_s, gains, first_g,
    second_g, tokens, gy, gh, weights, first_w, second_w,
):
    vmem = pl.BlockSpec(memory_space=pltpu.VMEM)
    anywhere = pl.BlockSpec(memory_space=pl.ANY)

    def like(value):
        return jax.ShapeDtypeStruct(value.shape, F32)

    kept = pltpu.VMEM(weights.shape, F32)
    return pl.pallas_call(
        functools.partial(update_kernel, group_count, group_width, count),
        out_shape=(
            jax.ShapeDtypeStruct((1, 1), F32), like(scale), like(scale), like(scale), like(gains),
            like(gains), like(gains), jax.ShapeDtypeStruct((1, 3), F32), like(gy), like(weights),
            like(weights), like(weights),
        ),
        in_specs=[vmem] * 10 + [anywhere] * 6,
        out_specs=[vmem] * 8 + [anywhere] * 4,
        scratch_shapes=[
            pltpu.VMEM(tokens.shape, LOW),
            pltpu.VMEM(gy.shape, F32),
            pltpu.VMEM(gh.shape, LOW),
            kept,
            kept,
            kept,
            pltpu.SemaphoreType.DMA((24,)),
        ],
        compiler_params=pltpu.CompilerParams(vmem_limit_bytes=62 * MIB),
        name="update",
    )(
        sums, gw, gw3, gain, scale, first_s, second_s, gains, first_g, second_g, tokens, gy, gh,
        weights, first_w, second_w,
    )


def body(
    n,
    nb,
    tokens,
    cotangent,
    weights,
    gains,
    query_scale,
    first_weights,
    second_weights,
    first_gains,
    second_gains,
    first_scale,
    second_scale,
    lengths,
):
    series_count, rows, width = tokens.shape
    size = query_scale.shape[0]
    group_count = n // 2
    heads = width // size // group_count
    group_width = heads * size
    fold = 640 // group_width
    shard = weights.shape[1]
    slab_width = (3 * group_width + 2 + LANES - 1) // LANES * LANES
    (
        normed_in, qkv, q_full, o_keep, lse, o_recv, w_all, wqkv, gain_rows, coef_row,
    ) = front(n, nb, heads, size, fold, lengths, query_scale[None], gains, tokens, weights)
    if w_all.ndim == 5:
        w_all = w_all.transpose(2, 0, 1, 3, 4).reshape(3, width, width)
    block_out, grad_middle, go_recv, layer_sums, w_half = layer(
        n, nb, fold, tokens, cotangent, o_recv, w_all, gain_rows
    )
    grad_normed, own_slab, own_three, sums = attend_back(
        n, nb, heads, size, fold, coef_row, qkv, go_recv, o_keep, lse, q_full, normed_in,
        wqkv, w_half, tokens, layer_sums, shard,
    )
    count = float(series_count * rows * width * nb * n)
    (
        grad_norm, new_scale, new_first_scale, new_second_scale, new_gains, new_first_gains,
        new_second_gains, rms_stats, input_grad, new_weights, new_first_weights, new_second_weights,
    ) = update(
        group_count, group_width, count, sums, own_slab, own_three, gain_rows, query_scale[None],
        first_scale[None], second_scale[None], gains, first_gains, second_gains, tokens, grad_middle,
        grad_normed, weights, first_weights, second_weights,
    )
    grad_norm = grad_norm.reshape(())
    new_scale, new_first_scale, new_second_scale = (
        new_scale.reshape(size), new_first_scale.reshape(size), new_second_scale.reshape(size)
    )
    rms_stats = rms_stats.reshape(3)
    return (
        block_out,
        input_grad,
        grad_norm,
        new_weights,
        new_first_weights,
        new_second_weights,
        new_gains,
        new_first_gains,
        new_second_gains,
        new_scale,
        new_first_scale,
        new_second_scale,
        rms_stats,
    )


def solution(mesh):
    return jax.shard_map(
        functools.partial(body, mesh.shape["seq"], mesh.shape["batch"]),
        mesh=mesh,
        in_specs=(
            P("batch", "seq", None),
            P("batch", "seq", None),
            P(None, ("batch", "seq"), None),
            P(None, ("batch", "seq")),
            P(),
            P(None, ("batch", "seq"), None),
            P(None, ("batch", "seq"), None),
            P(None, ("batch", "seq")),
            P(None, ("batch", "seq")),
            P(),
            P(),
            P("batch"),
        ),
        out_specs=(
            P("batch", "seq", None),
            P("batch", "seq", None),
            P(),
            P(None, ("batch", "seq"), None),
            P(None, ("batch", "seq"), None),
            P(None, ("batch", "seq"), None),
            P(None, ("batch", "seq")),
            P(None, ("batch", "seq")),
            P(None, ("batch", "seq")),
            P(),
            P(),
            P(),
            P(),
        ),
        check_vma=False,
    )
```

```python
import functools
import math

import jax
import jax.numpy as jnp
from jax import lax
from jax.experimental import pallas as pl
from jax.experimental.pallas import tpu as pltpu
from jax.sharding import PartitionSpec as P

STEP = 10

NORM_EPS = 1e-06
LOG_TWO_E = 1.442695
BETA_FIRST = 0.9
BETA_SECOND = 0.999
ADAM_EPS = 1e-08
MATRIX_RATE = 0.05
GAIN_RATE = 0.5
MATRIX_DECAY = 0.1
CLIP_NORM = 1.0
MASKED = -1e30

MESH = pl.DeviceIdType.MESH
LANES = 128
F32 = jnp.float32
LOW = jnp.bfloat16
MIB = 1024 * 1024


def rms_factor(values):
    return lax.rsqrt(jnp.mean(values * values, axis=-1, keepdims=True) + NORM_EPS)


def norm_back(grad_normed, normed, factor):
    return factor * (grad_normed - normed * jnp.mean(grad_normed * normed, axis=-1, keepdims=True))


def silu_slope(values):
    logistic = jax.nn.sigmoid(values)
    return logistic * (1.0 + values * (1.0 - logistic))


def adam_update(current, gradient, moment_one, moment_two, step_rate, decay_rate):
    new_one = BETA_FIRST * moment_one + (1.0 - BETA_FIRST) * gradient
    new_two = BETA_SECOND * moment_two + (1.0 - BETA_SECOND) * gradient * gradient
    first_hat = new_one / (1.0 - BETA_FIRST**STEP)
    second_hat = new_two / (1.0 - BETA_SECOND**STEP)
    updated = current - step_rate * (
        first_hat / (jnp.sqrt(second_hat) + ADAM_EPS) + decay_rate * current
    )
    return (updated, new_one, new_two)


def dot(left, right, left_axis=1, right_axis=0):
    return lax.dot_general(
        left, right, (((left_axis,), (right_axis,)), ((), ())), preferred_element_type=F32
    )


def greet(seq_count, batch_count):
    barrier = pltpu.get_barrier_semaphore()
    me_seq, me_batch = lax.axis_index("seq"), lax.axis_index("batch")
    for k in range(1, seq_count):
        pl.semaphore_signal(
            barrier,
            inc=1,
            device_id={"seq": lax.rem(me_seq + k, seq_count)},
            device_id_type=MESH,
        )
    for k in range(1, batch_count):
        pl.semaphore_signal(
            barrier,
            inc=1,
            device_id={"batch": lax.rem(me_batch + k, batch_count)},
            device_id_type=MESH,
        )
    pl.semaphore_wait(barrier, seq_count - 1 + batch_count - 1)


def push(source, target, send_sem, recv_sem, **where):
    return pltpu.make_async_remote_copy(
        source, target, send_sem, recv_sem, device_id=where, device_id_type=MESH
    )


def place(seq_count):
    me = lax.axis_index("seq")
    chips = seq_count // 2
    half_chips = chips // 2
    core = lax.rem(me, 2)
    chip = me // 2
    half = chip // half_chips
    base = half * half_chips
    gate_mine = half_chips - 1 + half
    gate_other = half_chips - half
    return me, core, chip, half, base, gate_mine, gate_other


def far_chip(step, half, half_chips):
    return (1 - half) * (half_chips + step) + half * (half_chips - 1 - step)


def batch_neighbours(batch):
    across = lax.rem(batch, 2)
    first = batch + 1 - 2 * across
    second = lax.rem(batch + 2, 4)
    return (first, second), lax.rem(first + 2, 4)


class Spread:
    def __init__(self, nb, block, send, recv):
        self.nb, self.block, self.send, self.recv = nb, block, send, recv
        self.batch = lax.axis_index("batch")
        self.copies = []

    def copy(self, owner, slot, j, lane, target, source=None):
        block = self.block(owner, slot)
        return push(
            block if source is None else source, block, self.send.at[j, lane],
            self.recv.at[j, lane], batch=target,
        )

    def route(self, lane):
        sides, across = batch_neighbours(self.batch)
        return sides[lane % 2], sides[1 - lane % 2], across

    def begin(self, slot, lane, source=None):
        if self.nb == 4:
            first, second, _ = self.route(lane)
            targets = [first, second]
        else:
            targets = [lax.rem(self.batch + j, self.nb) for j in range(1, self.nb)]
        new = [
            self.copy(self.batch, slot, j, lane, target, source) for j, target in enumerate(targets)
        ]
        for copy in new:
            copy.start()
        self.copies += new

    def relay(self, slot, lane):
        if self.nb == 4:
            first, second, _ = self.route(lane)
            self.copy(first, slot, 0, lane, first).wait_recv()
            copy = self.copy(first, slot, 2, lane, second)
            copy.start()
            self.copies.append(copy)
            return [first]
        return []

    def finish(self, slot, lane):
        if self.nb == 4:
            _, second, across = self.route(lane)
            self.copy(second, slot, 1, lane, second).wait_recv()
            self.copy(across, slot, 2, lane, second).wait_recv()
            return [second, across]
        owners = []
        for j in range(1, self.nb):
            owner = lax.rem(self.batch + self.nb - j, self.nb)
            self.copy(owner, slot, j - 1, lane, owner).wait_recv()
            owners.append(owner)
        return owners

    def drain(self):
        for copy in self.copies:
            copy.wait_send()


def widen(values):
    rows, width = values.shape
    return jnp.concatenate([values, jnp.zeros((rows, LANES - width), values.dtype)], axis=1)


def front_kernel(
    n, nb, heads, size, fold, chunks, joined, len_ref, scale_ref, gain_in, tok, w_in, h_out, qkv_out,
    q_out, keep_out, lse_out, o_out, w_all, wq_out, gain_out, coef_out,
    w_f, own_w, slab, x_s, h_s, zin, wq, chip_w, sib_w, qkv_s, q_s, keep_s, o_s, s_s, m_s, acc_s, sum_s,
    far_sem, own_sem, pass_sem, sib_sem, same_recv, sib_recv, z_send, z_recv, b_send, b_recv,
    h_sem, qkv_sem, q_sem, keep_sem, local_sem, o_send, o_recv, wz_send, wz_recv, wb_send, wb_recv,
    ws_send, ws_recv, wx_send, wx_recv,
):
    chips, half_chips = n // 2, n // 4
    me, core, chip, half, base, gate_mine, gate_other = place(n)
    group_count = n // 2
    batch = lax.axis_index("batch")
    sibling = 2 * chip + 1 - core
    block = tok.shape[1]
    width = tok.shape[2]
    rows = block // chunks
    group = range(heads)
    shard = own_w.shape[1]
    line = n * shard
    half_width = width // 2
    w_load = pltpu.make_async_copy(w_in, w_f, local_sem.at[8])
    w_load.start()
    greet(n, nb)
    w_load.wait()
    for m in range(3):
        own_w[m] = w_f[3 + m].astype(LOW)
    span = heads * size
    turned_gains = jnp.concatenate(
        [
            jnp.concatenate([gain_in[...], jnp.zeros((6, shard), F32)], axis=0),
            jnp.zeros((8, LANES - shard), F32),
        ],
        axis=1,
    ).T[:shard, :2]
    behind = jnp.zeros((shard, slab.shape[2] - 3 * span - 2), F32)
    for g in range(group_count):
        columns = [w_f[m, :, g * span : (g + 1) * span] for m in range(3)]
        slab[g] = jnp.concatenate(columns + [turned_gains, behind], axis=1).astype(LOW)

    sends = []
    z_copies = []
    for k in range(1, n):
        target = lax.rem(me + k, n)
        copy = push(
            slab.at[lax.rem(target, group_count)], zin.at[me], z_send.at[k], z_recv.at[k], seq=target
        )
        copy.start()
        z_copies.append(copy)
    slab_copy = pltpu.make_async_copy(
        slab.at[lax.rem(me, group_count)], zin.at[me], local_sem.at[0]
    )
    slab_copy.start()

    x_copy = None
    if joined:
        theirs = pl.ds(pl.multiple_of((1 - core) * half_width, LANES), half_width)
        ours = pl.ds(pl.multiple_of(core * half_width, LANES), half_width)
        x_copy = push(own_w.at[:, :, theirs], sib_w.at[0], wx_send, wx_recv, seq=sibling)
        x_copy.start()
        own_half = pltpu.make_async_copy(own_w.at[:, :, ours], sib_w.at[1], local_sem.at[1])
        own_half.start()

    def part(ref, lead, c):
        return ref.at[lead, pl.ds(c * rows, rows)]

    def tok_copy(source, slot, c, send_sem, recv_sem, target):
        return push(source, part(x_s, slot, c), send_sem, recv_sem.at[slot, c], seq=target)

    def send_tokens(c):
        copy = tok_copy(
            part(tok, 1 - half, c), me, c, far_sem.at[c], same_recv, 2 * gate_other + core
        )
        copy.start()
        sends.append(copy)
        for k in range(1, half_chips):
            other = base + lax.rem(chip - base + k, half_chips)
            copy = tok_copy(
                part(tok, half, c), me, c, own_sem.at[k, c], same_recv, 2 * other + core
            )
            copy.start()
            sends.append(copy)
        copy = tok_copy(part(tok, half, c), me, c, sib_sem.at[0, c], sib_recv, sibling)
        copy.start()
        sends.append(copy)

    for c in range(chunks):
        send_tokens(c)
    own_tok = pltpu.make_async_copy(tok.at[half], x_s.at[me], local_sem.at[2])
    own_tok.start()
    length = len_ref[half]
    scale = jnp.concatenate([scale_ref[...], jnp.zeros((1, LANES - size), F32)], axis=1)
    spot = lax.broadcasted_iota(jnp.int32, (1, LANES), 1)
    coef = jnp.where(
        spot < size,
        LOG_TWO_E / math.sqrt(size) * (jnp.maximum(scale, 0.0) + jnp.log1p(jnp.exp(-jnp.abs(scale)))),
        0.0,
    )
    coef_out[...] = coef

    def w_block(m, owner, p, c):
        if joined:
            start = pl.multiple_of((owner * chips + p) * 2 * shard, 16)
            return w_all.at[
                m, pl.ds(start, 2 * shard),
                pl.ds(pl.multiple_of(c * half_width, LANES), half_width),
            ]
        return w_all.at[owner, 2 * p + c, m]

    def w_source(m):
        return chip_w.at[m] if joined else own_w.at[m]

    matrices = [
        Spread(
            nb, lambda owner, p, m=m: w_block(m, owner, p, core), wb_send.at[m], wb_recv.at[m]
        )
        for m in range(3)
    ]
    w_line = []
    w_own = [
        pltpu.make_async_copy(w_source(m), w_block(m, batch, chip, core), local_sem.at[3 + m])
        for m in range(3)
    ]

    def chip_slot(k):
        return lax.rem(chip + chips - k, chips)

    def to_sibling(m, owner, k, j, source=None):
        piece = w_block(m, owner, chip_slot(k), core)
        copy = push(
            piece if source is None else source, piece, ws_send.at[m, j, k],
            ws_recv.at[m, owner, chip_slot(k)], seq=sibling,
        )
        copy.start()
        sends.append(copy)

    def w_send_line(m):
        for k in range(1, chips):
            target = 2 * lax.rem(chip + k, chips) + core
            copy = push(
                w_source(m), w_block(m, batch, chip, core), wz_send.at[m, k], wz_recv.at[m, k],
                seq=target,
            )
            copy.start()
            w_line.append(copy)
        w_own[m].start()
        matrices[m].begin(chip, 0, w_source(m))
        to_sibling(m, batch, 0, 0, w_source(m))

    def w_begin(m):
        for k in range(1, chips):
            slot = chip_slot(k)
            push(
                w_source(m), w_block(m, batch, slot, core), wz_send.at[m, k], wz_recv.at[m, k],
                seq=sibling,
            ).wait_recv()
            matrices[m].begin(slot, k)
            to_sibling(m, batch, k, 0)

    def w_relay(m):
        for k in range(chips):
            for j, owner in enumerate(matrices[m].relay(chip_slot(k), k)):
                to_sibling(m, owner, k, 1 + j)

    def w_finish(m):
        for k in range(chips):
            owners = matrices[m].finish(chip_slot(k), k)
            for j, owner in enumerate(owners):
                to_sibling(m, owner, k, nb - len(owners) + j)

    if joined:
        x_copy.wait_recv()
        own_half.wait()
        for m in range(3):
            other, mine = sib_w[0, m].astype(F32), sib_w[1, m].astype(F32)
            upper = jnp.where(core == 0, mine, other)
            lower = jnp.where(core == 0, other, mine)
            chip_w[m] = jnp.concatenate([upper, lower], axis=0).astype(LOW)
    w_send_line(0)

    slab_copy.wait()
    for copy in z_copies:
        copy.wait_recv()
    parts = [zin[k].astype(F32) for k in range(n)]
    line_start = pl.multiple_of(batch * line, 16)
    wq[pl.ds(line_start, line)] = jnp.concatenate(parts, axis=0).astype(LOW)
    pieces = 2 if nb == 4 else 1
    piece_rows = line // pieces

    def wq_block(owner, slot):
        return wq.at[pl.ds(pl.multiple_of(owner * line + slot * piece_rows, 16), piece_rows)]

    slices = Spread(nb, wq_block, b_send, b_recv)
    for k in range(pieces):
        slices.begin(k, k)

    def pass_near(c):
        for k in range(1, half_chips):
            slot = 2 * (base + lax.rem(chip - base + half_chips - k, half_chips)) + core
            tok_copy(part(x_s, slot, c), slot, c, sib_sem.at[k, c], same_recv, sibling).wait_recv()
            copy = tok_copy(part(x_s, slot, c), slot, c, sib_sem.at[k, c], sib_recv, sibling)
            copy.start()
            sends.append(copy)

    def pass_far(c):
        for k in range(half_chips):
            slot = 2 * far_chip(k, half, half_chips) + core
            lane = half_chips + k
            tok_copy(part(x_s, slot, c), slot, c, sib_sem.at[lane, c], same_recv, sibling).wait_recv()

            @pl.when(chip == gate_mine)
            def _():
                for j in range(1, half_chips):
                    other = base + lax.rem(chip - base + j, half_chips)
                    tok_copy(
                        part(x_s, slot, c), slot, c, pass_sem.at[k, j, c], same_recv,
                        2 * other + core,
                    ).start()

            copy = tok_copy(part(x_s, slot, c), slot, c, sib_sem.at[lane, c], sib_recv, sibling)
            copy.start()
            sends.append(copy)

    pass_near(0)
    pass_near(1)
    pass_far(0)
    for k in range(pieces):
        slices.relay(k, k)
    pass_near(2)
    pass_near(3)
    pass_far(1)
    w_begin(0)
    pass_far(2)
    for k in range(pieces):
        slices.finish(k, k)
    w_relay(0)
    wq_copy = pltpu.make_async_copy(wq, wq_out, local_sem.at[6])
    wq_copy.start()
    columns = 3 * heads * size
    tile = columns // LANES * LANES
    turned = wq[:, tile : tile + LANES].astype(F32).T
    gains = jnp.concatenate(
        [turned[columns - tile + k : columns - tile + k + 1] for k in range(2)], axis=0
    )
    gain_out[...] = gains
    gain = gains[:1]

    def kept(i):
        return [
            pltpu.make_async_copy(qkv_s.at[i], qkv_out.at[i], qkv_sem.at[i]),
            pltpu.make_async_copy(q_s.at[i], q_out.at[i], q_sem.at[i]),
        ]

    def h_copy(i, lane):
        return pltpu.make_async_copy(h_s.at[lane], h_out.at[i], h_sem.at[lane])

    def keep_copy(i):
        return pltpu.make_async_copy(keep_s.at[i], keep_out.at[i], keep_sem.at[i])

    def o_push(i):
        return push(o_s.at[i], o_out.at[me], o_send.at[i], o_recv.at[me], seq=i)

    own_o = pltpu.make_async_copy(o_s.at[me], o_out.at[me], local_sem.at[7])

    def project(i, lane):
        x = x_s[i].astype(F32)
        h = (x * rms_factor(x) * gain).astype(LOW)
        h_s[lane] = h
        h_copy(i, lane).start()
        out = dot(h, wq[...])
        place_in = lax.broadcasted_iota(jnp.int32, (block, LANES), 1)
        row = i * block + lax.broadcasted_iota(jnp.int32, (block, LANES), 0)
        mark = jnp.where(place_in == size, 1.0, 0.0)
        hide = jnp.where((place_in == size) & (row >= length), MASKED, 0.0)
        for a in group:
            q = widen(out[:, a * size : (a + 1) * size])
            q_s[i, a] = q
            qkv_s[i, a] = (q * coef + mark).astype(LOW)
        for a in range(heads, 2 * heads):
            qkv_s[i, a] = (widen(out[:, a * size : (a + 1) * size]) + hide).astype(LOW)
        for a in range(2 * heads, 3 * heads):
            qkv_s[i, a] = widen(out[:, a * size : (a + 1) * size].astype(LOW))
        for copy in kept(i):
            copy.start()

    own_tok.wait()

    def project_chips(first, last):
        @pl.loop(first, last)
        def _(k):
            q = half * (chips - 1 - k) + (1 - half) * k
            for lane in range(2):
                slot = 2 * q + (core if lane == 0 else 1 - core)
                if lane == 1:
                    for c in range(chunks):
                        tok_copy(
                            part(x_s, slot, c), slot, c, sib_sem.at[0, c], sib_recv, sibling
                        ).wait_recv()

                @pl.when(k > 0)
                def _():
                    h_copy(slot, lane).wait()

                project(slot, lane)

    @pl.when(chip != gate_mine)
    def _():
        project_chips(0, half_chips)

    pass_far(3)
    w_send_line(1)
    w_send_line(2)

    @pl.when(chip == gate_mine)
    def _():
        project_chips(0, half_chips)

    w_finish(0)
    project_chips(half_chips, chips)
    for lane in range(2):
        h_copy(me, lane).wait()

    def score(i, j, diagonal):
        if diagonal:
            row = lax.broadcasted_iota(jnp.int32, (block, block), 0)
            col = lax.broadcasted_iota(jnp.int32, (block, block), 1)
            visible = col <= row
        for a in group:
            s = dot(qkv_s[i, a], qkv_s[j, heads + a], 1, 1)
            if diagonal:
                s = jnp.where(visible, s, MASKED)
            s_s[a, j] = s
            best = m_s[a]
            for lane in range(block // LANES):
                best = jnp.maximum(best, s[:, lane * LANES : (lane + 1) * LANES])
            m_s[a] = best

    def mix(j):
        for a in group:
            best = m_s[a]
            count = sum_s[a]
            terms = []
            for lane in range(block // LANES):
                e = jnp.exp(s_s[a, j, :, lane * LANES : (lane + 1) * LANES] - best)
                count = count + e
                terms.append(e.astype(LOW))
            sum_s[a] = count
            acc_s[a] += dot(jnp.concatenate(terms, axis=1), qkv_s[j, 2 * heads + a])

    def query_block(t):
        i = lax.rem(me + 1 + t, n)
        m_s[...] = jnp.full_like(m_s, MASKED)
        sum_s[...] = jnp.zeros_like(sum_s)
        acc_s[...] = jnp.zeros_like(acc_s)
        pl.loop(0, i)(lambda j: score(i, j, False))
        score(i, i, True)
        for a in group:
            m_s[a] = jnp.broadcast_to(jnp.max(m_s[a], axis=1, keepdims=True), (block, LANES))
        pl.loop(0, i + 1)(mix)
        outs = []
        for a in group:
            count = jnp.sum(sum_s[a], axis=1, keepdims=True)
            out = acc_s[a] / count
            keep_s[i, a] = out
            outs.append(out[:, :size])
            lse_out[i, a] = (m_s[a] + jnp.log(count)).T[:8]
        low = jnp.concatenate(outs, axis=1).astype(LOW)
        piece = block // fold
        o_s[i] = jnp.concatenate([low[f * piece : (f + 1) * piece] for f in range(fold)], axis=1)
        keep_copy(i).start()

        @pl.when(i != me)
        def _():
            o_push(i).start()

        @pl.when(i == me)
        def _():
            own_o.start()

    bounds = [0, 3, 4, n - 2, n - 1, n] if n > 4 else [0, 1, 1, 2, 2, n]
    events = [lambda: w_begin(1), lambda: w_begin(2), lambda: w_relay(1), lambda: w_relay(2), None]
    for first, last, event in zip(bounds[:-1], bounds[1:], events):
        if last > first:
            pl.loop(first, last)(query_block)
        if event is not None:
            event()
    w_finish(1)
    w_finish(2)

    for k in range(1, n):
        source = lax.rem(me + k, n)
        push(
            o_s.at[source], o_out.at[source], o_send.at[source], o_recv.at[source], seq=source
        ).wait()
    own_o.wait()
    for m in range(3):
        for owner in range(nb):
            for q in range(chips):
                piece = w_block(m, owner, q, 1 - core)
                push(
                    piece, piece, ws_send.at[0, 0, 0], ws_recv.at[m, owner, q], seq=sibling
                ).wait_recv()
        matrices[m].drain()
        w_own[m].wait()
    slices.drain()
    if joined:
        x_copy.wait_send()
    wq_copy.wait()
    for copy in sends + z_copies + w_line:
        copy.wait_send()

    @pl.when(chip == gate_mine)
    def _():
        for c in range(chunks):
            for k in range(half_chips):
                for j in range(1, half_chips):
                    tok_copy(
                        part(x_s, me, c), me, c, pass_sem.at[k, j, c], same_recv, sibling
                    ).wait_send()

    @pl.loop(0, n)
    def _(i):
        keep_copy(i).wait()
        for copy in kept(i):
            copy.wait()


def front(n, nb, heads, size, fold, lengths, scale, gains, tokens, weights):
    chunks = 4
    _, rows, width = tokens.shape
    chips, half_chips = n // 2, n // 4
    shard = weights.shape[1]
    joined = 2 * shard % 16 == 0
    folded = (n, rows // fold, heads * size * fold)
    many, one = (n, 3 * heads, rows, LANES), (n, heads, rows, LANES)
    slab_width = (3 * heads * size + 2 + LANES - 1) // LANES * LANES
    pieces = 2 if nb == 4 else 1
    all_shape = (3, width, width) if joined else (nb, n, 3, shard, width)
    pair = (3, 2 * shard, width // 2) if joined else (3, 16, LANES)
    single = (2, 3, shard, width // 2) if joined else (2, 3, 16, LANES)
    dma = pltpu.SemaphoreType.DMA
    vmem = pl.BlockSpec(memory_space=pltpu.VMEM)
    smem = pl.BlockSpec(memory_space=pltpu.SMEM)
    anywhere = pl.BlockSpec(memory_space=pl.ANY)
    state = pltpu.VMEM((heads, rows, LANES), F32)
    return pl.pallas_call(
        functools.partial(front_kernel, n, nb, heads, size, fold, chunks, joined),
        out_shape=(
            jax.ShapeDtypeStruct((n, rows, width), LOW),
            jax.ShapeDtypeStruct(many, LOW),
            jax.ShapeDtypeStruct(one, F32),
            jax.ShapeDtypeStruct(one, F32),
            jax.ShapeDtypeStruct((n, heads, 8, rows), F32),
            jax.ShapeDtypeStruct(folded, LOW),
            jax.ShapeDtypeStruct(all_shape, LOW),
            jax.ShapeDtypeStruct((width, slab_width), LOW),
            jax.ShapeDtypeStruct((2, width), F32),
            jax.ShapeDtypeStruct((1, LANES), F32),
        ),
        in_specs=[smem, vmem, vmem, anywhere, anywhere],
        out_specs=[anywhere] * 4 + [vmem] + [anywhere] * 3 + [vmem, vmem],
        scratch_shapes=[
            pltpu.VMEM(weights.shape, F32),
            pltpu.VMEM((3, shard, width), LOW),
            pltpu.VMEM((n // 2, shard, slab_width), LOW),
            pltpu.VMEM((n, rows, width), LOW),
            pltpu.VMEM((2, rows, width), LOW),
            pltpu.VMEM((n, shard, slab_width), LOW),
            pltpu.VMEM((width, slab_width), LOW),
            pltpu.VMEM(pair, LOW),
            pltpu.VMEM(single, LOW),
            pltpu.VMEM(many, LOW),
            pltpu.VMEM(one, F32),
            pltpu.VMEM(one, F32),
            pltpu.VMEM(folded, LOW),
            pltpu.VMEM((heads, n, rows, rows), F32),
            state,
            state,
            state,
            dma((chunks,)),
            dma((half_chips, chunks)),
            dma((half_chips, half_chips, chunks)),
            dma((chips, chunks)),
            dma((n, chunks)),
            dma((n, chunks)),
            dma((n,)),
            dma((n,)),
            dma((nb, pieces)),
            dma((nb, pieces)),
            dma((2,)),
            dma((n,)),
            dma((n,)),
            dma((n,)),
            dma((9,)),
            dma((n,)),
            dma((n,)),
            dma((3, chips)),
            dma((3, chips)),
            dma((3, nb, chips)),
            dma((3, nb, chips)),
            dma((3, nb, chips)),
            dma((3, nb, chips)),
            dma,
            dma,
        ],
        compiler_params=pltpu.CompilerParams(
            collective_id=2, has_side_effects=True, vmem_limit_bytes=62 * MIB
        ),
        name="front",
    )(lengths, scale, gains, tokens, weights)


def fold_rows(values):
    rows, width = values.shape
    return jnp.sum(values.reshape(rows // 8, 8, width), axis=0)


def layer_kernel(
    n, nb, fold, tok, cot, o_in, w_in, gain_ref, y_out, gy_out, go_out, small_out, half_out,
    w, y_s, o_s, hidden_s, act_s, gu_s, ga_s, go_s, gw_s, sib_in, w_sem, send_sem, recv_sem, local_sem,
    sib_send, sib_recv,
):
    group_count = n // 2
    me, core, chip, half, base, gate_mine, gate_other = place(n)
    sibling = 2 * chip + 1 - core
    _, rows, width = tok.shape
    group_width = width // group_count
    piece = rows // fold
    barrier = pltpu.get_barrier_semaphore()
    for k in range(1, n):
        pl.semaphore_signal(
            barrier, inc=1, device_id={"seq": lax.rem(me + k, n)}, device_id_type=MESH
        )
    loads = [pltpu.make_async_copy(w_in.at[m], w.at[m], w_sem.at[m]) for m in range(3)]
    for load in loads:
        load.start()
    small_out[...] = jnp.zeros_like(small_out)
    gain = gain_ref[1:2]

    def go_push(target):
        return push(
            go_s.at[target], go_out.at[me], send_sem.at[target], recv_sem.at[me], seq=target
        )

    own_go = pltpu.make_async_copy(go_s.at[me], go_out.at[me], local_sem)

    for step in range(2):
        t = half if step else 1 - half
        parts = [
            jnp.concatenate(
                [
                    o_in[t * group_count + g, :, f * group_width : (f + 1) * group_width]
                    for g in range(group_count)
                ],
                axis=1,
            )
            for f in range(fold)
        ]
        o = jnp.concatenate(parts, axis=0)
        o_s[t] = o
        if step == 0:
            loads[0].wait()
        a = dot(o, w[0])
        small_out[1] += fold_rows(a * a)
        y1 = tok[t].astype(F32) + a
        factor = rms_factor(y1)
        normed = y1 * factor
        hidden = (normed * gain).astype(LOW)
        hidden_s[t] = hidden
        if step == 0:
            loads[1].wait()
        u = dot(hidden, w[1])
        logistic = 1.0 / (1.0 + jnp.exp(-u))
        act = (u * logistic).astype(LOW)
        act_s[t] = act
        y_s[t] = y1
        if step == 0:
            loads[2].wait()
        gz = dot(cot[t], w[2], 1, 1)
        gu = (gz * (logistic * (1.0 + u * (1.0 - logistic)))).astype(LOW)
        gu_s[t] = gu
        gh = dot(gu, w[1], 1, 1)
        small_out[0] += fold_rows(gh * normed)
        gy = cot[t].astype(F32) + norm_back(gh * gain, normed, factor)
        gy_out[t] = gy
        ga = gy.astype(LOW)
        ga_s[t] = ga
        go = dot(ga, w[0], 1, 1).astype(LOW)
        for g in range(group_count):
            block = go[:, g * group_width : (g + 1) * group_width]
            go_s[t * group_count + g] = jnp.concatenate(
                [block[f * piece : (f + 1) * piece] for f in range(fold)], axis=1
            )
        if step == 0:
            pl.semaphore_wait(barrier, n - 1)
        for g in range(group_count):
            target = t * group_count + g

            @pl.when(target != me)
            def _():
                go_push(target).start()

            @pl.when(target == me)
            def _():
                own_go.start()

    @pl.loop(0, 2)
    def _(t):
        f = dot(act_s[t], w[2])
        small_out[2] += fold_rows(f * f)
        y = y_s[t] + f
        small_out[3] += fold_rows(y * y)
        y_out[t] = y.astype(LOW)

    tile = 256
    half_rows = width // nb // 2
    sib_copies = []
    pairs = ((act_s, cot, 2), (hidden_s, gu_s, 1), (o_s, ga_s, 0))
    for left, right, m in pairs:

        @pl.loop(0, width // tile)
        def _(k):
            cols = pl.ds(pl.multiple_of(k * tile, tile), tile)
            total = dot(left[0, :, cols], right[0], 0, 0) + dot(left[1, :, cols], right[1], 0, 0)
            gw_s[m, cols] = total.astype(LOW)

        for b in range(nb):
            start = pl.multiple_of((2 * b + 1 - core) * half_rows, 16)
            copy = push(
                gw_s.at[m, pl.ds(start, half_rows)], sib_in.at[b, m], sib_send.at[b, m],
                sib_recv.at[b, m], seq=sibling,
            )
            copy.start()
            sib_copies.append(copy)
    index = 0
    for _, _, m in pairs:
        for b in range(nb):
            sib_copies[index].wait_recv()
            index += 1
            start = pl.multiple_of((2 * b + core) * half_rows, 16)
            half_out[b, m] = (
                gw_s[m, pl.ds(start, half_rows)].astype(F32) + sib_in[b, m].astype(F32)
            ).astype(LOW)
    for k in range(1, n):
        source = lax.rem(me + k, n)
        push(
            go_s.at[source], go_out.at[source], send_sem.at[source], recv_sem.at[source], seq=source
        ).wait()
    own_go.wait()
    for copy in sib_copies:
        copy.wait_send()


def layer(n, nb, fold, tokens, cotangent, o_recv, w_all, gain):
    _, rows, width = tokens.shape
    half_rows = width // nb // 2
    dma = pltpu.SemaphoreType.DMA
    vmem = pl.BlockSpec(memory_space=pltpu.VMEM)
    anywhere = pl.BlockSpec(memory_space=pl.ANY)
    kept = pltpu.VMEM((2, rows, width), LOW)
    return pl.pallas_call(
        functools.partial(layer_kernel, n, nb, fold),
        out_shape=(
            jax.ShapeDtypeStruct((2, rows, width), LOW),
            jax.ShapeDtypeStruct((2, rows, width), F32),
            jax.ShapeDtypeStruct(o_recv.shape, LOW),
            jax.ShapeDtypeStruct((4, 8, width), F32),
            jax.ShapeDtypeStruct((nb, 3, half_rows, width), LOW),
        ),
        in_specs=[vmem, vmem, vmem, anywhere, vmem],
        out_specs=[vmem, vmem, anywhere, vmem, vmem],
        scratch_shapes=[
            pltpu.VMEM((3, width, width), LOW),
            pltpu.VMEM((2, rows, width), F32),
            kept,
            kept,
            kept,
            kept,
            kept,
            pltpu.VMEM(o_recv.shape, LOW),
            pltpu.VMEM((3, width, width), LOW),
            pltpu.VMEM((nb, 3, half_rows, width), LOW),
            dma((3,)),
            dma((n,)),
            dma((n,)),
            dma,
            dma((nb, 3)),
            dma((nb, 3)),
        ],
        compiler_params=pltpu.CompilerParams(
            collective_id=3, has_side_effects=True, vmem_limit_bytes=63 * MIB
        ),
        name="layer",
    )(tokens, cotangent, o_recv, w_all, gain)


def back_kernel(
    n, nb, heads, size, fold, coef_ref, qkv_in, go_ref, keep_in, lse_ref, q_in, h_in, w_in,
    half_in, tok, sums_ref, out, own_gw, own_w, sums_out, cross_in, turn_in,
    qkv, kt, g_s, delta, gq, gk, gv, q_s, h_s, w_s, gw, gh_own, gh_out, from_sib, gate_in, peer_in,
    stage, cross_out, w_line, w_parts, gw_low, near_in, near_out, near_turn, line_out, line_in,
    load_sem, block_sem, sib_send, sib_recv, gate_send, gate_recv, peer_send, peer_recv, far_send,
    far_recv, c_send, c_recv, t_send, t_recv, w_send, w_recv, b_send, b_recv, bt_send, bt_recv,
    z_send, z_recv, stage_sem, scale_sum, sum_mine, sum_line, sum_batch, s_send, s_recv, u_send,
    u_recv,
):
    chips, half_chips = n // 2, n // 4
    me, core, chip, half, base, gate_mine, gate_other = place(n)
    group_count = n // 2
    batch = lax.axis_index("batch")
    sibling = 2 * chip + 1 - core
    block = qkv.shape[2]
    group = range(heads)
    sides, across = batch_neighbours(batch)
    is_gate = chip == gate_mine
    paired = nb == 4
    keep_load = pltpu.make_async_copy(keep_in, gk, load_sem.at[0])
    qkv_load = pltpu.make_async_copy(qkv_in, qkv, load_sem.at[1])
    w_load = pltpu.make_async_copy(w_in, w_s, load_sem.at[2])
    for load in (keep_load, qkv_load, w_load):
        load.start()
    greet(n, nb)

    w_rows = stage.shape[2]

    def w_piece(owner, h):
        return half_in.at[owner, :, pl.ds(h * w_rows, w_rows)]

    w_copies = []
    if paired:
        for h in range(2):
            for j, owner in enumerate((across, sides[h])):
                w_copies.append(
                    push(
                        w_piece(owner, h), cross_in.at[h, j], c_send.at[h, j], c_recv.at[h, j],
                        batch=sides[h],
                    )
                )
    else:
        for k in range(1, nb):
            target = lax.rem(batch + k, nb)
            w_copies.append(
                push(
                    w_piece(target, 0), cross_in.at[0, k], c_send.at[0, k], c_recv.at[0, k],
                    batch=target,
                )
            )
    for copy in w_copies:
        copy.start()

    own_terms = []
    if paired:
        for slot, (owner, h) in enumerate(((sides[1], 0), (sides[0], 1), (batch, 0), (batch, 1))):
            load = pltpu.make_async_copy(w_piece(owner, h), stage.at[slot], stage_sem.at[slot])
            own_terms.append(load)

    for load in own_terms:
        load.start()
    scale_sum[...] = jnp.zeros_like(scale_sum)
    gv[...] = jnp.zeros_like(gv)
    gq[...] = jnp.zeros_like(gq)
    keep_load.wait()

    @pl.loop(0, n)
    def _(i):
        for a in group:
            g = widen(
                jnp.concatenate(
                    [
                        go_ref[i, :, (f * heads + a) * size : (f * heads + a + 1) * size]
                        for f in range(fold)
                    ],
                    axis=0,
                )
            )
            g_s[i, a] = g
            delta[i, a] = jnp.broadcast_to(
                jnp.sum((g.astype(F32) * gk[i, a]).T, axis=0, keepdims=True), (8, block)
            )
            gk[i, a] = jnp.zeros_like(gk[i, a])

    qkv_load.wait()

    @pl.loop(0, n)
    def _(j):
        for a in group:
            kt[j, a] = qkv[j, heads + a].T

    w_load.wait()

    def pair_block(i, j, diagonal):
        if diagonal:
            col = lax.broadcasted_iota(jnp.int32, (block, block), 0)
            row = lax.broadcasted_iota(jnp.int32, (block, block), 1)
            visible = col <= row
        for a in group:
            s = dot(qkv[j, heads + a], qkv[i, a], 1, 1)
            p = jnp.exp(s - lse_ref[i, a, :1])
            if diagonal:
                p = jnp.where(visible, p, 0.0)
            dp = dot(qkv[j, 2 * heads + a], g_s[i, a], 1, 1)
            ds = (p * (dp - delta[i, a, :1])).astype(LOW)
            gk[j, a] += dot(ds, qkv[i, a])
            gv[j, a] += dot(p.astype(LOW), g_s[i, a])
            gq[i, a] += dot(kt[j, a], ds)

    def sib_copy(t):
        return push(
            gh_out.at[t % 2], from_sib.at[t], sib_send.at[t], sib_recv.at[t], seq=sibling
        )

    def step(t, u):
        r = half * t + (1 - half) * (n - 1 - t)
        loads = [
            pltpu.make_async_copy(q_in.at[r], q_s, block_sem.at[0]),
            pltpu.make_async_copy(h_in.at[r], h_s, block_sem.at[1]),
        ]
        for load in loads:
            load.start()
        pair_block(r, r, True)
        pl.loop(1, n - t)(lambda v: pair_block(r + half * v, r - (1 - half) * v, False))
        for load in loads:
            load.wait()
        pieces = []
        for a in group:
            grad = gq[r, a].T.astype(LOW).astype(F32)
            scale_sum[...] += fold_rows(grad * q_s[a])
            pieces.append((grad * coef_ref[...])[:, :size].astype(LOW))
        pieces += [gk[r, a][:, :size].astype(LOW) for a in group]
        pieces += [gv[r, a][:, :size].astype(LOW) for a in group]
        spare = w_s.shape[1] - 3 * heads * size
        pieces.append(jnp.zeros((block, spare), LOW))
        grads = jnp.concatenate(pieces, axis=1)
        gh = dot(grads, w_s[...], 1, 1).astype(LOW)
        tp = t // 2
        mine = lax.rem(r, 2) == core

        @pl.when(mine)
        def _():
            gh_own[tp] = gh

        @pl.when(jnp.logical_not(mine))
        def _():
            gh_out[tp % 2] = gh
            sib_copy(tp).start()

        part = dot(h_s[...], grads, 0, 0)
        if t == 0:
            gw[...] = part
        else:
            gw[...] += part

    def far_chip_of(tp):
        return half * tp + (1 - half) * (chips - 1 - tp)

    def gate_copy(tp):
        after = lax.rem(chip - gate_mine + half_chips, half_chips)
        return push(
            gh_own.at[tp], gate_in.at[after - 1, tp], gate_send.at[tp],
            gate_recv.at[after - 1, tp], seq=2 * gate_mine + core,
        )

    def far_copy(tp):
        return push(
            gh_own.at[tp], out.at[half], far_send.at[tp], far_recv.at[0],
            seq=2 * far_chip_of(tp) + core,
        )

    def peer_copy(tp):
        q = far_chip_of(tp)
        after = lax.rem(chip - q + half_chips, half_chips)
        return push(
            gh_own.at[tp], peer_in.at[after - 1], peer_send.at[tp], peer_recv.at[after - 1],
            seq=2 * q + core,
        )

    def relay(tp):
        @pl.when(is_gate)
        def _():
            value = gh_own[tp].astype(F32)
            for j in range(half_chips - 1):
                push(
                    gh_own.at[tp], gate_in.at[j, tp], gate_send.at[tp], gate_recv.at[j, tp],
                    seq=sibling,
                ).wait_recv()
                value = value + gate_in[j, tp].astype(F32)
            gh_own[tp] = value.astype(LOW)
            far_copy(tp).start()

    shard = own_w.shape[1]

    def staged(*sources):
        value = None
        for first in range(0, len(sources), 3):
            loads = [
                pltpu.make_async_copy(source, stage.at[j], stage_sem.at[j])
                for j, source in enumerate(sources[first : first + 3])
            ]
            for load in loads:
                load.start()
            for load in loads:
                load.wait()
            for j in range(len(loads)):
                term = stage[j].astype(F32)
                value = term if value is None else value + term
        return value

    t_copies = []

    def turn():
        if paired:
            for h in range(2):
                w_copies[2 * h].wait_recv()
                own_terms[h].wait()
                cross_out[h] = (stage[h].astype(F32) + cross_in[h, 0].astype(F32)).astype(LOW)
                copy = push(
                    cross_out.at[h], turn_in.at[h], t_send.at[h], t_recv.at[h], batch=sides[1 - h]
                )
                copy.start()
                t_copies.append(copy)

    def w_push(i):
        target = core * group_count + i
        return push(w_line.at[i], w_parts.at[chip], w_send.at[i], w_recv.at[chip], seq=target)

    def to_owners():
        for copy in w_copies[1::2] if paired else w_copies:
            copy.wait_recv()
        for copy in t_copies:
            copy.wait_recv()
        splits = 2 if paired else 1
        each = group_count // splits
        for h in range(splits):
            if paired:
                own_terms[2 + h].wait()
                value = stage[2 + h].astype(F32) + cross_in[h, 1].astype(F32) + turn_in[h].astype(F32)
            else:
                value = staged(w_piece(batch, 0), *[cross_in.at[0, k] for k in range(1, nb)])
            for i in range(each):
                w_line[h * each + i] = value[:, i * shard : (i + 1) * shard].astype(LOW)
        for i in range(group_count):
            own = core * group_count + i == me

            @pl.when(own)
            def _():
                w_parts[chip] = w_line[i]

            @pl.when(jnp.logical_not(own))
            def _():
                w_push(i).start()

    line_rows = gw.shape[0] // nb
    near_rows = near_in.shape[2]

    def near_piece(owner, h):
        return gw_low.at[owner, pl.ds(h * near_rows, near_rows)]

    b_copies = []

    def begin_slices():
        for b in range(nb):
            gw_low[b] = gw[b * line_rows : (b + 1) * line_rows].astype(LOW)
        if paired:
            for h in range(2):
                for j, owner in enumerate((across, sides[h])):
                    b_copies.append(
                        push(
                            near_piece(owner, h), near_in.at[h, j], b_send.at[h, j], b_recv.at[h, j],
                            batch=sides[h],
                        )
                    )
        else:
            for k in range(1, nb):
                target = lax.rem(batch + k, nb)
                b_copies.append(
                    push(
                        near_piece(target, 0), near_in.at[0, k], b_send.at[0, k], b_recv.at[0, k],
                        batch=target,
                    )
                )
        for copy in b_copies:
            copy.start()

    for tp in range(chips):
        if tp >= 2:
            sib_copy(tp - 2).wait_send()
        step(2 * tp, 0)
        if tp == 1:
            to_owners()
        step(2 * tp + 1, 1)
        if tp == 0:
            turn()
        if tp == chips - 1:
            begin_slices()
        sib_copy(tp).wait_recv()
        gh_own[tp] = (gh_own[tp].astype(F32) + from_sib[tp].astype(F32)).astype(LOW)
        if tp < half_chips:

            @pl.when(jnp.logical_not(is_gate))
            def _():
                gate_copy(tp).start()

        else:

            @pl.when(far_chip_of(tp) != chip)
            def _():
                peer_copy(tp).start()

        if 1 <= tp < half_chips:
            relay(tp - 1)

    relay(half_chips - 1)
    bt_copies = []
    if paired:
        for h in range(2):
            b_copies[2 * h].wait_recv()
            near_out[h] = (
                gw_low[sides[1 - h], pl.ds(h * near_rows, near_rows)].astype(F32)
                + near_in[h, 0].astype(F32)
            ).astype(LOW)
            copy = push(
                near_out.at[h], near_turn.at[h], bt_send.at[h], bt_recv.at[h], batch=sides[1 - h]
            )
            copy.start()
            bt_copies.append(copy)
    z_copies = []

    def z_copy(target):
        return push(
            line_out.at[target], line_in.at[me], z_send.at[target], z_recv.at[me], seq=target
        )

    splits = 2 if paired else 1
    each = n // splits
    for h in range(splits):
        value = gw_low[batch, pl.ds(h * near_rows, near_rows)].astype(F32)
        if paired:
            b_copies[2 * h + 1].wait_recv()
            bt_copies[h].wait_recv()
            value = value + near_in[h, 1].astype(F32) + near_turn[h].astype(F32)
        else:
            for k in range(1, nb):
                b_copies[k - 1].wait_recv()
                value = value + near_in[0, k].astype(F32)
        for i in range(each):
            target = h * each + i
            line_out[target] = value[i * shard : (i + 1) * shard].astype(LOW)

            @pl.when(target != me)
            def _():
                z_copy(target).start()

            @pl.when(target == me)
            def _():
                line_in[me] = line_out[target]

    value = gh_own[half * chip + (1 - half) * (chips - 1 - chip)].astype(F32)
    for j in range(half_chips - 1):
        push(
            gh_own.at[0], peer_in.at[j], peer_send.at[0], peer_recv.at[j], seq=sibling
        ).wait_recv()
        value = value + peer_in[j].astype(F32)
    out[half] = value.astype(LOW)
    push(gh_own.at[0], out.at[1 - half], far_send.at[0], far_recv.at[0], seq=sibling).wait_recv()

    tiles = out.shape[2] // LANES
    gain_sum = None
    for t in range(2):
        load = pltpu.make_async_copy(tok.at[t], h_s, block_sem.at[1])
        load.start()
        load.wait()
        x = h_s[...].astype(F32)
        term = fold_rows(out[t].astype(F32) * (x * rms_factor(x)))
        gain_sum = term if gain_sum is None else gain_sum + term

    def lanes(row):
        return [row[:, k * LANES : (k + 1) * LANES] for k in range(row.shape[1] // LANES)]

    def squeeze(row):
        total = None
        for piece in lanes(row):
            total = piece if total is None else total + piece
        return total

    rows_out = lanes(jnp.sum(gain_sum, axis=0, keepdims=True))
    rows_out += lanes(jnp.sum(sums_ref[0], axis=0, keepdims=True))
    rows_out.append(jnp.sum(scale_sum[...], axis=0, keepdims=True))
    for k in range(1, 4):
        rows_out.append(squeeze(jnp.sum(sums_ref[k], axis=0, keepdims=True)))

    for q in range(chips):

        @pl.when(2 * q + half != me)
        def _():
            push(w_line.at[0], w_parts.at[q], w_send.at[0], w_recv.at[q], seq=sibling).wait_recv()

    value = w_parts[0].astype(F32)
    for q in range(1, chips):
        value = value + w_parts[q].astype(F32)
    own_w[...] = value

    for k in range(1, n):
        source = lax.rem(me + k, n)
        push(
            line_out.at[source], line_in.at[source], z_send.at[source], z_recv.at[source], seq=source
        ).wait()
    for g in range(group_count):
        own_gw[g] = line_in[g].astype(F32) + line_in[g + group_count].astype(F32)

    squares = None
    for value in [own_gw[g] for g in range(group_count)] + [own_w[m] for m in range(3)]:
        term = squeeze(jnp.sum(value * value, axis=0, keepdims=True))
        squares = term if squares is None else squares + term
    rows_out.append(squares)
    sum_mine[0] = jnp.zeros_like(sum_mine[0])
    for k, row in enumerate(rows_out):
        sum_mine[0, k : k + 1, :] = row
    s_copies = []
    for k in range(1, n):
        copy = push(
            sum_mine.at[0], sum_line.at[k], s_send.at[k], s_recv.at[k], seq=lax.rem(me + k, n)
        )
        copy.start()
        s_copies.append(copy)
    sum_line[0] = sum_mine[0]
    for copy in s_copies:
        copy.wait_recv()
    value = jnp.zeros_like(sum_mine[0])
    for k in range(n):
        value = value + sum_line[lax.rem(me - k + n, n)]
    sum_mine[1] = value
    for k in range(1, nb):
        copy = push(
            sum_mine.at[1], sum_batch.at[k], u_send.at[k], u_recv.at[k],
            batch=lax.rem(batch + k, nb),
        )
        copy.start()
        s_copies.append(copy)
    sum_batch[0] = value
    for copy in s_copies[n - 1 :]:
        copy.wait_recv()
    value = jnp.zeros_like(value)
    for k in range(nb):
        value = value + sum_batch[lax.rem(batch - k + nb, nb)]
    sums_out[...] = value

    for i in range(group_count):

        @pl.when(core * group_count + i != me)
        def _():
            w_push(i).wait_send()

    for tp in range(max(chips - 2, 0), chips):
        sib_copy(tp).wait_send()
    for copy in w_copies + t_copies + b_copies + bt_copies + s_copies:
        copy.wait_send()
    for tp in range(chips):
        if tp < half_chips:

            @pl.when(is_gate)
            def _():
                far_copy(tp).wait_send()

            @pl.when(jnp.logical_not(is_gate))
            def _():
                gate_copy(tp).wait_send()

        else:

            @pl.when(far_chip_of(tp) != chip)
            def _():
                peer_copy(tp).wait_send()


def attend_back(
    n, nb, heads, size, fold, coef, qkv, go, keep, lse, q_full, h, wqkv, w_half, tokens,
    layer_sums, shard,
):
    _, rows, width = h.shape
    chips, half_chips = n // 2, n // 4
    paired = nb == 4
    split = 2 if paired else 1
    steps = 2 if paired else nb
    w_rows = w_half.shape[2] // split
    line_rows = width // nb
    slab = wqkv.shape[1]
    dma = pltpu.SemaphoreType.DMA
    vmem = pl.BlockSpec(memory_space=pltpu.VMEM)
    anywhere = pl.BlockSpec(memory_space=pl.ANY)
    one = (n, heads, rows, LANES)
    peers = max(half_chips - 1, 1)
    near = (line_rows // split, slab)
    landing = ((split, steps, 3, w_rows, width), (split, 3, w_rows, width))
    small_rows = (2 * (width // LANES) + 5 + 7) // 8 * 8
    result = pl.pallas_call(
        functools.partial(back_kernel, n, nb, heads, size, fold),
        out_shape=(
            jax.ShapeDtypeStruct((2, rows, width), LOW),
            jax.ShapeDtypeStruct((n // 2, shard, slab), F32),
            jax.ShapeDtypeStruct((3, shard, width), F32),
            jax.ShapeDtypeStruct((small_rows, LANES), F32),
        )
        + (() if paired else tuple(jax.ShapeDtypeStruct(shape, LOW) for shape in landing)),
        in_specs=[vmem, anywhere, vmem, anywhere, vmem]
        + [anywhere] * 5
        + [vmem],
        out_specs=[vmem] * 4 + ([] if paired else [anywhere] * 2),
        scratch_shapes=([pltpu.VMEM(shape, LOW) for shape in landing] if paired else [])
        + [
            pltpu.VMEM(qkv.shape, LOW),
            pltpu.VMEM((n, heads, LANES, rows), LOW),
            pltpu.VMEM(one, LOW),
            pltpu.VMEM((n, heads, 8, rows), F32),
            pltpu.VMEM((n, heads, LANES, rows), F32),
            pltpu.VMEM(one, F32),
            pltpu.VMEM(one, F32),
            pltpu.VMEM((heads, rows, LANES), F32),
            pltpu.VMEM((rows, width), LOW),
            pltpu.VMEM(wqkv.shape, LOW),
            pltpu.VMEM(wqkv.shape, F32),
            pltpu.VMEM((chips, rows, width), LOW),
            pltpu.VMEM((2, rows, width), LOW),
            pltpu.VMEM((chips, rows, width), LOW),
            pltpu.VMEM((peers, half_chips, rows, width), LOW),
            pltpu.VMEM((peers, rows, width), LOW),
            pltpu.VMEM((4 if paired else 3, 3, w_rows, width), LOW),
            pltpu.VMEM((split, 3, w_rows, width), LOW),
            pltpu.VMEM((n // 2, 3, shard, width), LOW),
            pltpu.VMEM((chips, 3, shard, width), LOW),
            pltpu.VMEM((nb, line_rows, slab), LOW),
            pltpu.VMEM((split, steps) + near, LOW),
            pltpu.VMEM((split,) + near, LOW),
            pltpu.VMEM((split,) + near, LOW),
            pltpu.VMEM((n, shard, slab), LOW),
            pltpu.VMEM((n, shard, slab), LOW),
            dma((3,)),
            dma((2,)),
            dma((chips,)),
            dma((chips,)),
            dma((half_chips,)),
            dma((peers, half_chips)),
            dma((chips,)),
            dma((peers,)),
            dma((half_chips,)),
            dma((1,)),
            dma((split, steps)),
            dma((split, steps)),
            dma((split,)),
            dma((split,)),
            dma((n // 2,)),
            dma((chips,)),
            dma((split, steps)),
            dma((split, steps)),
            dma((split,)),
            dma((split,)),
            dma((n,)),
            dma((n,)),
            dma((4,)),
            pltpu.VMEM((8, LANES), F32),
            pltpu.VMEM((2, small_rows, LANES), F32),
            pltpu.VMEM((n, small_rows, LANES), F32),
            pltpu.VMEM((nb, small_rows, LANES), F32),
            dma((n,)),
            dma((n,)),
            dma((nb,)),
            dma((nb,)),
        ],
        compiler_params=pltpu.CompilerParams(
            collective_id=4, has_side_effects=True, vmem_limit_bytes=63 * MIB
        ),
        name="attend_back",
    )(coef, qkv, go, keep, lse, q_full, h, wqkv, w_half, tokens, layer_sums)
    return result[:4]


def update_kernel(
    group_count, group_width, count, sums, gw, gw3, gain_ref, scale, first_s, second_s, gains, first_g,
    second_g, tok_in, gy_in, gh_in, w_in, m_in, s_in, norm_out, scale_out, first_s_out, second_s_out,
    gains_out, first_g_out, second_g_out, rms_out, grad_out, w_out, m_out, s_out,
    tok, gy, gh, w, m, v, sems,
):
    pairs = [(tok_in, tok), (gh_in, gh), (gy_in, gy), (w_in, w), (m_in, m), (s_in, v)]
    loads = [pltpu.make_async_copy(a, b, sems.at[k]) for k, (a, b) in enumerate(pairs)]
    for load in loads:
        load.start()
    width = tok.shape[2]
    tiles = width // LANES
    size = scale.shape[1]
    shard = gains.shape[1]
    gain_sums = [
        jnp.concatenate([sums[k * tiles + j : k * tiles + j + 1] for j in range(tiles)], axis=1)
        for k in range(2)
    ]
    slope = LOG_TWO_E / math.sqrt(size) / (1.0 + jnp.exp(-scale[...]))
    scale_grad = sums[2 * tiles : 2 * tiles + 1, :size] * slope

    def add_up(row):
        return jnp.sum(row, axis=1, keepdims=True)

    stats = [add_up(sums[2 * tiles + 1 + k : 2 * tiles + 2 + k]) for k in range(4)]
    for k in range(3):
        rms_out[:, k : k + 1] = jnp.sqrt(stats[k] / count)
    norm = jnp.sqrt(
        stats[3]
        + add_up(gain_sums[0] * gain_sums[0])
        + add_up(gain_sums[1] * gain_sums[1])
        + add_up(scale_grad * scale_grad)
    )
    norm_out[...] = norm
    clip = CLIP_NORM / jnp.maximum(norm, CLIP_NORM)

    def adam(outs, current, gradient, one, two, rate, decay):
        for out, value in zip(outs, adam_update(current, gradient * clip, one, two, rate, decay)):
            out[...] = value

    adam(
        (scale_out, first_s_out, second_s_out), scale[...], scale_grad, first_s[...], second_s[...],
        GAIN_RATE, 0.0,
    )
    index = lax.axis_index("batch") * lax.axis_size("seq") + lax.axis_index("seq")
    own = jnp.concatenate(gain_sums + [jnp.zeros((6, width), F32)], axis=0)
    own = pltpu.roll(own, lax.rem(width - index * shard, width), 1)[:2, :shard]
    adam(
        (gains_out, first_g_out, second_g_out), gains[...], own, first_g[...], second_g[...],
        GAIN_RATE, 0.0,
    )

    for load in loads[:3]:
        load.wait()
    for t in range(2):
        x = tok[t].astype(F32)
        factor = rms_factor(x)
        grad = gh[t].astype(F32) * gain_ref[:1]
        gy[t] = gy[t] + norm_back(grad, x * factor, factor)
    stores = [pltpu.make_async_copy(gy, grad_out, sems.at[0])]
    stores[0].start()
    for load in loads[3:]:
        load.wait()
    for k in range(6):
        if k < 3:
            span = slice(k * group_width, (k + 1) * group_width)
            gradient = jnp.concatenate([gw[g][:, span] for g in range(group_count)], axis=1)
        else:
            gradient = gw3[k - 3]
        w[k], m[k], v[k] = adam_update(w[k], gradient * clip, m[k], v[k], MATRIX_RATE, MATRIX_DECAY)
        for j, (a, b) in enumerate(((w, w_out), (m, m_out), (v, s_out))):
            copy = pltpu.make_async_copy(a.at[k], b.at[k], sems.at[6 + 3 * k + j])
            copy.start()
            stores.append(copy)
    for copy in stores:
        copy.wait()


def update(
    group_count, group_width, count, sums, gw, gw3, gain, scale, first_s, second_s, gains, first_g,
    second_g, tokens, gy, gh, weights, first_w, second_w,
):
    vmem = pl.BlockSpec(memory_space=pltpu.VMEM)
    anywhere = pl.BlockSpec(memory_space=pl.ANY)

    def like(value):
        return jax.ShapeDtypeStruct(value.shape, F32)

    kept = pltpu.VMEM(weights.shape, F32)
    return pl.pallas_call(
        functools.partial(update_kernel, group_count, group_width, count),
        out_shape=(
            jax.ShapeDtypeStruct((1, 1), F32), like(scale), like(scale), like(scale), like(gains),
            like(gains), like(gains), jax.ShapeDtypeStruct((1, 3), F32), like(gy), like(weights),
            like(weights), like(weights),
        ),
        in_specs=[vmem] * 10 + [anywhere] * 6,
        out_specs=[vmem] * 8 + [anywhere] * 4,
        scratch_shapes=[
            pltpu.VMEM(tokens.shape, LOW),
            pltpu.VMEM(gy.shape, F32),
            pltpu.VMEM(gh.shape, LOW),
            kept,
            kept,
            kept,
            pltpu.SemaphoreType.DMA((24,)),
        ],
        compiler_params=pltpu.CompilerParams(vmem_limit_bytes=62 * MIB),
        name="update",
    )(
        sums, gw, gw3, gain, scale, first_s, second_s, gains, first_g, second_g, tokens, gy, gh,
        weights, first_w, second_w,
    )


def body(
    n,
    nb,
    tokens,
    cotangent,
    weights,
    gains,
    query_scale,
    first_weights,
    second_weights,
    first_gains,
    second_gains,
    first_scale,
    second_scale,
    lengths,
):
    series_count, rows, width = tokens.shape
    size = query_scale.shape[0]
    group_count = n // 2
    heads = width // size // group_count
    group_width = heads * size
    fold = 640 // group_width
    shard = weights.shape[1]
    slab_width = (3 * group_width + 2 + LANES - 1) // LANES * LANES
    (
        normed_in, qkv, q_full, o_keep, lse, o_recv, w_all, wqkv, gain_rows, coef_row,
    ) = front(n, nb, heads, size, fold, lengths, query_scale[None], gains, tokens, weights)
    if w_all.ndim == 5:
        w_all = w_all.transpose(2, 0, 1, 3, 4).reshape(3, width, width)
    block_out, grad_middle, go_recv, layer_sums, w_half = layer(
        n, nb, fold, tokens, cotangent, o_recv, w_all, gain_rows
    )
    grad_normed, own_slab, own_three, sums = attend_back(
        n, nb, heads, size, fold, coef_row, qkv, go_recv, o_keep, lse, q_full, normed_in,
        wqkv, w_half, tokens, layer_sums, shard,
    )
    count = float(series_count * rows * width * nb * n)
    (
        grad_norm, new_scale, new_first_scale, new_second_scale, new_gains, new_first_gains,
        new_second_gains, rms_stats, input_grad, new_weights, new_first_weights, new_second_weights,
    ) = update(
        group_count, group_width, count, sums, own_slab, own_three, gain_rows, query_scale[None],
        first_scale[None], second_scale[None], gains, first_gains, second_gains, tokens, grad_middle,
        grad_normed, weights, first_weights, second_weights,
    )
    grad_norm = grad_norm.reshape(())
    new_scale, new_first_scale, new_second_scale = (
        new_scale.reshape(size), new_first_scale.reshape(size), new_second_scale.reshape(size)
    )
    rms_stats = rms_stats.reshape(3)
    return (
        block_out,
        input_grad,
        grad_norm,
        new_weights,
        new_first_weights,
        new_second_weights,
        new_gains,
        new_first_gains,
        new_second_gains,
        new_scale,
        new_first_scale,
        new_second_scale,
        rms_stats,
    )


def solution(mesh):
    return jax.shard_map(
        functools.partial(body, mesh.shape["seq"], mesh.shape["batch"]),
        mesh=mesh,
        in_specs=(
            P("batch", "seq", None),
            P("batch", "seq", None),
            P(None, ("batch", "seq"), None),
            P(None, ("batch", "seq")),
            P(),
            P(None, ("batch", "seq"), None),
            P(None, ("batch", "seq"), None),
            P(None, ("batch", "seq")),
            P(None, ("batch", "seq")),
            P(),
            P(),
            P("batch"),
        ),
        out_specs=(
            P("batch", "seq", None),
            P("batch", "seq", None),
            P(),
            P(None, ("batch", "seq"), None),
            P(None, ("batch", "seq"), None),
            P(None, ("batch", "seq"), None),
            P(None, ("batch", "seq")),
            P(None, ("batch", "seq")),
            P(None, ("batch", "seq")),
            P(),
            P(),
            P(),
            P(),
        ),
        check_vma=False,
    )
```
